32 devices in a mesh: dp: 8 (over y, x, core), zero: 4 (over z).
Axes of the slice: x: 2, y: 2, z: 4, core: 2. Of those that a mesh axis runs over, the one named last changes fastest.
Arguments:
- images: bfloat16 [256, 196, 512], P(('dp', 'zero')), may hold values from -6 to 6
- cotangent: bfloat16 [256, 196, 512], P(('dp', 'zero')), may hold values from -6 to 6
- counts: int32 [32], P(('dp', 'zero')), may hold values from 1 to 8, 160 in all
- rel_index: int32 [49, 49], replicated, may hold values from 0 to 168
- regions: int32 [196], replicated, may hold values from 0 to 2
- mat_w: float32 [2, 512, 6144], P(None, 'zero'), may hold values from -6 to 6
- mat_m: float32 [2, 512, 6144], P(None, 'zero'), may hold values from -112 to 112
- mat_v: float32 [2, 512, 6144], P(None, 'zero'), may hold values from 15.68 to 62.72
- vec_w: float32 [2, 12, 512], P(None, None, 'zero'), may hold values from -1.2 to 1.6
- vec_m: float32 [2, 12, 512], P(None, None, 'zero'), may hold values from -224 to 224
- vec_v: float32 [2, 12, 512], P(None, None, 'zero'), may hold values from 62.72 to 250.88
- tab_w: float32 [2, 16, 169], P(None, 'zero'), may hold values from -3 to 3
- tab_m: float32 [2, 16, 169], P(None, 'zero'), may hold values from -40 to 40
- tab_v: float32 [2, 16, 169], P(None, 'zero'), may hold values from 3.2 to 12.8
Outputs:
- activations: bfloat16 [256, 196, 512], P(('dp', 'zero'))
- grad_images: float32 [256, 196, 512], P(('dp', 'zero'))
- new_mat_w: float32 [2, 512, 6144], P(None, 'zero')
- new_mat_m: float32 [2, 512, 6144], P(None, 'zero')
- new_mat_v: float32 [2, 512, 6144], P(None, 'zero')
- new_vec_w: float32 [2, 12, 512], P(None, None, 'zero')
- new_vec_m: float32 [2, 12, 512], P(None, None, 'zero')
- new_vec_v: float32 [2, 12, 512], P(None, None, 'zero')
- new_tab_w: float32 [2, 16, 169], P(None, 'zero')
- new_tab_m: float32 [2, 16, 169], P(None, 'zero')
- new_tab_v: float32 [2, 16, 169], P(None, 'zero')
The draws below stay inside these ranges and needn't reach their ends.
Inputs may be any that keep to these rules, and one draw needn't show every extreme that they name: Device d holds its live images in its slots 0 to counts[d] - 1; the other slots are ignored. The counts sum to 160.
All inputs are finite; a program needn't handle non-finite values.
Results may differ from the reference program's by a relative error of at most 0.025.
Values may be sent and summed in bfloat16 or wider, within the bound.
No kernel may reach another device: no remote copies, remote signals or barrier semaphores. Data moves between devices by JAX's collectives and lax.ppermute only.
A program may use at most 384 MiB of HBM per device.

```python
import math
import jax
import jax.numpy as jnp
import numpy as np
from jax import lax

C = 512
HEADS = 16
HIDDEN_SIZE = 2048
WIN = 7
SIDE = 14
LAYERS = 2
STEP = 10
SLOTS = 8
NREL = 169
COLS = 6144
VROWS = 12
BUFFER = 256
IMAGES = 160
N_DP = 8
N_ZERO = 4


def draw_mat_w(key, part):
    key = jax.random.fold_in(key, 11)
    columns = 4 * C + 2 * HIDDEN_SIZE
    column = jnp.arange(columns)
    fan_in = jnp.where(column < 3 * C, C, jnp.where(column < 4 * C, C // 7, jnp.where(column < 4 * C + HIDDEN_SIZE, C, HIDDEN_SIZE)))
    base = jnp.clip(jax.random.normal(key, (LAYERS, C, columns), jnp.float32), -6.0, 6.0)
    return base * lax.rsqrt(fan_in.astype(jnp.float32))


def draw_vec_w(key, part):
    key = jax.random.fold_in(key, 12)
    row_count = 8 + HIDDEN_SIZE // C
    base = jnp.clip(jax.random.normal(key, (LAYERS, row_count, C), jnp.float32), -6.0, 6.0)
    row_id = jnp.arange(row_count)[None, :, None]
    gain_rows = (row_id == 0) | (row_id == 5)
    return jnp.where(gain_rows, 1.0 + 0.1 * base, 0.2 * base)


def plant(values, stream_key, low, largest):
    place = [jax.random.randint(jax.random.fold_in(stream_key, axis), (), 0, length) for axis, length in enumerate(values.shape)]
    longest = values.shape.index(max(values.shape))
    next_to = place[:longest] + [(place[longest] + 1) % values.shape[longest]] + place[longest + 1:]
    return values.at[tuple(place)].set(low).at[tuple(next_to)].set(largest)


def levels(rng, shape, split, least, largest):
    def one(axis_at, shards_of):
        heights = jax.random.uniform(jax.random.fold_in(jax.random.fold_in(rng, 6), axis_at), (shards_of,), jnp.float32, least / len(split), largest / len(split))
        return jnp.repeat(jnp.exp(heights), shape[axis_at] // shards_of).reshape((-1,) + (1,) * (len(shape) - axis_at - 1))

    loudness = one(*split[0])
    for cut in split[1:]:
        loudness = loudness * one(*cut)
    return loudness


def split_up(number_of, total, most, slope):
    weights = [(1 << 20) // math.isqrt(rank ** slope) + 1 for rank in range(2, number_of + 1)]
    surplus, given = total - most - (number_of - 1), [1] * (number_of - 1)
    while surplus > 0:
        movable = [i for i in range(number_of - 1) if given[i] < most]
        whole, left = sum([weights[i] for i in movable]), surplus
        for i in movable:
            extra = min(most - given[i], max(1, left * weights[i] // whole), surplus)
            given[i] = given[i] + extra
            surplus = surplus - extra
    return np.array([most] + given)


def uneven(stream_key, count, total, bound, lean):
    if count == 2:
        one = jax.random.randint(stream_key, (), max(1, total - bound), min(bound, total - 1) + 1)
        return jnp.stack([one, total - one])
    tallies = jnp.asarray(split_up(count, total, bound, lean), jnp.int32)
    twos = (count - 1) // 2
    source_of, receiver = tallies[1:1 + 2 * twos:2], tallies[2:2 + 2 * twos:2]
    margin = jnp.minimum(source_of - 1, bound - receiver)
    moved = jax.random.randint(jax.random.fold_in(stream_key, 1), (twos,), 0, 1 << 20) % (margin + 1)
    tallies = tallies.at[1:1 + 2 * twos:2].set(source_of - moved).at[2:2 + 2 * twos:2].set(receiver + moved)
    return tallies[jax.random.permutation(jax.random.fold_in(stream_key, 2), count)]


def noise(rng, extent, scale, limit, split=(), held_as=jnp.bfloat16):
    level = levels(rng, extent, split, -0.22, 0.18) if split else 1.0
    values = jax.random.normal(rng, extent, jnp.float32) * scale * level
    return jnp.minimum(jnp.maximum(values, -limit), limit).astype(held_as)


def setup_inputs(seed: int = 0) -> dict:
    key_of = jax.random.split(jax.random.key(seed), 15)
    return {
        "images": noise(key_of[0], (BUFFER, SIDE * SIDE, C), 1.0, 6.0, ((0, 32),)),
        "cotangent": noise(key_of[1], (BUFFER, SIDE * SIDE, C), 1.0, 6.0, ((0, 32),)),
        "counts": uneven(key_of[2], N_DP * N_ZERO, IMAGES, SLOTS, 2).astype(jnp.int32),
        "rel_index": plant(jax.random.randint(key_of[3], (WIN * WIN, WIN * WIN), 0, NREL), jax.random.fold_in(key_of[3], 1), 0, NREL - 1).astype(jnp.int32),
        "regions": plant(jax.random.randint(key_of[4], (SIDE * SIDE,), 0, 3), jax.random.fold_in(key_of[4], 1), 0, 2).astype(jnp.int32),
        "mat_w": draw_mat_w(jax.random.fold_in(key_of[14], 71), 0),
        "mat_m": noise(key_of[6], (LAYERS, C, COLS), (0.1 * (SIDE * SIDE * IMAGES) ** 0.5), 112.0, ((1, 4),), jnp.float32),
        "mat_v": jnp.clip(jnp.exp(math.log(62.72) - 1.3862944 * jax.random.uniform(key_of[7], (LAYERS, C, COLS), jnp.float32) ** levels(key_of[7], (LAYERS, C, COLS), ((1, 4),), -0.2, 0.2)), 15.68, 62.72),
        "vec_w": draw_vec_w(jax.random.fold_in(key_of[14], 71), 0),
        "vec_m": noise(key_of[9], (LAYERS, VROWS, C), (0.2 * (SIDE * SIDE * IMAGES) ** 0.5), 224.0, ((2, 4),), jnp.float32),
        "vec_v": jnp.clip(jnp.exp(math.log(250.88) - 1.3862944 * jax.random.uniform(key_of[10], (LAYERS, VROWS, C), jnp.float32) ** levels(key_of[10], (LAYERS, VROWS, C), ((2, 4),), -0.2, 0.2)), 62.72, 250.88),
        "tab_w": noise(key_of[11], (LAYERS, HEADS, NREL), 0.5, 3.0, ((1, 4),), jnp.float32),
        "tab_m": noise(key_of[12], (LAYERS, HEADS, NREL), (0.5 * IMAGES ** 0.5), 40.0, ((1, 4),), jnp.float32),
        "tab_v": jnp.clip(jnp.exp(math.log(12.8) - 1.3862944 * jax.random.uniform(key_of[13], (LAYERS, HEADS, NREL), jnp.float32) ** levels(key_of[13], (LAYERS, HEADS, NREL), ((1, 4),), -0.2, 0.2)), 3.2, 12.8),
    }


@jax.custom_vjp
def low(v):
    return lax.optimization_barrier(v.astype(jnp.bfloat16)).astype(jnp.float32)

@jax.custom_vjp
def low_back(v):
    return v

def low_keep(v):
    return (low(v), None)

def low_pass(kept, grad):
    return (grad,)

def back_keep(v):
    return (v, None)

def back_low(kept, grad):
    return (low(grad),)
low.defvjp(low_keep, low_pass)
low_back.defvjp(back_keep, back_low)
norm_eps = 1e-05
mask_value = -100.0
beta_one = 0.9
beta_two = 0.999
adam_eps = 1e-08
weight_decay = 0.05
rate_matrix = 0.1
rate_vector = 0.5
rate_table = 1.0
highest = lax.Precision.HIGHEST

def to_windows(values_in, shifted):
    channels = values_in.shape[-1]
    images_here = values_in.shape[0] // (SIDE * SIDE)
    lattice = values_in.reshape(images_here, SIDE, SIDE, channels)
    if shifted:
        lattice = jnp.roll(lattice, (-(WIN // 2), -(WIN // 2)), (1, 2))
    lattice = lattice.reshape(images_here, SIDE // WIN, WIN, SIDE // WIN, WIN, channels)
    return lattice.transpose(0, 1, 3, 2, 4, 5).reshape(-1, WIN * WIN, channels)

def from_windows(values_in, shifted):
    channels = values_in.shape[-1]
    images_here = values_in.shape[0] // (SIDE // WIN * (SIDE // WIN))
    lattice = values_in.reshape(images_here, SIDE // WIN, SIDE // WIN, WIN, WIN, channels)
    lattice = lattice.transpose(0, 1, 3, 2, 4, 5).reshape(images_here, SIDE, SIDE, channels)
    if shifted:
        lattice = jnp.roll(lattice, (WIN // 2, WIN // 2), (1, 2))
    return lattice.reshape(images_here * SIDE * SIDE, channels)

def normalize(stream, gain_row, offset):
    centred = stream - lax.optimization_barrier(jnp.mean(stream, -1, keepdims=True))
    spread = lax.rsqrt(lax.optimization_barrier(jnp.mean(centred * centred, -1, keepdims=True)) + norm_eps)
    return centred * spread * gain_row + offset

def block(stream, matrix, vector, table, rel_index, mask_add, shifted):
    channels = stream.shape[-1]
    head_count = table.shape[0]
    head_size = channels // head_count
    hidden_units = (matrix.shape[1] - 4 * channels) // 2
    matrix = low(matrix)
    vector = low(vector)
    table = low(table)
    normed = low(normalize(stream, vector[0], vector[1]))
    qkv_bias = jnp.concatenate([vector[2], jnp.zeros_like(vector[2]), vector[3]])
    packed = low(low_back(jnp.dot(normed, matrix[:, :3 * channels], precision=highest) + qkv_bias))
    framed = to_windows(packed, shifted).reshape(-1, WIN * WIN, 3, head_count, head_size)
    queries = framed[:, :, 0]
    keys_win = framed[:, :, 1]
    values_win = framed[:, :, 2]
    bias_full = table[:, rel_index]
    scores = jnp.einsum('wihd,wjhd->whij', queries, keys_win, precision=highest) * head_size ** (-0.5) + bias_full[None]
    if shifted:
        windows_each = mask_add.shape[0]
        shape_now = scores.shape
        scores = (scores.reshape(-1, windows_each, head_count, WIN * WIN, WIN * WIN) + mask_add[None, :, None]).reshape(shape_now)
    scores = low_back(scores)
    weights_soft = low(jax.nn.softmax(scores, axis=-1))
    attended = jnp.einsum('whij,wjhd->wihd', weights_soft, values_win, precision=highest)
    attended = low(low_back(attended))
    merged = from_windows(attended.reshape(-1, WIN * WIN, channels), shifted)
    middle = stream + low_back(jnp.dot(merged, matrix[:, 3 * channels:4 * channels], precision=highest) + vector[4])
    normed_two = low(normalize(middle, vector[5], vector[6]))
    inner = low_back(jnp.dot(normed_two, matrix[:, 4 * channels:4 * channels + hidden_units], precision=highest) + vector[8:].reshape(-1))
    activated = low(jax.nn.gelu(inner, approximate=False))
    return middle + low_back(jnp.dot(activated, matrix[:, 4 * channels + hidden_units:].T, precision=highest) + vector[7])

def adam_step(weight, first, second, gradient, rate, decay):
    first_new = beta_one * first + (1.0 - beta_one) * gradient
    second_new = beta_two * second + (1.0 - beta_two) * gradient * gradient
    first_hat = first_new / (1.0 - beta_one ** STEP)
    second_hat = second_new / (1.0 - beta_two ** STEP)
    weight_new = weight - rate * (first_hat / (jnp.sqrt(second_hat) + adam_eps) + decay * weight)
    return (weight_new, first_new, second_new)

def reference(images, cotangent, counts, rel_index, regions, mat_w, mat_m, mat_v, vec_w, vec_m, vec_v, tab_w, tab_m, tab_v):
    device_count = counts.shape[0]
    channels = images.shape[-1]
    live_mask = (jnp.arange(SLOTS)[None, :] < counts[:, None]).astype(jnp.float32)
    pictures = images.astype(jnp.float32).reshape(device_count, SLOTS * SIDE * SIDE, channels)
    cotangents = cotangent.astype(jnp.float32).reshape(device_count, SLOTS, SIDE * SIDE, channels) * live_mask[:, :, None, None]
    cotangents = cotangents.reshape(device_count, SLOTS * SIDE * SIDE, channels)
    zones = to_windows(regions.reshape(SIDE * SIDE, 1), False)[:, :, 0]
    mask_add = jnp.where(zones[:, :, None] == zones[:, None, :], 0.0, mask_value).astype(jnp.float32)

    def forward(params, stream):
        matrices, vectors, tables = params
        for layer_num in range(LAYERS):
            stream = block(stream, matrices[layer_num], vectors[layer_num], tables[layer_num], rel_index, mask_add, layer_num % 2 == 1)
        return stream

    def visit(totals, item):
        stream, grad_out = item
        result, pull = jax.vjp(forward, (mat_w, vec_w, tab_w), stream)
        grads, grad_in = pull(grad_out)
        totals = jax.tree.map(jnp.add, totals, grads)
        return (totals, (result, grad_in))
    starting = jax.tree.map(jnp.zeros_like, (mat_w, vec_w, tab_w))
    totals, (results, grads_in) = lax.scan(visit, starting, (pictures, cotangents))
    activations = (results.reshape(device_count, SLOTS, SIDE * SIDE, channels) * live_mask[:, :, None, None]).astype(jnp.bfloat16).reshape(images.shape)
    grad_images = grads_in.reshape(images.shape)
    new_mat = adam_step(mat_w, mat_m, mat_v, totals[0], rate_matrix, weight_decay)
    new_vec = adam_step(vec_w, vec_m, vec_v, totals[1], rate_vector, 0.0)
    new_tab = adam_step(tab_w, tab_m, tab_v, totals[2], rate_table, 0.0)
    return (activations, grad_images, new_mat[0], new_mat[1], new_mat[2], new_vec[0], new_vec[1], new_vec[2], new_tab[0], new_tab[1], new_tab[2])
```

```python
from functools import partial

import jax
import jax.numpy as jnp
import numpy as np
from jax import lax
from jax.experimental import pallas as pl
from jax.experimental.pallas import tpu as pltpu
from jax.sharding import PartitionSpec as P

WIN = 7
SIDE = 14
STEP = 10
NREL = 169
C = 512
HID = 2048
TOKENS = SIDE * SIDE
ROWS = 208
FRAME = 256
CELL = 64
QUAD = 4
BLOCK = 256
EXTRA = 32
SMALL = 16

norm_eps = 1e-05
mask_value = -100.0
beta_one = 0.9
beta_two = 0.999
adam_eps = 1e-08
weight_decay = 0.05
rate_matrix = 0.1
rate_vector = 0.5
rate_table = 1.0
scale = 32 ** (-0.5)

bf16 = jnp.bfloat16
f32 = jnp.float32
NN = (((1,), (0,)), ((), ()))
NT = (((1,), (1,)), ((), ()))
TN = (((0,), (0,)), ((), ()))


def mm(left, right, dims=NN):
    return lax.dot_general(left, right, dims, preferred_element_type=f32)


def frames(shifted):
    move = WIN // 2 if shifted else 0
    placed = np.zeros((FRAME, ROWS), np.float32)
    for wy in range(2):
        for wx in range(2):
            for iy in range(WIN):
                for ix in range(WIN):
                    y = (wy * WIN + iy + move) % SIDE
                    x = (wx * WIN + ix + move) % SIDE
                    placed[(wy * 2 + wx) * CELL + iy * WIN + ix, y * SIDE + x] = 1
    return placed


def head_rows():
    rows = np.zeros((QUAD * CELL, 128), np.float32)
    for h in range(QUAD):
        rows[h * CELL : (h + 1) * CELL, h * 32 : (h + 1) * 32] = 1
    return rows


def head_spread(rows):
    out = np.zeros((rows, QUAD * CELL), np.float32)
    for h in range(QUAD):
        out[h, h * CELL : (h + 1) * CELL] = 1
    return out


def norm(rows):
    centred = rows - jnp.mean(rows, -1, keepdims=True)
    spread = lax.rsqrt(jnp.mean(centred * centred, -1, keepdims=True) + norm_eps)
    return centred * spread, spread


def norm_back(grad_unit, unit, spread):
    return spread * (
        grad_unit
        - jnp.mean(grad_unit, -1, keepdims=True)
        - unit * jnp.mean(grad_unit * unit, -1, keepdims=True)
    )


def column_sum(rows):
    return jnp.sum(rows, 0, keepdims=True)


def gelu_pair(u):
    size = jnp.abs(u)
    below = 1.0 + (0.3275911 * 0.5**0.5) * size
    t = pl.reciprocal(below, approx=True)
    t = t * (2.0 - below * t)
    bell = jnp.exp2(u * u * (-0.5 * 1.4426950408889634))
    poly = t * (
        0.127414796 + t * (-0.142248368 + t * (0.710706871 + t * (-0.726576013 + t * 0.530702714)))
    )
    tail = poly * bell
    phi = jnp.where(u >= 0, 1.0 - tail, tail)
    return u * phi, phi + u * bell * 0.3989422804014327


def quad_rows(part, heads):
    return jnp.concatenate([part] * QUAD, 0) * heads


def pick_heads(stacked, lane_head):
    low = jnp.where(lane_head == 0, stacked[:CELL], stacked[CELL : 2 * CELL])
    high = jnp.where(lane_head == 2, stacked[2 * CELL : 3 * CELL], stacked[3 * CELL :])
    return jnp.where(lane_head < 2, low, high)


def lane_heads():
    return lax.broadcasted_iota(jnp.int32, (CELL, 128), 1) // 32


def whole(shape):
    zero = (0,) * len(shape)
    return pl.BlockSpec(shape, lambda *_: zero, pipeline_mode=pl.Buffered(1))


def per_image(rows, cols):
    return pl.BlockSpec((1, rows, cols), lambda i, *_: (i, 0, 0))


def call(body, name, grid, ins, outs, out_shapes, scratch, flops, moved, prefetch=0, aliases=None):
    return pl.pallas_call(
        body,
        name=name,
        grid_spec=pltpu.PrefetchScalarGridSpec(
            num_scalar_prefetch=prefetch,
            grid=grid,
            in_specs=ins,
            out_specs=outs,
            scratch_shapes=scratch,
        ),
        out_shape=out_shapes,
        input_output_aliases=aliases or {},
        compiler_params=pltpu.CompilerParams(
            dimension_semantics=("arbitrary",) * len(grid), vmem_limit_bytes=58 * 1024 * 1024
        ),
        cost_estimate=pl.CostEstimate(flops=flops, bytes_accessed=moved, transcendentals=0),
    )


def shape(dims, kind):
    return jax.ShapeDtypeStruct(dims, kind)


def pack_body(place, mat, rel, tab, vec, spread, out, spread_tab, small):
    rows = mat.shape[1]
    out[0:rows, :] = mat[0].astype(bf16)
    for layer in range(2):
        spread_tab[layer, 0:NREL, :] = mm(tab[layer].astype(bf16), spread[...], TN)
    pairs = rel[...]

    def step(r, sums):
        hit = pairs == r
        return tuple(
            jnp.where(hit, spread_tab[layer, pl.ds(r, 1), :], sums[layer]) for layer in range(2)
        )

    start = jnp.zeros((8, QUAD * CELL), f32)
    first, second = lax.fori_loop(0, NREL, step, (start, start))
    out[rows : rows + 16, :] = jnp.concatenate([first, second], 0).astype(bf16)
    small[...] = jnp.zeros_like(small)
    row = jnp.minimum(place[0] * 2, 10)
    for layer in range(2):
        for k in range(2):
            small[k : k + 1, layer * 128 : (layer + 1) * 128] = vec[layer, pl.ds(row + k, 1), :]
    out[rows + 16 : rows + 32, :] = small[...].astype(bf16)


def pack(place, rows, mat_w, rel, tab_w, vec_w):
    return call(
        pack_body,
        "pack",
        (1,),
        [
            pl.BlockSpec((1, rows, BLOCK), lambda i, place: (0, place[1], place[0])),
            pl.BlockSpec((8, QUAD * CELL), lambda i, place: (place[0], 0)),
            whole(tab_w.shape),
            whole(vec_w.shape),
            whole((QUAD, QUAD * CELL)),
        ],
        pl.BlockSpec((rows + EXTRA, BLOCK), lambda i, place: (0, 0)),
        shape((rows + EXTRA, BLOCK), bf16),
        [pltpu.VMEM((2, 176, QUAD * CELL), f32), pltpu.VMEM((16, 256), f32)],
        0,
        400000,
        prefetch=1,
    )(place, mat_w, rel, tab_w, vec_w, jnp.asarray(head_spread(QUAD), bf16))


def attention_forward_body(
    layer, x, weight, extra, mask, perm, perm_back, heads,
    mid, qkv, merged, totals, table, vec, x_rows, framed,
):
    @pl.when(pl.program_id(0) == 0)
    def _():
        x_rows[...] = jnp.zeros_like(x_rows)
        vec[...] = jnp.zeros_like(vec)
        for z in range(4):
            for d in range(8):
                pair = extra[d, z, 0:16, :].astype(f32)
                bias = pair[8 * layer : 8 * layer + 8]
                for w in range(table.shape[0]):
                    table[w, z, 8 * d : 8 * d + 8, :] = bias + mask[w, 8 * d : 8 * d + 8, :]
                if d < 6:
                    rows = extra[d, z, 16:32, 128 * layer : 128 * layer + 128].astype(f32)
                    vec[2 * d : 2 * d + 2, 128 * z : 128 * z + 128] = rows[0:2]

    if x.shape[1] == ROWS:
        stream = x[0]
    else:
        x_rows[0:TOKENS, :] = x[0].astype(f32)
        stream = x_rows[...]
    unit, _ = norm(stream)
    normed = (unit * vec[0:1, :] + vec[1:2, :]).astype(bf16)
    normed = mm(perm[...], normed).astype(bf16)
    for c in range(6):
        part = mm(normed, weight[c].reshape(C, BLOCK))
        if c < 2:
            part = part + vec[2:3, 256 * c : 256 * c + 256]
        if c >= 4:
            part = part + vec[3:4, 256 * (c - 4) : 256 * (c - 4) + 256]
        qkv[0, :, 256 * c : 256 * c + 256] = part.astype(bf16)
    lane_head = lane_heads()
    for w in range(4):
        rows = slice(CELL * w, CELL * w + CELL)
        for g in range(4):
            at = 128 * g
            query = quad_rows(qkv[0, rows, at : at + 128], heads[...])
            key = qkv[0, rows, C + at : C + at + 128]
            value = qkv[0, rows, 2 * C + at : 2 * C + at + 128]
            scores = mm(key, query, NT) * scale + table[w % table.shape[0], g]
            top = jnp.max(scores, 0, keepdims=True)
            raised = jnp.exp(scores - top)
            total = jnp.sum(raised, 0, keepdims=True)
            totals[0, 4 * w + g : 4 * w + g + 1, :] = top + jnp.log(total)
            probs = (raised * (1.0 / total)).astype(bf16)
            stacked = mm(probs, value, TN)
            framed[rows, at : at + 128] = pick_heads(stacked, lane_head).astype(bf16)
    gathered = mm(perm_back[...], framed[...]).astype(bf16)
    merged[0] = gathered
    for c in range(2):
        cols = slice(256 * c, 256 * c + 256)
        mid[0, :, cols] = (
            stream[:, cols] + mm(gathered, weight[6 + c].reshape(C, BLOCK)) + vec[4:5, cols]
        )


def attention_forward(layer, x, weight, extra, mask, perm):
    images = x.shape[0]
    tables = mask.shape[0]
    return call(
        partial(attention_forward_body, layer),
        f"attention_forward_{layer}",
        (images,),
        [
            per_image(x.shape[1], C),
            whole((8, 4, 128, BLOCK)),
            pl.BlockSpec((8, 4, EXTRA, BLOCK), lambda i: (0, 0, 4, 0), pipeline_mode=pl.Buffered(1)),
            whole(mask.shape),
            whole((FRAME, ROWS)),
            whole((ROWS, FRAME)),
            whole((QUAD * CELL, 128)),
        ],
        [
            per_image(ROWS, C),
            per_image(FRAME, 3 * C),
            per_image(ROWS, C),
            per_image(16, QUAD * CELL),
            pl.BlockSpec((tables, 4, CELL, QUAD * CELL), lambda i: (0, 0, 0, 0)),
            pl.BlockSpec((16, C), lambda i: (0, 0)),
        ],
        [
            shape((images, ROWS, C), f32),
            shape((images, FRAME, 3 * C), bf16),
            shape((images, ROWS, C), bf16),
            shape((images, 16, QUAD * CELL), f32),
            shape((tables, 4, CELL, QUAD * CELL), f32),
            shape((16, C), f32),
        ],
        [pltpu.VMEM((ROWS, C), f32), pltpu.VMEM((FRAME, C), bf16)],
        images * 256 * C * 2048 * 4,
        images * 2500000,
    )(
        x,
        weight,
        extra,
        mask,
        jnp.asarray(perm, bf16),
        jnp.asarray(perm.T, bf16),
        jnp.asarray(head_rows(), bf16),
    )


def mlp_forward_body(last, count, mid, first, second, vec, result, act, slope):
    unit, _ = norm(mid[0])
    normed = (unit * vec[5:6, :] + vec[6:7, :]).astype(bf16)
    total = mid[0] + vec[7:8, :]
    for c in range(8):
        bias = vec[8 + c // 2 : 9 + c // 2, 256 * (c % 2) : 256 * (c % 2) + 256]
        value, pull = gelu_pair(mm(normed, first[c]) + bias)
        value = value.astype(bf16)
        act[0, :, 256 * c : 256 * c + 256] = value
        slope[0, :, 256 * c : 256 * c + 256] = pull.astype(bf16)
        total = total + mm(value, second[c], NT)
    if last:
        alive = (pl.program_id(0) < count[0]).astype(f32)
        result[0] = (total * alive)[:TOKENS].astype(bf16)
    else:
        result[0] = total


def mlp_forward(layer, last, count, mid, first, second, vec):
    images = mid.shape[0]
    out = (images, TOKENS, C) if last else (images, ROWS, C)
    return call(
        partial(mlp_forward_body, last),
        f"mlp_forward_{layer}",
        (images,),
        [per_image(ROWS, C), whole(first.shape), whole(second.shape), whole(vec.shape)],
        [per_image(out[1], C), per_image(ROWS, HID), per_image(ROWS, HID)],
        [
            shape(out, bf16 if last else f32),
            shape((images, ROWS, HID), bf16),
            shape((images, ROWS, HID), bf16),
        ],
        [],
        images * ROWS * C * HID * 4,
        images * 3000000,
        prefetch=1,
    )(count, mid, first, second, vec)


def mlp_backward_body(
    count, grad, act, slope, mid, first, second, vec,
    grad_mid, grad_first, grad_second, small,
    grad_rows, all_grad, all_act, all_inner, all_normed,
):
    i = pl.program_id(0)

    @pl.when(i == 0)
    def _():
        grad_rows[...] = jnp.zeros_like(grad_rows)
        small[...] = jnp.zeros_like(small)

    if grad.shape[1] == ROWS:
        grad_out = grad[0]
    else:
        alive = (i < count[0]).astype(f32)
        grad_rows[0:TOKENS, :] = grad[0].astype(f32) * alive
        grad_out = grad_rows[...]
    here = pl.ds(pl.multiple_of(i * ROWS, 16), ROWS)
    low = grad_out.astype(bf16)
    all_grad[here, :] = low
    small[7:8, :] += column_sum(low.astype(f32))
    all_act[here, :] = act[0]
    unit, spread = norm(mid[0])
    all_normed[here, :] = (unit * vec[5:6, :] + vec[6:7, :]).astype(bf16)
    back = jnp.zeros((ROWS, C), f32)
    for c in range(8):
        cols = slice(256 * c, 256 * c + 256)
        inner = (mm(low, second[c]) * slope[0, :, cols].astype(f32)).astype(bf16)
        all_inner[here, cols] = inner
        row, lane = 8 + c // 2, 256 * (c % 2)
        small[row : row + 1, lane : lane + 256] += column_sum(inner.astype(f32))
        back = back + mm(inner, first[c], NT)
    small[5:6, :] += column_sum(back * unit)
    small[6:7, :] += column_sum(back)
    grad_mid[0] = grad_out + norm_back(back * vec[5:6, :], unit, spread)

    @pl.when(i == pl.num_programs(0) - 1)
    def _():
        grad_across = all_grad[...].T
        normed_across = all_normed[...].T
        for c in range(8):
            cols = slice(256 * c, 256 * c + 256)
            grad_second[c] = mm(grad_across, all_act[:, cols]).astype(bf16)
            grad_first[c] = mm(normed_across, all_inner[:, cols]).astype(bf16)


def mlp_backward(layer, count, grad, act, slope, mid, first, second, vec):
    images = mid.shape[0]
    total = images * ROWS
    return call(
        mlp_backward_body,
        f"mlp_backward_{layer}",
        (images,),
        [
            per_image(grad.shape[1], C),
            per_image(ROWS, HID),
            per_image(ROWS, HID),
            per_image(ROWS, C),
            whole(first.shape),
            whole(second.shape),
            whole(vec.shape),
        ],
        [per_image(ROWS, C), whole(first.shape), whole(second.shape), whole((16, C))],
        [
            shape((images, ROWS, C), f32),
            shape(first.shape, bf16),
            shape(second.shape, bf16),
            shape((16, C), f32),
        ],
        [
            pltpu.VMEM((ROWS, C), f32),
            pltpu.VMEM((total, C), bf16),
            pltpu.VMEM((total, HID), bf16),
            pltpu.VMEM((total, HID), bf16),
            pltpu.VMEM((total, C), bf16),
        ],
        total * C * HID * 8,
        images * 4000000,
        prefetch=1,
    )(count, grad, act, slope, mid, first, second, vec)


def attention_backward_body(
    grad, x, qkv, merged, totals, table, weight, vec, before, perm, perm_back, heads, rel, spread,
    result, pieces,
    x_rows, framed, grad_framed, all_normed, all_packed, all_merged, all_grad, pairs, small, hits,
):
    i = pl.program_id(0)

    @pl.when(i == 0)
    def _():
        x_rows[...] = jnp.zeros_like(x_rows)
        small[...] = before[...]
        pairs[...] = jnp.zeros_like(pairs)

    if x.shape[1] == ROWS:
        stream = x[0]
    else:
        x_rows[0:TOKENS, :] = x[0].astype(f32)
        stream = x_rows[...]
    here = pl.ds(pl.multiple_of(i * ROWS, 16), ROWS)
    unit, spread_one = norm(stream)
    all_normed[here, :] = (unit * vec[0:1, :] + vec[1:2, :]).astype(bf16)
    low = grad[0].astype(bf16)
    all_grad[here, :] = low
    all_merged[here, :] = merged[0]
    small[4:5, :] += column_sum(low.astype(f32))
    moved = mm(perm[...], low).astype(bf16)
    from_heads = mm(moved[:, :BLOCK], weight[6].reshape(C, BLOCK), NT)
    from_heads = from_heads + mm(moved[:, BLOCK:], weight[7].reshape(C, BLOCK), NT)
    framed[...] = from_heads.astype(bf16)
    lane_head = lane_heads()
    for w in range(4):
        rows = slice(CELL * w, CELL * w + CELL)
        for g in range(4):
            at = 128 * g
            query = quad_rows(qkv[0, rows, at : at + 128], heads[...])
            key = qkv[0, rows, C + at : C + at + 128]
            value = qkv[0, rows, 2 * C + at : 2 * C + at + 128]
            pull = quad_rows(framed[rows, at : at + 128], heads[...])
            scores = mm(key, query, NT) * scale + table[w % table.shape[0], g]
            probs = jnp.exp(scores - totals[0, 4 * w + g : 4 * w + g + 1, :])
            grad_probs = mm(value, pull, NT)
            mean = jnp.sum(probs * grad_probs, 0, keepdims=True)
            grad_scores = (probs * (grad_probs - mean)).astype(bf16)
            pairs[g] += grad_scores.astype(f32)
            grad_value = mm(probs.astype(bf16), pull)
            grad_key = mm(grad_scores, query) * scale
            grad_query = pick_heads(mm(grad_scores, key, TN), lane_head) * scale
            grad_framed[rows, at : at + 128] = grad_query.astype(bf16)
            grad_framed[rows, C + at : C + at + 128] = grad_key.astype(bf16)
            grad_framed[rows, 2 * C + at : 2 * C + at + 128] = grad_value.astype(bf16)
    back = jnp.zeros((ROWS, C), f32)
    for c in range(6):
        cols = slice(256 * c, 256 * c + 256)
        part_wide = mm(perm_back[...], grad_framed[:, cols])
        part = part_wide.astype(bf16)
        all_packed[here, cols] = part
        if c < 2:
            small[2:3, cols] += column_sum(part_wide)
        if c >= 4:
            small[3:4, 256 * (c - 4) : 256 * (c - 4) + 256] += column_sum(part_wide)
        back = back + mm(part, weight[c].reshape(C, BLOCK), NT)
    small[0:1, :] += column_sum(back * unit)
    small[1:2, :] += column_sum(back)
    total = grad[0] + norm_back(back * vec[0:1, :], unit, spread_one)
    result[0] = total[: result.shape[1]]

    @pl.when(i == pl.num_programs(0) - 1)
    def _():
        normed_across = all_normed[...].T
        merged_across = all_merged[...].T
        for c in range(8):
            if c < 6:
                block = mm(normed_across, all_packed[:, 256 * c : 256 * c + 256])
            else:
                block = mm(merged_across, all_grad[:, 256 * (c - 6) : 256 * (c - 6) + 256])
            pieces[c, :, 0:128, :] = block.astype(bf16).reshape(4, 128, BLOCK)
        hits[...] = jnp.zeros_like(hits)

        def step(r, carry):
            same = rel[...] == r
            for g in range(4):
                kept = jnp.where(same, pairs[g], 0.0)
                hits[pl.ds(r, 1), 256 * g : 256 * g + 256] = column_sum(kept)
            return carry

        lax.fori_loop(0, NREL, step, 0)
        for z in range(4):
            for c in range(2, 8):
                pieces[c, z, 128:144, :] = jnp.zeros((SMALL, BLOCK), bf16)
            pieces[0, z, 128:144, :] = lax.dot_general(
                spread[...],
                hits[:, 256 * z : 256 * z + 256],
                NT,
                precision=lax.Precision.HIGHEST,
                preferred_element_type=f32,
            ).astype(bf16)
            pieces[1, z, 128:144, 0:128] = small[:, 128 * z : 128 * z + 128].astype(bf16)
            pieces[1, z, 128:144, 128:256] = jnp.zeros((SMALL, 128), bf16)


def attention_backward(layer, grad, x, qkv, merged, totals, table, weight, vec, before, perm, rel):
    images = grad.shape[0]
    total = images * ROWS
    out_rows = TOKENS if layer == 0 else ROWS
    return call(
        attention_backward_body,
        f"attention_backward_{layer}",
        (images,),
        [
            per_image(ROWS, C),
            per_image(x.shape[1], C),
            per_image(FRAME, 3 * C),
            per_image(ROWS, C),
            per_image(16, QUAD * CELL),
            whole(table.shape),
            whole((8, 4, 128, BLOCK)),
            whole(vec.shape),
            whole((16, C)),
            whole((FRAME, ROWS)),
            whole((ROWS, FRAME)),
            whole((QUAD * CELL, 128)),
            whole(rel.shape),
            whole((SMALL, QUAD * CELL)),
        ],
        [per_image(out_rows, C), whole((8, 4, 128 + SMALL, BLOCK))],
        [shape((images, out_rows, C), f32), shape((8, 4, 128 + SMALL, BLOCK), bf16)],
        [
            pltpu.VMEM((ROWS, C), f32),
            pltpu.VMEM((FRAME, C), bf16),
            pltpu.VMEM((FRAME, 3 * C), bf16),
            pltpu.VMEM((total, C), bf16),
            pltpu.VMEM((total, 3 * C), bf16),
            pltpu.VMEM((total, C), bf16),
            pltpu.VMEM((total, C), bf16),
            pltpu.VMEM((4, CELL, QUAD * CELL), f32),
            pltpu.VMEM((16, C), f32),
            pltpu.VMEM((256, 4 * QUAD * CELL), f32),
        ],
        total * C * 2048 * 10,
        images * 4000000,
    )(
        grad,
        x,
        qkv,
        merged,
        totals,
        table,
        weight,
        vec,
        before,
        jnp.asarray(perm, bf16),
        jnp.asarray(perm.T, bf16),
        jnp.asarray(head_rows(), bf16),
        rel,
        jnp.asarray(head_spread(SMALL), f32),
    )


def adam_step(weight, first, second, gradient, rate, decay):
    first_new = beta_one * first + (1.0 - beta_one) * gradient
    second_new = beta_two * second + (1.0 - beta_two) * gradient * gradient
    first_hat = first_new / (1.0 - beta_one**STEP)
    second_hat = second_new / (1.0 - beta_two**STEP)
    weight_new = weight - rate * (first_hat / (jnp.sqrt(second_hat) + adam_eps) + decay * weight)
    return (weight_new, first_new, second_new)


def adam_body(grad, weight, first, second, *refs):
    outs = refs[-3:]
    for k in range(grad.shape[0]):
        cols = slice(BLOCK * k, BLOCK * k + BLOCK)
        news = adam_step(
            weight[0, :, cols], first[0, :, cols], second[0, :, cols],
            grad[k].astype(f32), rate_matrix, weight_decay,
        )
        for out, new in zip(outs, news):
            out[0, :, cols] = new


def adam(layer, part, grad, state, done):
    wide = 4
    spec = pl.BlockSpec((1, 128, wide * BLOCK), lambda i: (layer, 0, part * (8 // wide) + i))
    kept = [] if done is None else list(done)
    return call(
        adam_body,
        f"adam_{layer}_{part}",
        (8 // wide,),
        [pl.BlockSpec((wide, 128, BLOCK), lambda i: (i, 0, 0)), spec, spec, spec]
        + [pl.BlockSpec(memory_space=pl.ANY)] * len(kept),
        [spec] * 3,
        [shape(state[0].shape, f32)] * 3,
        [],
        0,
        7000000,
        aliases={4 + k: k for k in range(len(kept))},
    )(grad, *state, *kept)


def gather(piece, dp, extra):
    out = lax.all_gather(piece, ("dp", "zero"), axis=0, tiled=False)
    fine = dp // 8
    if fine == 1:
        return out.reshape(8, 4, *piece.shape)
    out = out.reshape(8, fine, 4, *piece.shape)
    rows = piece.shape[0] - extra
    main = out[:, :, :, :rows].transpose(0, 2, 1, 3, 4).reshape(8, 4, 128, BLOCK)
    return jnp.concatenate([main, out[:, 0, :, rows:]], 2)


def reduce(blocks, dp, extra):
    fine = dp // 8
    if fine > 1:
        rows = 128 // fine
        main = blocks[:, :, :128].reshape(8, 4, fine, rows, BLOCK).transpose(0, 2, 1, 3, 4)
        beside = jnp.broadcast_to(
            blocks[:, None, :, 128:], (8, fine, 4, extra, BLOCK)
        )
        blocks = jnp.concatenate([main, beside], 3)
    flat = blocks.reshape(dp * 4, -1, BLOCK)
    own = lax.psum_scatter(flat, ("dp", "zero"), scatter_dimension=0, tiled=True)
    out = lax.all_gather(own[0], "dp", axis=0, tiled=False)
    beside = out[::fine, out.shape[1] - extra :]
    if fine > 1:
        out = out[:, : out.shape[1] - extra].reshape(8, 128, BLOCK)
    return out, beside


def shards(
    dp, images, cotangent, counts, rel_index, regions,
    mat_w, mat_m, mat_v, vec_w, vec_m, vec_v, tab_w, tab_m, tab_v,
):
    fine = dp // 8
    rows = 128 // fine
    me = lax.axis_index("dp")
    place = jnp.stack([me // fine, me % fine]).astype(jnp.int32)

    inside = np.arange(CELL) < WIN * WIN
    pair_ids = jnp.pad(rel_index.T, ((0, 15), (0, 15)), constant_values=-1)
    rel = jnp.tile(pair_ids, (1, QUAD))
    zones = regions.reshape(2, WIN, 2, WIN).transpose(0, 2, 1, 3).reshape(4, WIN * WIN)
    zones = jnp.pad(zones, ((0, 0), (0, 15)))
    differ = (zones[:, :, None] != zones[:, None, :]) & inside[None, None, :]
    outside = jnp.asarray(np.where(inside, 0.0, -1e30), f32)[None, :, None]
    mask_shifted = jnp.tile(jnp.where(differ, mask_value, 0.0) + outside, (1, 1, QUAD)).astype(f32)
    mask_plain = jnp.broadcast_to(outside, (1, CELL, QUAD * CELL))
    masks = (mask_plain, mask_shifted)
    perms = (frames(False), frames(True))

    def piece(layer, part):
        taken = lax.dynamic_slice(
            mat_w, (layer, place[1] * rows, part * HID + place[0] * BLOCK), (1, rows, BLOCK)
        )
        return taken[0].astype(bf16)

    packed = pack(place, rows, mat_w, rel, tab_w, vec_w)
    heads0 = gather(packed, dp, EXTRA)
    first0 = gather(piece(0, 1), dp, 0).reshape(8, C, BLOCK)
    second0 = gather(piece(0, 2), dp, 0).reshape(8, C, BLOCK)
    heads1 = gather(piece(1, 0), dp, 0)
    first1 = gather(piece(1, 1), dp, 0).reshape(8, C, BLOCK)
    second1 = gather(piece(1, 2), dp, 0).reshape(8, C, BLOCK)
    attention_w = (heads0, heads1)
    first_w = (first0, first1)
    second_w = (second0, second1)

    stream = images
    saved = []
    for layer in range(2):
        mid, qkv, merged, totals, table, vec = attention_forward(
            layer, stream, attention_w[layer], heads0, masks[layer], perms[layer]
        )
        result, act, slope = mlp_forward(
            layer, layer == 1, counts, mid, first_w[layer], second_w[layer], vec
        )
        saved.append((stream, mid, qkv, merged, totals, table, vec, act, slope))
        stream = result
    activations = stream
    gradient = cotangent
    state = (mat_w, mat_m, mat_v)
    done = None
    vec_parts = []
    tab_parts = []
    mat_parts = []
    for layer in (1, 0):
        x, mid, qkv, merged, totals, table, vec, act, slope = saved[layer]
        grad_mid, grad_first, grad_second, small = mlp_backward(
            layer, counts, gradient, act, slope, mid, first_w[layer], second_w[layer], vec
        )
        sum_first, _ = reduce(grad_first.reshape(8, 4, 128, BLOCK), dp, 0)
        sum_second, _ = reduce(grad_second.reshape(8, 4, 128, BLOCK), dp, 0)
        gradient, pieces = attention_backward(
            layer, grad_mid, x, qkv, merged, totals, table, attention_w[layer], vec, small,
            perms[layer], rel,
        )
        sum_heads, beside = reduce(pieces, dp, SMALL)
        mat_parts += [(layer, 1, sum_first), (layer, 2, sum_second), (layer, 0, sum_heads)]
        tab_parts.insert(0, beside[0, 0:4, 0:NREL])
        vec_parts.insert(0, beside[1, 0:12, 0:128])
    for layer, part, total in mat_parts:
        done = adam(layer, part, total, state, done)
    new_vec = adam_step(vec_w, vec_m, vec_v, jnp.stack(vec_parts).astype(f32), rate_vector, 0.0)
    new_tab = adam_step(tab_w, tab_m, tab_v, jnp.stack(tab_parts).astype(f32), rate_table, 0.0)
    return (activations, gradient, *done, *new_vec, *new_tab)


def solution(mesh):
    images = P(("dp", "zero"), None, None)
    rows = P(None, "zero", None)
    lanes = P(None, None, "zero")
    return jax.shard_map(
        partial(shards, mesh.shape["dp"]),
        mesh=mesh,
        in_specs=(images, images, P(("dp", "zero")), P(), P())
        + (rows,) * 3 + (lanes,) * 3 + (rows,) * 3,
        out_specs=(images, images) + (rows,) * 3 + (lanes,) * 3 + (rows,) * 3,
        check_vma=False,
    )
```

```python
from functools import partial

import jax
import jax.numpy as jnp
import numpy as np
from jax import lax
from jax.experimental import pallas as pl
from jax.experimental.pallas import tpu as pltpu
from jax.sharding import PartitionSpec as P

WIN = 7
SIDE = 14
STEP = 10
NREL = 169
C = 512
HID = 2048
TOKENS = SIDE * SIDE
ROWS = 208
FRAME = 256
CELL = 64
QUAD = 4
BLOCK = 256
EXTRA = 32
SMALL = 16

norm_eps = 1e-05
mask_value = -100.0
beta_one = 0.9
beta_two = 0.999
adam_eps = 1e-08
weight_decay = 0.05
rate_matrix = 0.1
rate_vector = 0.5
rate_table = 1.0
scale = 32 ** (-0.5)

bf16 = jnp.bfloat16
f32 = jnp.float32
NN = (((1,), (0,)), ((), ()))
NT = (((1,), (1,)), ((), ()))
TN = (((0,), (0,)), ((), ()))


def mm(left, right, dims=NN):
    return lax.dot_general(left, right, dims, preferred_element_type=f32)


def frames(shifted):
    move = WIN // 2 if shifted else 0
    placed = np.zeros((FRAME, ROWS), np.float32)
    for wy in range(2):
        for wx in range(2):
            for iy in range(WIN):
                for ix in range(WIN):
                    y = (wy * WIN + iy + move) % SIDE
                    x = (wx * WIN + ix + move) % SIDE
                    placed[(wy * 2 + wx) * CELL + iy * WIN + ix, y * SIDE + x] = 1
    return placed


def head_rows():
    rows = np.zeros((QUAD * CELL, 128), np.float32)
    for h in range(QUAD):
        rows[h * CELL : (h + 1) * CELL, h * 32 : (h + 1) * 32] = 1
    return rows


def head_spread(rows):
    out = np.zeros((rows, QUAD * CELL), np.float32)
    for h in range(QUAD):
        out[h, h * CELL : (h + 1) * CELL] = 1
    return out


def norm(rows):
    centred = rows - jnp.mean(rows, -1, keepdims=True)
    spread = lax.rsqrt(jnp.mean(centred * centred, -1, keepdims=True) + norm_eps)
    return centred * spread, spread


def norm_back(grad_unit, unit, spread):
    return spread * (
        grad_unit
        - jnp.mean(grad_unit, -1, keepdims=True)
        - unit * jnp.mean(grad_unit * unit, -1, keepdims=True)
    )


def column_sum(rows):
    return jnp.sum(rows, 0, keepdims=True)


def gelu_pair(u):
    size = jnp.abs(u)
    below = 1.0 + (0.3275911 * 0.5**0.5) * size
    t = pl.reciprocal(below, approx=True)
    t = t * (2.0 - below * t)
    bell = jnp.exp2(u * u * (-0.5 * 1.4426950408889634))
    poly = t * (
        0.127414796 + t * (-0.142248368 + t * (0.710706871 + t * (-0.726576013 + t * 0.530702714)))
    )
    tail = poly * bell
    phi = jnp.where(u >= 0, 1.0 - tail, tail)
    return u * phi, phi + u * bell * 0.3989422804014327


def quad_rows(part, heads):
    return jnp.concatenate([part] * QUAD, 0) * heads


def pick_heads(stacked, lane_head):
    low = jnp.where(lane_head == 0, stacked[:CELL], stacked[CELL : 2 * CELL])
    high = jnp.where(lane_head == 2, stacked[2 * CELL : 3 * CELL], stacked[3 * CELL :])
    return jnp.where(lane_head < 2, low, high)


def lane_heads():
    return lax.broadcasted_iota(jnp.int32, (CELL, 128), 1) // 32


def whole(shape):
    zero = (0,) * len(shape)
    return pl.BlockSpec(shape, lambda *_: zero, pipeline_mode=pl.Buffered(1))


def per_image(rows, cols):
    return pl.BlockSpec((1, rows, cols), lambda i, *_: (i, 0, 0))


HBM = pl.BlockSpec(memory_space=pl.ANY)


def weight_copies(place, arrays, kept, sems, first_row=0):
    copies = []
    parts, rows = kept.shape[0], kept.shape[3]
    for k in range(2):
        for j in range(4):
            block = place[0] ^ (2 * j + k)
            for s in range(4):
                owner = (place[1] + 4 - s) & 3
                for p in range(parts):
                    copies.append(
                        pltpu.make_async_copy(
                            arrays[4 * k + j].at[s, p, pl.ds(first_row, rows), :],
                            kept.at[p, block, owner],
                            sems.at[k * 4 + j, s, p],
                        )
                    )
    return copies


def fetch(copies):
    for copy in copies:
        copy.start()
    for copy in copies:
        copy.wait()


def call(body, name, grid, ins, outs, out_shapes, scratch, flops, moved, prefetch=0, aliases=None):
    return pl.pallas_call(
        body,
        name=name,
        grid_spec=pltpu.PrefetchScalarGridSpec(
            num_scalar_prefetch=prefetch,
            grid=grid,
            in_specs=ins,
            out_specs=outs,
            scratch_shapes=scratch,
        ),
        out_shape=out_shapes,
        input_output_aliases=aliases or {},
        compiler_params=pltpu.CompilerParams(
            dimension_semantics=("arbitrary",) * len(grid), vmem_limit_bytes=58 * 1024 * 1024
        ),
        cost_estimate=pl.CostEstimate(flops=flops, bytes_accessed=moved, transcendentals=0),
    )


def shape(dims, kind):
    return jax.ShapeDtypeStruct(dims, kind)


def pack_body(place, mat, rel, tab, vec, spread, out, spread_tab, small):
    rows = mat.shape[1]
    out[0:rows, :] = mat[0].astype(bf16)
    for layer in range(2):
        spread_tab[layer, 0:NREL, :] = mm(tab[layer].astype(bf16), spread[...], TN)
    pairs = rel[...]

    def step(r, sums):
        hit = pairs == r
        return tuple(
            jnp.where(hit, spread_tab[layer, pl.ds(r, 1), :], sums[layer]) for layer in range(2)
        )

    start = jnp.zeros((8, QUAD * CELL), f32)
    first, second = lax.fori_loop(0, NREL, step, (start, start))
    out[rows : rows + 16, :] = jnp.concatenate([first, second], 0).astype(bf16)
    small[...] = jnp.zeros_like(small)
    row = jnp.minimum(place[0] * 2, 10)
    for layer in range(2):
        for k in range(2):
            small[k : k + 1, layer * 128 : (layer + 1) * 128] = vec[layer, pl.ds(row + k, 1), :]
    out[rows + 16 : rows + 32, :] = small[...].astype(bf16)


def pack(place, rows, mat_w, rel, tab_w, vec_w):
    return call(
        pack_body,
        "pack",
        (1,),
        [
            pl.BlockSpec((1, rows, BLOCK), lambda i, place: (0, place[1], place[0])),
            pl.BlockSpec((8, QUAD * CELL), lambda i, place: (place[0], 0)),
            whole(tab_w.shape),
            whole(vec_w.shape),
            whole((QUAD, QUAD * CELL)),
        ],
        pl.BlockSpec((rows + EXTRA, BLOCK), lambda i, place: (0, 0)),
        shape((rows + EXTRA, BLOCK), bf16),
        [pltpu.VMEM((2, 176, QUAD * CELL), f32), pltpu.VMEM((16, 256), f32)],
        0,
        400000,
        prefetch=1,
    )(place, mat_w, rel, tab_w, vec_w, jnp.asarray(head_spread(QUAD), bf16))


def attention_forward_body(layer, waits, place, *refs):
    arrays, extras, refs = refs[:8], refs[8:16], refs[16 + waits :]
    x, mask, perm, perm_back, heads = refs[:5]
    mid, qkv, merged, totals, table, vec, x_rows, framed, kept, extra_kept, sems, more_sems = refs[5:]
    weight, extra = kept.at[0], extra_kept.at[0]

    @pl.when(pl.program_id(0) == 0)
    def _():
        fetch(
            weight_copies(place, arrays, kept, sems)
            + weight_copies(place, extras, extra_kept, more_sems, 128)
        )
        x_rows[...] = jnp.zeros_like(x_rows)
        vec[...] = jnp.zeros_like(vec)
        for z in range(4):
            for d in range(8):
                pair = extra[d, z, 0:16, :].astype(f32)
                bias = pair[8 * layer : 8 * layer + 8]
                for w in range(table.shape[0]):
                    table[w, z, 8 * d : 8 * d + 8, :] = bias + mask[w, 8 * d : 8 * d + 8, :]
                if d < 6:
                    rows = extra[d, z, 16:32, 128 * layer : 128 * layer + 128].astype(f32)
                    vec[2 * d : 2 * d + 2, 128 * z : 128 * z + 128] = rows[0:2]

    if x.shape[1] == ROWS:
        stream = x[0]
    else:
        x_rows[0:TOKENS, :] = x[0].astype(f32)
        stream = x_rows[...]
    unit, _ = norm(stream)
    normed = (unit * vec[0:1, :] + vec[1:2, :]).astype(bf16)
    normed = mm(perm[...], normed).astype(bf16)
    for c in range(6):
        part = mm(normed, weight[c].reshape(C, BLOCK))
        if c < 2:
            part = part + vec[2:3, 256 * c : 256 * c + 256]
        if c >= 4:
            part = part + vec[3:4, 256 * (c - 4) : 256 * (c - 4) + 256]
        qkv[0, :, 256 * c : 256 * c + 256] = part.astype(bf16)
    lane_head = lane_heads()
    for w in range(4):
        rows = slice(CELL * w, CELL * w + CELL)
        for g in range(4):
            at = 128 * g
            query = quad_rows(qkv[0, rows, at : at + 128], heads[...])
            key = qkv[0, rows, C + at : C + at + 128]
            value = qkv[0, rows, 2 * C + at : 2 * C + at + 128]
            scores = mm(key, query, NT) * scale + table[w % table.shape[0], g]
            top = jnp.max(scores, 0, keepdims=True)
            raised = jnp.exp(scores - top)
            total = jnp.sum(raised, 0, keepdims=True)
            totals[0, 4 * w + g : 4 * w + g + 1, :] = top + jnp.log(total)
            probs = (raised * (1.0 / total)).astype(bf16)
            stacked = mm(probs, value, TN)
            framed[rows, at : at + 128] = pick_heads(stacked, lane_head).astype(bf16)
    gathered = mm(perm_back[...], framed[...]).astype(bf16)
    merged[0] = gathered
    for c in range(2):
        cols = slice(256 * c, 256 * c + 256)
        mid[0, :, cols] = (
            stream[:, cols] + mm(gathered, weight[6 + c].reshape(C, BLOCK)) + vec[4:5, cols]
        )


def attention_forward(layer, place, x, weight, extra, mask, perm, after):
    images = x.shape[0]
    tables = mask.shape[0]
    return call(
        partial(attention_forward_body, layer, len(after)),
        f"attention_forward_{layer}",
        (images,),
        [HBM] * (16 + len(after))
        + [
            per_image(x.shape[1], C),
            whole(mask.shape),
            whole((FRAME, ROWS)),
            whole((ROWS, FRAME)),
            whole((QUAD * CELL, 128)),
        ],
        [
            per_image(ROWS, C),
            per_image(FRAME, 3 * C),
            per_image(ROWS, C),
            per_image(16, QUAD * CELL),
            pl.BlockSpec((tables, 4, CELL, QUAD * CELL), lambda i, *_: (0, 0, 0, 0)),
            pl.BlockSpec((16, C), lambda i, *_: (0, 0)),
        ],
        [
            shape((images, ROWS, C), f32),
            shape((images, FRAME, 3 * C), bf16),
            shape((images, ROWS, C), bf16),
            shape((images, 16, QUAD * CELL), f32),
            shape((tables, 4, CELL, QUAD * CELL), f32),
            shape((16, C), f32),
        ],
        [
            pltpu.VMEM((ROWS, C), f32),
            pltpu.VMEM((FRAME, C), bf16),
            pltpu.VMEM((1, 8, 4, 128, BLOCK), bf16),
            pltpu.VMEM((1, 8, 4, EXTRA, BLOCK), bf16),
            pltpu.SemaphoreType.DMA((8, 4, 1)),
            pltpu.SemaphoreType.DMA((8, 4, 1)),
        ],
        images * 256 * C * 2048 * 4,
        images * 2500000,
        prefetch=1,
    )(
        place,
        *weight,
        *extra,
        *after,
        x,
        mask,
        jnp.asarray(perm, bf16),
        jnp.asarray(perm.T, bf16),
        jnp.asarray(head_rows(), bf16),
    )


def mlp_forward_body(last, waits, place, *refs):
    arrays, refs = refs[:8], refs[8 + waits :]
    mid, vec, result, act, slope, kept, sems = refs
    first, second = kept.at[0], kept.at[1]

    @pl.when(pl.program_id(0) == 0)
    def _():
        fetch(weight_copies(place, arrays, kept, sems))

    unit, _ = norm(mid[0])
    normed = (unit * vec[5:6, :] + vec[6:7, :]).astype(bf16)
    total = mid[0] + vec[7:8, :]
    for c in range(8):
        bias = vec[8 + c // 2 : 9 + c // 2, 256 * (c % 2) : 256 * (c % 2) + 256]
        value, pull = gelu_pair(mm(normed, first[c].reshape(C, BLOCK)) + bias)
        value = value.astype(bf16)
        act[0, :, 256 * c : 256 * c + 256] = value
        slope[0, :, 256 * c : 256 * c + 256] = pull.astype(bf16)
        total = total + mm(value, second[c].reshape(C, BLOCK), NT)
    if last:
        alive = (pl.program_id(0) < place[2]).astype(f32)
        result[0] = (total * alive)[:TOKENS].astype(bf16)
    else:
        result[0] = total


def mlp_forward(layer, last, place, mid, weight, vec, after):
    images = mid.shape[0]
    out = (images, TOKENS, C) if last else (images, ROWS, C)
    return call(
        partial(mlp_forward_body, last, len(after)),
        f"mlp_forward_{layer}",
        (images,),
        [HBM] * (8 + len(after)) + [per_image(ROWS, C), whole(vec.shape)],
        [per_image(out[1], C), per_image(ROWS, HID), per_image(ROWS, HID)],
        [
            shape(out, bf16 if last else f32),
            shape((images, ROWS, HID), bf16),
            shape((images, ROWS, HID), bf16),
        ],
        [pltpu.VMEM((2, 8, 4, 128, BLOCK), bf16), pltpu.SemaphoreType.DMA((8, 4, 2))],
        images * ROWS * C * HID * 4,
        images * 3000000,
        prefetch=1,
    )(place, *weight, *after, mid, vec)


def mlp_backward_body(waits, place, *refs):
    arrays, refs = refs[:8], refs[8 + waits :]
    grad, act, slope, mid, vec, grad_mid, own, other, small = refs[:9]
    grad_rows, all_grad, all_act, all_inner, all_normed, kept, sems = refs[9:]
    first, second = kept.at[0], kept.at[1]
    i = pl.program_id(0)

    @pl.when(i == 0)
    def _():
        fetch(weight_copies(place, arrays, kept, sems))
        grad_rows[...] = jnp.zeros_like(grad_rows)
        small[...] = jnp.zeros_like(small)

    if grad.shape[1] == ROWS:
        grad_out = grad[0]
    else:
        alive = (i < place[2]).astype(f32)
        grad_rows[0:TOKENS, :] = grad[0].astype(f32) * alive
        grad_out = grad_rows[...]
    here = pl.ds(pl.multiple_of(i * ROWS, 16), ROWS)
    low = grad_out.astype(bf16)
    all_grad[here, :] = low
    small[7:8, :] += column_sum(low.astype(f32))
    all_act[here, :] = act[0]
    unit, spread = norm(mid[0])
    all_normed[here, :] = (unit * vec[5:6, :] + vec[6:7, :]).astype(bf16)
    back = jnp.zeros((ROWS, C), f32)
    for c in range(8):
        cols = slice(256 * c, 256 * c + 256)
        inner = (mm(low, second[c].reshape(C, BLOCK)) * slope[0, :, cols].astype(f32)).astype(bf16)
        all_inner[here, cols] = inner
        row, lane = 8 + c // 2, 256 * (c % 2)
        small[row : row + 1, lane : lane + 256] += column_sum(inner.astype(f32))
        back = back + mm(inner, first[c].reshape(C, BLOCK), NT)
    small[5:6, :] += column_sum(back * unit)
    small[6:7, :] += column_sum(back)
    grad_mid[0] = grad_out + norm_back(back * vec[5:6, :], unit, spread)

    @pl.when(i == pl.num_programs(0) - 1)
    def _():
        grad_across = all_grad[...].T
        normed_across = all_normed[...].T
        for m in range(8):
            cols = pl.ds(pl.multiple_of((place[0] ^ m) * BLOCK, BLOCK), BLOCK)
            out = other if m % 2 else own
            for p, block in enumerate(
                (mm(normed_across, all_inner[:, cols]), mm(grad_across, all_act[:, cols]))
            ):
                block = block.astype(bf16)
                for z in range(4):
                    out[m // 2, (z + 4 - place[1]) & 3, p] = block[128 * z : 128 * z + 128]


def mlp_backward(layer, place, grad, act, slope, mid, weight, vec, after):
    images = mid.shape[0]
    total = images * ROWS
    pieces = (4, 4, 2, 128, BLOCK)
    return call(
        partial(mlp_backward_body, len(after)),
        f"mlp_backward_{layer}",
        (images,),
        [HBM] * (8 + len(after))
        + [
            per_image(grad.shape[1], C),
            per_image(ROWS, HID),
            per_image(ROWS, HID),
            per_image(ROWS, C),
            whole(vec.shape),
        ],
        [per_image(ROWS, C), whole(pieces), whole(pieces), whole((16, C))],
        [
            shape((images, ROWS, C), f32),
            shape(pieces, bf16),
            shape(pieces, bf16),
            shape((16, C), f32),
        ],
        [
            pltpu.VMEM((ROWS, C), f32),
            pltpu.VMEM((total, C), bf16),
            pltpu.VMEM((total, HID), bf16),
            pltpu.VMEM((total, HID), bf16),
            pltpu.VMEM((total, C), bf16),
            pltpu.VMEM((2, 8, 4, 128, BLOCK), bf16),
            pltpu.SemaphoreType.DMA((8, 4, 2)),
        ],
        total * C * HID * 8,
        images * 4000000,
        prefetch=1,
    )(place, *weight, *after, grad, act, slope, mid, vec)


def attention_backward_body(waits, place, *refs):
    arrays, refs = refs[:8], refs[8 + waits :]
    grad, x, qkv, merged, totals, table, vec, before = refs[:8]
    perm, perm_back, heads, rel, spread, result, own, other = refs[8:16]
    x_rows, framed, grad_framed, all_normed, all_packed, all_merged = refs[16:22]
    across, pairs, small, hits, beside, kept, sems = refs[22:]
    weight = kept.at[0]
    i = pl.program_id(0)

    @pl.when(i == 0)
    def _():
        fetch(weight_copies(place, arrays, kept, sems))
        x_rows[...] = jnp.zeros_like(x_rows)
        small[...] = before[...]
        pairs[...] = jnp.zeros_like(pairs)

    if x.shape[1] == ROWS:
        stream = x[0]
    else:
        x_rows[0:TOKENS, :] = x[0].astype(f32)
        stream = x_rows[...]
    here = pl.ds(pl.multiple_of(i * ROWS, 16), ROWS)
    unit, spread_one = norm(stream)
    all_normed[here, :] = (unit * vec[0:1, :] + vec[1:2, :]).astype(bf16)
    low = grad[0].astype(bf16)
    all_packed[here, 3 * C :] = low
    all_merged[here, :] = merged[0]
    small[4:5, :] += column_sum(low.astype(f32))
    moved = mm(perm[...], low).astype(bf16)
    from_heads = mm(moved[:, :BLOCK], weight[6].reshape(C, BLOCK), NT)
    from_heads = from_heads + mm(moved[:, BLOCK:], weight[7].reshape(C, BLOCK), NT)
    framed[...] = from_heads.astype(bf16)
    lane_head = lane_heads()
    for w in range(4):
        rows = slice(CELL * w, CELL * w + CELL)
        for g in range(4):
            at = 128 * g
            query = quad_rows(qkv[0, rows, at : at + 128], heads[...])
            key = qkv[0, rows, C + at : C + at + 128]
            value = qkv[0, rows, 2 * C + at : 2 * C + at + 128]
            pull = quad_rows(framed[rows, at : at + 128], heads[...])
            scores = mm(key, query, NT) * scale + table[w % table.shape[0], g]
            probs = jnp.exp(scores - totals[0, 4 * w + g : 4 * w + g + 1, :])
            grad_probs = mm(value, pull, NT)
            mean = jnp.sum(probs * grad_probs, 0, keepdims=True)
            grad_scores = (probs * (grad_probs - mean)).astype(bf16)
            pairs[g] += grad_scores.astype(f32)
            grad_value = mm(probs.astype(bf16), pull)
            grad_key = mm(grad_scores, query) * scale
            grad_query = pick_heads(mm(grad_scores, key, TN), lane_head) * scale
            grad_framed[rows, at : at + 128] = grad_query.astype(bf16)
            grad_framed[rows, C + at : C + at + 128] = grad_key.astype(bf16)
            grad_framed[rows, 2 * C + at : 2 * C + at + 128] = grad_value.astype(bf16)
    back = jnp.zeros((ROWS, C), f32)
    for c in range(6):
        cols = slice(256 * c, 256 * c + 256)
        part_wide = mm(perm_back[...], grad_framed[:, cols])
        part = part_wide.astype(bf16)
        all_packed[here, cols] = part
        if c < 2:
            small[2:3, cols] += column_sum(part_wide)
        if c >= 4:
            small[3:4, 256 * (c - 4) : 256 * (c - 4) + 256] += column_sum(part_wide)
        back = back + mm(part, weight[c].reshape(C, BLOCK), NT)
    small[0:1, :] += column_sum(back * unit)
    small[1:2, :] += column_sum(back)
    total = grad[0] + norm_back(back * vec[0:1, :], unit, spread_one)
    result[0] = total[: result.shape[1]]

    @pl.when(i == pl.num_programs(0) - 1)
    def _():
        across[0] = all_normed[...].T
        across[1] = all_merged[...].T
        hits[...] = jnp.zeros_like(hits)

        def step(r, carry):
            same = rel[...] == r
            for g in range(4):
                kept_pairs = jnp.where(same, pairs[g], 0.0)
                hits[pl.ds(r, 1), 256 * g : 256 * g + 256] = column_sum(kept_pairs)
            return carry

        lax.fori_loop(0, NREL, step, 0)
        beside[...] = jnp.zeros_like(beside)
        for z in range(4):
            beside[0, z] = lax.dot_general(
                spread[...],
                hits[:, 256 * z : 256 * z + 256],
                NT,
                precision=lax.Precision.HIGHEST,
                preferred_element_type=f32,
            ).astype(bf16)
            beside[1, z, :, 0:128] = small[:, 128 * z : 128 * z + 128].astype(bf16)
        for m in range(8):
            b = place[0] ^ m
            left = across[jnp.where(b < 6, 0, 1)]
            right = all_packed[:, pl.ds(pl.multiple_of(b * BLOCK, BLOCK), BLOCK)]
            block = mm(left, right).astype(bf16)
            out = other if m % 2 else own
            for z in range(4):
                to = (z + 4 - place[1]) & 3
                out[m // 2, to, 0, 0:128, :] = block[128 * z : 128 * z + 128]
                out[m // 2, to, 0, 128:144, :] = beside[jnp.minimum(b, 2), z]


def attention_backward(
    layer, place, grad, x, qkv, merged, totals, table, weight, vec, before, perm, rel, after
):
    images = grad.shape[0]
    pieces = (4, 4, 1, 128 + SMALL, BLOCK)
    total = images * ROWS
    out_rows = TOKENS if layer == 0 else ROWS
    return call(
        partial(attention_backward_body, len(after)),
        f"attention_backward_{layer}",
        (images,),
        [HBM] * (8 + len(after))
        + [
            per_image(ROWS, C),
            per_image(x.shape[1], C),
            per_image(FRAME, 3 * C),
            per_image(ROWS, C),
            per_image(16, QUAD * CELL),
            whole(table.shape),
            whole(vec.shape),
            whole((16, C)),
            whole((FRAME, ROWS)),
            whole((ROWS, FRAME)),
            whole((QUAD * CELL, 128)),
            whole(rel.shape),
            whole((SMALL, QUAD * CELL)),
        ],
        [per_image(out_rows, C), whole(pieces), whole(pieces)],
        [shape((images, out_rows, C), f32), shape(pieces, bf16), shape(pieces, bf16)],
        [
            pltpu.VMEM((ROWS, C), f32),
            pltpu.VMEM((FRAME, C), bf16),
            pltpu.VMEM((FRAME, 3 * C), bf16),
            pltpu.VMEM((total, C), bf16),
            pltpu.VMEM((total, 4 * C), bf16),
            pltpu.VMEM((total, C), bf16),
            pltpu.VMEM((2, C, total), bf16),
            pltpu.VMEM((4, CELL, QUAD * CELL), f32),
            pltpu.VMEM((16, C), f32),
            pltpu.VMEM((256, 4 * QUAD * CELL), f32),
            pltpu.VMEM((3, 4, SMALL, BLOCK), bf16),
            pltpu.VMEM((1, 8, 4, 128, BLOCK), bf16),
            pltpu.SemaphoreType.DMA((8, 4, 1)),
        ],
        total * C * 2048 * 10,
        images * 4000000,
        prefetch=1,
    )(
        place,
        *weight,
        *after,
        grad,
        x,
        qkv,
        merged,
        totals,
        table,
        vec,
        before,
        jnp.asarray(perm, bf16),
        jnp.asarray(perm.T, bf16),
        jnp.asarray(head_rows(), bf16),
        rel,
        jnp.asarray(head_spread(SMALL), f32),
    )


def adam_step(weight, first, second, gradient, rate, decay):
    first_new = beta_one * first + (1.0 - beta_one) * gradient
    second_new = beta_two * second + (1.0 - beta_two) * gradient * gradient
    first_hat = first_new / (1.0 - beta_one**STEP)
    second_hat = second_new / (1.0 - beta_two**STEP)
    weight_new = weight - rate * (first_hat / (jnp.sqrt(second_hat) + adam_eps) + decay * weight)
    return (weight_new, first_new, second_new)


def adam_body(place, near, far, weight, first, second, *refs):
    outs = refs[-3:]
    even = place[0] % 2 == 0
    for k in range(2):
        cols = slice(BLOCK * k, BLOCK * k + BLOCK)
        grad = jnp.where(even, near[0, 0], far[0, 0]) if k == 0 else jnp.where(even, far[0, 0], near[0, 0])
        news = adam_step(
            weight[0, :, cols], first[0, :, cols], second[0, :, cols],
            grad.astype(f32), rate_matrix, weight_decay,
        )
        for out, new in zip(outs, news):
            out[0, :, cols] = new


def adam(layer, part, place, near, far, state, done):
    parts = near.shape[1]
    spec = pl.BlockSpec(
        (1, 128, 2 * BLOCK), lambda p, j, place: (layer, 0, (part + p) * 4 + ((place[0] // 2) ^ j))
    )
    piece = pl.BlockSpec((1, 1, 128, BLOCK), lambda p, j, place: (j, p, 0, 0))
    kept = [] if done is None else list(done)
    return call(
        adam_body,
        f"adam_{layer}_{part}",
        (parts, 4),
        [piece, piece, spec, spec, spec] + [HBM] * len(kept),
        [spec] * 3,
        [shape(state[0].shape, f32)] * 3,
        [],
        0,
        7000000 * parts,
        prefetch=1,
        aliases={6 + k: k for k in range(len(kept))},
    )(place, near, far, *state, *kept)


def swap(value, bits):
    return lax.ppermute(value, "dp", [(i, i ^ bits) for i in range(8)])


def shift(value, steps):
    return lax.ppermute(value, "zero", [(i, (i + steps) % 4) for i in range(4)])


def gather_z(piece):
    return jnp.stack([piece] + [shift(piece, s) for s in range(1, 4)])


def gather_plane(stack):
    return [stack] + [swap(stack, 2 * j) for j in range(1, 4)]


def gather_core(blocks):
    return blocks + [swap(block, 1) for block in blocks]


def gather_wide(piece, dp, extra):
    fine = dp // 8
    parts, rows = piece.shape[0], piece.shape[1] - extra
    out = lax.all_gather(piece, ("dp", "zero"), axis=0, tiled=False)
    out = out.reshape(8, fine, 4, *piece.shape)
    main = out[..., :rows, :].transpose(0, 2, 3, 1, 4, 5).reshape(8, 4, parts, 128, BLOCK)
    out = jnp.concatenate([main, out[:, 0, ..., rows:, :]], 3)
    order = np.array([0, 3, 2, 1])
    return [out[2 * j + k][order] for k in range(2) for j in range(4)]


def summed(values):
    total = values[0].astype(f32)
    for value in values[1:]:
        total = total + value.astype(f32)
    return total.astype(bf16)


def reduce_core(own, other):
    return summed([own, swap(other, 1)])


def reduce_plane(stack):
    return summed([stack[0]] + [swap(stack[j], 2 * j) for j in range(1, 4)])


def reduce_z(stack):
    return summed([stack[0]] + [shift(stack[s], s) for s in range(1, 4)])


def spread_sum(piece):
    near = jnp.stack(gather_plane(piece))
    return near, swap(near, 1)


def reduce_wide(own, other, dp, extra):
    fine = dp // 8
    blocks = jnp.stack([own, other], 1).reshape(8, 4, *own.shape[2:])
    parts, rows = own.shape[2], 128 // fine
    main = blocks[..., :128, :].reshape(8, 4, parts, fine, rows, BLOCK).transpose(0, 3, 1, 2, 4, 5)
    beside = jnp.broadcast_to(
        blocks[:, None, ..., 128:, :], (8, fine, 4, parts, extra, BLOCK)
    )
    flat = jnp.concatenate([main, beside], 4).reshape(dp * 4, parts, rows + extra, BLOCK)
    mine = lax.psum_scatter(flat, ("dp", "zero"), scatter_dimension=0, tiled=True)
    out = lax.all_gather(mine[0], "dp", axis=0, tiled=False)
    out = out.reshape(8, fine, parts, rows + extra, BLOCK)
    main = out[..., :rows, :].transpose(0, 2, 1, 3, 4).reshape(8, parts, 128, BLOCK)
    out = jnp.concatenate([main, out[:, 0, :, rows:]], 2)
    return out[0::2], out[1::2]


def shards(
    dp, images, cotangent, counts, rel_index, regions,
    mat_w, mat_m, mat_v, vec_w, vec_m, vec_v, tab_w, tab_m, tab_v,
):
    near = dp == 8
    fine = dp // 8
    rows = 128 // fine
    me = lax.axis_index("dp")
    taken_from = jnp.stack([me // fine, me % fine]).astype(jnp.int32)
    spot = [me, lax.axis_index("zero")] if near else [0 * me, 0 * me]
    place = jnp.stack(spot + [counts[0]]).astype(jnp.int32)

    inside = np.arange(CELL) < WIN * WIN
    pair_ids = jnp.pad(rel_index.T, ((0, 15), (0, 15)), constant_values=-1)
    rel = jnp.tile(pair_ids, (1, QUAD))
    zones = regions.reshape(2, WIN, 2, WIN).transpose(0, 2, 1, 3).reshape(4, WIN * WIN)
    zones = jnp.pad(zones, ((0, 0), (0, 15)))
    differ = (zones[:, :, None] != zones[:, None, :]) & inside[None, None, :]
    outside = jnp.asarray(np.where(inside, 0.0, -1e30), f32)[None, :, None]
    mask_shifted = jnp.tile(jnp.where(differ, mask_value, 0.0) + outside, (1, 1, QUAD)).astype(f32)
    mask_plain = jnp.broadcast_to(outside, (1, CELL, QUAD * CELL))
    masks = (mask_plain, mask_shifted)
    perms = (frames(False), frames(True))

    def piece(layer, part, parts):
        at = (layer, taken_from[1] * rows, taken_from[0] * BLOCK)
        pieces = [
            lax.dynamic_slice(mat_w, (at[0], at[1], (part + p) * HID + at[2]), (1, rows, BLOCK))
            for p in range(parts)
        ]
        return jnp.concatenate(pieces, 0).astype(bf16)

    packed = pack(taken_from, rows, mat_w, rel, tab_w, vec_w)[None]
    if near:
        z_heads0 = gather_z(packed)
        z_mlp0 = gather_z(piece(0, 1, 2))
        p_heads0 = gather_plane(z_heads0)
        heads0 = gather_core(p_heads0)
        p_mlp0 = gather_plane(z_mlp0)
        z_heads1 = gather_z(piece(1, 0, 1))
        z_mlp1 = gather_z(piece(1, 1, 2))
        mlp0 = gather_core(p_mlp0)
        p_heads1 = gather_plane(z_heads1)
        heads1 = gather_core(p_heads1)
        p_mlp1 = gather_plane(z_mlp1)
        mlp1 = gather_core(p_mlp1)
    else:
        heads0 = gather_wide(packed, dp, EXTRA)
        mlp0 = gather_wide(piece(0, 1, 2), dp, 0)
        heads1 = gather_wide(piece(1, 0, 1), dp, 0)
        mlp1 = gather_wide(piece(1, 1, 2), dp, 0)
        p_heads1, p_mlp1 = [], []
    attention_w = (heads0, heads1)
    mlp_w = (mlp0, mlp1)

    stream = images
    saved = []
    for layer in range(2):
        mid, qkv, merged, totals, table, vec = attention_forward(
            layer, place, stream, attention_w[layer], heads0, masks[layer], perms[layer],
            p_mlp1 if layer else [],
        )
        result, act, slope = mlp_forward(
            layer, layer == 1, place, mid, mlp_w[layer], vec, [] if layer else p_heads1
        )
        saved.append((stream, mid, qkv, merged, totals, table, vec, act, slope))
        stream = result
    activations = stream

    def backward(layer, gradient, after_mlp, after_attention):
        x, mid, qkv, merged, totals, table, vec, act, slope = saved[layer]
        grad_mid, own, other, small = mlp_backward(
            layer, place, gradient, act, slope, mid, mlp_w[layer], vec, after_mlp
        )
        later = after_attention(own, other)
        gradient, own, other = attention_backward(
            layer, place, grad_mid, x, qkv, merged, totals, table, attention_w[layer], vec, small,
            perms[layer], rel, later,
        )
        return gradient, (own, other)

    sums = {}
    if near:
        held = {}

        def first_window(own, other):
            held["mlp1"] = (own, other)
            return []

        gradient, heads = backward(1, cotangent, [], first_window)
        core_mlp1 = reduce_core(*held["mlp1"])
        x, mid, qkv, merged, totals, table, vec, act, slope = saved[0]

        def second_window(own, other):
            held["mlp0"] = (own, other)
            held["plane_mlp1"] = reduce_plane(core_mlp1)
            held["core_heads1"] = reduce_core(*heads)
            return [held["plane_mlp1"], held["core_heads1"]]

        gradient, heads_last = backward(0, gradient, [core_mlp1], second_window)
        sums[1, 1] = spread_sum(reduce_z(held["plane_mlp1"]))
        sums[1, 0] = spread_sum(reduce_z(reduce_plane(held["core_heads1"])))
        sums[0, 1] = spread_sum(reduce_z(reduce_plane(reduce_core(*held["mlp0"]))))
        sums[0, 0] = spread_sum(reduce_z(reduce_plane(reduce_core(*heads_last))))
    else:
        gradient = cotangent
        for layer in (1, 0):
            held = []
            gradient, heads = backward(layer, gradient, [], lambda *pair: held.append(pair) or [])
            sums[layer, 1] = reduce_wide(*held[0], dp, 0)
            sums[layer, 0] = reduce_wide(*heads, dp, SMALL)

    state = (mat_w, mat_m, mat_v)
    done = None
    for layer, part in ((1, 1), (1, 0), (0, 1), (0, 0)):
        done = adam(layer, part, place, *sums[layer, part], state, done)

    def beside(block):
        m = place[0] ^ block
        found = []
        for layer in range(2):
            both = jnp.concatenate([half[:, 0, 128:] for half in sums[layer, 0]])
            found.append(lax.dynamic_index_in_dim(both, (m % 2) * 4 + m // 2, 0, False))
        return jnp.stack(found).astype(f32)

    new_vec = adam_step(vec_w, vec_m, vec_v, beside(1)[:, 0:12, 0:128], rate_vector, 0.0)
    new_tab = adam_step(tab_w, tab_m, tab_v, beside(0)[:, 0:4, 0:NREL], rate_table, 0.0)
    return (activations, gradient, *done, *new_vec, *new_tab)


def solution(mesh):
    images = P(("dp", "zero"), None, None)
    rows = P(None, "zero", None)
    lanes = P(None, None, "zero")
    return jax.shard_map(
        partial(shards, mesh.shape["dp"]),
        mesh=mesh,
        in_specs=(images, images, P(("dp", "zero")), P(), P())
        + (rows,) * 3 + (lanes,) * 3 + (rows,) * 3,
        out_specs=(images, images) + (rows,) * 3 + (lanes,) * 3 + (rows,) * 3,
        check_vma=False,
    )
```

```python
from functools import partial

import jax
import jax.numpy as jnp
import numpy as np
from jax import lax
from jax.experimental import pallas as pl
from jax.experimental.pallas import tpu as pltpu
from jax.sharding import PartitionSpec as P

WIN = 7
SIDE = 14
STEP = 10
NREL = 169
C = 512
HID = 2048
TOKENS = SIDE * SIDE
PAIR = 2
ROWS = 208
FRAME = 256
CELL = 64
QUAD = 4
BLOCK = 256
EXTRA = 32
SMALL = 16

norm_eps = 1e-05
mask_value = -100.0
beta_one = 0.9
beta_two = 0.999
adam_eps = 1e-08
weight_decay = 0.05
rate_matrix = 0.1
rate_vector = 0.5
rate_table = 1.0
scale = 32 ** (-0.5)

bf16 = jnp.bfloat16
f32 = jnp.float32
NN = (((1,), (0,)), ((), ()))
NT = (((1,), (1,)), ((), ()))
TN = (((0,), (0,)), ((), ()))


def mm(left, right, dims=NN):
    return lax.dot_general(left, right, dims, preferred_element_type=f32)


def frames(shifted):
    move = WIN // 2 if shifted else 0
    placed = np.zeros((FRAME, ROWS), np.float32)
    for wy in range(2):
        for wx in range(2):
            for iy in range(WIN):
                for ix in range(WIN):
                    y = (wy * WIN + iy + move) % SIDE
                    x = (wx * WIN + ix + move) % SIDE
                    placed[(wy * 2 + wx) * CELL + iy * WIN + ix, y * SIDE + x] = 1
    return placed


def head_rows():
    rows = np.zeros((QUAD * CELL, 128), np.float32)
    for h in range(QUAD):
        rows[h * CELL : (h + 1) * CELL, h * 32 : (h + 1) * 32] = 1
    return rows


def head_spread(rows):
    out = np.zeros((rows, QUAD * CELL), np.float32)
    for h in range(QUAD):
        out[h, h * CELL : (h + 1) * CELL] = 1
    return out


def norm(rows):
    centred = rows - jnp.mean(rows, -1, keepdims=True)
    spread = lax.rsqrt(jnp.mean(centred * centred, -1, keepdims=True) + norm_eps)
    return centred * spread, spread


def norm_back(grad_unit, unit, spread):
    return spread * (
        grad_unit
        - jnp.mean(grad_unit, -1, keepdims=True)
        - unit * jnp.mean(grad_unit * unit, -1, keepdims=True)
    )


def column_sum(rows):
    return jnp.sum(rows, 0, keepdims=True)


def gelu_pair(u):
    size = jnp.abs(u)
    below = 1.0 + (0.3275911 * 0.5**0.5) * size
    t = pltpu.reciprocal(below, approx=True)
    bell = jnp.exp2(u * u * (-0.5 * 1.4426950408889634))
    poly = t * (
        0.127414796 + t * (-0.142248368 + t * (0.710706871 + t * (-0.726576013 + t * 0.530702714)))
    )
    tail = poly * bell
    phi = jnp.where(u >= 0, 1.0 - tail, tail)
    return u * phi, phi + u * bell * 0.3989422804014327


def quad_rows(part, heads):
    return jnp.concatenate([part] * QUAD, 0) * heads


def pick_heads(stacked, lane_head):
    low = jnp.where(lane_head == 0, stacked[:CELL], stacked[CELL : 2 * CELL])
    high = jnp.where(lane_head == 2, stacked[2 * CELL : 3 * CELL], stacked[3 * CELL :])
    return jnp.where(lane_head < 2, low, high)


def lane_heads():
    return lax.broadcasted_iota(jnp.int32, (CELL, 128), 1) // 32


def whole(shape):
    zero = (0,) * len(shape)
    return pl.BlockSpec(shape, lambda *_: zero, pipeline_mode=pl.Buffered(1))


def per_image(rows, cols):
    return pl.BlockSpec((1, rows, cols), lambda i, *_: (i, 0, 0))


def per_pair(rows, cols):
    return pl.BlockSpec((PAIR, rows, cols), lambda i, *_: (i, 0, 0))


HBM = pl.BlockSpec(memory_space=pl.ANY)


def weight_copies(place, stacks, kept, sems, first_row=0):
    copies = []
    parts, rows = kept.shape[0], kept.shape[3]
    for k in range(2):
        for j in range(4):
            block = place[0] ^ (2 * j + k)
            for s in range(4):
                owner = (place[1] + 4 - s) & 3
                for p in range(parts):
                    copies.append(
                        pltpu.make_async_copy(
                            stacks[k].at[j, s, p, pl.ds(first_row, rows), :],
                            kept.at[p, block, owner],
                            sems.at[k * 4 + j, s, p],
                        )
                    )
    return copies


def fetch(copies):
    for copy in copies:
        copy.start()
    for copy in copies:
        copy.wait()


def call(body, name, grid, ins, outs, out_shapes, scratch, flops, moved, prefetch=0, aliases=None):
    return pl.pallas_call(
        body,
        name=name,
        grid_spec=pltpu.PrefetchScalarGridSpec(
            num_scalar_prefetch=prefetch,
            grid=grid,
            in_specs=ins,
            out_specs=outs,
            scratch_shapes=scratch,
        ),
        out_shape=out_shapes,
        input_output_aliases=aliases or {},
        compiler_params=pltpu.CompilerParams(
            dimension_semantics=("arbitrary",) * len(grid), vmem_limit_bytes=58 * 1024 * 1024
        ),
        cost_estimate=pl.CostEstimate(flops=flops, bytes_accessed=moved, transcendentals=0),
    )


def shape(dims, kind):
    return jax.ShapeDtypeStruct(dims, kind)


def pack_body(place, mat, pair_index, tab, vec, spread, out, rel, spread_tab, small):
    rows = mat.shape[1]
    out[0, 0:rows, :] = mat[0].astype(bf16)
    rel[...] = jnp.full(rel.shape, -1, jnp.int32)
    across = pair_index[...].astype(f32).T.astype(jnp.int32)
    for h in range(QUAD):
        rel[0 : WIN * WIN, CELL * h : CELL * h + WIN * WIN] = across
    for layer in range(2):
        spread_tab[layer, 0:NREL, :] = mm(tab[layer].astype(bf16), spread[...], TN)
    pairs = rel[pl.ds(pl.multiple_of(place[0] * 8, 8), 8), :]

    def step(r, sums):
        hit = pairs == r
        return tuple(
            jnp.where(hit, spread_tab[layer, pl.ds(r, 1), :], sums[layer]) for layer in range(2)
        )

    start = jnp.zeros((8, QUAD * CELL), f32)
    first, second = lax.fori_loop(0, NREL, step, (start, start))
    out[0, rows : rows + 16, :] = jnp.concatenate([first, second], 0).astype(bf16)
    small[...] = jnp.zeros_like(small)
    row = jnp.minimum(place[0] * 2, 10)
    for layer in range(2):
        for k in range(2):
            small[k : k + 1, layer * 128 : (layer + 1) * 128] = vec[row + k, layer : layer + 1, :]
    out[0, rows + 16 : rows + 32, :] = small[...].astype(bf16)


def pack(place, rows, mat_w, rel_index, tab_w, vec_w):
    vec_w = vec_w.transpose(1, 0, 2)
    return call(
        pack_body,
        "pack",
        (1,),
        [
            pl.BlockSpec((1, rows, BLOCK), lambda i, place: (0, place[1], place[0])),
            whole(rel_index.shape),
            whole(tab_w.shape),
            whole(vec_w.shape),
            whole((QUAD, QUAD * CELL)),
        ],
        [whole((1, rows + EXTRA, BLOCK)), whole((CELL, QUAD * CELL))],
        [shape((1, rows + EXTRA, BLOCK), bf16), shape((CELL, QUAD * CELL), jnp.int32)],
        [pltpu.VMEM((2, 176, QUAD * CELL), f32), pltpu.VMEM((16, 256), f32)],
        0,
        400000,
        prefetch=1,
    )(place, mat_w, rel_index, tab_w, vec_w, jnp.asarray(head_spread(QUAD), bf16))


def cut_body(place, mat, *refs):
    refs[-1][0] = mat[0].astype(bf16)


def cut(place, rows, mat_w, layer, part, parts, after):
    return call(
        cut_body,
        f"cut_{layer}_{part}",
        (parts,),
        [
            pl.BlockSpec(
                (1, rows, BLOCK), lambda i, place: (layer, place[1], (part + i) * 8 + place[0])
            )
        ]
        + [HBM] * len(after),
        pl.BlockSpec((1, rows, BLOCK), lambda i, place: (i, 0, 0)),
        shape((parts, rows, BLOCK), bf16),
        [],
        0,
        200000 * parts,
        prefetch=1,
    )(place, mat_w, *after)


def attention_forward_body(layer, waits, place, *refs):
    arrays, extras, refs = refs[:2], refs[2:4], refs[4 + waits :]
    x, mask, perm, perm_back, heads = refs[:5]
    mid, qkv, merged, totals, table, vec, x_rows, framed, kept, extra_kept, sems, more_sems = refs[5:]
    weight, extra = kept.at[0], extra_kept.at[0]

    @pl.when(pl.program_id(0) == 0)
    def _():
        fetch(
            weight_copies(place, arrays, kept, sems)
            + weight_copies(place, extras, extra_kept, more_sems, 128)
        )
        x_rows[...] = jnp.zeros_like(x_rows)
        vec[...] = jnp.zeros_like(vec)
        for z in range(4):
            for d in range(8):
                pair = extra[d, z, 0:16, :].astype(f32)
                bias = pair[8 * layer : 8 * layer + 8]
                for w in range(table.shape[0]):
                    table[w, z, 8 * d : 8 * d + 8, :] = bias + mask[w, 8 * d : 8 * d + 8, :]
                if d < 6:
                    rows = extra[d, z, 16:32, 128 * layer : 128 * layer + 128].astype(f32)
                    vec[2 * d : 2 * d + 2, 128 * z : 128 * z + 128] = rows[0:2]

    if x.shape[1] == ROWS:
        stream = x[0]
    else:
        x_rows[0:TOKENS, :] = x[0].astype(f32)
        stream = x_rows[...]
    unit, _ = norm(stream)
    normed = (unit * vec[0:1, :] + vec[1:2, :]).astype(bf16)
    normed = mm(perm[...], normed).astype(bf16)
    for c in range(6):
        part = mm(normed, weight[c].reshape(C, BLOCK))
        if c < 2:
            part = part + vec[2:3, 256 * c : 256 * c + 256]
        if c >= 4:
            part = part + vec[3:4, 256 * (c - 4) : 256 * (c - 4) + 256]
        qkv[0, :, 256 * c : 256 * c + 256] = part.astype(bf16)
    lane_head = lane_heads()
    for w in range(4):
        rows = slice(CELL * w, CELL * w + CELL)
        at = [128 * g for g in range(4)]
        query = [quad_rows(qkv[0, rows, c : c + 128], heads[...]) for c in at]
        scores = [mm(qkv[0, rows, C + at[g] : C + at[g] + 128], query[g], NT) for g in range(4)]
        probs = []
        for g in range(4):
            shifted = scores[g] * scale + table[w % table.shape[0], g]
            top = jnp.max(shifted, 0, keepdims=True)
            raised = jnp.exp(shifted - top)
            total = jnp.sum(raised, 0, keepdims=True)
            totals[0, 4 * w + g : 4 * w + g + 1, :] = top + jnp.log(total)
            probs.append((raised * (1.0 / total)).astype(bf16))
        stacked = [mm(probs[g], qkv[0, rows, 2 * C + at[g] : 2 * C + at[g] + 128], TN) for g in range(4)]
        for g in range(4):
            framed[rows, at[g] : at[g] + 128] = pick_heads(stacked[g], lane_head).astype(bf16)
    gathered = mm(perm_back[...], framed[...]).astype(bf16)
    merged[0] = gathered
    for c in range(2):
        cols = slice(256 * c, 256 * c + 256)
        mid[0, :, cols] = (
            stream[:, cols] + mm(gathered, weight[6 + c].reshape(C, BLOCK)) + vec[4:5, cols]
        )


def attention_forward(layer, place, x, weight, extra, mask, perm, after):
    images = x.shape[0]
    tables = mask.shape[0]
    return call(
        partial(attention_forward_body, layer, len(after)),
        f"attention_forward_{layer}",
        (images,),
        [HBM] * (4 + len(after))
        + [
            per_image(x.shape[1], C),
            whole(mask.shape),
            whole((FRAME, ROWS)),
            whole((ROWS, FRAME)),
            whole((QUAD * CELL, 128)),
        ],
        [
            per_image(ROWS, C),
            per_image(FRAME, 3 * C),
            per_image(ROWS, C),
            per_image(16, QUAD * CELL),
            pl.BlockSpec((tables, 4, CELL, QUAD * CELL), lambda i, *_: (0, 0, 0, 0)),
            pl.BlockSpec((16, C), lambda i, *_: (0, 0)),
        ],
        [
            shape((images, ROWS, C), f32),
            shape((images, FRAME, 3 * C), bf16),
            shape((images, ROWS, C), bf16),
            shape((images, 16, QUAD * CELL), f32),
            shape((tables, 4, CELL, QUAD * CELL), f32),
            shape((16, C), f32),
        ],
        [
            pltpu.VMEM((ROWS, C), f32),
            pltpu.VMEM((FRAME, C), bf16),
            pltpu.VMEM((1, 8, 4, 128, BLOCK), bf16),
            pltpu.VMEM((1, 8, 4, EXTRA, BLOCK), bf16),
            pltpu.SemaphoreType.DMA((8, 4, 1)),
            pltpu.SemaphoreType.DMA((8, 4, 1)),
        ],
        images * 256 * C * 2048 * 4,
        images * 2500000,
        prefetch=1,
    )(
        place,
        *weight,
        *extra,
        *after,
        x,
        mask,
        jnp.asarray(perm, bf16),
        jnp.asarray(perm.T, bf16),
        jnp.asarray(head_rows(), bf16),
    )


def mlp_forward_body(last, waits, place, *refs):
    arrays, refs = refs[:2], refs[2 + waits :]
    mid, vec, result, act, slope, kept, sems = refs
    first, second = kept.at[0], kept.at[1]

    @pl.when(pl.program_id(0) == 0)
    def _():
        fetch(weight_copies(place, arrays, kept, sems))

    rows = PAIR * ROWS
    stream = mid[...].reshape(rows, C)
    unit, _ = norm(stream)
    normed = (unit * vec[5:6, :] + vec[6:7, :]).astype(bf16)
    total = stream + vec[7:8, :]
    for c in range(8):
        bias = vec[8 + c // 2 : 9 + c // 2, 256 * (c % 2) : 256 * (c % 2) + 256]
        value, pull = gelu_pair(mm(normed, first[c].reshape(C, BLOCK)) + bias)
        value = value.astype(bf16)
        act[:, :, 256 * c : 256 * c + 256] = value.reshape(PAIR, ROWS, BLOCK)
        slope[:, :, 256 * c : 256 * c + 256] = pull.astype(bf16).reshape(PAIR, ROWS, BLOCK)
        total = total + mm(value, second[c].reshape(C, BLOCK), NT)
    if last:
        for n in range(PAIR):
            alive = (pl.program_id(0) * PAIR + n < place[2]).astype(f32)
            result[n] = (total[n * ROWS : n * ROWS + TOKENS] * alive).astype(bf16)
    else:
        result[...] = total.reshape(PAIR, ROWS, C)


def mlp_forward(layer, last, place, mid, weight, vec, after):
    images = mid.shape[0]
    out = (images, TOKENS, C) if last else (images, ROWS, C)
    return call(
        partial(mlp_forward_body, last, len(after)),
        f"mlp_forward_{layer}",
        (images // PAIR,),
        [HBM] * (2 + len(after)) + [per_pair(ROWS, C), whole(vec.shape)],
        [per_pair(out[1], C), per_pair(ROWS, HID), per_pair(ROWS, HID)],
        [
            shape(out, bf16 if last else f32),
            shape((images, ROWS, HID), bf16),
            shape((images, ROWS, HID), bf16),
        ],
        [pltpu.VMEM((2, 8, 4, 128, BLOCK), bf16), pltpu.SemaphoreType.DMA((8, 4, 2))],
        images * ROWS * C * HID * 4,
        images * 3000000,
        prefetch=1,
    )(place, *weight, *after, mid, vec)


def mlp_backward_body(waits, place, *refs):
    arrays, refs = refs[:2], refs[2 + waits :]
    grad, act, slope, mid, vec, grad_mid, own, other, small = refs[:9]
    grad_rows, all_grad, all_act, all_inner, all_normed, kept, sems = refs[9:]
    first, second = kept.at[0], kept.at[1]
    i = pl.program_id(0)

    @pl.when(i == 0)
    def _():
        fetch(weight_copies(place, arrays, kept, sems))
        grad_rows[...] = jnp.zeros_like(grad_rows)
        small[...] = jnp.zeros_like(small)

    rows = PAIR * ROWS
    if grad.shape[1] == ROWS:
        grad_out = grad[...].reshape(rows, C)
    else:
        for n in range(PAIR):
            alive = (i * PAIR + n < place[2]).astype(f32)
            grad_rows[n * ROWS : n * ROWS + TOKENS, :] = grad[n].astype(f32) * alive
        grad_out = grad_rows[...]
    here = pl.ds(pl.multiple_of(i * rows, 32), rows)
    low = grad_out.astype(bf16)
    all_grad[here, :] = low
    small[7:8, :] += column_sum(low.astype(f32))
    all_act[here, :] = act[...].reshape(rows, HID)
    unit, spread = norm(mid[...].reshape(rows, C))
    all_normed[here, :] = (unit * vec[5:6, :] + vec[6:7, :]).astype(bf16)
    back = jnp.zeros((rows, C), f32)
    for c in range(8):
        cols = slice(256 * c, 256 * c + 256)
        pull = slope[:, :, cols].reshape(rows, BLOCK).astype(f32)
        inner = (mm(low, second[c].reshape(C, BLOCK)) * pull).astype(bf16)
        all_inner[here, cols] = inner
        row, lane = 8 + c // 2, 256 * (c % 2)
        small[row : row + 1, lane : lane + 256] += column_sum(inner.astype(f32))
        back = back + mm(inner, first[c].reshape(C, BLOCK), NT)
    small[5:6, :] += column_sum(back * unit)
    small[6:7, :] += column_sum(back)
    grad_mid[...] = (grad_out + norm_back(back * vec[5:6, :], unit, spread)).reshape(PAIR, ROWS, C)

    @pl.when(i == pl.num_programs(0) - 1)
    def _():
        grad_across = all_grad[...].T
        normed_across = all_normed[...].T
        for m in range(8):
            cols = pl.ds(pl.multiple_of((place[0] ^ m) * BLOCK, BLOCK), BLOCK)
            out = other if m % 2 else own
            for p, block in enumerate(
                (mm(normed_across, all_inner[:, cols]), mm(grad_across, all_act[:, cols]))
            ):
                block = block.astype(bf16)
                for z in range(4):
                    out[m // 2, (z + 4 - place[1]) & 3, p] = block[128 * z : 128 * z + 128]


def mlp_backward(layer, place, grad, act, slope, mid, weight, vec, after):
    images = mid.shape[0]
    total = images * ROWS
    pieces = (4, 4, 2, 128, BLOCK)
    return call(
        partial(mlp_backward_body, len(after)),
        f"mlp_backward_{layer}",
        (images // PAIR,),
        [HBM] * (2 + len(after))
        + [
            per_pair(grad.shape[1], C),
            per_pair(ROWS, HID),
            per_pair(ROWS, HID),
            per_pair(ROWS, C),
            whole(vec.shape),
        ],
        [per_pair(ROWS, C), whole(pieces), whole(pieces), whole((16, C))],
        [
            shape((images, ROWS, C), f32),
            shape(pieces, bf16),
            shape(pieces, bf16),
            shape((16, C), f32),
        ],
        [
            pltpu.VMEM((PAIR * ROWS, C), f32),
            pltpu.VMEM((total, C), bf16),
            pltpu.VMEM((total, HID), bf16),
            pltpu.VMEM((total, HID), bf16),
            pltpu.VMEM((total, C), bf16),
            pltpu.VMEM((2, 8, 4, 128, BLOCK), bf16),
            pltpu.SemaphoreType.DMA((8, 4, 2)),
        ],
        total * C * HID * 8,
        images * 4000000,
        prefetch=1,
    )(place, *weight, *after, grad, act, slope, mid, vec)


def attention_backward_body(waits, resumed, ends, place, *refs):
    arrays, refs = refs[:2], refs[2 + waits :]
    if resumed:
        (own_before, other_before, pairs_before), refs = refs[1:4], refs[4:]
    grad, x, qkv, merged, totals, table, vec, before = refs[:8]
    perm, perm_back, heads, rel, spread, result, own, other, pairs, small = refs[8:18]
    x_rows, framed, grad_framed, all_normed, all_packed, all_merged = refs[18:24]
    across, hits, beside, kept, sems = refs[24:]
    weight = kept.at[0]
    i = pl.program_id(0)

    @pl.when(i == 0)
    def _():
        fetch(weight_copies(place, arrays, kept, sems))
        x_rows[...] = jnp.zeros_like(x_rows)
        small[...] = before[...]
        pairs[...] = pairs_before[...] if resumed else jnp.zeros_like(pairs)

    if x.shape[1] == ROWS:
        stream = x[0]
    else:
        x_rows[0:TOKENS, :] = x[0].astype(f32)
        stream = x_rows[...]
    here = pl.ds(pl.multiple_of(i * ROWS, 16), ROWS)
    unit, spread_one = norm(stream)
    all_normed[here, :] = (unit * vec[0:1, :] + vec[1:2, :]).astype(bf16)
    low = grad[0].astype(bf16)
    all_packed[here, 3 * C :] = low
    all_merged[here, :] = merged[0]
    small[4:5, :] += column_sum(low.astype(f32))
    moved = mm(perm[...], low).astype(bf16)
    from_heads = mm(moved[:, :BLOCK], weight[6].reshape(C, BLOCK), NT)
    from_heads = from_heads + mm(moved[:, BLOCK:], weight[7].reshape(C, BLOCK), NT)
    framed[...] = from_heads.astype(bf16)
    lane_head = lane_heads()
    for w in range(4):
        rows = slice(CELL * w, CELL * w + CELL)
        at = [128 * g for g in range(4)]
        keys = [qkv[0, rows, C + c : C + c + 128] for c in at]
        query = [quad_rows(qkv[0, rows, c : c + 128], heads[...]) for c in at]
        pull = [quad_rows(framed[rows, c : c + 128], heads[...]) for c in at]
        scores = [mm(keys[g], query[g], NT) for g in range(4)]
        grad_probs = [
            mm(qkv[0, rows, 2 * C + at[g] : 2 * C + at[g] + 128], pull[g], NT) for g in range(4)
        ]
        probs, grad_scores = [], []
        for g in range(4):
            shifted = scores[g] * scale + table[w % table.shape[0], g]
            prob = jnp.exp(shifted - totals[0, 4 * w + g : 4 * w + g + 1, :])
            mean = jnp.sum(prob * grad_probs[g], 0, keepdims=True)
            grad_score = (prob * (grad_probs[g] - mean)).astype(bf16)
            pairs[g] += grad_score.astype(f32)
            probs.append(prob.astype(bf16))
            grad_scores.append(grad_score)
        for g in range(4):
            grad_value = mm(probs[g], pull[g])
            grad_framed[rows, 2 * C + at[g] : 2 * C + at[g] + 128] = grad_value.astype(bf16)
        for g in range(4):
            grad_key = mm(grad_scores[g], query[g]) * scale
            grad_framed[rows, C + at[g] : C + at[g] + 128] = grad_key.astype(bf16)
        for g in range(4):
            grad_query = pick_heads(mm(grad_scores[g], keys[g], TN), lane_head) * scale
            grad_framed[rows, at[g] : at[g] + 128] = grad_query.astype(bf16)
    back = jnp.zeros((ROWS, C), f32)
    for c in range(6):
        cols = slice(256 * c, 256 * c + 256)
        part_wide = mm(perm_back[...], grad_framed[:, cols])
        part = part_wide.astype(bf16)
        all_packed[here, cols] = part
        if c < 2:
            small[2:3, cols] += column_sum(part_wide)
        if c >= 4:
            small[3:4, 256 * (c - 4) : 256 * (c - 4) + 256] += column_sum(part_wide)
        back = back + mm(part, weight[c].reshape(C, BLOCK), NT)
    small[0:1, :] += column_sum(back * unit)
    small[1:2, :] += column_sum(back)
    total = grad[0] + norm_back(back * vec[0:1, :], unit, spread_one)
    result[0] = total[: result.shape[1]]

    @pl.when(i == pl.num_programs(0) - 1)
    def _():
        across[0] = all_normed[...].T
        across[1] = all_merged[...].T
        beside[...] = jnp.zeros_like(beside)
        if ends:
            hits[...] = jnp.zeros_like(hits)

            def step(r, carry):
                same = rel[...] == r
                for g in range(4):
                    kept_pairs = jnp.where(same, pairs[g], 0.0)
                    hits[pl.ds(r, 1), 256 * g : 256 * g + 256] = column_sum(kept_pairs)
                return carry

            lax.fori_loop(0, NREL, step, 0)
            for z in range(4):
                beside[0, z] = lax.dot_general(
                    spread[...],
                    hits[:, 256 * z : 256 * z + 256],
                    NT,
                    precision=lax.Precision.HIGHEST,
                    preferred_element_type=f32,
                ).astype(bf16)
                beside[1, z, :, 0:128] = small[:, 128 * z : 128 * z + 128].astype(bf16)
        for m in range(8):
            b = place[0] ^ m
            left = across[jnp.where(b < 6, 0, 1)]
            right = all_packed[:, pl.ds(pl.multiple_of(b * BLOCK, BLOCK), BLOCK)]
            block = mm(left, right)
            out = other if m % 2 else own
            for z in range(4):
                to = (z + 4 - place[1]) & 3
                new = block[128 * z : 128 * z + 128]
                if resumed:
                    old = other_before if m % 2 else own_before
                    new = new + old[m // 2, to, 0, 0:128, :].astype(f32)
                out[m // 2, to, 0, 0:128, :] = new.astype(bf16)
                out[m // 2, to, 0, 128:144, :] = beside[jnp.minimum(b, 2), z]


def attention_backward(
    layer, place, grad, x, qkv, merged, totals, table, weight, vec, small, perm, rel, after,
    first=0, count=None, resume=None,
):
    images = grad.shape[0]
    count = count or images
    pieces = (4, 4, 1, 128 + SMALL, BLOCK)
    pairs = (4, CELL, QUAD * CELL)
    total = count * ROWS
    out_rows = TOKENS if layer == 0 else ROWS

    def image(rows, cols):
        return pl.BlockSpec((1, rows, cols), lambda i, *_: (i + first, 0, 0))

    resumed = list(resume or [])
    return call(
        partial(
            attention_backward_body, len(after), bool(resumed), first + count == images
        ),
        f"attention_backward_{layer}_{first}",
        (count,),
        [HBM] * (2 + len(after))
        + ([HBM, whole(pieces), whole(pieces), whole(pairs)] if resumed else [])
        + [
            image(ROWS, C),
            image(x.shape[1], C),
            image(FRAME, 3 * C),
            image(ROWS, C),
            image(16, QUAD * CELL),
            whole(table.shape),
            whole(vec.shape),
            whole((16, C)),
            whole((FRAME, ROWS)),
            whole((ROWS, FRAME)),
            whole((QUAD * CELL, 128)),
            whole(rel.shape),
            whole((SMALL, QUAD * CELL)),
        ],
        [image(out_rows, C), whole(pieces), whole(pieces), whole(pairs), whole((16, C))],
        [
            shape((images, out_rows, C), f32),
            shape(pieces, bf16),
            shape(pieces, bf16),
            shape(pairs, f32),
            shape((16, C), f32),
        ],
        [
            pltpu.VMEM((ROWS, C), f32),
            pltpu.VMEM((FRAME, C), bf16),
            pltpu.VMEM((FRAME, 3 * C), bf16),
            pltpu.VMEM((total, C), bf16),
            pltpu.VMEM((total, 4 * C), bf16),
            pltpu.VMEM((total, C), bf16),
            pltpu.VMEM((2, C, total), bf16),
            pltpu.VMEM((256, 4 * QUAD * CELL), f32),
            pltpu.VMEM((3, 4, SMALL, BLOCK), bf16),
            pltpu.VMEM((1, 8, 4, 128, BLOCK), bf16),
            pltpu.SemaphoreType.DMA((8, 4, 1)),
        ],
        total * C * 2048 * 10,
        images * 4000000,
        prefetch=1,
        aliases={3 + len(after): 0} if resumed else None,
    )(
        place,
        *weight,
        *after,
        *resumed,
        grad,
        x,
        qkv,
        merged,
        totals,
        table,
        vec,
        small,
        jnp.asarray(perm, bf16),
        jnp.asarray(perm.T, bf16),
        jnp.asarray(head_rows(), bf16),
        rel,
        jnp.asarray(head_spread(SMALL), f32),
    )


def adam_step(weight, first, second, gradient, rate, decay):
    first_new = beta_one * first + (1.0 - beta_one) * gradient
    second_new = beta_two * second + (1.0 - beta_two) * gradient * gradient
    first_hat = first_new / (1.0 - beta_one**STEP)
    second_hat = second_new / (1.0 - beta_two**STEP)
    weight_new = weight - rate * (first_hat / (jnp.sqrt(second_hat) + adam_eps) + decay * weight)
    return (weight_new, first_new, second_new)


def adam_body(place, near, far, weight, first, second, *refs):
    outs = refs[-3:]
    for j in range(2):
        for k in range(2):
            block = (((place[0] // 2) & 1) ^ j) * 2 + ((place[0] & 1) ^ k)
            cols = pl.ds(pl.multiple_of(block * BLOCK, BLOCK), BLOCK)
            grad = (far if k else near)[j, 0].astype(f32)
            news = adam_step(
                weight[0, :, cols], first[0, :, cols], second[0, :, cols],
                grad, rate_matrix, weight_decay,
            )
            for out, new in zip(outs, news):
                out[0, :, cols] = new


def adam(layer, part, place, near, far, state, done):
    parts = near.shape[1]
    spec = pl.BlockSpec(
        (1, 128, 4 * BLOCK), lambda p, j, place: (layer, 0, (part + p) * 2 + ((place[0] // 4) ^ j))
    )
    piece = pl.BlockSpec((2, 1, 128, BLOCK), lambda p, j, place: (j, p, 0, 0))
    kept = [] if done is None else list(done)
    return call(
        adam_body,
        f"adam_{layer}_{part}",
        (parts, 2),
        [piece, piece, spec, spec, spec] + [HBM] * len(kept),
        [spec] * 3,
        [shape(state[0].shape, f32)] * 3,
        [],
        0,
        7000000 * parts,
        prefetch=1,
        aliases={6 + k: k for k in range(len(kept))},
    )(place, near, far, *state, *kept)


def swap(value, bits):
    return lax.ppermute(value, "dp", [(i, i ^ bits) for i in range(8)])


def shift(value, steps):
    return lax.ppermute(value, "zero", [(i, (i + steps) % 4) for i in range(4)])


def gather_z(piece):
    return jnp.stack([piece] + [shift(piece, s) for s in range(1, 4)])


def gather_plane(stack):
    return jnp.stack([stack] + [swap(stack, 2 * j) for j in range(1, 4)])


def gather_core(blocks):
    return [blocks, swap(blocks, 1)]


def gather_wide(piece, dp, extra):
    fine = dp // 8
    parts, rows = piece.shape[0], piece.shape[1] - extra
    out = lax.all_gather(piece, ("dp", "zero"), axis=0, tiled=False)
    out = out.reshape(8, fine, 4, *piece.shape)
    main = out[..., :rows, :].transpose(0, 2, 3, 1, 4, 5).reshape(8, 4, parts, 128, BLOCK)
    out = jnp.concatenate([main, out[:, 0, ..., rows:, :]], 3)
    order = np.array([0, 3, 2, 1])
    return [out[k::2][:, order] for k in range(2)]


def summed(values):
    total = values[0].astype(f32)
    for value in values[1:]:
        total = total + value.astype(f32)
    return total.astype(bf16)


def reduce_core(own, other):
    return summed([own, swap(other, 1)])


def reduce_plane(stack):
    return summed([stack[0]] + [swap(stack[j], 2 * j) for j in range(1, 4)])


def reduce_z(stack):
    return summed([stack[0]] + [shift(stack[s], s) for s in range(1, 4)])


def spread_sum(piece):
    near = gather_plane(piece)
    return near, swap(near, 1)


def reduce_wide(own, other, dp, extra):
    fine = dp // 8
    blocks = jnp.stack([own, other], 1).reshape(8, 4, *own.shape[2:])
    parts, rows = own.shape[2], 128 // fine
    main = blocks[..., :128, :].reshape(8, 4, parts, fine, rows, BLOCK).transpose(0, 3, 1, 2, 4, 5)
    beside = jnp.broadcast_to(
        blocks[:, None, ..., 128:, :], (8, fine, 4, parts, extra, BLOCK)
    )
    flat = jnp.concatenate([main, beside], 4).reshape(dp * 4, parts, rows + extra, BLOCK)
    mine = lax.psum_scatter(flat, ("dp", "zero"), scatter_dimension=0, tiled=True)
    out = lax.all_gather(mine[0], "dp", axis=0, tiled=False)
    out = out.reshape(8, fine, parts, rows + extra, BLOCK)
    main = out[..., :rows, :].transpose(0, 2, 1, 3, 4).reshape(8, parts, 128, BLOCK)
    out = jnp.concatenate([main, out[:, 0, :, rows:]], 2)
    return out[0::2], out[1::2]


def shards(
    dp, images, cotangent, counts, rel_index, regions,
    mat_w, mat_m, mat_v, vec_w, vec_m, vec_v, tab_w, tab_m, tab_v,
):
    near = dp == 8
    fine = dp // 8
    rows = 128 // fine
    me = lax.axis_index("dp")
    taken_from = jnp.stack([me // fine, me % fine]).astype(jnp.int32)
    spot = [me, lax.axis_index("zero")] if near else [0 * me, 0 * me]
    place = jnp.stack(spot + [counts[0]]).astype(jnp.int32)

    inside = np.arange(CELL) < WIN * WIN
    zones = regions.reshape(2, WIN, 2, WIN).transpose(0, 2, 1, 3).reshape(4, WIN * WIN)
    zones = jnp.pad(zones, ((0, 0), (0, 15)))
    differ = (zones[:, :, None] != zones[:, None, :]) & inside[None, None, :]
    outside = jnp.asarray(np.where(inside, 0.0, -1e30), f32)[None, :, None]
    mask_shifted = jnp.tile(jnp.where(differ, mask_value, 0.0) + outside, (1, 1, QUAD)).astype(f32)
    mask_plain = jnp.broadcast_to(outside, (1, CELL, QUAD * CELL))
    masks = (mask_plain, mask_shifted)
    perms = (frames(False), frames(True))

    packed, rel = pack(taken_from, rows, mat_w, rel_index, tab_w, vec_w)
    piece = partial(cut, taken_from, rows, mat_w)
    if near:
        z_heads0 = gather_z(packed)
        z_mlp0 = gather_z(piece(0, 1, 2, [z_heads0]))
        p_heads0 = gather_plane(z_heads0)
        heads0 = gather_core(p_heads0)
        p_mlp0 = gather_plane(z_mlp0)
        z_heads1 = gather_z(piece(1, 0, 1, [p_heads0]))
        mlp0 = gather_core(p_mlp0)
        p_heads1 = gather_plane(z_heads1)
        z_mlp1 = gather_z(piece(1, 1, 2, [p_mlp0]))
        heads1 = gather_core(p_heads1)
        p_mlp1 = gather_plane(z_mlp1)
        mlp1 = gather_core(p_mlp1)
        waits = [[z_mlp0], [z_heads1], [z_mlp1], []]
    else:
        heads0 = gather_wide(packed, dp, EXTRA)
        mlp0 = gather_wide(piece(0, 1, 2, []), dp, 0)
        heads1 = gather_wide(piece(1, 0, 1, []), dp, 0)
        mlp1 = gather_wide(piece(1, 1, 2, []), dp, 0)
        waits = [[], [], [], []]
    attention_w = (heads0, heads1)
    mlp_w = (mlp0, mlp1)

    stream = images
    saved = []
    for layer in range(2):
        mid, qkv, merged, totals, table, vec = attention_forward(
            layer, place, stream, attention_w[layer], heads0, masks[layer], perms[layer],
            waits[2 * layer],
        )
        result, act, slope = mlp_forward(
            layer, layer == 1, place, mid, mlp_w[layer], vec, waits[2 * layer + 1]
        )
        saved.append((stream, mid, qkv, merged, totals, table, vec, act, slope))
        stream = result
    activations = stream

    def backward_mlp(layer, gradient, after):
        x, mid, qkv, merged, totals, table, vec, act, slope = saved[layer]
        return mlp_backward(layer, place, gradient, act, slope, mid, mlp_w[layer], vec, after)

    def backward_attention(layer, gradient, small, after, *span):
        x, mid, qkv, merged, totals, table, vec, act, slope = saved[layer]
        return attention_backward(
            layer, place, gradient, x, qkv, merged, totals, table, attention_w[layer], vec, small,
            perms[layer], rel, after, *span,
        )

    sums = {}
    if near:
        half = images.shape[0] // 2
        grad_mid, *mlp1, small = backward_mlp(1, cotangent, [])
        gradient, *heads1, _, _ = backward_attention(1, grad_mid, small, [])
        core_mlp1 = reduce_core(*mlp1)
        grad_mid, *mlp0, small = backward_mlp(0, gradient, [core_mlp1])
        plane_mlp1 = reduce_plane(core_mlp1)
        core_heads1 = reduce_core(*heads1)
        gradient, *heads0, pairs, small = backward_attention(
            0, grad_mid, small, [plane_mlp1, core_heads1], 0, half
        )
        z_mlp1 = reduce_z(plane_mlp1)
        plane_heads1 = reduce_plane(core_heads1)
        core_mlp0 = reduce_core(*mlp0)
        gradient, *heads0, _, _ = backward_attention(
            0, grad_mid, small, [z_mlp1, plane_heads1, core_mlp0], half, half,
            [gradient, *heads0, pairs],
        )
        sums[1, 1] = spread_sum(z_mlp1)
        sums[1, 0] = spread_sum(reduce_z(plane_heads1))
        sums[0, 1] = spread_sum(reduce_z(reduce_plane(core_mlp0)))
        sums[0, 0] = spread_sum(reduce_z(reduce_plane(reduce_core(*heads0))))
    else:
        gradient = cotangent
        for layer in (1, 0):
            gradient, *mlp, small = backward_mlp(layer, gradient, [])
            gradient, *heads, _, _ = backward_attention(layer, gradient, small, [])
            sums[layer, 1] = reduce_wide(*mlp, dp, 0)
            sums[layer, 0] = reduce_wide(*heads, dp, SMALL)

    state = (mat_w, mat_m, mat_v)
    done = None
    for layer, part in ((1, 1), (1, 0), (0, 1), (0, 0)):
        done = adam(layer, part, place, *sums[layer, part], state, done)

    def beside(block):
        m = place[0] ^ block
        found = []
        for layer in range(2):
            both = jnp.concatenate([half[:, 0, 128:] for half in sums[layer, 0]])
            found.append(lax.dynamic_index_in_dim(both, (m % 2) * 4 + m // 2, 0, False))
        return jnp.stack(found).astype(f32)

    new_vec = adam_step(vec_w, vec_m, vec_v, beside(1)[:, 0:12, 0:128], rate_vector, 0.0)
    new_tab = adam_step(tab_w, tab_m, tab_v, beside(0)[:, 0:4, 0:NREL], rate_table, 0.0)
    return (activations, gradient, *done, *new_vec, *new_tab)


def solution(mesh):
    images = P(("dp", "zero"), None, None)
    rows = P(None, "zero", None)
    lanes = P(None, None, "zero")
    return jax.shard_map(
        partial(shards, mesh.shape["dp"]),
        mesh=mesh,
        in_specs=(images, images, P(("dp", "zero")), P(), P())
        + (rows,) * 3 + (lanes,) * 3 + (rows,) * 3,
        out_specs=(images, images) + (rows,) * 3 + (lanes,) * 3 + (rows,) * 3,
        check_vma=False,
    )
```

```python
from functools import partial

import jax
import jax.numpy as jnp
import numpy as np
from jax import lax
from jax.experimental import pallas as pl
from jax.experimental.pallas import tpu as pltpu
from jax.sharding import PartitionSpec as P

WIN = 7
SIDE = 14
STEP = 10
NREL = 169
C = 512
HID = 2048
TOKENS = SIDE * SIDE
PAIR = 2
ROWS = 208
FRAME = 256
CELL = 64
QUAD = 4
BLOCK = 256
EXTRA = 32
SMALL = 16

norm_eps = 1e-05
mask_value = -100.0
beta_one = 0.9
beta_two = 0.999
adam_eps = 1e-08
weight_decay = 0.05
rate_matrix = 0.1
rate_vector = 0.5
rate_table = 1.0
scale = 32 ** (-0.5)

bf16 = jnp.bfloat16
f32 = jnp.float32
NN = (((1,), (0,)), ((), ()))
NT = (((1,), (1,)), ((), ()))
TN = (((0,), (0,)), ((), ()))


def mm(left, right, dims=NN):
    return lax.dot_general(left, right, dims, preferred_element_type=f32)


def frames(shifted):
    move = WIN // 2 if shifted else 0
    placed = np.zeros((FRAME, ROWS), np.float32)
    for wy in range(2):
        for wx in range(2):
            for iy in range(WIN):
                for ix in range(WIN):
                    y = (wy * WIN + iy + move) % SIDE
                    x = (wx * WIN + ix + move) % SIDE
                    placed[(wy * 2 + wx) * CELL + iy * WIN + ix, y * SIDE + x] = 1
    return placed


def head_rows():
    rows = np.zeros((QUAD * CELL, 128), np.float32)
    for h in range(QUAD):
        rows[h * CELL : (h + 1) * CELL, h * 32 : (h + 1) * 32] = 1
    return rows


def head_spread(rows):
    out = np.zeros((rows, QUAD * CELL), np.float32)
    for h in range(QUAD):
        out[h, h * CELL : (h + 1) * CELL] = 1
    return out


def norm(rows):
    centred = rows - jnp.mean(rows, -1, keepdims=True)
    spread = lax.rsqrt(jnp.mean(centred * centred, -1, keepdims=True) + norm_eps)
    return centred * spread, spread


def norm_back(grad_unit, unit, spread):
    return spread * (
        grad_unit
        - jnp.mean(grad_unit, -1, keepdims=True)
        - unit * jnp.mean(grad_unit * unit, -1, keepdims=True)
    )


def column_sum(rows):
    return jnp.sum(rows, 0, keepdims=True)


def gelu_pair(u):
    size = jnp.abs(u)
    below = 1.0 + (0.3275911 * 0.5**0.5) * size
    t = pltpu.reciprocal(below, approx=True)
    bell = jnp.exp2(u * u * (-0.5 * 1.4426950408889634))
    poly = t * (
        0.127414796 + t * (-0.142248368 + t * (0.710706871 + t * (-0.726576013 + t * 0.530702714)))
    )
    tail = poly * bell
    phi = jnp.where(u >= 0, 1.0 - tail, tail)
    return u * phi, phi + u * bell * 0.3989422804014327


def quad_rows(part, heads):
    return jnp.concatenate([part] * QUAD, 0) * heads


def pick_heads(stacked, lane_head):
    low = jnp.where(lane_head == 0, stacked[:CELL], stacked[CELL : 2 * CELL])
    high = jnp.where(lane_head == 2, stacked[2 * CELL : 3 * CELL], stacked[3 * CELL :])
    return jnp.where(lane_head < 2, low, high)


def lane_heads():
    return lax.broadcasted_iota(jnp.int32, (CELL, 128), 1) // 32


def whole(shape):
    zero = (0,) * len(shape)
    return pl.BlockSpec(shape, lambda *_: zero, pipeline_mode=pl.Buffered(1))


def per_image(rows, cols):
    return pl.BlockSpec((1, rows, cols), lambda i, *_: (i, 0, 0))


def per_pair(rows, cols):
    return pl.BlockSpec((PAIR, rows, cols), lambda i, *_: (i, 0, 0))


HBM = pl.BlockSpec(memory_space=pl.ANY)


def weight_copies(place, stacks, kept, sems, first_row=0):
    copies = []
    parts, rows = kept.shape[0], kept.shape[3]
    for m in range(8):
        for s in range(4):
            for p in range(parts):
                if len(stacks) == 1:
                    source, block, owner = stacks[0].at[m, s, p], m, s
                else:
                    source = stacks[m % 2].at[m // 2, s, p]
                    block, owner = place[0] ^ m, (place[1] + 4 - s) & 3
                copies.append(
                    pltpu.make_async_copy(
                        source.at[pl.ds(first_row, rows), :],
                        kept.at[p, block, owner],
                        sems.at[m, s, p],
                    )
                )
    return copies


def fetch(copies):
    for copy in copies:
        copy.start()
    for copy in copies:
        copy.wait()


def call(body, name, grid, ins, outs, out_shapes, scratch, cost_us, prefetch=0, aliases=None):
    return pl.pallas_call(
        body,
        name=name,
        grid_spec=pltpu.PrefetchScalarGridSpec(
            num_scalar_prefetch=prefetch,
            grid=grid,
            in_specs=ins,
            out_specs=outs,
            scratch_shapes=scratch,
        ),
        out_shape=out_shapes,
        input_output_aliases=aliases or {},
        compiler_params=pltpu.CompilerParams(
            dimension_semantics=("arbitrary",) * len(grid), vmem_limit_bytes=58 * 1024 * 1024
        ),
        cost_estimate=pl.CostEstimate(
            flops=0, bytes_accessed=int(cost_us * 3.69e6), transcendentals=0
        ),
    )


def shape(dims, kind):
    return jax.ShapeDtypeStruct(dims, kind)


def pack_body(place, mat, pair_index, tab, vec, spread, out, rel, spread_tab, small):
    rows = mat.shape[1]
    out[0, 0:rows, :] = mat[0].astype(bf16)
    rel[...] = jnp.full(rel.shape, -1, jnp.int32)
    across = pair_index[...].astype(f32).T.astype(jnp.int32)
    for h in range(QUAD):
        rel[0 : WIN * WIN, CELL * h : CELL * h + WIN * WIN] = across
    for layer in range(2):
        spread_tab[layer, 0:NREL, :] = mm(tab[layer].astype(bf16), spread[...], TN)
    pairs = rel[pl.ds(pl.multiple_of(place[0] * 8, 8), 8), :]

    def step(r, sums):
        hit = pairs == r
        return tuple(
            jnp.where(hit, spread_tab[layer, pl.ds(r, 1), :], sums[layer]) for layer in range(2)
        )

    start = jnp.zeros((8, QUAD * CELL), f32)
    first, second = lax.fori_loop(0, NREL, step, (start, start))
    out[0, rows : rows + 16, :] = jnp.concatenate([first, second], 0).astype(bf16)
    small[...] = jnp.zeros_like(small)
    row = jnp.minimum(place[0] * 2, 10)
    for layer in range(2):
        for k in range(2):
            small[k : k + 1, layer * 128 : (layer + 1) * 128] = vec[row + k, layer : layer + 1, :]
    out[0, rows + 16 : rows + 32, :] = small[...].astype(bf16)


def pack(place, rows, mat_w, rel_index, tab_w, vec_w):
    vec_w = vec_w.transpose(1, 0, 2)
    return call(
        pack_body,
        "pack",
        (1,),
        [
            pl.BlockSpec((1, rows, BLOCK), lambda i, place: (0, place[1], place[0])),
            whole(rel_index.shape),
            whole(tab_w.shape),
            whole(vec_w.shape),
            whole((QUAD, QUAD * CELL)),
        ],
        [whole((1, rows + EXTRA, BLOCK)), whole((CELL, QUAD * CELL))],
        [shape((1, rows + EXTRA, BLOCK), bf16), shape((CELL, QUAD * CELL), jnp.int32)],
        [pltpu.VMEM((2, 176, QUAD * CELL), f32), pltpu.VMEM((16, 256), f32)],
        4,
        prefetch=1,
    )(place, mat_w, rel_index, tab_w, vec_w, jnp.asarray(head_spread(QUAD), bf16))


def cut_body(place, mat, *refs):
    refs[-1][0] = mat[0].astype(bf16)


def cut(place, rows, mat_w, layer, part, parts, after):
    return call(
        cut_body,
        f"cut_{layer}_{part}",
        (parts,),
        [
            pl.BlockSpec(
                (1, rows, BLOCK), lambda i, place: (layer, place[1], (part + i) * 8 + place[0])
            )
        ]
        + [HBM] * len(after),
        pl.BlockSpec((1, rows, BLOCK), lambda i, place: (i, 0, 0)),
        shape((parts, rows, BLOCK), bf16),
        [],
        2,
        prefetch=1,
    )(place, mat_w, *after)


def attention_forward_body(layer, stacks, waits, place, *refs):
    arrays, refs = refs[: stacks[0]], refs[stacks[0] :]
    extras, refs = refs[: stacks[1]], refs[stacks[1] + waits :]
    x, mask, perm, perm_back, heads = refs[:5]
    mid, qkv, merged, totals, table, vec, x_rows, framed, kept, extra_kept, sems, more_sems = refs[5:]
    weight, extra = kept.at[0], extra_kept.at[0]

    @pl.when(pl.program_id(0) == 0)
    def _():
        fetch(
            weight_copies(place, arrays, kept, sems)
            + weight_copies(place, extras, extra_kept, more_sems, 128)
        )
        x_rows[...] = jnp.zeros_like(x_rows)
        vec[...] = jnp.zeros_like(vec)
        for z in range(4):
            for d in range(8):
                pair = extra[d, z, 0:16, :].astype(f32)
                bias = pair[8 * layer : 8 * layer + 8]
                for w in range(table.shape[0]):
                    table[w, z, 8 * d : 8 * d + 8, :] = bias + mask[w, 8 * d : 8 * d + 8, :]
                if d < 6:
                    rows = extra[d, z, 16:32, 128 * layer : 128 * layer + 128].astype(f32)
                    vec[2 * d : 2 * d + 2, 128 * z : 128 * z + 128] = rows[0:2]

    if x.shape[1] == ROWS:
        stream = x[0]
    else:
        x_rows[0:TOKENS, :] = x[0].astype(f32)
        stream = x_rows[...]
    unit, _ = norm(stream)
    normed = (unit * vec[0:1, :] + vec[1:2, :]).astype(bf16)
    normed = mm(perm[...], normed).astype(bf16)
    for c in range(6):
        part = mm(normed, weight[c].reshape(C, BLOCK))
        if c < 2:
            part = part + vec[2:3, 256 * c : 256 * c + 256]
        if c >= 4:
            part = part + vec[3:4, 256 * (c - 4) : 256 * (c - 4) + 256]
        qkv[0, :, 256 * c : 256 * c + 256] = part.astype(bf16)
    lane_head = lane_heads()

    def score(unit):
        rows, at = slice(CELL * (unit // 4), CELL * (unit // 4) + CELL), 128 * (unit % 4)
        query = quad_rows(qkv[0, rows, at : at + 128], heads[...])
        return mm(qkv[0, rows, C + at : C + at + 128], query, NT)

    ahead = score(0)
    for n in range(16):
        w, g = n // 4, n % 4
        rows, at = slice(CELL * w, CELL * w + CELL), 128 * g
        scores = ahead * scale + table[w % table.shape[0], g]
        if n < 15:
            ahead = score(n + 1)
        top = jnp.max(scores, 0, keepdims=True)
        raised = jnp.exp(scores - top)
        total = jnp.sum(raised, 0, keepdims=True)
        totals[0, n : n + 1, :] = top + jnp.log(total)
        probs = (raised * (1.0 / total)).astype(bf16)
        stacked = mm(probs, qkv[0, rows, 2 * C + at : 2 * C + at + 128], TN)
        framed[rows, at : at + 128] = pick_heads(stacked, lane_head).astype(bf16)
    gathered = mm(perm_back[...], framed[...]).astype(bf16)
    merged[0] = gathered
    for c in range(2):
        cols = slice(256 * c, 256 * c + 256)
        mid[0, :, cols] = (
            stream[:, cols] + mm(gathered, weight[6 + c].reshape(C, BLOCK)) + vec[4:5, cols]
        )


def attention_forward(layer, place, x, weight, extra, mask, perm, after):
    images = x.shape[0]
    tables = mask.shape[0]
    return call(
        partial(attention_forward_body, layer, (len(weight), len(extra)), len(after)),
        f"attention_forward_{layer}",
        (images,),
        [HBM] * (len(weight) + len(extra) + len(after))
        + [
            per_image(x.shape[1], C),
            whole(mask.shape),
            whole((FRAME, ROWS)),
            whole((ROWS, FRAME)),
            whole((QUAD * CELL, 128)),
        ],
        [
            per_image(ROWS, C),
            per_image(FRAME, 3 * C),
            per_image(ROWS, C),
            per_image(16, QUAD * CELL),
            pl.BlockSpec((tables, 4, CELL, QUAD * CELL), lambda i, *_: (0, 0, 0, 0)),
            pl.BlockSpec((16, C), lambda i, *_: (0, 0)),
        ],
        [
            shape((images, ROWS, C), f32),
            shape((images, FRAME, 3 * C), bf16),
            shape((images, ROWS, C), bf16),
            shape((images, 16, QUAD * CELL), f32),
            shape((tables, 4, CELL, QUAD * CELL), f32),
            shape((16, C), f32),
        ],
        [
            pltpu.VMEM((ROWS, C), f32),
            pltpu.VMEM((FRAME, C), bf16),
            pltpu.VMEM((1, 8, 4, 128, BLOCK), bf16),
            pltpu.VMEM((1, 8, 4, EXTRA, BLOCK), bf16),
            pltpu.SemaphoreType.DMA((8, 4, 1)),
            pltpu.SemaphoreType.DMA((8, 4, 1)),
        ],
        20,
        prefetch=1,
    )(
        place,
        *weight,
        *extra,
        *after,
        x,
        mask,
        jnp.asarray(perm, bf16),
        jnp.asarray(perm.T, bf16),
        jnp.asarray(head_rows(), bf16),
    )


def mlp_forward_body(stacks, waits, place, *refs):
    arrays, refs = refs[:stacks], refs[stacks + waits :]
    mid, vec, result, act, slope, kept, sems = refs
    first, second = kept.at[0], kept.at[1]

    @pl.when(pl.program_id(0) == 0)
    def _():
        fetch(weight_copies(place, arrays, kept, sems))

    rows = PAIR * ROWS
    stream = mid[...].reshape(rows, C)
    unit, _ = norm(stream)
    normed = (unit * vec[5:6, :] + vec[6:7, :]).astype(bf16)
    total = stream + vec[7:8, :]
    for c in range(8):
        bias = vec[8 + c // 2 : 9 + c // 2, 256 * (c % 2) : 256 * (c % 2) + 256]
        value, pull = gelu_pair(mm(normed, first[c].reshape(C, BLOCK)) + bias)
        value = value.astype(bf16)
        act[:, :, 256 * c : 256 * c + 256] = value.reshape(PAIR, ROWS, BLOCK)
        slope[:, :, 256 * c : 256 * c + 256] = pull.astype(bf16).reshape(PAIR, ROWS, BLOCK)
        total = total + mm(value, second[c].reshape(C, BLOCK), NT)
    result[...] = total.reshape(PAIR, ROWS, C)


def mlp_forward(layer, place, mid, weight, vec, after):
    images = mid.shape[0]
    return call(
        partial(mlp_forward_body, len(weight), len(after)),
        f"mlp_forward_{layer}",
        (images // PAIR,),
        [HBM] * (len(weight) + len(after)) + [per_pair(ROWS, C), whole(vec.shape)],
        [per_pair(ROWS, C), per_pair(ROWS, HID), per_pair(ROWS, HID)],
        [
            shape((images, ROWS, C), f32),
            shape((images, ROWS, HID), bf16),
            shape((images, ROWS, HID), bf16),
        ],
        [pltpu.VMEM((2, 8, 4, 128, BLOCK), bf16), pltpu.SemaphoreType.DMA((8, 4, 2))],
        22,
        prefetch=1,
    )(place, *weight, *after, mid, vec)


def mlp_both_body(stacks, waits, place, *refs):
    arrays, refs = refs[:stacks], refs[stacks + waits :]
    grad, mid, vec, result, grad_mid, own, other, small = refs[:8]
    grad_rows, all_grad, all_act, all_inner, all_normed, kept, sems = refs[8:]
    first, second = kept.at[0], kept.at[1]
    i = pl.program_id(0)

    @pl.when(i == 0)
    def _():
        fetch(weight_copies(place, arrays, kept, sems))
        grad_rows[...] = jnp.zeros_like(grad_rows)
        small[...] = jnp.zeros_like(small)

    rows = PAIR * ROWS
    alive = [(i * PAIR + n < place[2]).astype(f32) for n in range(PAIR)]
    for n in range(PAIR):
        grad_rows[n, 0:TOKENS, :] = grad[n].astype(f32) * alive[n]
    grad_out = grad_rows[...].reshape(rows, C)
    here = pl.ds(pl.multiple_of(i * rows, 32), rows)
    low = grad_out.astype(bf16)
    all_grad[here, :] = low
    small[7:8, :] += column_sum(grad_out)
    stream = mid[...].reshape(rows, C)
    unit, spread = norm(stream)
    normed = (unit * vec[5:6, :] + vec[6:7, :]).astype(bf16)
    all_normed[here, :] = normed
    total = stream + vec[7:8, :]
    back = jnp.zeros((rows, C), f32)
    for c in range(8):
        cols = slice(256 * c, 256 * c + 256)
        row, lane = 8 + c // 2, 256 * (c % 2)
        bias = vec[row : row + 1, lane : lane + 256]
        value, pull = gelu_pair(mm(normed, first[c].reshape(C, BLOCK)) + bias)
        value = value.astype(bf16)
        all_act[here, cols] = value
        inner = (mm(low, second[c].reshape(C, BLOCK)) * pull).astype(bf16)
        all_inner[here, cols] = inner
        small[row : row + 1, lane : lane + 256] += column_sum(inner.astype(f32))
        total = total + mm(value, second[c].reshape(C, BLOCK), NT)
        back = back + mm(inner, first[c].reshape(C, BLOCK), NT)
    small[5:6, :] += column_sum(back * unit)
    small[6:7, :] += column_sum(back)
    grad_mid[...] = (grad_out + norm_back(back * vec[5:6, :], unit, spread)).reshape(PAIR, ROWS, C)
    total = total.reshape(PAIR, ROWS, C)
    for n in range(PAIR):
        result[n] = (total[n, :TOKENS] * alive[n]).astype(bf16)

    @pl.when(i == pl.num_programs(0) - 1)
    def _():
        mlp_weight_grads(place, False, all_grad, all_act, all_inner, all_normed, own, other)


def mlp_weight_grads(place, rotate, all_grad, all_act, all_inner, all_normed, own, other):
    grad_across = all_grad[...].T
    normed_across = all_normed[...].T
    for m in range(8):
        cols = pl.ds(pl.multiple_of((place[0] ^ m) * BLOCK, BLOCK), BLOCK)
        out = other if m % 2 else own
        for p, block in enumerate(
            (mm(normed_across, all_inner[:, cols]), mm(grad_across, all_act[:, cols]))
        ):
            block = block.astype(bf16)
            for z in range(4):
                to = (z + 4 - place[1]) & 3 if rotate else z
                out[m // 2, to, p] = block[128 * z : 128 * z + 128]


def mlp_both(place, grad, mid, weight, vec, after):
    images = mid.shape[0]
    total = images * ROWS
    pieces = (4, 4, 2, 128, BLOCK)
    return call(
        partial(mlp_both_body, len(weight), len(after)),
        "mlp_both",
        (images // PAIR,),
        [HBM] * (len(weight) + len(after)) + [per_pair(TOKENS, C), per_pair(ROWS, C), whole(vec.shape)],
        [per_pair(TOKENS, C), per_pair(ROWS, C), whole(pieces), whole(pieces), whole((16, C))],
        [
            shape((images, TOKENS, C), bf16),
            shape((images, ROWS, C), f32),
            shape(pieces, bf16),
            shape(pieces, bf16),
            shape((16, C), f32),
        ],
        [
            pltpu.VMEM((PAIR, ROWS, C), f32),
            pltpu.VMEM((total, C), bf16),
            pltpu.VMEM((total, HID), bf16),
            pltpu.VMEM((total, HID), bf16),
            pltpu.VMEM((total, C), bf16),
            pltpu.VMEM((2, 8, 4, 128, BLOCK), bf16),
            pltpu.SemaphoreType.DMA((8, 4, 2)),
        ],
        45,
        prefetch=1,
    )(place, *weight, *after, grad, mid, vec)


def mlp_backward_body(stacks, waits, place, *refs):
    arrays, refs = refs[:stacks], refs[stacks + waits :]
    grad, act, slope, mid, vec, grad_mid, own, other, small = refs[:9]
    all_grad, all_act, all_inner, all_normed, kept, sems = refs[9:]
    first, second = kept.at[0], kept.at[1]
    i = pl.program_id(0)

    @pl.when(i == 0)
    def _():
        fetch(weight_copies(place, arrays, kept, sems))
        small[...] = jnp.zeros_like(small)

    rows = PAIR * ROWS
    grad_out = grad[...].reshape(rows, C)
    here = pl.ds(pl.multiple_of(i * rows, 32), rows)
    low = grad_out.astype(bf16)
    all_grad[here, :] = low
    small[7:8, :] += column_sum(low.astype(f32))
    all_act[here, :] = act[...].reshape(rows, HID)
    unit, spread = norm(mid[...].reshape(rows, C))
    all_normed[here, :] = (unit * vec[5:6, :] + vec[6:7, :]).astype(bf16)
    back = jnp.zeros((rows, C), f32)
    for c in range(8):
        cols = slice(256 * c, 256 * c + 256)
        pull = slope[:, :, cols].reshape(rows, BLOCK).astype(f32)
        inner = (mm(low, second[c].reshape(C, BLOCK)) * pull).astype(bf16)
        all_inner[here, cols] = inner
        row, lane = 8 + c // 2, 256 * (c % 2)
        small[row : row + 1, lane : lane + 256] += column_sum(inner.astype(f32))
        back = back + mm(inner, first[c].reshape(C, BLOCK), NT)
    small[5:6, :] += column_sum(back * unit)
    small[6:7, :] += column_sum(back)
    grad_mid[...] = (grad_out + norm_back(back * vec[5:6, :], unit, spread)).reshape(PAIR, ROWS, C)

    @pl.when(i == pl.num_programs(0) - 1)
    def _():
        mlp_weight_grads(place, True, all_grad, all_act, all_inner, all_normed, own, other)


def mlp_backward(layer, place, grad, act, slope, mid, weight, vec, after):
    images = mid.shape[0]
    total = images * ROWS
    pieces = (4, 4, 2, 128, BLOCK)
    return call(
        partial(mlp_backward_body, len(weight), len(after)),
        f"mlp_backward_{layer}",
        (images // PAIR,),
        [HBM] * (len(weight) + len(after))
        + [
            per_pair(grad.shape[1], C),
            per_pair(ROWS, HID),
            per_pair(ROWS, HID),
            per_pair(ROWS, C),
            whole(vec.shape),
        ],
        [per_pair(ROWS, C), whole(pieces), whole(pieces), whole((16, C))],
        [
            shape((images, ROWS, C), f32),
            shape(pieces, bf16),
            shape(pieces, bf16),
            shape((16, C), f32),
        ],
        [
            pltpu.VMEM((total, C), bf16),
            pltpu.VMEM((total, HID), bf16),
            pltpu.VMEM((total, HID), bf16),
            pltpu.VMEM((total, C), bf16),
            pltpu.VMEM((2, 8, 4, 128, BLOCK), bf16),
            pltpu.SemaphoreType.DMA((8, 4, 2)),
        ],
        30,
        prefetch=1,
    )(place, *weight, *after, grad, act, slope, mid, vec)


def attention_backward_body(layer, stacks, waits, resumed, ends, place, *refs):
    arrays, refs = refs[:stacks], refs[stacks + waits :]
    if resumed:
        (own_before, other_before, pairs_before), refs = refs[1:4], refs[4:]
    grad, x, qkv, merged, totals, table, vec, before = refs[:8]
    perm, perm_back, heads, rel, spread, result, own, other, pairs, small = refs[8:18]
    x_rows, framed, grad_framed, all_normed, all_packed, all_merged = refs[18:24]
    across, hits, beside, kept, sems = refs[24:]
    weight = kept.at[0]
    i = pl.program_id(0)

    @pl.when(i == 0)
    def _():
        fetch(weight_copies(place, arrays, kept, sems))
        x_rows[...] = jnp.zeros_like(x_rows)
        small[...] = before[...]
        pairs[...] = pairs_before[...] if resumed else jnp.zeros_like(pairs)

    if x.shape[1] == ROWS:
        stream = x[0]
    else:
        x_rows[0:TOKENS, :] = x[0].astype(f32)
        stream = x_rows[...]
    here = pl.ds(pl.multiple_of(i * ROWS, 16), ROWS)
    unit, spread_one = norm(stream)
    all_normed[here, :] = (unit * vec[0:1, :] + vec[1:2, :]).astype(bf16)
    low = grad[0].astype(bf16)
    all_packed[here, 3 * C :] = low
    all_merged[here, :] = merged[0]
    small[4:5, :] += column_sum(low.astype(f32))
    moved = mm(perm[...], low).astype(bf16)
    from_heads = mm(moved[:, :BLOCK], weight[6].reshape(C, BLOCK), NT)
    from_heads = from_heads + mm(moved[:, BLOCK:], weight[7].reshape(C, BLOCK), NT)
    framed[...] = from_heads.astype(bf16)
    lane_head = lane_heads()
    for w in range(4):
        rows = slice(CELL * w, CELL * w + CELL)
        at = [128 * g for g in range(4)]
        keys = [qkv[0, rows, C + c : C + c + 128] for c in at]
        query = [quad_rows(qkv[0, rows, c : c + 128], heads[...]) for c in at]
        pull = [quad_rows(framed[rows, c : c + 128], heads[...]) for c in at]
        scores = [mm(keys[g], query[g], NT) for g in range(4)]
        grad_probs = [
            mm(qkv[0, rows, 2 * C + at[g] : 2 * C + at[g] + 128], pull[g], NT) for g in range(4)
        ]
        probs, grad_scores = [], []
        for g in range(4):
            shifted = scores[g] * scale + table[w % table.shape[0], g]
            prob = jnp.exp(shifted - totals[0, 4 * w + g : 4 * w + g + 1, :])
            mean = jnp.sum(prob * grad_probs[g], 0, keepdims=True)
            grad_score = (prob * (grad_probs[g] - mean)).astype(bf16)
            pairs[g] += grad_score.astype(f32)
            probs.append(prob.astype(bf16))
            grad_scores.append(grad_score)
        for g in range(4):
            grad_value = mm(probs[g], pull[g])
            grad_framed[rows, 2 * C + at[g] : 2 * C + at[g] + 128] = grad_value.astype(bf16)
        for g in range(4):
            grad_key = mm(grad_scores[g], query[g]) * scale
            grad_framed[rows, C + at[g] : C + at[g] + 128] = grad_key.astype(bf16)
        for g in range(4):
            grad_query = pick_heads(mm(grad_scores[g], keys[g], TN), lane_head) * scale
            grad_framed[rows, at[g] : at[g] + 128] = grad_query.astype(bf16)
    back = jnp.zeros((ROWS, C), f32)
    for c in range(6):
        cols = slice(256 * c, 256 * c + 256)
        part_wide = mm(perm_back[...], grad_framed[:, cols])
        part = part_wide.astype(bf16)
        all_packed[here, cols] = part
        if c < 2:
            small[2:3, cols] += column_sum(part_wide)
        if c >= 4:
            small[3:4, 256 * (c - 4) : 256 * (c - 4) + 256] += column_sum(part_wide)
        back = back + mm(part, weight[c].reshape(C, BLOCK), NT)
    small[0:1, :] += column_sum(back * unit)
    small[1:2, :] += column_sum(back)
    total = grad[0] + norm_back(back * vec[0:1, :], unit, spread_one)
    result[0] = total[: result.shape[1]]

    @pl.when(i == pl.num_programs(0) - 1)
    def _():
        across[0] = all_normed[...].T
        across[1] = all_merged[...].T
        beside[...] = jnp.zeros_like(beside)
        if ends:
            hits[...] = jnp.zeros_like(hits)

            def step(r, carry):
                same = rel[...] == r
                for g in range(4):
                    kept_pairs = jnp.where(same, pairs[g], 0.0)
                    hits[pl.ds(r, 1), 256 * g : 256 * g + 256] = column_sum(kept_pairs)
                return carry

            lax.fori_loop(0, NREL, step, 0)
            for z in range(4):
                beside[0, z] = lax.dot_general(
                    spread[...],
                    hits[:, 256 * z : 256 * z + 256],
                    NT,
                    precision=lax.Precision.HIGHEST,
                    preferred_element_type=f32,
                ).astype(bf16)
                beside[1, z, :, 0:128] = small[:, 128 * z : 128 * z + 128].astype(bf16)
        for m in range(8):
            b = place[0] ^ m
            left = across[jnp.where(b < 6, 0, 1)]
            right = all_packed[:, pl.ds(pl.multiple_of(b * BLOCK, BLOCK), BLOCK)]
            block = mm(left, right)
            out = other if m % 2 else own
            for z in range(4):
                to = (z + 4 - place[1]) & 3 if layer == 0 else z
                new = block[128 * z : 128 * z + 128]
                if resumed:
                    old = other_before if m % 2 else own_before
                    new = new + old[m // 2, to, 0, 0:128, :].astype(f32)
                out[m // 2, to, 0, 0:128, :] = new.astype(bf16)
                out[m // 2, to, 0, 128:144, :] = beside[jnp.minimum(b, 2), z]


def attention_backward(
    layer, place, grad, x, qkv, merged, totals, table, weight, vec, small, perm, rel, after,
    first=0, count=None, resume=None,
):
    images = grad.shape[0]
    count = count or images
    pieces = (4, 4, 1, 128 + SMALL, BLOCK)
    pairs = (4, CELL, QUAD * CELL)
    total = count * ROWS
    out_rows = TOKENS if layer == 0 else ROWS

    def image(rows, cols):
        return pl.BlockSpec((1, rows, cols), lambda i, *_: (i + first, 0, 0))

    resumed = list(resume or [])
    return call(
        partial(
            attention_backward_body, layer, len(weight), len(after), bool(resumed),
            first + count == images,
        ),
        f"attention_backward_{layer}_{first}",
        (count,),
        [HBM] * (len(weight) + len(after))
        + ([HBM, whole(pieces), whole(pieces), whole(pairs)] if resumed else [])
        + [
            image(ROWS, C),
            image(x.shape[1], C),
            image(FRAME, 3 * C),
            image(ROWS, C),
            image(16, QUAD * CELL),
            whole(table.shape),
            whole(vec.shape),
            whole((16, C)),
            whole((FRAME, ROWS)),
            whole((ROWS, FRAME)),
            whole((QUAD * CELL, 128)),
            whole(rel.shape),
            whole((SMALL, QUAD * CELL)),
        ],
        [image(out_rows, C), whole(pieces), whole(pieces), whole(pairs), whole((16, C))],
        [
            shape((images, out_rows, C), f32),
            shape(pieces, bf16),
            shape(pieces, bf16),
            shape(pairs, f32),
            shape((16, C), f32),
        ],
        [
            pltpu.VMEM((ROWS, C), f32),
            pltpu.VMEM((FRAME, C), bf16),
            pltpu.VMEM((FRAME, 3 * C), bf16),
            pltpu.VMEM((total, C), bf16),
            pltpu.VMEM((total, 4 * C), bf16),
            pltpu.VMEM((total, C), bf16),
            pltpu.VMEM((2, C, total), bf16),
            pltpu.VMEM((256, 4 * QUAD * CELL), f32),
            pltpu.VMEM((3, 4, SMALL, BLOCK), bf16),
            pltpu.VMEM((1, 8, 4, 128, BLOCK), bf16),
            pltpu.SemaphoreType.DMA((8, 4, 1)),
        ],
        6 * count,
        prefetch=1,
        aliases={1 + len(weight) + len(after): 0} if resumed else None,
    )(
        place,
        *weight,
        *after,
        *resumed,
        grad,
        x,
        qkv,
        merged,
        totals,
        table,
        vec,
        small,
        jnp.asarray(perm, bf16),
        jnp.asarray(perm.T, bf16),
        jnp.asarray(head_rows(), bf16),
        rel,
        jnp.asarray(head_spread(SMALL), f32),
    )


def adam_step(weight, first, second, gradient, rate, decay):
    first_new = beta_one * first + (1.0 - beta_one) * gradient
    second_new = beta_two * second + (1.0 - beta_two) * gradient * gradient
    first_hat = first_new / (1.0 - beta_one**STEP)
    second_hat = second_new / (1.0 - beta_two**STEP)
    weight_new = weight - rate * (first_hat / (jnp.sqrt(second_hat) + adam_eps) + decay * weight)
    return (weight_new, first_new, second_new)


def adam_block(grad, weight, first, second, outs, cols):
    news = adam_step(
        weight[0, :, cols], first[0, :, cols], second[0, :, cols],
        grad.astype(f32), rate_matrix, weight_decay,
    )
    for out, new in zip(outs, news):
        out[0, :, cols] = new


def adam_body(place, near, far, weight, first, second, *refs):
    for j in range(2):
        for k in range(2):
            block = (((place[0] // 2) & 1) ^ j) * 2 + ((place[0] & 1) ^ k)
            cols = pl.ds(pl.multiple_of(block * BLOCK, BLOCK), BLOCK)
            adam_block((far if k else near)[j, 0], weight, first, second, refs[-3:], cols)


def adam_body_plain(place, sums, weight, first, second, *refs):
    for k in range(4):
        cols = slice(BLOCK * k, BLOCK * k + BLOCK)
        adam_block(sums[k], weight, first, second, refs[-3:], cols)


def adam(layer, part, place, sums, state, done, after):
    kept = [] if done is None else list(done)
    if len(sums) == 2:
        parts = sums[0].shape[1]
        body = adam_body
        spec = pl.BlockSpec(
            (1, 128, 4 * BLOCK),
            lambda p, j, place: (layer, 0, (part + p) % 3 * 2 + ((place[0] // 4) ^ j)),
        )
        piece = pl.BlockSpec((2, 1, 128, BLOCK), lambda p, j, place: (j, p, 0, 0))
    else:
        parts = sums[0].shape[1] // 128
        body = adam_body_plain
        spec = pl.BlockSpec(
            (1, 128, 4 * BLOCK), lambda p, j, place: (layer, 0, (part + p) % 3 * 2 + j)
        )
        piece = pl.BlockSpec((4, 128, BLOCK), lambda p, j, place: (j, p, 0))
    return call(
        body,
        f"adam_{layer}_{part}",
        (parts, 2),
        [piece] * len(sums) + [spec] * 3 + [HBM] * (len(kept) + len(after)),
        [spec] * 3,
        [shape(state[0].shape, f32)] * 3,
        [],
        3 * parts,
        prefetch=1,
        aliases={4 + len(sums) + k: k for k in range(len(kept))},
    )(place, *sums, *state, *kept, *after)


def swap(value, bits):
    return lax.ppermute(value, "dp", [(i, i ^ bits) for i in range(8)])


def shift(value, steps):
    return lax.ppermute(value, "zero", [(i, (i + steps) % 4) for i in range(4)])


def stack_body(count, *refs):
    out, sems = refs[-2:]
    fetch([pltpu.make_async_copy(refs[k], out.at[k], sems.at[k]) for k in range(count)])


def stack(values, after=()):
    dims = (len(values), *values[0].shape)
    return call(
        partial(stack_body, len(values)),
        "stack",
        (1,),
        [HBM] * (len(values) + len(after)),
        HBM,
        shape(dims, bf16),
        [pltpu.SemaphoreType.DMA((len(values),))],
        10,
    )(*values, *after)


def add_body(count, *refs):
    total = refs[0][...].astype(f32)
    for k in range(1, count):
        total = total + refs[k][...].astype(f32)
    refs[-1][...] = total.astype(bf16)


def add(values, after=()):
    dims = values[0].shape
    return call(
        partial(add_body, len(values)),
        "add",
        (1,),
        [whole(dims)] * len(values) + [HBM] * len(after),
        whole(dims),
        shape(dims, bf16),
        [],
        10,
    )(*values, *after)


def add_split_body(count, lead, *refs):
    for k in range(4):
        total = refs[0][k].astype(f32)
        for v in range(1, count):
            total = total + refs[v][k].astype(f32)
        refs[len(refs) - 4 + k][...] = total.astype(bf16)


def add_split(values, after=()):
    dims = values[0].shape
    steps = dims[1] if len(dims) == 5 else 1
    ins = (4, dims[1] // steps, *dims[2:])
    outs = dims[1:]
    zeros = (0,) * (len(dims) - 2)
    return call(
        partial(add_split_body, len(values), True),
        "add_split",
        (steps,),
        [pl.BlockSpec(ins, lambda i: (0, i, *zeros))] * len(values) + [HBM] * len(after),
        [pl.BlockSpec((outs[0] // steps, *outs[1:]), lambda i: (i, *zeros))] * 4,
        [shape(outs, bf16)] * 4,
        [],
        10,
    )(*values, *after)


def add_join_body(*refs):
    out = refs[-1]
    at = 0
    for group in (refs[:1], refs[1:5]):
        parts, rows = group[0].shape[1:3]
        for p in range(parts):
            total = group[0][0, p].astype(f32)
            for ref in group[1:]:
                total = total + ref[0, p].astype(f32)
            out[0, at : at + rows, :] = total.astype(bf16)
            at += rows


def add_join(first, second, after):
    rows = sum(group[0].shape[1] * group[0].shape[2] for group in (first, second))

    def spec(value):
        return pl.BlockSpec((1, *value.shape[1:]), lambda i: (i, 0, 0, 0))

    return call(
        add_join_body,
        "add_join",
        (4,),
        [spec(v) for v in [*first, *second]] + [HBM] * len(after),
        pl.BlockSpec((1, rows, BLOCK), lambda i: (i, 0, 0)),
        shape((4, rows, BLOCK), bf16),
        [],
        10,
    )(*first, *second, *after)


def send_z(piece):
    return [piece] + [shift(piece, s) for s in range(1, 4)]


def send_plane(piece):
    return [piece] + [swap(piece, 2 * j) for j in range(1, 4)]


def give_plane(parts):
    return [parts[0]] + [swap(parts[j], 2 * j) for j in range(1, 4)]


def give_z(parts):
    return [parts[0]] + [shift(parts[s], s) for s in range(1, 4)]


def gather_wide(piece, dp, extra):
    fine = dp // 8
    parts, rows = piece.shape[0], piece.shape[1] - extra
    out = lax.all_gather(piece, ("dp", "zero"), axis=0, tiled=False)
    out = out.reshape(8, fine, 4, *piece.shape)
    main = out[..., :rows, :].transpose(0, 2, 3, 1, 4, 5).reshape(8, 4, parts, 128, BLOCK)
    return [jnp.concatenate([main, out[:, 0, ..., rows:, :]], 3)]


def reduce_wide(own, other, dp, extra):
    fine = dp // 8
    blocks = jnp.stack([own, other], 1).reshape(8, 4, *own.shape[2:])
    parts, rows = own.shape[2], 128 // fine
    main = blocks[..., :128, :].reshape(8, 4, parts, fine, rows, BLOCK).transpose(0, 3, 1, 2, 4, 5)
    beside = jnp.broadcast_to(
        blocks[:, None, ..., 128:, :], (8, fine, 4, parts, extra, BLOCK)
    )
    flat = jnp.concatenate([main, beside], 4).reshape(dp * 4, parts, rows + extra, BLOCK)
    mine = lax.psum_scatter(flat, ("dp", "zero"), scatter_dimension=0, tiled=True)
    out = lax.all_gather(mine[0], "dp", axis=0, tiled=False)
    out = out.reshape(8, fine, parts, rows + extra, BLOCK)
    main = out[..., :rows, :].transpose(0, 2, 1, 3, 4).reshape(8, parts, 128, BLOCK)
    out = jnp.concatenate([main, out[:, 0, :, rows:]], 2)
    return out.reshape(8, -1, BLOCK)


def shards(
    dp, images, cotangent, counts, rel_index, regions,
    mat_w, mat_m, mat_v, vec_w, vec_m, vec_v, tab_w, tab_m, tab_v,
):
    near = dp == 8
    fine = dp // 8
    rows = 128 // fine
    me = lax.axis_index("dp")
    taken_from = jnp.stack([me // fine, me % fine]).astype(jnp.int32)
    spot = [me, lax.axis_index("zero")] if near else [0 * me, 0 * me]
    place = jnp.stack(spot + [counts[0]]).astype(jnp.int32)

    inside = np.arange(CELL) < WIN * WIN
    zones = regions.reshape(2, WIN, 2, WIN).transpose(0, 2, 1, 3).reshape(4, WIN * WIN)
    zones = jnp.pad(zones, ((0, 0), (0, 15)))
    differ = (zones[:, :, None] != zones[:, None, :]) & inside[None, None, :]
    outside = jnp.asarray(np.where(inside, 0.0, -1e30), f32)[None, :, None]
    mask_shifted = jnp.tile(jnp.where(differ, mask_value, 0.0) + outside, (1, 1, QUAD)).astype(f32)
    mask_plain = jnp.broadcast_to(outside, (1, CELL, QUAD * CELL))
    masks = (mask_plain, mask_shifted)
    perms = (frames(False), frames(True))

    packed, rel = pack(taken_from, rows, mat_w, rel_index, tab_w, vec_w)
    piece = partial(cut, taken_from, rows, mat_w)

    def attention(layer, stream, weight, after):
        return attention_forward(
            layer, place, stream, weight, heads0, masks[layer], perms[layer], after
        )

    half = images.shape[0] // 2
    if near:
        z_heads0 = stack(send_z(packed))
        sent_heads0 = send_plane(z_heads0)
        cut_mlp0 = piece(0, 1, 2, [z_heads0])
        sent_mlp0 = send_z(cut_mlp0)
        p_heads0 = stack(sent_heads0, sent_mlp0)
        heads0 = [p_heads0, swap(p_heads0, 1)]
        z_mlp0 = stack(sent_mlp0, [p_heads0])
        sent_mlp0 = send_plane(z_mlp0)
        cut_heads1 = piece(1, 0, 1, [z_mlp0])
        sent_heads1 = send_z(cut_heads1)
        cut_mlp1 = piece(1, 1, 2, [z_mlp0])
        mlp1 = gather_wide(cut_mlp1, dp, 0)
        kept0 = attention(0, images, heads0, [cut_heads1, cut_mlp1])
        p_mlp0 = stack(sent_mlp0, [kept0[0]])
        mlp0 = [p_mlp0, swap(p_mlp0, 1)]
        z_heads1 = stack(sent_heads1, [p_mlp0])
        sent_heads1 = send_plane(z_heads1)
        stream, act, slope = mlp_forward(0, place, kept0[0], mlp0, kept0[5], [z_heads1])
        p_heads1 = stack(sent_heads1, [stream])
        heads1 = [p_heads1, swap(p_heads1, 1)]
        kept1 = attention(1, stream, heads1, [])
    else:
        heads0 = gather_wide(packed, dp, EXTRA)
        mlp0 = gather_wide(piece(0, 1, 2, []), dp, 0)
        heads1 = gather_wide(piece(1, 0, 1, []), dp, 0)
        mlp1 = gather_wide(piece(1, 1, 2, []), dp, 0)
        kept0 = attention(0, images, heads0, [])
        stream, act, slope = mlp_forward(0, place, kept0[0], mlp0, kept0[5], [])
        kept1 = attention(1, stream, heads1, [])
    kept = (kept0, kept1)
    inputs = (images, stream)
    attention_w = (heads0, heads1)

    def backward_attention(layer, gradient, small, after, *span):
        mid, qkv, merged, totals, table, vec = kept[layer]
        return attention_backward(
            layer, place, gradient, inputs[layer], qkv, merged, totals, table, attention_w[layer],
            vec, small, perms[layer], rel, after, *span,
        )

    activations, grad_mid, *parts_mlp1, small = mlp_both(
        place, cotangent, kept1[0], mlp1, kept1[5], []
    )

    def backward_mlp0(gradient, after):
        return mlp_backward(0, place, gradient, act, slope, kept0[0], mlp0, kept0[5], after)

    state = (mat_w, mat_m, mat_v)
    def exchange(parts):
        return [parts[0], swap(parts[1], 1)]

    if near:
        gone_mlp1 = exchange(parts_mlp1)
        gradient, *parts_heads1, _, _ = backward_attention(1, grad_mid, small, [])
        s_mlp1 = add_split(gone_mlp1, [gradient])
        gone_mlp1 = give_plane(s_mlp1)
        gone_heads1 = exchange(parts_heads1)
        grad_mid, *parts_mlp0, small = backward_mlp0(gradient, [s_mlp1[0]])

        t_mlp1 = add(gone_mlp1, [grad_mid])
        s_heads1 = add_split(gone_heads1, [t_mlp1])
        gone_heads1 = give_plane(s_heads1)
        gone_mlp0 = exchange(lax.optimization_barrier((*parts_mlp0, s_heads1[0]))[:2])
        gradient, *parts_heads0, pairs, small = backward_attention(
            0, grad_mid, small, [s_heads1[0]], 0, half
        )

        t_all1 = add_join([t_mlp1], gone_heads1, [gradient])
        g_all1 = lax.psum_scatter(t_all1, "zero", scatter_dimension=0, tiled=True)
        s_mlp0 = add_split(gone_mlp0, [gradient])
        gone_mlp0 = give_plane(s_mlp0)
        gradient, *parts_heads0, _, small = backward_attention(
            0, grad_mid, small, [t_all1, s_mlp0[0]], half, half, [gradient, *parts_heads0, pairs]
        )

        n_all1 = lax.all_gather(g_all1[0], "dp", axis=0, tiled=False)
        t_mlp0 = add_split(gone_mlp0, [small])
        gone_heads0 = exchange(lax.optimization_barrier((*parts_heads0, t_mlp0[0]))[:2])
        gone_mlp0 = give_z(t_mlp0)
        s_heads0 = add_split(gone_heads0, [t_mlp0[0]])
        gone_heads0 = give_plane(s_heads0)
        g_mlp0 = add(gone_mlp0, [s_heads0[0]])
        gone_mlp0 = send_plane(g_mlp0)
        t_heads0 = add_split(gone_heads0, [g_mlp0])
        gone_heads0 = give_z(t_heads0)
        n_mlp0 = stack(gone_mlp0, [t_heads0[0]])
        sums_mlp0 = [n_mlp0, swap(n_mlp0, 1)]
        g_heads0 = add(gone_heads0, [n_mlp0])
        gone_heads0 = send_plane(g_heads0)
        done = adam(1, 1, place, [n_all1], state, None, [g_heads0])
        n_heads0 = stack(gone_heads0, [done[0]])
        sums_heads0 = [n_heads0, swap(n_heads0, 1)]
        done = adam(0, 1, place, sums_mlp0, state, done, [n_heads0])
        m = place[0] ^ np.arange(2)
        both = jnp.concatenate([half[:, 0, 128:] for half in sums_heads0])
        beside0 = [lax.dynamic_index_in_dim(both, (m[b] % 2) * 4 + m[b] // 2, 0, False) for b in range(2)]
    else:
        gradient, *parts_heads1, _, _ = backward_attention(1, grad_mid, small, [])
        grad_mid, *parts_mlp0, small = backward_mlp0(gradient, [])
        gradient, *parts_heads0, _, _ = backward_attention(0, grad_mid, small, [])
        n_mlp1 = reduce_wide(*parts_mlp1, dp, 0)
        n_heads1 = reduce_wide(*parts_heads1, dp, SMALL)
        n_all1 = jnp.concatenate([n_mlp1, n_heads1], 1)
        done = adam(1, 1, place, [n_all1], state, None, [])
        done = adam(0, 1, place, [reduce_wide(*parts_mlp0, dp, 0)], state, done, [])
        sums_heads0 = [reduce_wide(*parts_heads0, dp, SMALL)]
        beside0 = sums_heads0[0][:2, 128:]
    done = adam(0, 0, place, sums_heads0, state, done, [])

    def beside(block):
        return jnp.stack([beside0[block], n_all1[block, 384:]]).astype(f32)

    new_vec = adam_step(vec_w, vec_m, vec_v, beside(1)[:, 0:12, 0:128], rate_vector, 0.0)
    new_tab = adam_step(tab_w, tab_m, tab_v, beside(0)[:, 0:4, 0:NREL], rate_table, 0.0)
    return (activations, gradient, *done, *new_vec, *new_tab)


def solution(mesh):
    images = P(("dp", "zero"), None, None)
    rows = P(None, "zero", None)
    lanes = P(None, None, "zero")
    return jax.shard_map(
        partial(shards, mesh.shape["dp"]),
        mesh=mesh,
        in_specs=(images, images, P(("dp", "zero")), P(), P())
        + (rows,) * 3 + (lanes,) * 3 + (rows,) * 3,
        out_specs=(images, images) + (rows,) * 3 + (lanes,) * 3 + (rows,) * 3,
        check_vma=False,
    )
```

```python
from functools import partial

import jax
import jax.numpy as jnp
import numpy as np
from jax import lax
from jax.experimental import pallas as pl
from jax.experimental.pallas import tpu as pltpu
from jax.sharding import PartitionSpec as P

WIN = 7
SIDE = 14
STEP = 10
NREL = 169
C = 512
HID = 2048
TOKENS = SIDE * SIDE
PAIR = 2
ROWS = 208
FRAME = 256
CELL = 64
QUAD = 4
BLOCK = 256
EXTRA = 32
SMALL = 16

norm_eps = 1e-05
mask_value = -100.0
beta_one = 0.9
beta_two = 0.999
adam_eps = 1e-08
weight_decay = 0.05
rate_matrix = 0.1
rate_vector = 0.5
rate_table = 1.0
scale = 32 ** (-0.5)

bf16 = jnp.bfloat16
f32 = jnp.float32
NN = (((1,), (0,)), ((), ()))
NT = (((1,), (1,)), ((), ()))
TN = (((0,), (0,)), ((), ()))


def mm(left, right, dims=NN):
    return lax.dot_general(left, right, dims, preferred_element_type=f32)


def frames(shifted):
    move = WIN // 2 if shifted else 0
    placed = np.zeros((FRAME, ROWS), np.float32)
    for wy in range(2):
        for wx in range(2):
            for iy in range(WIN):
                for ix in range(WIN):
                    y = (wy * WIN + iy + move) % SIDE
                    x = (wx * WIN + ix + move) % SIDE
                    placed[(wy * 2 + wx) * CELL + iy * WIN + ix, y * SIDE + x] = 1
    return placed


def head_rows():
    rows = np.zeros((QUAD * CELL, 128), np.float32)
    for h in range(QUAD):
        rows[h * CELL : (h + 1) * CELL, h * 32 : (h + 1) * 32] = 1
    return rows


def head_spread(rows):
    out = np.zeros((rows, QUAD * CELL), np.float32)
    for h in range(QUAD):
        out[h, h * CELL : (h + 1) * CELL] = 1
    return out


def norm(rows):
    centred = rows - jnp.mean(rows, -1, keepdims=True)
    spread = lax.rsqrt(jnp.mean(centred * centred, -1, keepdims=True) + norm_eps)
    return centred * spread, spread


def norm_back(grad_unit, unit, spread):
    return spread * (
        grad_unit
        - jnp.mean(grad_unit, -1, keepdims=True)
        - unit * jnp.mean(grad_unit * unit, -1, keepdims=True)
    )


def column_sum(rows):
    return jnp.sum(rows, 0, keepdims=True)


def gelu_pair(u):
    size = jnp.abs(u)
    below = 1.0 + (0.3275911 * 0.5**0.5) * size
    t = pltpu.reciprocal(below, approx=True)
    bell = jnp.exp2(u * u * (-0.5 * 1.4426950408889634))
    poly = t * (
        0.127414796 + t * (-0.142248368 + t * (0.710706871 + t * (-0.726576013 + t * 0.530702714)))
    )
    tail = poly * bell
    phi = jnp.where(u >= 0, 1.0 - tail, tail)
    return u * phi, phi + u * bell * 0.3989422804014327


def quad_rows(part, heads):
    return jnp.concatenate([part] * QUAD, 0) * heads


def pick_heads(stacked, lane_head):
    low = jnp.where(lane_head == 0, stacked[:CELL], stacked[CELL : 2 * CELL])
    high = jnp.where(lane_head == 2, stacked[2 * CELL : 3 * CELL], stacked[3 * CELL :])
    return jnp.where(lane_head < 2, low, high)


def lane_heads():
    return lax.broadcasted_iota(jnp.int32, (CELL, 128), 1) // 32


def whole(shape):
    zero = (0,) * len(shape)
    return pl.BlockSpec(shape, lambda *_: zero, pipeline_mode=pl.Buffered(1))


def per_image(rows, cols):
    return pl.BlockSpec((1, rows, cols), lambda i, *_: (i, 0, 0))


def per_pair(rows, cols):
    return pl.BlockSpec((PAIR, rows, cols), lambda i, *_: (i, 0, 0))


HBM = pl.BlockSpec(memory_space=pl.ANY)


def weight_copies(place, stacks, kept, sems):
    copies = []
    for m in range(8):
        for s in range(4):
            for p in range(kept.shape[0]):
                if len(stacks) == 1:
                    source, block, owner = stacks[0].at[m, s, p], m, s
                else:
                    source = stacks[m % 2].at[m // 2, s, p]
                    block, owner = place[0] ^ m, (place[1] + 4 - s) & 3
                rows = pl.ds(pl.multiple_of(owner * 128, 128), 128)
                cols = pl.ds(pl.multiple_of(block * BLOCK, BLOCK), BLOCK)
                copies.append(
                    pltpu.make_async_copy(
                        source.at[pl.ds(0, 128), :], kept.at[p, rows, cols], sems.at[m, s, p]
                    )
                )
    return copies


def extra_copies(place, stacks, kept, sems):
    copies = []
    for m in range(8):
        for s in range(4):
            if len(stacks) == 1:
                source, block, owner = stacks[0].at[m, s, 0], m, s
            else:
                source = stacks[m % 2].at[m // 2, s, 0]
                block, owner = place[0] ^ m, (place[1] + 4 - s) & 3
            copies.append(
                pltpu.make_async_copy(
                    source.at[pl.ds(128, EXTRA), :], kept.at[block, owner], sems.at[m, s, 0]
                )
            )
    return copies


def fetch(copies):
    for copy in copies:
        copy.start()
    for copy in copies:
        copy.wait()


def call(body, name, grid, ins, outs, out_shapes, scratch, cost_us, prefetch=0, aliases=None):
    return pl.pallas_call(
        body,
        name=name,
        grid_spec=pltpu.PrefetchScalarGridSpec(
            num_scalar_prefetch=prefetch,
            grid=grid,
            in_specs=ins,
            out_specs=outs,
            scratch_shapes=scratch,
        ),
        out_shape=out_shapes,
        input_output_aliases=aliases or {},
        compiler_params=pltpu.CompilerParams(
            dimension_semantics=("arbitrary",) * len(grid), vmem_limit_bytes=58 * 1024 * 1024
        ),
        cost_estimate=pl.CostEstimate(
            flops=0, bytes_accessed=int(cost_us * 3.69e6), transcendentals=0
        ),
    )


def shape(dims, kind):
    return jax.ShapeDtypeStruct(dims, kind)


def pack_body(place, *refs):
    mats, (pair_index, tab, vec, spread) = refs[:6], refs[6:10]
    out, mlp0, heads1, mlp1, rel, spread_tab, small = refs[10:]
    rows = mats[0].shape[1]
    out[0, 0:rows, :] = mats[0][0].astype(bf16)
    for ref, at, n in ((mlp0, 0, 1), (mlp0, 1, 2), (heads1, 0, 3), (mlp1, 0, 4), (mlp1, 1, 5)):
        ref[at] = mats[n][0].astype(bf16)
    rel[...] = jnp.full(rel.shape, -1, jnp.int32)
    across = pair_index[...].astype(f32).T.astype(jnp.int32)
    for h in range(QUAD):
        rel[0 : WIN * WIN, CELL * h : CELL * h + WIN * WIN] = across
    for layer in range(2):
        spread_tab[layer, 0:NREL, :] = mm(tab[layer].astype(bf16), spread[...], TN)
    pairs = rel[pl.ds(pl.multiple_of(place[0] * 8, 8), 8), :]

    def step(r, sums):
        hit = pairs == r
        return tuple(
            jnp.where(hit, spread_tab[layer, pl.ds(r, 1), :], sums[layer]) for layer in range(2)
        )

    start = jnp.zeros((8, QUAD * CELL), f32)
    first, second = lax.fori_loop(0, NREL, step, (start, start), unroll=13)
    out[0, rows : rows + 16, :] = jnp.concatenate([first, second], 0).astype(bf16)
    small[...] = jnp.zeros_like(small)
    row = jnp.minimum(place[0] * 2, 10)
    for layer in range(2):
        for k in range(2):
            small[k : k + 1, layer * 128 : (layer + 1) * 128] = vec[row + k, layer : layer + 1, :]
    out[0, rows + 16 : rows + 32, :] = small[...].astype(bf16)


def pack(place, rows, mat_w, rel_index, tab_w, vec_w):
    vec_w = vec_w.transpose(1, 0, 2)

    def block(layer, part):
        return pl.BlockSpec(
            (1, rows, BLOCK), lambda i, place: (layer, place[1], part * 8 + place[0])
        )

    dims = [(1, rows + EXTRA, BLOCK), (2, rows, BLOCK), (1, rows, BLOCK), (2, rows, BLOCK)]
    return call(
        pack_body,
        "pack",
        (1,),
        [block(layer, part) for layer in range(2) for part in range(3)]
        + [
            whole(rel_index.shape),
            whole(tab_w.shape),
            whole(vec_w.shape),
            whole((QUAD, QUAD * CELL)),
        ],
        [whole(d) for d in dims] + [whole((CELL, QUAD * CELL))],
        [shape(d, bf16) for d in dims] + [shape((CELL, QUAD * CELL), jnp.int32)],
        [pltpu.VMEM((2, 176, QUAD * CELL), f32), pltpu.VMEM((16, 256), f32)],
        4,
        prefetch=1,
    )(place, *[mat_w] * 6, rel_index, tab_w, vec_w, jnp.asarray(head_spread(QUAD), bf16))


def attention_forward_body(layer, stacks, waits, place, *refs):
    arrays, refs = refs[: stacks[0]], refs[stacks[0] :]
    extras, refs = refs[: stacks[1]], refs[stacks[1] + waits :]
    x, mask, perm, perm_back, heads = refs[:5]
    mid, qkv, merged, totals, table, vec, framed, kept, extra_kept, sems, more_sems = refs[5:]
    weight, extra = kept.at[0], extra_kept

    @pl.when(pl.program_id(0) == 0)
    def _():
        fetch(
            weight_copies(place, arrays, kept, sems)
            + extra_copies(place, extras, extra_kept, more_sems)
        )
        vec[...] = jnp.zeros_like(vec)
        for z in range(4):
            for d in range(8):
                pair = extra[d, z, 0:16, :].astype(f32)
                bias = pair[8 * layer : 8 * layer + 8]
                for w in range(table.shape[0]):
                    table[w, z, 8 * d : 8 * d + 8, :] = bias + mask[w, 8 * d : 8 * d + 8, :]
                if d < 6:
                    rows = extra[d, z, 16:32, 128 * layer : 128 * layer + 128].astype(f32)
                    vec[2 * d : 2 * d + 2, 128 * z : 128 * z + 128] = rows[0:2]

    stream = x[0]
    unit, _ = norm(stream)
    normed = (unit * vec[0:1, :] + vec[1:2, :]).astype(bf16)
    normed = mm(perm[...], normed).astype(bf16)
    for c in range(6):
        part = mm(normed, weight[:, 256 * c : 256 * c + 256])
        if c < 2:
            part = part + vec[2:3, 256 * c : 256 * c + 256]
        if c >= 4:
            part = part + vec[3:4, 256 * (c - 4) : 256 * (c - 4) + 256]
        qkv[0, :, 256 * c : 256 * c + 256] = part.astype(bf16)
    lane_head = lane_heads()

    def score(unit):
        rows, at = slice(CELL * (unit // 4), CELL * (unit // 4) + CELL), 128 * (unit % 4)
        query = quad_rows(qkv[0, rows, at : at + 128], heads[...])
        return mm(qkv[0, rows, C + at : C + at + 128], query, NT)

    ahead = score(0)
    for n in range(16):
        w, g = n // 4, n % 4
        rows, at = slice(CELL * w, CELL * w + CELL), 128 * g
        scores = ahead * scale + table[w % table.shape[0], g]
        if n < 15:
            ahead = score(n + 1)
        top = jnp.max(scores, 0, keepdims=True)
        raised = jnp.exp(scores - top)
        total = jnp.sum(raised, 0, keepdims=True)
        totals[0, n : n + 1, :] = top + jnp.log(total)
        probs = (raised * (1.0 / total)).astype(bf16)
        stacked = mm(probs, qkv[0, rows, 2 * C + at : 2 * C + at + 128], TN)
        framed[rows, at : at + 128] = pick_heads(stacked, lane_head).astype(bf16)
    gathered = mm(perm_back[...], framed[...]).astype(bf16)
    merged[0] = gathered
    mid[0] = stream + mm(gathered, weight[:, 3 * C :]) + vec[4:5, :]


def attention_forward(layer, place, x, weight, extra, mask, perm, after):
    images = x.shape[0]
    tables = mask.shape[0]
    return call(
        partial(attention_forward_body, layer, (len(weight), len(extra)), len(after)),
        f"attention_forward_{layer}",
        (images,),
        [HBM] * (len(weight) + len(extra) + len(after))
        + [
            per_image(x.shape[1], C),
            whole(mask.shape),
            whole((FRAME, ROWS)),
            whole((ROWS, FRAME)),
            whole((QUAD * CELL, 128)),
        ],
        [
            per_image(ROWS, C),
            per_image(FRAME, 3 * C),
            per_image(ROWS, C),
            per_image(16, QUAD * CELL),
            pl.BlockSpec((tables, 4, CELL, QUAD * CELL), lambda i, *_: (0, 0, 0, 0)),
            pl.BlockSpec((16, C), lambda i, *_: (0, 0)),
        ],
        [
            shape((images, ROWS, C), f32),
            shape((images, FRAME, 3 * C), bf16),
            shape((images, ROWS, C), bf16),
            shape((images, 16, QUAD * CELL), f32),
            shape((tables, 4, CELL, QUAD * CELL), f32),
            shape((16, C), f32),
        ],
        [
            pltpu.VMEM((FRAME, C), bf16),
            pltpu.VMEM((1, C, HID), bf16),
            pltpu.VMEM((8, 4, EXTRA, BLOCK), bf16),
            pltpu.SemaphoreType.DMA((8, 4, 1)),
            pltpu.SemaphoreType.DMA((8, 4, 1)),
        ],
        20,
        prefetch=1,
    )(
        place,
        *weight,
        *extra,
        *after,
        x,
        mask,
        jnp.asarray(perm, bf16),
        jnp.asarray(perm.T, bf16),
        jnp.asarray(head_rows(), bf16),
    )


def mlp_forward_body(stacks, waits, place, *refs):
    arrays, refs = refs[:stacks], refs[stacks + waits :]
    mid, vec, result, act, slope, kept, sems = refs
    first, second = kept.at[0], kept.at[1]

    @pl.when(pl.program_id(0) == 0)
    def _():
        fetch(weight_copies(place, arrays, kept, sems))

    rows = PAIR * ROWS
    stream = mid[...].reshape(rows, C)
    unit, _ = norm(stream)
    normed = (unit * vec[5:6, :] + vec[6:7, :]).astype(bf16)
    for c in range(8):
        cols = slice(256 * c, 256 * c + 256)
        bias = vec[8 + c // 2 : 9 + c // 2, 256 * (c % 2) : 256 * (c % 2) + 256]
        value, pull = gelu_pair(mm(normed, first[:, cols]) + bias)
        act[:, :, cols] = value.astype(bf16).reshape(PAIR, ROWS, BLOCK)
        slope[:, :, cols] = pull.astype(bf16).reshape(PAIR, ROWS, BLOCK)
    total = stream + vec[7:8, :] + mm(act[...].reshape(rows, HID), second[...], NT)
    result[...] = total.reshape(PAIR, ROWS, C)


def mlp_forward(layer, place, mid, weight, vec, after):
    images = mid.shape[0]
    return call(
        partial(mlp_forward_body, len(weight), len(after)),
        f"mlp_forward_{layer}",
        (images // PAIR,),
        [HBM] * (len(weight) + len(after)) + [per_pair(ROWS, C), whole(vec.shape)],
        [per_pair(ROWS, C), per_pair(ROWS, HID), per_pair(ROWS, HID)],
        [
            shape((images, ROWS, C), f32),
            shape((images, ROWS, HID), bf16),
            shape((images, ROWS, HID), bf16),
        ],
        [pltpu.VMEM((2, C, HID), bf16), pltpu.SemaphoreType.DMA((8, 4, 2))],
        22,
        prefetch=1,
    )(place, *weight, *after, mid, vec)


def mlp_both_body(stacks, waits, place, *refs):
    arrays, refs = refs[:stacks], refs[stacks + waits :]
    grad, mid, vec, result, grad_mid, own, other, small = refs[:8]
    all_grad, all_act, all_inner, all_normed, kept, sems = refs[8:]
    first, second = kept.at[0], kept.at[1]
    i = pl.program_id(0)

    @pl.when(i == 0)
    def _():
        fetch(weight_copies(place, arrays, kept, sems))
        small[...] = jnp.zeros_like(small)

    rows = PAIR * ROWS
    grad_out = grad[...].reshape(rows, C)
    here = pl.ds(pl.multiple_of(i * rows, 32), rows)
    low = grad_out.astype(bf16)
    all_grad[here, :] = low
    small[7:8, :] += column_sum(grad_out)
    stream = mid[...].reshape(rows, C)
    unit, spread = norm(stream)
    normed = (unit * vec[5:6, :] + vec[6:7, :]).astype(bf16)
    all_normed[here, :] = normed
    for c in range(8):
        cols = slice(256 * c, 256 * c + 256)
        row, lane = 8 + c // 2, 256 * (c % 2)
        bias = vec[row : row + 1, lane : lane + 256]
        value, pull = gelu_pair(mm(normed, first[:, cols]) + bias)
        all_act[here, cols] = value.astype(bf16)
        inner = (mm(low, second[:, cols]) * pull).astype(bf16)
        all_inner[here, cols] = inner
        small[row : row + 1, lane : lane + 256] += column_sum(inner.astype(f32))
    back = mm(all_inner[here, :], first[...], NT)
    small[5:6, :] += column_sum(back * unit)
    small[6:7, :] += column_sum(back)
    grad_mid[...] = (grad_out + norm_back(back * vec[5:6, :], unit, spread)).reshape(PAIR, ROWS, C)
    total = stream + vec[7:8, :] + mm(all_act[here, :], second[...], NT)
    for n in range(PAIR):
        alive = (i * PAIR + n < place[2]).astype(f32)
        result[n] = (total[n * ROWS : n * ROWS + TOKENS] * alive).astype(bf16)

    @pl.when(i == pl.num_programs(0) - 1)
    def _():
        mlp_weight_grads(place, False, all_grad, all_act, all_inner, all_normed, own, other)


def mlp_weight_grads(place, rotate, all_grad, all_act, all_inner, all_normed, own, other):
    grad_across = all_grad[...].T
    normed_across = all_normed[...].T
    for m in range(8):
        cols = pl.ds(pl.multiple_of((place[0] ^ m) * BLOCK, BLOCK), BLOCK)
        out = other if m % 2 else own
        for p, block in enumerate(
            (mm(normed_across, all_inner[:, cols]), mm(grad_across, all_act[:, cols]))
        ):
            block = block.astype(bf16)
            for z in range(4):
                to = (z + 4 - place[1]) & 3 if rotate else z
                out[m // 2, to, p] = block[128 * z : 128 * z + 128]


def mlp_both(place, grad, mid, weight, vec, after):
    images = mid.shape[0]
    total = images * ROWS
    pieces = (4, 4, 2, 128, BLOCK)
    return call(
        partial(mlp_both_body, len(weight), len(after)),
        "mlp_both",
        (images // PAIR,),
        [HBM] * (len(weight) + len(after)) + [per_pair(ROWS, C), per_pair(ROWS, C), whole(vec.shape)],
        [per_pair(TOKENS, C), per_pair(ROWS, C), whole(pieces), whole(pieces), whole((16, C))],
        [
            shape((images, TOKENS, C), bf16),
            shape((images, ROWS, C), f32),
            shape(pieces, bf16),
            shape(pieces, bf16),
            shape((16, C), f32),
        ],
        [
            pltpu.VMEM((total, C), bf16),
            pltpu.VMEM((total, HID), bf16),
            pltpu.VMEM((total, HID), bf16),
            pltpu.VMEM((total, C), bf16),
            pltpu.VMEM((2, C, HID), bf16),
            pltpu.SemaphoreType.DMA((8, 4, 2)),
        ],
        45,
        prefetch=1,
    )(place, *weight, *after, grad, mid, vec)


def mlp_backward_body(stacks, waits, place, *refs):
    arrays, refs = refs[:stacks], refs[stacks + waits :]
    grad, act, slope, mid, vec, grad_mid, own, other, small = refs[:9]
    all_grad, all_act, all_inner, all_normed, kept, sems = refs[9:]
    first, second = kept.at[0], kept.at[1]
    i = pl.program_id(0)

    @pl.when(i == 0)
    def _():
        fetch(weight_copies(place, arrays, kept, sems))
        small[...] = jnp.zeros_like(small)

    rows = PAIR * ROWS
    grad_out = grad[...].reshape(rows, C)
    here = pl.ds(pl.multiple_of(i * rows, 32), rows)
    low = grad_out.astype(bf16)
    all_grad[here, :] = low
    small[7:8, :] += column_sum(low.astype(f32))
    all_act[here, :] = act[...].reshape(rows, HID)
    unit, spread = norm(mid[...].reshape(rows, C))
    all_normed[here, :] = (unit * vec[5:6, :] + vec[6:7, :]).astype(bf16)
    for c in range(8):
        cols = slice(256 * c, 256 * c + 256)
        pull = slope[:, :, cols].reshape(rows, BLOCK).astype(f32)
        inner = (mm(low, second[:, cols]) * pull).astype(bf16)
        all_inner[here, cols] = inner
        row, lane = 8 + c // 2, 256 * (c % 2)
        small[row : row + 1, lane : lane + 256] += column_sum(inner.astype(f32))
    back = mm(all_inner[here, :], first[...], NT)
    small[5:6, :] += column_sum(back * unit)
    small[6:7, :] += column_sum(back)
    grad_mid[...] = (grad_out + norm_back(back * vec[5:6, :], unit, spread)).reshape(PAIR, ROWS, C)

    @pl.when(i == pl.num_programs(0) - 1)
    def _():
        mlp_weight_grads(place, True, all_grad, all_act, all_inner, all_normed, own, other)


def mlp_backward(layer, place, grad, act, slope, mid, weight, vec, after):
    images = mid.shape[0]
    total = images * ROWS
    pieces = (4, 4, 2, 128, BLOCK)
    return call(
        partial(mlp_backward_body, len(weight), len(after)),
        f"mlp_backward_{layer}",
        (images // PAIR,),
        [HBM] * (len(weight) + len(after))
        + [
            per_pair(grad.shape[1], C),
            per_pair(ROWS, HID),
            per_pair(ROWS, HID),
            per_pair(ROWS, C),
            whole(vec.shape),
        ],
        [per_pair(ROWS, C), whole(pieces), whole(pieces), whole((16, C))],
        [
            shape((images, ROWS, C), f32),
            shape(pieces, bf16),
            shape(pieces, bf16),
            shape((16, C), f32),
        ],
        [
            pltpu.VMEM((total, C), bf16),
            pltpu.VMEM((total, HID), bf16),
            pltpu.VMEM((total, HID), bf16),
            pltpu.VMEM((total, C), bf16),
            pltpu.VMEM((2, C, HID), bf16),
            pltpu.SemaphoreType.DMA((8, 4, 2)),
        ],
        30,
        prefetch=1,
    )(place, *weight, *after, grad, act, slope, mid, vec)


def attention_backward_body(layer, stacks, waits, resumed, ends, place, *refs):
    arrays, refs = refs[:stacks], refs[stacks + waits :]
    if resumed:
        (own_before, other_before, pairs_before), refs = refs[1:4], refs[4:]
    grad, x, qkv, merged, totals, table, vec, before = refs[:8]
    perm, perm_back, heads, rel, spread, result, own, other, pairs, small = refs[8:18]
    framed, grad_framed, all_normed, all_packed, all_merged = refs[18:23]
    across, hits, beside, kept, sems = refs[23:]
    weight = kept.at[0]
    i = pl.program_id(0)

    @pl.when(i == 0)
    def _():
        fetch(weight_copies(place, arrays, kept, sems))
        small[...] = before[...]
        pairs[...] = pairs_before[...] if resumed else jnp.zeros_like(pairs)

    stream = x[0]
    here = pl.ds(pl.multiple_of(i * ROWS, 16), ROWS)
    unit, spread_one = norm(stream)
    all_normed[here, :] = (unit * vec[0:1, :] + vec[1:2, :]).astype(bf16)
    low = grad[0].astype(bf16)
    all_packed[here, 3 * C :] = low
    all_merged[here, :] = merged[0]
    small[4:5, :] += column_sum(low.astype(f32))
    moved = mm(perm[...], low).astype(bf16)
    framed[...] = mm(moved, weight[:, 3 * C :], NT).astype(bf16)
    lane_head = lane_heads()
    for w in range(4):
        rows = slice(CELL * w, CELL * w + CELL)
        at = [128 * g for g in range(4)]
        keys = [qkv[0, rows, C + c : C + c + 128] for c in at]
        query = [quad_rows(qkv[0, rows, c : c + 128], heads[...]) for c in at]
        pull = [quad_rows(framed[rows, c : c + 128], heads[...]) for c in at]
        scores = [mm(keys[g], query[g], NT) for g in range(4)]
        grad_probs = [
            mm(qkv[0, rows, 2 * C + at[g] : 2 * C + at[g] + 128], pull[g], NT) for g in range(4)
        ]
        probs, grad_scores = [], []
        for g in range(4):
            shifted = scores[g] * scale + table[w % table.shape[0], g]
            prob = jnp.exp(shifted - totals[0, 4 * w + g : 4 * w + g + 1, :])
            mean = jnp.sum(prob * grad_probs[g], 0, keepdims=True)
            grad_score = (prob * (grad_probs[g] - mean)).astype(bf16)
            pairs[g] += grad_score.astype(f32)
            probs.append(prob.astype(bf16))
            grad_scores.append(grad_score)
        for g in range(4):
            grad_value = mm(probs[g], pull[g])
            grad_framed[rows, 2 * C + at[g] : 2 * C + at[g] + 128] = grad_value.astype(bf16)
        for g in range(4):
            grad_key = mm(grad_scores[g], query[g]) * scale
            grad_framed[rows, C + at[g] : C + at[g] + 128] = grad_key.astype(bf16)
        for g in range(4):
            grad_query = pick_heads(mm(grad_scores[g], keys[g], TN), lane_head) * scale
            grad_framed[rows, at[g] : at[g] + 128] = grad_query.astype(bf16)
    for c in range(6):
        cols = slice(256 * c, 256 * c + 256)
        part = mm(perm_back[...], grad_framed[:, cols])
        all_packed[here, cols] = part.astype(bf16)
        if c < 2:
            small[2:3, cols] += column_sum(part)
        if c >= 4:
            small[3:4, 256 * (c - 4) : 256 * (c - 4) + 256] += column_sum(part)
    back = mm(all_packed[here, : 3 * C], weight[:, : 3 * C], NT)
    small[0:1, :] += column_sum(back * unit)
    small[1:2, :] += column_sum(back)
    total = grad[0] + norm_back(back * vec[0:1, :], unit, spread_one)
    result[0] = total[: result.shape[1]]

    @pl.when(i == pl.num_programs(0) - 1)
    def _():
        across[0] = all_normed[...].T
        across[1] = all_merged[...].T
        beside[...] = jnp.zeros_like(beside)
        if ends:
            hits[...] = jnp.zeros_like(hits)

            def step(r, carry):
                same = rel[...] == r
                for g in range(4):
                    kept_pairs = jnp.where(same, pairs[g], 0.0)
                    hits[pl.ds(r, 1), 256 * g : 256 * g + 256] = column_sum(kept_pairs)
                return carry

            lax.fori_loop(0, NREL, step, 0)
            for z in range(4):
                beside[0, z] = lax.dot_general(
                    spread[...],
                    hits[:, 256 * z : 256 * z + 256],
                    NT,
                    precision=lax.Precision.HIGHEST,
                    preferred_element_type=f32,
                ).astype(bf16)
                beside[1, z, :, 0:128] = small[:, 128 * z : 128 * z + 128].astype(bf16)
        for m in range(8):
            b = place[0] ^ m
            left = across[jnp.where(b < 6, 0, 1)]
            right = all_packed[:, pl.ds(pl.multiple_of(b * BLOCK, BLOCK), BLOCK)]
            block = mm(left, right)
            out = other if m % 2 else own
            for z in range(4):
                to = (z + 4 - place[1]) & 3 if layer == 0 else z
                new = block[128 * z : 128 * z + 128]
                if resumed:
                    old = other_before if m % 2 else own_before
                    new = new + old[m // 2, to, 0, 0:128, :].astype(f32)
                out[m // 2, to, 0, 0:128, :] = new.astype(bf16)
                out[m // 2, to, 0, 128:144, :] = beside[jnp.minimum(b, 2), z]


def attention_backward(
    layer, place, grad, x, qkv, merged, totals, table, weight, vec, small, perm, rel, after,
    first=0, count=None, resume=None,
):
    images = grad.shape[0]
    count = count or images
    pieces = (4, 4, 1, 128 + SMALL, BLOCK)
    pairs = (4, CELL, QUAD * CELL)
    total = count * ROWS
    out_rows = TOKENS if layer == 0 else ROWS

    def image(rows, cols):
        return pl.BlockSpec((1, rows, cols), lambda i, *_: (i + first, 0, 0))

    resumed = list(resume or [])
    return call(
        partial(
            attention_backward_body, layer, len(weight), len(after), bool(resumed),
            first + count == images,
        ),
        f"attention_backward_{layer}_{first}",
        (count,),
        [HBM] * (len(weight) + len(after))
        + ([HBM, whole(pieces), whole(pieces), whole(pairs)] if resumed else [])
        + [
            image(ROWS, C),
            image(x.shape[1], C),
            image(FRAME, 3 * C),
            image(ROWS, C),
            image(16, QUAD * CELL),
            whole(table.shape),
            whole(vec.shape),
            whole((16, C)),
            whole((FRAME, ROWS)),
            whole((ROWS, FRAME)),
            whole((QUAD * CELL, 128)),
            whole(rel.shape),
            whole((SMALL, QUAD * CELL)),
        ],
        [image(out_rows, C), whole(pieces), whole(pieces), whole(pairs), whole((16, C))],
        [
            shape((images, out_rows, C), f32),
            shape(pieces, bf16),
            shape(pieces, bf16),
            shape(pairs, f32),
            shape((16, C), f32),
        ],
        [
            pltpu.VMEM((FRAME, C), bf16),
            pltpu.VMEM((FRAME, 3 * C), bf16),
            pltpu.VMEM((total, C), bf16),
            pltpu.VMEM((total, 4 * C), bf16),
            pltpu.VMEM((total, C), bf16),
            pltpu.VMEM((2, C, total), bf16),
            pltpu.VMEM((256, 4 * QUAD * CELL), f32),
            pltpu.VMEM((3, 4, SMALL, BLOCK), bf16),
            pltpu.VMEM((1, C, HID), bf16),
            pltpu.SemaphoreType.DMA((8, 4, 1)),
        ],
        6 * count,
        prefetch=1,
        aliases={1 + len(weight) + len(after): 0} if resumed else None,
    )(
        place,
        *weight,
        *after,
        *resumed,
        grad,
        x,
        qkv,
        merged,
        totals,
        table,
        vec,
        small,
        jnp.asarray(perm, bf16),
        jnp.asarray(perm.T, bf16),
        jnp.asarray(head_rows(), bf16),
        rel,
        jnp.asarray(head_spread(SMALL), f32),
    )


def adam_step(weight, first, second, gradient, rate, decay):
    first_new = beta_one * first + (1.0 - beta_one) * gradient
    second_new = beta_two * second + (1.0 - beta_two) * gradient * gradient
    first_hat = first_new / (1.0 - beta_one**STEP)
    second_hat = second_new / (1.0 - beta_two**STEP)
    weight_new = weight - rate * (first_hat / (jnp.sqrt(second_hat) + adam_eps) + decay * weight)
    return (weight_new, first_new, second_new)


def adam_block(grad, weight, first, second, outs, cols):
    news = adam_step(
        weight[0, :, cols], first[0, :, cols], second[0, :, cols],
        grad.astype(f32), rate_matrix, weight_decay,
    )
    for out, new in zip(outs, news):
        out[0, :, cols] = new


def adam_body(place, near, far, weight, first, second, *refs):
    for j in range(2):
        for k in range(2):
            block = (((place[0] // 2) & 1) ^ j) * 2 + ((place[0] & 1) ^ k)
            cols = pl.ds(pl.multiple_of(block * BLOCK, BLOCK), BLOCK)
            adam_block((far if k else near)[j, 0], weight, first, second, refs[-3:], cols)


def adam_body_plain(place, sums, weight, first, second, *refs):
    for k in range(4):
        cols = slice(BLOCK * k, BLOCK * k + BLOCK)
        adam_block(sums[k], weight, first, second, refs[-3:], cols)


def adam(layer, part, place, sums, state, done, after):
    kept = [] if done is None else list(done)
    if len(sums) == 2:
        parts = sums[0].shape[1]
        body = adam_body
        spec = pl.BlockSpec(
            (1, 128, 4 * BLOCK),
            lambda p, j, place: (layer, 0, (part + p) % 3 * 2 + ((place[0] // 4) ^ j)),
        )
        piece = pl.BlockSpec((2, 1, 128, BLOCK), lambda p, j, place: (j, p, 0, 0))
    else:
        parts = sums[0].shape[1] // 128
        body = adam_body_plain
        spec = pl.BlockSpec(
            (1, 128, 4 * BLOCK), lambda p, j, place: (layer, 0, (part + p) % 3 * 2 + j)
        )
        piece = pl.BlockSpec((4, 128, BLOCK), lambda p, j, place: (j, p, 0))
    return call(
        body,
        f"adam_{layer}_{part}",
        (parts, 2),
        [piece] * len(sums) + [spec] * 3 + [HBM] * (len(kept) + len(after)),
        [spec] * 3,
        [shape(state[0].shape, f32)] * 3,
        [],
        3 * parts,
        prefetch=1,
        aliases={4 + len(sums) + k: k for k in range(len(kept))},
    )(place, *sums, *state, *kept, *after)


def swap(value, bits):
    return lax.ppermute(value, "dp", [(i, i ^ bits) for i in range(8)])


def shift(value, steps):
    return lax.ppermute(value, "zero", [(i, (i + steps) % 4) for i in range(4)])


def tie(values, after):
    values = list(values)
    return list(lax.optimization_barrier((*values, *after))[: len(values)])


def stack(values, after=()):
    return jnp.stack(tie(values, after) if after else values)


def add_body(count, *refs):
    total = refs[0][...].astype(f32)
    for k in range(1, count):
        total = total + refs[k][...].astype(f32)
    refs[-1][...] = total.astype(bf16)


def add(values, after=()):
    dims = values[0].shape
    return call(
        partial(add_body, len(values)),
        "add",
        (1,),
        [whole(dims)] * len(values) + [HBM] * len(after),
        whole(dims),
        shape(dims, bf16),
        [],
        10,
    )(*values, *after)


def add_split_body(count, lead, *refs):
    for k in range(4):
        total = refs[0][k].astype(f32)
        for v in range(1, count):
            total = total + refs[v][k].astype(f32)
        refs[len(refs) - 4 + k][...] = total.astype(bf16)


def add_split(values, after=()):
    dims = values[0].shape
    steps = dims[1] if len(dims) == 5 else 1
    ins = (4, dims[1] // steps, *dims[2:])
    outs = dims[1:]
    zeros = (0,) * (len(dims) - 2)
    return call(
        partial(add_split_body, len(values), True),
        "add_split",
        (steps,),
        [pl.BlockSpec(ins, lambda i: (0, i, *zeros))] * len(values) + [HBM] * len(after),
        [pl.BlockSpec((outs[0] // steps, *outs[1:]), lambda i: (i, *zeros))] * 4,
        [shape(outs, bf16)] * 4,
        [],
        10,
    )(*values, *after)


def add_join_body(*refs):
    out = refs[-1]
    at = 0
    for group in (refs[:1], refs[1:5]):
        parts, rows = group[0].shape[1:3]
        for p in range(parts):
            total = group[0][0, p].astype(f32)
            for ref in group[1:]:
                total = total + ref[0, p].astype(f32)
            out[0, at : at + rows, :] = total.astype(bf16)
            at += rows


def add_join(first, second, after):
    rows = sum(group[0].shape[1] * group[0].shape[2] for group in (first, second))

    def spec(value):
        return pl.BlockSpec((1, *value.shape[1:]), lambda i: (i, 0, 0, 0))

    return call(
        add_join_body,
        "add_join",
        (4,),
        [spec(v) for v in [*first, *second]] + [HBM] * len(after),
        pl.BlockSpec((1, rows, BLOCK), lambda i: (i, 0, 0)),
        shape((4, rows, BLOCK), bf16),
        [],
        10,
    )(*first, *second, *after)


def send_z(piece):
    return [piece] + [shift(piece, s) for s in range(1, 4)]


def send_plane(piece):
    return [piece] + [swap(piece, 2 * j) for j in range(1, 4)]


def give_plane(parts):
    return [parts[0]] + [swap(parts[j], 2 * j) for j in range(1, 4)]


def give_z(parts):
    return [parts[0]] + [shift(parts[s], s) for s in range(1, 4)]


def gather_wide(piece, dp, extra):
    fine = dp // 8
    parts, rows = piece.shape[0], piece.shape[1] - extra
    out = lax.all_gather(piece, ("dp", "zero"), axis=0, tiled=False)
    out = out.reshape(8, fine, 4, *piece.shape)
    main = out[..., :rows, :].transpose(0, 2, 3, 1, 4, 5).reshape(8, 4, parts, 128, BLOCK)
    return [jnp.concatenate([main, out[:, 0, ..., rows:, :]], 3)]


def reduce_wide(own, other, dp, extra):
    fine = dp // 8
    blocks = jnp.stack([own, other], 1).reshape(8, 4, *own.shape[2:])
    parts, rows = own.shape[2], 128 // fine
    main = blocks[..., :128, :].reshape(8, 4, parts, fine, rows, BLOCK).transpose(0, 3, 1, 2, 4, 5)
    beside = jnp.broadcast_to(
        blocks[:, None, ..., 128:, :], (8, fine, 4, parts, extra, BLOCK)
    )
    flat = jnp.concatenate([main, beside], 4).reshape(dp * 4, parts, rows + extra, BLOCK)
    mine = lax.psum_scatter(flat, ("dp", "zero"), scatter_dimension=0, tiled=True)
    out = lax.all_gather(mine[0], "dp", axis=0, tiled=False)
    out = out.reshape(8, fine, parts, rows + extra, BLOCK)
    main = out[..., :rows, :].transpose(0, 2, 1, 3, 4).reshape(8, parts, 128, BLOCK)
    out = jnp.concatenate([main, out[:, 0, :, rows:]], 2)
    return out.reshape(8, -1, BLOCK)


def shards(
    dp, images, cotangent, counts, rel_index, regions,
    mat_w, mat_m, mat_v, vec_w, vec_m, vec_v, tab_w, tab_m, tab_v,
):
    near = dp == 8
    fine = dp // 8
    rows = 128 // fine
    me = lax.axis_index("dp")
    taken_from = jnp.stack([me // fine, me % fine]).astype(jnp.int32)
    spot = [me, lax.axis_index("zero")] if near else [0 * me, 0 * me]
    place = jnp.stack(spot + [counts[0]]).astype(jnp.int32)

    inside = np.arange(CELL) < WIN * WIN
    zones = regions.reshape(2, WIN, 2, WIN).transpose(0, 2, 1, 3).reshape(4, WIN * WIN)
    zones = jnp.pad(zones, ((0, 0), (0, 15)))
    differ = (zones[:, :, None] != zones[:, None, :]) & inside[None, None, :]
    outside = jnp.asarray(np.where(inside, 0.0, -1e30), f32)[None, :, None]
    mask_shifted = jnp.tile(jnp.where(differ, mask_value, 0.0) + outside, (1, 1, QUAD)).astype(f32)
    mask_plain = jnp.broadcast_to(outside, (1, CELL, QUAD * CELL))
    masks = (mask_plain, mask_shifted)
    perms = (frames(False), frames(True))

    packed, cut_mlp0, cut_heads1, cut_mlp1, rel = pack(
        taken_from, rows, mat_w, rel_index, tab_w, vec_w
    )
    alive = (jnp.arange(images.shape[0]) < counts[0]).astype(f32)[:, None, None]
    pad = ((0, 0), (0, ROWS - TOKENS), (0, 0))
    images = jnp.pad(images.astype(f32), pad)
    cotangent = jnp.pad(cotangent.astype(f32) * alive, pad)

    def attention(layer, stream, weight, after):
        return attention_forward(
            layer, place, stream, weight, heads0, masks[layer], perms[layer], after
        )

    half = images.shape[0] // 2
    if near:
        sent_heads0 = send_z(packed)
        *sent_heads0, images, cotangent, mask_shifted = tie(
            [*sent_heads0, images, cotangent, mask_shifted], []
        )
        masks = (mask_plain, mask_shifted)
        z_heads0 = stack(sent_heads0)
        sent_heads0 = send_plane(z_heads0)
        sent_mlp0 = send_z(tie([cut_mlp0], [z_heads0])[0])
        p_heads0 = stack(sent_heads0, sent_mlp0)
        heads0 = [p_heads0, swap(p_heads0, 1)]
        z_mlp0 = stack(sent_mlp0, [p_heads0])
        sent_mlp0 = send_plane(z_mlp0)
        cut_heads1, cut_mlp1 = tie([cut_heads1, cut_mlp1], [z_mlp0])
        sent_heads1 = send_z(cut_heads1)
        mlp1 = gather_wide(cut_mlp1, dp, 0)
        kept0 = attention(0, images, heads0, [z_mlp0])
        p_mlp0 = stack(sent_mlp0, [kept0[0]])
        mlp0 = [p_mlp0, swap(p_mlp0, 1)]
        z_heads1 = stack(sent_heads1, [p_mlp0])
        sent_heads1 = send_plane(z_heads1)
        stream, act, slope = mlp_forward(0, place, kept0[0], mlp0, kept0[5], [z_heads1])
        p_heads1 = stack(sent_heads1, [stream])
        heads1 = [p_heads1, swap(p_heads1, 1)]
        kept1 = attention(1, stream, heads1, [])
    else:
        heads0 = gather_wide(packed, dp, EXTRA)
        mlp0 = gather_wide(cut_mlp0, dp, 0)
        heads1 = gather_wide(cut_heads1, dp, 0)
        mlp1 = gather_wide(cut_mlp1, dp, 0)
        kept0 = attention(0, images, heads0, [])
        stream, act, slope = mlp_forward(0, place, kept0[0], mlp0, kept0[5], [])
        kept1 = attention(1, stream, heads1, [])
    kept = (kept0, kept1)
    inputs = (images, stream)
    attention_w = (heads0, heads1)

    def backward_attention(layer, gradient, small, after, *span):
        mid, qkv, merged, totals, table, vec = kept[layer]
        return attention_backward(
            layer, place, gradient, inputs[layer], qkv, merged, totals, table, attention_w[layer],
            vec, small, perms[layer], rel, after, *span,
        )

    activations, grad_mid, *parts_mlp1, small = mlp_both(
        place, cotangent, kept1[0], mlp1, kept1[5], []
    )

    def backward_mlp0(gradient, after):
        return mlp_backward(0, place, gradient, act, slope, kept0[0], mlp0, kept0[5], after)

    state = (mat_w, mat_m, mat_v)
    def exchange(parts):
        return [parts[0], swap(parts[1], 1)]

    if near:
        gone_mlp1 = exchange(parts_mlp1)
        gradient, *parts_heads1, _, _ = backward_attention(1, grad_mid, small, [])
        s_mlp1 = add_split(gone_mlp1, [gradient])
        gone_mlp1 = give_plane(s_mlp1)
        gone_heads1 = exchange(parts_heads1)
        grad_mid, *parts_mlp0, small = backward_mlp0(gradient, [s_mlp1[0]])

        t_mlp1 = add(gone_mlp1, [grad_mid])
        s_heads1 = add_split(gone_heads1, [t_mlp1])
        gone_heads1 = give_plane(s_heads1)
        gone_mlp0 = exchange(tie(parts_mlp0, [s_heads1[0]]))
        gradient, *parts_heads0, pairs, small = backward_attention(
            0, grad_mid, small, [s_heads1[0]], 0, half
        )

        t_all1 = add_join([t_mlp1], gone_heads1, [gradient])
        g_all1 = lax.psum_scatter(t_all1, "zero", scatter_dimension=0, tiled=True)
        s_mlp0 = add_split(gone_mlp0, [gradient])
        gone_mlp0 = give_plane(s_mlp0)
        gradient, *parts_heads0, _, small = backward_attention(
            0, grad_mid, small, [t_all1, s_mlp0[0]], half, half, [gradient, *parts_heads0, pairs]
        )

        g_all1 = tie([g_all1], [small])[0]
        n_all1 = lax.all_gather(g_all1[0], "dp", axis=0, tiled=False)
        t_mlp0 = add_split(gone_mlp0, [small])
        gone_heads0 = exchange(tie(parts_heads0, [t_mlp0[0]]))
        gone_mlp0 = give_z(t_mlp0)
        s_heads0 = add_split(gone_heads0, [t_mlp0[0]])
        gone_heads0 = give_plane(s_heads0)
        g_mlp0 = add(gone_mlp0, [s_heads0[0]])
        gone_mlp0 = send_plane(g_mlp0)
        done = adam(1, 1, place, [n_all1], state, None, [g_mlp0])
        t_heads0 = add_split(gone_heads0, [done[0]])
        gone_heads0 = give_z(t_heads0)
        n_mlp0 = stack(gone_mlp0, [t_heads0[0]])
        sums_mlp0 = [n_mlp0, swap(n_mlp0, 1)]
        g_heads0 = add(gone_heads0, [n_mlp0])
        gone_heads0 = send_plane(g_heads0)
        n_heads0 = stack(gone_heads0)
        sums_heads0 = [n_heads0, swap(n_heads0, 1)]
        done = adam(0, 1, place, sums_mlp0, state, done, [n_heads0])
        m = place[0] ^ np.arange(2)
        both = jnp.concatenate([half[:, 0, 128:] for half in sums_heads0])
        beside0 = [lax.dynamic_index_in_dim(both, (m[b] % 2) * 4 + m[b] // 2, 0, False) for b in range(2)]
    else:
        gradient, *parts_heads1, _, _ = backward_attention(1, grad_mid, small, [])
        grad_mid, *parts_mlp0, small = backward_mlp0(gradient, [])
        gradient, *parts_heads0, _, _ = backward_attention(0, grad_mid, small, [])
        n_mlp1 = reduce_wide(*parts_mlp1, dp, 0)
        n_heads1 = reduce_wide(*parts_heads1, dp, SMALL)
        n_all1 = jnp.concatenate([n_mlp1, n_heads1], 1)
        done = adam(1, 1, place, [n_all1], state, None, [])
        done = adam(0, 1, place, [reduce_wide(*parts_mlp0, dp, 0)], state, done, [])
        sums_heads0 = [reduce_wide(*parts_heads0, dp, SMALL)]
        beside0 = sums_heads0[0][:2, 128:]
    done = adam(0, 0, place, sums_heads0, state, done, [])

    def beside(block):
        return jnp.stack([beside0[block], n_all1[block, 384:]]).astype(f32)

    new_vec = adam_step(vec_w, vec_m, vec_v, beside(1)[:, 0:12, 0:128], rate_vector, 0.0)
    new_tab = adam_step(tab_w, tab_m, tab_v, beside(0)[:, 0:4, 0:NREL], rate_table, 0.0)
    return (activations, gradient, *done, *new_vec, *new_tab)


def solution(mesh):
    images = P(("dp", "zero"), None, None)
    rows = P(None, "zero", None)
    lanes = P(None, None, "zero")
    return jax.shard_map(
        partial(shards, mesh.shape["dp"]),
        mesh=mesh,
        in_specs=(images, images, P(("dp", "zero")), P(), P())
        + (rows,) * 3 + (lanes,) * 3 + (rows,) * 3,
        out_specs=(images, images) + (rows,) * 3 + (lanes,) * 3 + (rows,) * 3,
        check_vma=False,
    )
```

```python
from functools import partial

import jax
import jax.numpy as jnp
import numpy as np
from jax import lax
from jax.experimental import pallas as pl
from jax.experimental.pallas import tpu as pltpu
from jax.sharding import PartitionSpec as P

WIN = 7
SIDE = 14
STEP = 10
NREL = 169
C = 512
HID = 2048
TOKENS = SIDE * SIDE
PAIR = 2
ROWS = 208
FRAME = 256
CELL = 64
QUAD = 4
BLOCK = 256
EXTRA = 32
SMALL = 16

norm_eps = 1e-05
mask_value = -100.0
beta_one = 0.9
beta_two = 0.999
adam_eps = 1e-08
weight_decay = 0.05
rate_matrix = 0.1
rate_vector = 0.5
rate_table = 1.0
scale = 32 ** (-0.5)

bf16 = jnp.bfloat16
f32 = jnp.float32
NN = (((1,), (0,)), ((), ()))
NT = (((1,), (1,)), ((), ()))
TN = (((0,), (0,)), ((), ()))


def mm(left, right, dims=NN):
    return lax.dot_general(left, right, dims, preferred_element_type=f32)


def frames(shifted):
    move = WIN // 2 if shifted else 0
    placed = np.zeros((FRAME, ROWS), np.float32)
    for wy in range(2):
        for wx in range(2):
            for iy in range(WIN):
                for ix in range(WIN):
                    y = (wy * WIN + iy + move) % SIDE
                    x = (wx * WIN + ix + move) % SIDE
                    placed[(wy * 2 + wx) * CELL + iy * WIN + ix, y * SIDE + x] = 1
    return placed


def head_rows():
    rows = np.zeros((QUAD * CELL, 128), np.float32)
    for h in range(QUAD):
        rows[h * CELL : (h + 1) * CELL, h * 32 : (h + 1) * 32] = 1
    return rows


def head_spread(rows):
    out = np.zeros((rows, QUAD * CELL), np.float32)
    for h in range(QUAD):
        out[h, h * CELL : (h + 1) * CELL] = 1
    return out


def norm(rows):
    centred = rows - jnp.mean(rows, -1, keepdims=True)
    spread = lax.rsqrt(jnp.mean(centred * centred, -1, keepdims=True) + norm_eps)
    return centred * spread, spread


def norm_back(grad_unit, unit, spread):
    return spread * (
        grad_unit
        - jnp.mean(grad_unit, -1, keepdims=True)
        - unit * jnp.mean(grad_unit * unit, -1, keepdims=True)
    )


def column_sum(rows):
    return jnp.sum(rows, 0, keepdims=True)


def gelu_pair(u):
    size = jnp.abs(u)
    below = 1.0 + (0.3275911 * 0.5**0.5) * size
    t = pltpu.reciprocal(below, approx=True)
    bell = jnp.exp2(u * u * (-0.5 * 1.4426950408889634))
    poly = t * (
        0.127414796 + t * (-0.142248368 + t * (0.710706871 + t * (-0.726576013 + t * 0.530702714)))
    )
    tail = poly * bell
    phi = jnp.where(u >= 0, 1.0 - tail, tail)
    return u * phi, phi + u * bell * 0.3989422804014327


def quad_rows(part, heads):
    return jnp.concatenate([part] * QUAD, 0) * heads


def pick_heads(stacked, lane_head):
    low = jnp.where(lane_head == 0, stacked[:CELL], stacked[CELL : 2 * CELL])
    high = jnp.where(lane_head == 2, stacked[2 * CELL : 3 * CELL], stacked[3 * CELL :])
    return jnp.where(lane_head < 2, low, high)


def lane_heads():
    return lax.broadcasted_iota(jnp.int32, (CELL, 128), 1) // 32


def whole(shape):
    zero = (0,) * len(shape)
    return pl.BlockSpec(shape, lambda *_: zero, pipeline_mode=pl.Buffered(1))


def per_image(rows, cols):
    return pl.BlockSpec((1, rows, cols), lambda i, *_: (i, 0, 0))


def per_pair(rows, cols):
    return pl.BlockSpec((PAIR, rows, cols), lambda i, *_: (i, 0, 0))


HBM = pl.BlockSpec(memory_space=pl.ANY)


def weight_copies(place, stacks, kept, sems, part=0):
    copies = []
    for m in range(8):
        for s in range(4):
            for p in range(kept.shape[0]):
                if len(stacks) == 1:
                    source, block, owner = stacks[0].at[m, s, part + p], m, s
                else:
                    source = stacks[m % 2].at[m // 2, s, p]
                    block, owner = place[0] ^ m, (place[1] + 4 - s) & 3
                rows = pl.ds(pl.multiple_of(owner * 128, 128), 128)
                cols = pl.ds(pl.multiple_of(block * BLOCK, BLOCK), BLOCK)
                copies.append(
                    pltpu.make_async_copy(
                        source.at[pl.ds(0, 128), :], kept.at[p, rows, cols], sems.at[m, s, p]
                    )
                )
    return copies


def extra_copies(place, stacks, kept, sems):
    copies = []
    for m in range(8):
        for s in range(4):
            if len(stacks) == 1:
                source, block, owner = stacks[0].at[m, s, 0], m, s
            else:
                source = stacks[m % 2].at[m // 2, s, 0]
                block, owner = place[0] ^ m, (place[1] + 4 - s) & 3
            copies.append(
                pltpu.make_async_copy(
                    source.at[pl.ds(128, EXTRA), :], kept.at[block, owner], sems.at[m, s, 0]
                )
            )
    return copies


def fetch(copies):
    for copy in copies:
        copy.start()
    for copy in copies:
        copy.wait()


def call(body, name, grid, ins, outs, out_shapes, scratch, cost_us, prefetch=0, aliases=None):
    return pl.pallas_call(
        body,
        name=name,
        grid_spec=pltpu.PrefetchScalarGridSpec(
            num_scalar_prefetch=prefetch,
            grid=grid,
            in_specs=ins,
            out_specs=outs,
            scratch_shapes=scratch,
        ),
        out_shape=out_shapes,
        input_output_aliases=aliases or {},
        compiler_params=pltpu.CompilerParams(
            dimension_semantics=("arbitrary",) * len(grid), vmem_limit_bytes=58 * 1024 * 1024
        ),
        cost_estimate=pl.CostEstimate(
            flops=0, bytes_accessed=int(cost_us * 3.69e4), transcendentals=0
        ),
    )


def shape(dims, kind):
    return jax.ShapeDtypeStruct(dims, kind)


def pack_body(place, *refs):
    mats, (pair_index, tab, vec, spread) = refs[:6], refs[6:10]
    out, mlp0, all1, rel, spread_tab, small = refs[10:]
    rows = mats[0].shape[1]
    out[0, 0:rows, :] = mats[0][0].astype(bf16)
    for ref, at, n in ((mlp0, 0, 1), (mlp0, 1, 2), (all1, 0, 3), (all1, 1, 4), (all1, 2, 5)):
        ref[at] = mats[n][0].astype(bf16)
    rel[...] = jnp.full(rel.shape, -1, jnp.int32)
    across = pair_index[...].astype(f32).T.astype(jnp.int32)
    for h in range(QUAD):
        rel[0 : WIN * WIN, CELL * h : CELL * h + WIN * WIN] = across
    for layer in range(2):
        spread_tab[layer, 0:NREL, :] = mm(tab[layer].astype(bf16), spread[...], TN)
    pairs = rel[pl.ds(pl.multiple_of(place[0] * 8, 8), 8), :]

    def step(r, sums):
        hit = pairs == r
        return tuple(
            jnp.where(hit, spread_tab[layer, pl.ds(r, 1), :], sums[layer]) for layer in range(2)
        )

    start = jnp.zeros((8, QUAD * CELL), f32)
    first, second = lax.fori_loop(0, NREL, step, (start, start), unroll=13)
    out[0, rows : rows + 16, :] = jnp.concatenate([first, second], 0).astype(bf16)
    small[...] = jnp.zeros_like(small)
    row = jnp.minimum(place[0] * 2, 10)
    for layer in range(2):
        for k in range(2):
            small[k : k + 1, layer * 128 : (layer + 1) * 128] = vec[row + k, layer : layer + 1, :]
    out[0, rows + 16 : rows + 32, :] = small[...].astype(bf16)


def pack(place, rows, mat_w, rel_index, tab_w, vec_w):
    vec_w = vec_w.transpose(1, 0, 2)

    def block(layer, part):
        return pl.BlockSpec(
            (1, rows, BLOCK), lambda i, place: (layer, place[1], part * 8 + place[0])
        )

    dims = [(1, rows + EXTRA, BLOCK), (2, rows, BLOCK), (3, rows, BLOCK)]
    return call(
        pack_body,
        "pack",
        (1,),
        [block(layer, part) for layer in range(2) for part in range(3)]
        + [
            whole(rel_index.shape),
            whole(tab_w.shape),
            whole(vec_w.shape),
            whole((QUAD, QUAD * CELL)),
        ],
        [whole(d) for d in dims] + [whole((CELL, QUAD * CELL))],
        [shape(d, bf16) for d in dims] + [shape((CELL, QUAD * CELL), jnp.int32)],
        [pltpu.VMEM((2, 176, QUAD * CELL), f32), pltpu.VMEM((16, 256), f32)],
        4,
        prefetch=1,
    )(place, *[mat_w] * 6, rel_index, tab_w, vec_w, jnp.asarray(head_spread(QUAD), bf16))


def attention_forward_body(layer, stacks, waits, place, *refs):
    arrays, refs = refs[: stacks[0]], refs[stacks[0] :]
    extras, refs = refs[: stacks[1]], refs[stacks[1] + waits :]
    x, mask, perm, perm_back, heads = refs[:5]
    mid, qkv, merged, totals, table, vec, framed, kept, extra_kept, sems, more_sems = refs[5:]
    weight, extra = kept.at[0], extra_kept

    @pl.when(pl.program_id(0) == 0)
    def _():
        fetch(
            weight_copies(place, arrays, kept, sems)
            + extra_copies(place, extras, extra_kept, more_sems)
        )
        vec[...] = jnp.zeros_like(vec)
        for z in range(4):
            for d in range(8):
                pair = extra[d, z, 0:16, :].astype(f32)
                bias = pair[8 * layer : 8 * layer + 8]
                for w in range(table.shape[0]):
                    table[w, z, 8 * d : 8 * d + 8, :] = bias + mask[w, 8 * d : 8 * d + 8, :]
                if d < 6:
                    rows = extra[d, z, 16:32, 128 * layer : 128 * layer + 128].astype(f32)
                    vec[2 * d : 2 * d + 2, 128 * z : 128 * z + 128] = rows[0:2]

    stream = x[0]
    unit, _ = norm(stream)
    normed = (unit * vec[0:1, :] + vec[1:2, :]).astype(bf16)
    normed = mm(perm[...], normed).astype(bf16)
    for c in range(6):
        part = mm(normed, weight[:, 256 * c : 256 * c + 256])
        if c < 2:
            part = part + vec[2:3, 256 * c : 256 * c + 256]
        if c >= 4:
            part = part + vec[3:4, 256 * (c - 4) : 256 * (c - 4) + 256]
        qkv[0, :, 256 * c : 256 * c + 256] = part.astype(bf16)
    lane_head = lane_heads()

    def score(unit):
        rows, at = slice(CELL * (unit // 4), CELL * (unit // 4) + CELL), 128 * (unit % 4)
        query = quad_rows(qkv[0, rows, at : at + 128], heads[...])
        return mm(qkv[0, rows, C + at : C + at + 128], query, NT)

    ahead = score(0)
    for n in range(16):
        w, g = n // 4, n % 4
        rows, at = slice(CELL * w, CELL * w + CELL), 128 * g
        scores = ahead * scale + table[w % table.shape[0], g]
        if n < 15:
            ahead = score(n + 1)
        top = jnp.max(scores, 0, keepdims=True)
        raised = jnp.exp(scores - top)
        total = jnp.sum(raised, 0, keepdims=True)
        totals[0, n : n + 1, :] = top + jnp.log(total)
        probs = (raised * (1.0 / total)).astype(bf16)
        stacked = mm(probs, qkv[0, rows, 2 * C + at : 2 * C + at + 128], TN)
        framed[rows, at : at + 128] = pick_heads(stacked, lane_head).astype(bf16)
    gathered = mm(perm_back[...], framed[...]).astype(bf16)
    merged[0] = gathered
    mid[0] = stream + mm(gathered, weight[:, 3 * C :]) + vec[4:5, :]


def attention_forward(layer, place, x, weight, extra, mask, perm, after):
    images = x.shape[0]
    tables = mask.shape[0]
    return call(
        partial(attention_forward_body, layer, (len(weight), len(extra)), len(after)),
        f"attention_forward_{layer}",
        (images,),
        [HBM] * (len(weight) + len(extra) + len(after))
        + [
            per_image(x.shape[1], C),
            whole(mask.shape),
            whole((FRAME, ROWS)),
            whole((ROWS, FRAME)),
            whole((QUAD * CELL, 128)),
        ],
        [
            per_image(ROWS, C),
            per_image(FRAME, 3 * C),
            per_image(ROWS, C),
            per_image(16, QUAD * CELL),
            pl.BlockSpec((tables, 4, CELL, QUAD * CELL), lambda i, *_: (0, 0, 0, 0)),
            pl.BlockSpec((16, C), lambda i, *_: (0, 0)),
        ],
        [
            shape((images, ROWS, C), f32),
            shape((images, FRAME, 3 * C), bf16),
            shape((images, ROWS, C), bf16),
            shape((images, 16, QUAD * CELL), f32),
            shape((tables, 4, CELL, QUAD * CELL), f32),
            shape((16, C), f32),
        ],
        [
            pltpu.VMEM((FRAME, C), bf16),
            pltpu.VMEM((1, C, HID), bf16),
            pltpu.VMEM((8, 4, EXTRA, BLOCK), bf16),
            pltpu.SemaphoreType.DMA((8, 4, 1)),
            pltpu.SemaphoreType.DMA((8, 4, 1)),
        ],
        20,
        prefetch=1,
    )(
        place,
        *weight,
        *extra,
        *after,
        x,
        mask,
        jnp.asarray(perm, bf16),
        jnp.asarray(perm.T, bf16),
        jnp.asarray(head_rows(), bf16),
    )


def mlp_forward_body(stacks, waits, place, *refs):
    arrays, refs = refs[:stacks], refs[stacks + waits :]
    mid, vec, result, act, slope, kept, sems = refs
    first, second = kept.at[0], kept.at[1]

    @pl.when(pl.program_id(0) == 0)
    def _():
        fetch(weight_copies(place, arrays, kept, sems))

    rows = PAIR * ROWS
    stream = mid[...].reshape(rows, C)
    unit, _ = norm(stream)
    normed = (unit * vec[5:6, :] + vec[6:7, :]).astype(bf16)
    for c in range(8):
        cols = slice(256 * c, 256 * c + 256)
        bias = vec[8 + c // 2 : 9 + c // 2, 256 * (c % 2) : 256 * (c % 2) + 256]
        value, pull = gelu_pair(mm(normed, first[:, cols]) + bias)
        act[:, :, cols] = value.astype(bf16).reshape(PAIR, ROWS, BLOCK)
        slope[:, :, cols] = pull.astype(bf16).reshape(PAIR, ROWS, BLOCK)
    total = stream + vec[7:8, :] + mm(act[...].reshape(rows, HID), second[...], NT)
    result[...] = total.reshape(PAIR, ROWS, C)


def mlp_forward(layer, place, mid, weight, vec, after):
    images = mid.shape[0]
    return call(
        partial(mlp_forward_body, len(weight), len(after)),
        f"mlp_forward_{layer}",
        (images // PAIR,),
        [HBM] * (len(weight) + len(after)) + [per_pair(ROWS, C), whole(vec.shape)],
        [per_pair(ROWS, C), per_pair(ROWS, HID), per_pair(ROWS, HID)],
        [
            shape((images, ROWS, C), f32),
            shape((images, ROWS, HID), bf16),
            shape((images, ROWS, HID), bf16),
        ],
        [pltpu.VMEM((2, C, HID), bf16), pltpu.SemaphoreType.DMA((8, 4, 2))],
        22,
        prefetch=1,
    )(place, *weight, *after, mid, vec)


def mlp_both_body(stacks, waits, place, *refs):
    arrays, refs = refs[:stacks], refs[stacks + waits :]
    grad, mid, vec, result, grad_mid, pieces, small = refs[:7]
    all_grad, all_act, all_inner, all_normed, kept, sems = refs[7:]
    first, second = kept.at[0], kept.at[1]
    i = pl.program_id(0)

    @pl.when(i == 0)
    def _():
        fetch(weight_copies(place, arrays, kept, sems, 1))
        small[...] = jnp.zeros_like(small)

    rows = PAIR * ROWS
    grad_out = grad[...].reshape(rows, C)
    here = pl.ds(pl.multiple_of(i * rows, 32), rows)
    low = grad_out.astype(bf16)
    all_grad[here, :] = low
    small[7:8, :] += column_sum(grad_out)
    stream = mid[...].reshape(rows, C)
    unit, spread = norm(stream)
    normed = (unit * vec[5:6, :] + vec[6:7, :]).astype(bf16)
    all_normed[here, :] = normed
    for c in range(8):
        cols = slice(256 * c, 256 * c + 256)
        row, lane = 8 + c // 2, 256 * (c % 2)
        bias = vec[row : row + 1, lane : lane + 256]
        value, pull = gelu_pair(mm(normed, first[:, cols]) + bias)
        all_act[here, cols] = value.astype(bf16)
        inner = (mm(low, second[:, cols]) * pull).astype(bf16)
        all_inner[here, cols] = inner
        small[row : row + 1, lane : lane + 256] += column_sum(inner.astype(f32))
    back = mm(all_inner[here, :], first[...], NT)
    small[5:6, :] += column_sum(back * unit)
    small[6:7, :] += column_sum(back)
    grad_mid[...] = (grad_out + norm_back(back * vec[5:6, :], unit, spread)).reshape(PAIR, ROWS, C)
    total = stream + vec[7:8, :] + mm(all_act[here, :], second[...], NT)
    for n in range(PAIR):
        alive = (i * PAIR + n < place[2]).astype(f32)
        result[n] = (total[n * ROWS : n * ROWS + TOKENS] * alive).astype(bf16)

    @pl.when(i == pl.num_programs(0) - 1)
    def _():
        mlp_weight_grads(place, all_grad, all_act, all_inner, all_normed, pieces)


def mlp_weight_grads(place, all_grad, all_act, all_inner, all_normed, *outs):
    grad_across = all_grad[...].T
    normed_across = all_normed[...].T
    for m in range(8):
        block = m if len(outs) == 1 else place[0] ^ m
        cols = pl.ds(pl.multiple_of(block * BLOCK, BLOCK), BLOCK)
        for p, total in enumerate(
            (mm(normed_across, all_inner[:, cols]), mm(grad_across, all_act[:, cols]))
        ):
            total = total.astype(bf16)
            for z in range(4):
                if len(outs) == 1:
                    outs[0][m, z, p] = total[128 * z : 128 * z + 128]
                else:
                    to = (z + 4 - place[1]) & 3
                    outs[m % 2][m // 2, to, p] = total[128 * z : 128 * z + 128]


def mlp_both(place, grad, mid, weight, vec, after):
    images = mid.shape[0]
    total = images * ROWS
    pieces = (8, 4, 2, 128, BLOCK)
    return call(
        partial(mlp_both_body, len(weight), len(after)),
        "mlp_both",
        (images // PAIR,),
        [HBM] * (len(weight) + len(after)) + [per_pair(ROWS, C), per_pair(ROWS, C), whole(vec.shape)],
        [per_pair(TOKENS, C), per_pair(ROWS, C), whole(pieces), whole((16, C))],
        [
            shape((images, TOKENS, C), bf16),
            shape((images, ROWS, C), f32),
            shape(pieces, bf16),
            shape((16, C), f32),
        ],
        [
            pltpu.VMEM((total, C), bf16),
            pltpu.VMEM((total, HID), bf16),
            pltpu.VMEM((total, HID), bf16),
            pltpu.VMEM((total, C), bf16),
            pltpu.VMEM((2, C, HID), bf16),
            pltpu.SemaphoreType.DMA((8, 4, 2)),
        ],
        45,
        prefetch=1,
    )(place, *weight, *after, grad, mid, vec)


def mlp_backward_body(stacks, waits, place, *refs):
    arrays, refs = refs[:stacks], refs[stacks + waits :]
    grad, act, slope, mid, vec, grad_mid, own, other, small = refs[:9]
    all_grad, all_act, all_inner, all_normed, kept, sems = refs[9:]
    first, second = kept.at[0], kept.at[1]
    i = pl.program_id(0)

    @pl.when(i == 0)
    def _():
        fetch(weight_copies(place, arrays, kept, sems))
        small[...] = jnp.zeros_like(small)

    rows = PAIR * ROWS
    grad_out = grad[...].reshape(rows, C)
    here = pl.ds(pl.multiple_of(i * rows, 32), rows)
    low = grad_out.astype(bf16)
    all_grad[here, :] = low
    small[7:8, :] += column_sum(low.astype(f32))
    all_act[here, :] = act[...].reshape(rows, HID)
    unit, spread = norm(mid[...].reshape(rows, C))
    all_normed[here, :] = (unit * vec[5:6, :] + vec[6:7, :]).astype(bf16)
    for c in range(8):
        cols = slice(256 * c, 256 * c + 256)
        pull = slope[:, :, cols].reshape(rows, BLOCK).astype(f32)
        inner = (mm(low, second[:, cols]) * pull).astype(bf16)
        all_inner[here, cols] = inner
        row, lane = 8 + c // 2, 256 * (c % 2)
        small[row : row + 1, lane : lane + 256] += column_sum(inner.astype(f32))
    back = mm(all_inner[here, :], first[...], NT)
    small[5:6, :] += column_sum(back * unit)
    small[6:7, :] += column_sum(back)
    grad_mid[...] = (grad_out + norm_back(back * vec[5:6, :], unit, spread)).reshape(PAIR, ROWS, C)

    @pl.when(i == pl.num_programs(0) - 1)
    def _():
        mlp_weight_grads(place, all_grad, all_act, all_inner, all_normed, own, other)


def mlp_backward(layer, place, grad, act, slope, mid, weight, vec, after):
    images = mid.shape[0]
    total = images * ROWS
    pieces = (4, 4, 2, 128, BLOCK)
    return call(
        partial(mlp_backward_body, len(weight), len(after)),
        f"mlp_backward_{layer}",
        (images // PAIR,),
        [HBM] * (len(weight) + len(after))
        + [
            per_pair(grad.shape[1], C),
            per_pair(ROWS, HID),
            per_pair(ROWS, HID),
            per_pair(ROWS, C),
            whole(vec.shape),
        ],
        [per_pair(ROWS, C), whole(pieces), whole(pieces), whole((16, C))],
        [
            shape((images, ROWS, C), f32),
            shape(pieces, bf16),
            shape(pieces, bf16),
            shape((16, C), f32),
        ],
        [
            pltpu.VMEM((total, C), bf16),
            pltpu.VMEM((total, HID), bf16),
            pltpu.VMEM((total, HID), bf16),
            pltpu.VMEM((total, C), bf16),
            pltpu.VMEM((2, C, HID), bf16),
            pltpu.SemaphoreType.DMA((8, 4, 2)),
        ],
        30,
        prefetch=1,
    )(place, *weight, *after, grad, act, slope, mid, vec)


def attention_backward_body(layer, stacks, waits, resumed, ends, place, *refs):
    arrays, refs = refs[:stacks], refs[stacks + waits :]
    if resumed:
        (own_before, other_before, pairs_before), refs = refs[1:4], refs[4:]
    grad, x, qkv, merged, totals, table, vec, before = refs[:8]
    perm, perm_back, heads, rel, spread, result = refs[8:14]
    outs, refs = (refs[14:15], refs[15:]) if layer else (refs[14:16], refs[16:])
    pairs, small, framed, grad_framed, all_normed, all_packed, all_merged = refs[:7]
    across, hits, beside, kept, sems = refs[7:]
    weight = kept.at[0]
    i = pl.program_id(0)

    @pl.when(i == 0)
    def _():
        fetch(weight_copies(place, arrays, kept, sems))
        small[...] = before[...]
        pairs[...] = pairs_before[...] if resumed else jnp.zeros_like(pairs)

    stream = x[0]
    here = pl.ds(pl.multiple_of(i * ROWS, 16), ROWS)
    unit, spread_one = norm(stream)
    all_normed[here, :] = (unit * vec[0:1, :] + vec[1:2, :]).astype(bf16)
    low = grad[0].astype(bf16)
    all_packed[here, 3 * C :] = low
    all_merged[here, :] = merged[0]
    small[4:5, :] += column_sum(low.astype(f32))
    moved = mm(perm[...], low).astype(bf16)
    framed[...] = mm(moved, weight[:, 3 * C :], NT).astype(bf16)
    lane_head = lane_heads()
    for w in range(4):
        rows = slice(CELL * w, CELL * w + CELL)
        at = [128 * g for g in range(4)]
        keys = [qkv[0, rows, C + c : C + c + 128] for c in at]
        query = [quad_rows(qkv[0, rows, c : c + 128], heads[...]) for c in at]
        pull = [quad_rows(framed[rows, c : c + 128], heads[...]) for c in at]
        scores = [mm(keys[g], query[g], NT) for g in range(4)]
        grad_probs = [
            mm(qkv[0, rows, 2 * C + at[g] : 2 * C + at[g] + 128], pull[g], NT) for g in range(4)
        ]
        probs, grad_scores = [], []
        for g in range(4):
            shifted = scores[g] * scale + table[w % table.shape[0], g]
            prob = jnp.exp(shifted - totals[0, 4 * w + g : 4 * w + g + 1, :])
            mean = jnp.sum(prob * grad_probs[g], 0, keepdims=True)
            grad_score = (prob * (grad_probs[g] - mean)).astype(bf16)
            pairs[g] += grad_score.astype(f32)
            probs.append(prob.astype(bf16))
            grad_scores.append(grad_score)
        for g in range(4):
            grad_value = mm(probs[g], pull[g])
            grad_framed[rows, 2 * C + at[g] : 2 * C + at[g] + 128] = grad_value.astype(bf16)
        for g in range(4):
            grad_key = mm(grad_scores[g], query[g]) * scale
            grad_framed[rows, C + at[g] : C + at[g] + 128] = grad_key.astype(bf16)
        for g in range(4):
            grad_query = pick_heads(mm(grad_scores[g], keys[g], TN), lane_head) * scale
            grad_framed[rows, at[g] : at[g] + 128] = grad_query.astype(bf16)
    for c in range(6):
        cols = slice(256 * c, 256 * c + 256)
        part = mm(perm_back[...], grad_framed[:, cols])
        all_packed[here, cols] = part.astype(bf16)
        if c < 2:
            small[2:3, cols] += column_sum(part)
        if c >= 4:
            small[3:4, 256 * (c - 4) : 256 * (c - 4) + 256] += column_sum(part)
    back = mm(all_packed[here, : 3 * C], weight[:, : 3 * C], NT)
    small[0:1, :] += column_sum(back * unit)
    small[1:2, :] += column_sum(back)
    total = grad[0] + norm_back(back * vec[0:1, :], unit, spread_one)
    result[0] = total[: result.shape[1]]

    @pl.when(i == pl.num_programs(0) - 1)
    def _():
        across[0] = all_normed[...].T
        across[1] = all_merged[...].T
        beside[...] = jnp.zeros_like(beside)
        if ends:
            hits[...] = jnp.zeros_like(hits)

            def step(r, carry):
                same = rel[...] == r
                for g in range(4):
                    kept_pairs = jnp.where(same, pairs[g], 0.0)
                    hits[pl.ds(r, 1), 256 * g : 256 * g + 256] = column_sum(kept_pairs)
                return carry

            lax.fori_loop(0, NREL, step, 0)
            for z in range(4):
                beside[0, z] = lax.dot_general(
                    spread[...],
                    hits[:, 256 * z : 256 * z + 256],
                    NT,
                    precision=lax.Precision.HIGHEST,
                    preferred_element_type=f32,
                ).astype(bf16)
                beside[1, z, :, 0:128] = small[:, 128 * z : 128 * z + 128].astype(bf16)
        for m in range(8):
            b = m if layer else place[0] ^ m
            left = across[jnp.where(b < 6, 0, 1)]
            right = all_packed[:, pl.ds(pl.multiple_of(b * BLOCK, BLOCK), BLOCK)]
            block = mm(left, right)
            for z in range(4):
                if layer:
                    out = outs[0].at[m, z, 0]
                else:
                    to = (z + 4 - place[1]) & 3
                    out = outs[m % 2].at[m // 2, to, 0]
                new = block[128 * z : 128 * z + 128]
                if resumed:
                    old = other_before if m % 2 else own_before
                    new = new + old[m // 2, to, 0, 0:128, :].astype(f32)
                out[0:128, :] = new.astype(bf16)
                out[128:144, :] = beside[jnp.minimum(b, 2), z]


def attention_backward(
    layer, place, grad, x, qkv, merged, totals, table, weight, vec, small, perm, rel, after,
    first=0, count=None, resume=None,
):
    images = grad.shape[0]
    count = count or images
    pieces = (8 if layer else 4, 4, 1, 128 + SMALL, BLOCK)
    pairs = (4, CELL, QUAD * CELL)
    total = count * ROWS
    out_rows = TOKENS if layer == 0 else ROWS

    def image(rows, cols):
        return pl.BlockSpec((1, rows, cols), lambda i, *_: (i + first, 0, 0))

    resumed = list(resume or [])
    return call(
        partial(
            attention_backward_body, layer, len(weight), len(after), bool(resumed),
            first + count == images,
        ),
        f"attention_backward_{layer}_{first}",
        (count,),
        [HBM] * (len(weight) + len(after))
        + ([HBM, whole(pieces), whole(pieces), whole(pairs)] if resumed else [])
        + [
            image(ROWS, C),
            image(x.shape[1], C),
            image(FRAME, 3 * C),
            image(ROWS, C),
            image(16, QUAD * CELL),
            whole(table.shape),
            whole(vec.shape),
            whole((16, C)),
            whole((FRAME, ROWS)),
            whole((ROWS, FRAME)),
            whole((QUAD * CELL, 128)),
            whole(rel.shape),
            whole((SMALL, QUAD * CELL)),
        ],
        [image(out_rows, C)]
        + [whole(pieces)] * (1 if layer else 2)
        + [whole(pairs), whole((16, C))],
        [shape((images, out_rows, C), f32)]
        + [shape(pieces, bf16)] * (1 if layer else 2)
        + [shape(pairs, f32), shape((16, C), f32)],
        [
            pltpu.VMEM((FRAME, C), bf16),
            pltpu.VMEM((FRAME, 3 * C), bf16),
            pltpu.VMEM((total, C), bf16),
            pltpu.VMEM((total, 4 * C), bf16),
            pltpu.VMEM((total, C), bf16),
            pltpu.VMEM((2, C, total), bf16),
            pltpu.VMEM((256, 4 * QUAD * CELL), f32),
            pltpu.VMEM((3, 4, SMALL, BLOCK), bf16),
            pltpu.VMEM((1, C, HID), bf16),
            pltpu.SemaphoreType.DMA((8, 4, 1)),
        ],
        6 * count,
        prefetch=1,
        aliases={1 + len(weight) + len(after): 0} if resumed else None,
    )(
        place,
        *weight,
        *after,
        *resumed,
        grad,
        x,
        qkv,
        merged,
        totals,
        table,
        vec,
        small,
        jnp.asarray(perm, bf16),
        jnp.asarray(perm.T, bf16),
        jnp.asarray(head_rows(), bf16),
        rel,
        jnp.asarray(head_spread(SMALL), f32),
    )


def adam_step(weight, first, second, gradient, rate, decay):
    first_new = beta_one * first + (1.0 - beta_one) * gradient
    second_new = beta_two * second + (1.0 - beta_two) * gradient * gradient
    first_hat = first_new / (1.0 - beta_one**STEP)
    second_hat = second_new / (1.0 - beta_two**STEP)
    weight_new = weight - rate * (first_hat / (jnp.sqrt(second_hat) + adam_eps) + decay * weight)
    return (weight_new, first_new, second_new)


def adam_block(grad, weight, first, second, outs, cols):
    news = adam_step(
        weight[0, :, cols], first[0, :, cols], second[0, :, cols],
        grad.astype(f32), rate_matrix, weight_decay,
    )
    for out, new in zip(outs, news):
        out[0, :, cols] = new


def adam_body(place, near, far, weight, first, second, *refs):
    for j in range(2):
        for k in range(2):
            block = (((place[0] // 2) & 1) ^ j) * 2 + ((place[0] & 1) ^ k)
            cols = pl.ds(pl.multiple_of(block * BLOCK, BLOCK), BLOCK)
            adam_block((far if k else near)[j, 0], weight, first, second, refs[-3:], cols)


def adam_body_plain(place, sums, weight, first, second, *refs):
    for k in range(4):
        cols = slice(BLOCK * k, BLOCK * k + BLOCK)
        adam_block(sums[k], weight, first, second, refs[-3:], cols)


def adam(layer, part, place, sums, state, done, after):
    kept = [] if done is None else list(done)
    if len(sums) == 2:
        parts = sums[0].shape[1]
        body = adam_body
        spec = pl.BlockSpec(
            (1, 128, 4 * BLOCK),
            lambda p, j, place: (layer, 0, (part + p) % 3 * 2 + ((place[0] // 4) ^ j)),
        )
        piece = pl.BlockSpec((2, 1, 128, BLOCK), lambda p, j, place: (j, p, 0, 0))
    else:
        parts = sums[0].shape[1] // 128
        body = adam_body_plain
        spec = pl.BlockSpec(
            (1, 128, 4 * BLOCK), lambda p, j, place: (layer, 0, (part + p) % 3 * 2 + j)
        )
        piece = pl.BlockSpec((4, 128, BLOCK), lambda p, j, place: (j, p, 0))
    return call(
        body,
        f"adam_{layer}_{part}",
        (parts, 2),
        [piece] * len(sums) + [spec] * 3 + [HBM] * (len(kept) + len(after)),
        [spec] * 3,
        [shape(state[0].shape, f32)] * 3,
        [],
        3 * parts,
        prefetch=1,
        aliases={4 + len(sums) + k: k for k in range(len(kept))},
    )(place, *sums, *state, *kept, *after)


def swap(value, bits):
    return lax.ppermute(value, "dp", [(i, i ^ bits) for i in range(8)])


def shift(value, steps):
    return lax.ppermute(value, "zero", [(i, (i + steps) % 4) for i in range(4)])


def tie(values, after):
    values = list(values)
    return list(lax.optimization_barrier((*values, *after))[: len(values)])


def stack(values, after=()):
    return jnp.stack(tie(values, after) if after else values)


def add_body(count, *refs):
    total = refs[0][...].astype(f32)
    for k in range(1, count):
        total = total + refs[k][...].astype(f32)
    refs[-1][...] = total.astype(bf16)


def add(values, after=()):
    dims = values[0].shape
    return call(
        partial(add_body, len(values)),
        "add",
        (1,),
        [whole(dims)] * len(values) + [HBM] * len(after),
        whole(dims),
        shape(dims, bf16),
        [],
        10,
    )(*values, *after)


def add_split_body(count, lead, *refs):
    for k in range(4):
        if count == 2:
            refs[len(refs) - 4 + k][...] = refs[0][k] + refs[1][k]
            continue
        total = refs[0][k].astype(f32)
        for v in range(1, count):
            total = total + refs[v][k].astype(f32)
        refs[len(refs) - 4 + k][...] = total.astype(bf16)


def add_split(values, after=()):
    dims = values[0].shape
    steps = dims[1] if len(dims) == 5 else 1
    ins = (4, dims[1] // steps, *dims[2:])
    outs = dims[1:]
    zeros = (0,) * (len(dims) - 2)
    return call(
        partial(add_split_body, len(values), True),
        "add_split",
        (steps,),
        [pl.BlockSpec(ins, lambda i: (0, i, *zeros))] * len(values) + [HBM] * len(after),
        [pl.BlockSpec((outs[0] // steps, *outs[1:]), lambda i: (i, *zeros))] * 4,
        [shape(outs, bf16)] * 4,
        [],
        10,
    )(*values, *after)


def join_body(*refs):
    out = refs[-1]
    at = 0
    for ref in refs[:2]:
        parts, rows = ref.shape[1:3]
        for p in range(parts):
            out[0, at : at + rows, :] = ref[0, p]
            at += rows


def join(first, second, after):
    rows = sum(value.shape[1] * value.shape[2] for value in (first, second))

    def spec(value):
        return pl.BlockSpec((1, *value.shape[1:]), lambda i: (i, 0, 0, 0))

    return call(
        join_body,
        "join",
        (4,),
        [spec(first), spec(second)] + [HBM] * len(after),
        pl.BlockSpec((1, rows, BLOCK), lambda i: (i, 0, 0)),
        shape((4, rows, BLOCK), bf16),
        [],
        5,
    )(first, second, *after)


def send_z(piece):
    return [piece] + [shift(piece, s) for s in range(1, 4)]


def send_plane(piece):
    return [piece] + [swap(piece, 2 * j) for j in range(1, 4)]


def give_plane(parts):
    return [parts[0]] + [swap(parts[j], 2 * j) for j in range(1, 4)]


def give_z(parts):
    return [parts[0]] + [shift(parts[s], s) for s in range(1, 4)]


def gather_wide(piece, dp, extra):
    fine = dp // 8
    parts, rows = piece.shape[0], piece.shape[1] - extra
    out = lax.all_gather(piece, ("dp", "zero"), axis=0, tiled=False)
    out = out.reshape(8, fine, 4, *piece.shape)
    main = out[..., :rows, :].transpose(0, 2, 3, 1, 4, 5).reshape(8, 4, parts, 128, BLOCK)
    return [jnp.concatenate([main, out[:, 0, ..., rows:, :]], 3)]


def reduce_wide(blocks, dp, extra):
    fine = dp // 8
    blocks = blocks.reshape(8, 4, *blocks.shape[-3:])
    parts, rows = blocks.shape[2], 128 // fine
    main = blocks[..., :128, :].reshape(8, 4, parts, fine, rows, BLOCK).transpose(0, 3, 1, 2, 4, 5)
    beside = jnp.broadcast_to(
        blocks[:, None, ..., 128:, :], (8, fine, 4, parts, extra, BLOCK)
    )
    flat = jnp.concatenate([main, beside], 4).reshape(dp * 4, parts, rows + extra, BLOCK)
    mine = lax.psum_scatter(flat, ("dp", "zero"), scatter_dimension=0, tiled=True)
    out = lax.all_gather(mine[0], "dp", axis=0, tiled=False)
    out = out.reshape(8, fine, parts, rows + extra, BLOCK)
    main = out[..., :rows, :].transpose(0, 2, 1, 3, 4).reshape(8, parts, 128, BLOCK)
    out = jnp.concatenate([main, out[:, 0, :, rows:]], 2)
    return out.reshape(8, -1, BLOCK)


def shards(
    dp, images, cotangent, counts, rel_index, regions,
    mat_w, mat_m, mat_v, vec_w, vec_m, vec_v, tab_w, tab_m, tab_v,
):
    near = dp == 8
    fine = dp // 8
    rows = 128 // fine
    me = lax.axis_index("dp")
    taken_from = jnp.stack([me // fine, me % fine]).astype(jnp.int32)
    spot = [me, lax.axis_index("zero")] if near else [0 * me, 0 * me]
    place = jnp.stack(spot + [counts[0]]).astype(jnp.int32)

    inside = np.arange(CELL) < WIN * WIN
    zones = regions.reshape(2, WIN, 2, WIN).transpose(0, 2, 1, 3).reshape(4, WIN * WIN)
    zones = jnp.pad(zones, ((0, 0), (0, 15)))
    differ = (zones[:, :, None] != zones[:, None, :]) & inside[None, None, :]
    outside = jnp.asarray(np.where(inside, 0.0, -1e30), f32)[None, :, None]
    mask_shifted = jnp.tile(jnp.where(differ, mask_value, 0.0) + outside, (1, 1, QUAD)).astype(f32)
    mask_plain = jnp.broadcast_to(outside, (1, CELL, QUAD * CELL))
    masks = (mask_plain, mask_shifted)
    perms = (frames(False), frames(True))

    packed, cut_mlp0, cut_all1, rel = pack(
        taken_from, rows, mat_w, rel_index, tab_w, vec_w
    )
    alive = (jnp.arange(images.shape[0]) < counts[0]).astype(f32)[:, None, None]
    pad = ((0, 0), (0, ROWS - TOKENS), (0, 0))
    images = jnp.pad(images.astype(f32), pad)
    cotangent = jnp.pad(cotangent.astype(f32) * alive, pad)

    def attention(layer, stream, weight, after):
        return attention_forward(
            layer, place, stream, weight, heads0, masks[layer], perms[layer], after
        )

    half = images.shape[0] // 2
    if near:
        sent_heads0 = send_z(packed)
        *sent_heads0, images = tie([*sent_heads0, images], [])
        z_heads0 = stack(sent_heads0)
        all1 = gather_wide(tie([cut_all1], [z_heads0])[0], dp, 0)
        sent_heads0 = send_plane(z_heads0)
        sent_mlp0 = send_z(tie([cut_mlp0], [z_heads0])[0])
        cotangent, mask_shifted = tie([cotangent, mask_shifted], [z_heads0])
        *sent_heads0, cotangent, mask_shifted = tie(
            [*sent_heads0, cotangent, mask_shifted], sent_mlp0
        )
        masks = (mask_plain, mask_shifted)
        p_heads0 = stack(sent_heads0)
        heads0 = [p_heads0, swap(p_heads0, 1)]
        z_mlp0 = stack(sent_mlp0, [p_heads0])
        sent_mlp0 = send_plane(z_mlp0)
        kept0 = attention(0, images, heads0, [z_mlp0])
        p_mlp0 = stack(sent_mlp0, [kept0[0]])
        mlp0 = [p_mlp0, swap(p_mlp0, 1)]
    else:
        heads0 = gather_wide(packed, dp, EXTRA)
        mlp0 = gather_wide(cut_mlp0, dp, 0)
        all1 = gather_wide(cut_all1, dp, 0)
        kept0 = attention(0, images, heads0, [])
    stream, act, slope = mlp_forward(0, place, kept0[0], mlp0, kept0[5], [])
    kept1 = attention(1, stream, all1, [])
    kept = (kept0, kept1)
    inputs = (images, stream)
    attention_w = (heads0, all1)

    def backward_attention(layer, gradient, small, after, *span):
        mid, qkv, merged, totals, table, vec = kept[layer]
        return attention_backward(
            layer, place, gradient, inputs[layer], qkv, merged, totals, table, attention_w[layer],
            vec, small, perms[layer], rel, after, *span,
        )

    activations, grad_mid, parts_mlp1, small = mlp_both(
        place, cotangent, kept1[0], all1, kept1[5], []
    )

    def backward_mlp0(gradient, after):
        return mlp_backward(0, place, gradient, act, slope, kept0[0], mlp0, kept0[5], after)

    state = (mat_w, mat_m, mat_v)
    def exchange(parts):
        return [parts[0], swap(parts[1], 1)]

    gradient, parts_heads1, _, small1 = backward_attention(1, grad_mid, small, [])
    grad_mid, *parts_mlp0, small = backward_mlp0(gradient, [])
    if near:
        t_mlp1 = lax.psum_scatter(parts_mlp1, "dp", scatter_dimension=0, tiled=True)[0]
        parts_heads1 = tie([parts_heads1], [t_mlp1])[0]
        t_heads1 = lax.psum_scatter(parts_heads1, "dp", scatter_dimension=0, tiled=True)[0]
        gone_mlp0 = exchange(parts_mlp0)
        gradient, *parts_heads0, pairs, small = backward_attention(0, grad_mid, small, [], 0, half)

        s_mlp0 = add_split(gone_mlp0, [gradient])
        gone_mlp0 = give_plane(s_mlp0)
        t_all1 = join(t_mlp1, t_heads1, [s_mlp0[0]])
        g_all1 = lax.psum_scatter(t_all1, "zero", scatter_dimension=0, tiled=True)
        gradient, *parts_heads0, _, small = backward_attention(
            0, grad_mid, small, [t_all1], half, half, [gradient, *parts_heads0, pairs]
        )

        gone_mlp0 = tie(gone_mlp0, [small])
        gone_heads0 = exchange(tie(parts_heads0, gone_mlp0))
        t_mlp0 = add_split(gone_mlp0)
        n_all1 = lax.all_gather(tie([g_all1], [t_mlp0[0]])[0][0], "dp", axis=0, tiled=False)
        gone_mlp0 = give_z(t_mlp0)
        s_heads0 = add_split(gone_heads0, [t_mlp0[0]])
        gone_heads0 = give_plane(s_heads0)
        g_mlp0 = add(gone_mlp0, [s_heads0[0]])
        gone_mlp0 = send_plane(g_mlp0)
        t_heads0 = add_split(gone_heads0, [g_mlp0])
        gone_heads0 = give_z(t_heads0)
        n_mlp0 = stack(gone_mlp0, [t_heads0[0]])
        sums_mlp0 = [n_mlp0, swap(n_mlp0, 1)]
        g_heads0 = add(gone_heads0, [n_mlp0])
        gone_heads0 = send_plane(g_heads0)
        done = adam(1, 1, place, [n_all1], state, None, [g_heads0])
        n_heads0 = stack(gone_heads0, [done[0]])
        sums_heads0 = [n_heads0, swap(n_heads0, 1)]
        done = adam(0, 1, place, sums_mlp0, state, done, [n_heads0])
        m = place[0] ^ np.arange(2)
        both = jnp.concatenate([half[:, 0, 128:] for half in sums_heads0])
        beside0 = [lax.dynamic_index_in_dim(both, (m[b] % 2) * 4 + m[b] // 2, 0, False) for b in range(2)]
    else:
        gradient, *parts_heads0, _, _ = backward_attention(0, grad_mid, small, [])
        n_mlp1 = reduce_wide(parts_mlp1, dp, 0)
        n_heads1 = reduce_wide(parts_heads1, dp, SMALL)
        n_all1 = jnp.concatenate([n_mlp1, n_heads1], 1)
        done = adam(1, 1, place, [n_all1], state, None, [])
        done = adam(0, 1, place, [reduce_wide(jnp.stack(parts_mlp0, 1), dp, 0)], state, done, [])
        sums_heads0 = [reduce_wide(jnp.stack(parts_heads0, 1), dp, SMALL)]
        beside0 = sums_heads0[0][:2, 128:]
    done = adam(0, 0, place, sums_heads0, state, done, [])

    def beside(block):
        return jnp.stack([beside0[block], n_all1[block, 384:]]).astype(f32)

    new_vec = adam_step(vec_w, vec_m, vec_v, beside(1)[:, 0:12, 0:128], rate_vector, 0.0)
    new_tab = adam_step(tab_w, tab_m, tab_v, beside(0)[:, 0:4, 0:NREL], rate_table, 0.0)
    return (activations, gradient, *done, *new_vec, *new_tab)


def solution(mesh):
    images = P(("dp", "zero"), None, None)
    rows = P(None, "zero", None)
    lanes = P(None, None, "zero")
    return jax.shard_map(
        partial(shards, mesh.shape["dp"]),
        mesh=mesh,
        in_specs=(images, images, P(("dp", "zero")), P(), P())
        + (rows,) * 3 + (lanes,) * 3 + (rows,) * 3,
        out_specs=(images, images) + (rows,) * 3 + (lanes,) * 3 + (rows,) * 3,
        check_vma=False,
    )
```

```python
from functools import partial

import jax
import jax.numpy as jnp
import numpy as np
from jax import lax
from jax.experimental import pallas as pl
from jax.experimental.pallas import tpu as pltpu
from jax.sharding import PartitionSpec as P

WIN = 7
SIDE = 14
STEP = 10
NREL = 169
C = 512
HID = 2048
TOKENS = SIDE * SIDE
PAIR = 2
CHUNK = 16
ROWS = 208
FRAME = 256
CELL = 64
QUAD = 4
BLOCK = 256
EXTRA = 32
SMALL = 16

norm_eps = 1e-05
mask_value = -100.0
beta_one = 0.9
beta_two = 0.999
adam_eps = 1e-08
weight_decay = 0.05
rate_matrix = 0.1
rate_vector = 0.5
rate_table = 1.0
scale = 32 ** (-0.5)

bf16 = jnp.bfloat16
f32 = jnp.float32
NN = (((1,), (0,)), ((), ()))
NT = (((1,), (1,)), ((), ()))
TN = (((0,), (0,)), ((), ()))


def mm(left, right, dims=NN):
    return lax.dot_general(left, right, dims, preferred_element_type=f32)


def frames(shifted):
    move = WIN // 2 if shifted else 0
    placed = np.zeros((FRAME, ROWS), np.float32)
    for wy in range(2):
        for wx in range(2):
            for iy in range(WIN):
                for ix in range(WIN):
                    y = (wy * WIN + iy + move) % SIDE
                    x = (wx * WIN + ix + move) % SIDE
                    placed[(wy * 2 + wx) * CELL + iy * WIN + ix, y * SIDE + x] = 1
    return placed


def head_rows():
    rows = np.zeros((QUAD * CELL, 128), np.float32)
    for h in range(QUAD):
        rows[h * CELL : (h + 1) * CELL, h * 32 : (h + 1) * 32] = 1
    return rows


def head_spread(rows):
    out = np.zeros((rows, QUAD * CELL), np.float32)
    for h in range(QUAD):
        out[h, h * CELL : (h + 1) * CELL] = 1
    return out


def norm(rows):
    centred = rows - jnp.mean(rows, -1, keepdims=True)
    spread = lax.rsqrt(jnp.mean(centred * centred, -1, keepdims=True) + norm_eps)
    return centred * spread, spread


def norm_back(grad_unit, unit, spread):
    return spread * (
        grad_unit
        - jnp.mean(grad_unit, -1, keepdims=True)
        - unit * jnp.mean(grad_unit * unit, -1, keepdims=True)
    )


def column_sum(rows):
    return jnp.sum(rows, 0, keepdims=True)


def gelu_pair(u):
    size = jnp.abs(u)
    below = 1.0 + (0.3275911 * 0.5**0.5) * size
    t = pltpu.reciprocal(below, approx=True)
    bell = jnp.exp2(u * u * (-0.5 * 1.4426950408889634))
    poly = t * (
        0.127414796 + t * (-0.142248368 + t * (0.710706871 + t * (-0.726576013 + t * 0.530702714)))
    )
    tail = poly * bell
    phi = jnp.where(u >= 0, 1.0 - tail, tail)
    return u * phi, phi + u * bell * 0.3989422804014327


def fold(rows):
    return rows[:8] + rows[8:]


def norm_chunks(stream, vec, gain, out, first=0):
    for r in range(0, stream.shape[0], CHUNK):
        unit, _ = norm(stream[r : r + CHUNK, :])
        scaled = unit * vec[gain : gain + 1, :] + vec[gain + 1 : gain + 2, :]
        out[pl.ds(first + r, CHUNK), :] = scaled.astype(bf16)


def norm_back_chunks(stream, back, through, vec, gain, out, limit):
    gains = jnp.zeros((8, C), f32)
    offsets = jnp.zeros((8, C), f32)
    for r in range(0, stream.shape[0], CHUNK):
        unit, spread = norm(stream[r : r + CHUNK, :])
        grad = back[r : r + CHUNK, :]
        gains = gains + fold(grad * unit)
        offsets = offsets + fold(grad)
        total = through[r : r + CHUNK, :] + norm_back(grad * vec[gain : gain + 1, :], unit, spread)
        size = min(CHUNK, limit - r)
        if size > 0:
            out[r : r + size, :] = total[:size]
    return gains, offsets


def quad_rows(part, heads):
    return jnp.concatenate([part] * QUAD, 0) * heads


def pick_heads(stacked, lane_head):
    low = jnp.where(lane_head == 0, stacked[:CELL], stacked[CELL : 2 * CELL])
    high = jnp.where(lane_head == 2, stacked[2 * CELL : 3 * CELL], stacked[3 * CELL :])
    return jnp.where(lane_head < 2, low, high)


def lane_heads():
    return lax.broadcasted_iota(jnp.int32, (CELL, 128), 1) // 32


def whole(shape):
    zero = (0,) * len(shape)
    return pl.BlockSpec(shape, lambda *_: zero, pipeline_mode=pl.Buffered(1))


def per_image(rows, cols):
    return pl.BlockSpec((1, rows, cols), lambda i, *_: (i, 0, 0))


def per_pair(rows, cols):
    return pl.BlockSpec((PAIR, rows, cols), lambda i, *_: (i, 0, 0))


HBM = pl.BlockSpec(memory_space=pl.ANY)


def weight_copies(place, stacks, kept, sems, part=0):
    copies = []
    for m in range(8):
        for s in range(4):
            for p in range(kept.shape[0]):
                if len(stacks) == 1:
                    source, block, owner = stacks[0].at[m, s, part + p], m, s
                else:
                    source = stacks[m % 2].at[m // 2, s, p]
                    block, owner = place[0] ^ m, (place[1] + 4 - s) & 3
                rows = pl.ds(pl.multiple_of(owner * 128, 128), 128)
                cols = pl.ds(pl.multiple_of(block * BLOCK, BLOCK), BLOCK)
                copies.append(
                    pltpu.make_async_copy(
                        source.at[pl.ds(0, 128), :], kept.at[p, rows, cols], sems.at[m, s, p]
                    )
                )
    return copies


def extra_copies(place, stacks, kept, sems):
    copies = []
    for m in range(8):
        for s in range(4):
            if len(stacks) == 1:
                source, block, owner = stacks[0].at[m, s, 0], m, s
            else:
                source = stacks[m % 2].at[m // 2, s, 0]
                block, owner = place[0] ^ m, (place[1] + 4 - s) & 3
            copies.append(
                pltpu.make_async_copy(
                    source.at[pl.ds(128, EXTRA), :], kept.at[block, owner], sems.at[m, s, 0]
                )
            )
    return copies


def fetch(copies):
    for copy in copies:
        copy.start()
    for copy in copies:
        copy.wait()


def call(body, name, grid, ins, outs, out_shapes, scratch, cost_us, prefetch=0, aliases=None):
    return pl.pallas_call(
        body,
        name=name,
        grid_spec=pltpu.PrefetchScalarGridSpec(
            num_scalar_prefetch=prefetch,
            grid=grid,
            in_specs=ins,
            out_specs=outs,
            scratch_shapes=scratch,
        ),
        out_shape=out_shapes,
        input_output_aliases=aliases or {},
        compiler_params=pltpu.CompilerParams(
            dimension_semantics=("arbitrary",) * len(grid), vmem_limit_bytes=58 * 1024 * 1024
        ),
        cost_estimate=pl.CostEstimate(
            flops=0, bytes_accessed=int(cost_us * 3.69e4), transcendentals=0
        ),
    )


def shape(dims, kind):
    return jax.ShapeDtypeStruct(dims, kind)


def pack_body(place, *refs):
    mats, (pair_index, tab, vec, spread) = refs[:6], refs[6:10]
    out, mlp0, all1, rel, spread_tab, small = refs[10:]
    rows = mats[0].shape[1]
    out[0, 0:rows, :] = mats[0][0].astype(bf16)
    for ref, at, n in ((mlp0, 0, 1), (mlp0, 1, 2), (all1, 0, 3), (all1, 1, 4), (all1, 2, 5)):
        ref[at] = mats[n][0].astype(bf16)
    rel[...] = jnp.full(rel.shape, -1, jnp.int32)
    across = pair_index[...].astype(f32).T.astype(jnp.int32)
    for h in range(QUAD):
        rel[0 : WIN * WIN, CELL * h : CELL * h + WIN * WIN] = across
    for layer in range(2):
        spread_tab[layer, 0:NREL, :] = mm(tab[layer].astype(bf16), spread[...], TN)
    pairs = rel[pl.ds(pl.multiple_of(place[0] * 8, 8), 8), :]

    def step(r, sums):
        hit = pairs == r
        return tuple(
            jnp.where(hit, spread_tab[layer, pl.ds(r, 1), :], sums[layer]) for layer in range(2)
        )

    start = jnp.zeros((8, QUAD * CELL), f32)
    first, second = lax.fori_loop(0, NREL, step, (start, start), unroll=13)
    out[0, rows : rows + 16, :] = jnp.concatenate([first, second], 0).astype(bf16)
    small[...] = jnp.zeros_like(small)
    row = jnp.minimum(place[0] * 2, 10)
    for layer in range(2):
        for k in range(2):
            small[k : k + 1, layer * 128 : (layer + 1) * 128] = vec[row + k, layer : layer + 1, :]
    out[0, rows + 16 : rows + 32, :] = small[...].astype(bf16)


def pack(place, rows, mat_w, rel_index, tab_w, vec_w):
    vec_w = vec_w.transpose(1, 0, 2)

    def block(layer, part):
        return pl.BlockSpec(
            (1, rows, BLOCK), lambda i, place: (layer, place[1], part * 8 + place[0])
        )

    dims = [(1, rows + EXTRA, BLOCK), (2, rows, BLOCK), (3, rows, BLOCK)]
    return call(
        pack_body,
        "pack",
        (1,),
        [block(layer, part) for layer in range(2) for part in range(3)]
        + [
            whole(rel_index.shape),
            whole(tab_w.shape),
            whole(vec_w.shape),
            whole((QUAD, QUAD * CELL)),
        ],
        [whole(d) for d in dims] + [whole((CELL, QUAD * CELL))],
        [shape(d, bf16) for d in dims] + [shape((CELL, QUAD * CELL), jnp.int32)],
        [pltpu.VMEM((2, 176, QUAD * CELL), f32), pltpu.VMEM((16, 256), f32)],
        4,
        prefetch=1,
    )(place, *[mat_w] * 6, rel_index, tab_w, vec_w, jnp.asarray(head_spread(QUAD), bf16))


def attention_forward_body(layer, stacks, waits, place, *refs):
    arrays, refs = refs[: stacks[0]], refs[stacks[0] :]
    extras, refs = refs[: stacks[1]], refs[stacks[1] + waits :]
    x, mask, perm, perm_back, heads = refs[:5]
    mid, qkv, merged, totals, table, vec, framed, normed_rows = refs[5:13]
    kept, extra_kept, sems, more_sems = refs[13:]
    weight, extra = kept.at[0], extra_kept

    @pl.when(pl.program_id(0) == 0)
    def _():
        fetch(
            weight_copies(place, arrays, kept, sems)
            + extra_copies(place, extras, extra_kept, more_sems)
        )
        vec[...] = jnp.zeros_like(vec)
        for z in range(4):
            for d in range(8):
                pair = extra[d, z, 0:16, :].astype(f32)
                bias = pair[8 * layer : 8 * layer + 8]
                for w in range(table.shape[0]):
                    table[w, z, 8 * d : 8 * d + 8, :] = bias + mask[w, 8 * d : 8 * d + 8, :]
                if d < 6:
                    rows = extra[d, z, 16:32, 128 * layer : 128 * layer + 128].astype(f32)
                    vec[2 * d : 2 * d + 2, 128 * z : 128 * z + 128] = rows[0:2]

    norm_chunks(x.at[0], vec, 0, normed_rows)
    normed = mm(perm[...], normed_rows[...]).astype(bf16)
    for c in range(6):
        part = mm(normed, weight[:, 256 * c : 256 * c + 256])
        if c < 2:
            part = part + vec[2:3, 256 * c : 256 * c + 256]
        if c >= 4:
            part = part + vec[3:4, 256 * (c - 4) : 256 * (c - 4) + 256]
        qkv[0, :, 256 * c : 256 * c + 256] = part.astype(bf16)
    lane_head = lane_heads()

    def score(unit):
        rows, at = slice(CELL * (unit // 4), CELL * (unit // 4) + CELL), 128 * (unit % 4)
        query = quad_rows(qkv[0, rows, at : at + 128], heads[...])
        return mm(qkv[0, rows, C + at : C + at + 128], query, NT)

    ahead = score(0)
    for n in range(16):
        w, g = n // 4, n % 4
        rows, at = slice(CELL * w, CELL * w + CELL), 128 * g
        scores = ahead * scale + table[w % table.shape[0], g]
        if n < 15:
            ahead = score(n + 1)
        top = jnp.max(scores, 0, keepdims=True)
        raised = jnp.exp(scores - top)
        total = jnp.sum(raised, 0, keepdims=True)
        totals[0, n : n + 1, :] = top + jnp.log(total)
        probs = (raised * (1.0 / total)).astype(bf16)
        stacked = mm(probs, qkv[0, rows, 2 * C + at : 2 * C + at + 128], TN)
        framed[rows, at : at + 128] = pick_heads(stacked, lane_head).astype(bf16)
    gathered = mm(perm_back[...], framed[...]).astype(bf16)
    merged[0] = gathered
    mid[0] = x[0] + mm(gathered, weight[:, 3 * C :]) + vec[4:5, :]


def attention_forward(layer, place, x, weight, extra, mask, perm, after):
    images = x.shape[0]
    tables = mask.shape[0]
    return call(
        partial(attention_forward_body, layer, (len(weight), len(extra)), len(after)),
        f"attention_forward_{layer}",
        (images,),
        [HBM] * (len(weight) + len(extra) + len(after))
        + [
            per_image(x.shape[1], C),
            whole(mask.shape),
            whole((FRAME, ROWS)),
            whole((ROWS, FRAME)),
            whole((QUAD * CELL, 128)),
        ],
        [
            per_image(ROWS, C),
            per_image(FRAME, 3 * C),
            per_image(ROWS, C),
            per_image(16, QUAD * CELL),
            pl.BlockSpec((tables, 4, CELL, QUAD * CELL), lambda i, *_: (0, 0, 0, 0)),
            pl.BlockSpec((16, C), lambda i, *_: (0, 0)),
        ],
        [
            shape((images, ROWS, C), f32),
            shape((images, FRAME, 3 * C), bf16),
            shape((images, ROWS, C), bf16),
            shape((images, 16, QUAD * CELL), f32),
            shape((tables, 4, CELL, QUAD * CELL), f32),
            shape((16, C), f32),
        ],
        [
            pltpu.VMEM((FRAME, C), bf16),
            pltpu.VMEM((ROWS, C), bf16),
            pltpu.VMEM((1, C, HID), bf16),
            pltpu.VMEM((8, 4, EXTRA, BLOCK), bf16),
            pltpu.SemaphoreType.DMA((8, 4, 1)),
            pltpu.SemaphoreType.DMA((8, 4, 1)),
        ],
        20,
        prefetch=1,
    )(
        place,
        *weight,
        *extra,
        *after,
        x,
        mask,
        jnp.asarray(perm, bf16),
        jnp.asarray(perm.T, bf16),
        jnp.asarray(head_rows(), bf16),
    )


def mlp_forward_body(stacks, waits, place, *refs):
    arrays, refs = refs[:stacks], refs[stacks + waits :]
    mid, vec, result, act, slope, normed, inners, kept, sems = refs
    first, second = kept.at[0], kept.at[1]

    @pl.when(pl.program_id(0) == 0)
    def _():
        fetch(weight_copies(place, arrays, kept, sems))

    rows = PAIR * ROWS
    for n in range(PAIR):
        norm_chunks(mid.at[n], vec, 5, normed, n * ROWS)
    inners[0] = mm(normed[...], first[:, 0:BLOCK])
    for c in range(8):
        cols = slice(256 * c, 256 * c + 256)
        if c < 7:
            inners[(c + 1) % 2] = mm(normed[...], first[:, 256 * c + 256 : 256 * c + 512])
        bias = vec[8 + c // 2 : 9 + c // 2, 256 * (c % 2) : 256 * (c % 2) + 256]
        for n in range(PAIR):
            for r in range(0, ROWS, CHUNK):
                value, pull = gelu_pair(inners[c % 2, n * ROWS + r : n * ROWS + r + CHUNK] + bias)
                act[n, r : r + CHUNK, cols] = value.astype(bf16)
                slope[n, r : r + CHUNK, cols] = pull.astype(bf16)
    total = mm(act[...].reshape(rows, HID), second[...], NT)
    result[...] = mid[...] + (total + vec[7:8, :]).reshape(PAIR, ROWS, C)


def mlp_forward(layer, place, mid, weight, vec, after):
    images = mid.shape[0]
    return call(
        partial(mlp_forward_body, len(weight), len(after)),
        f"mlp_forward_{layer}",
        (images // PAIR,),
        [HBM] * (len(weight) + len(after)) + [per_pair(ROWS, C), whole(vec.shape)],
        [per_pair(ROWS, C), per_pair(ROWS, HID), per_pair(ROWS, HID)],
        [
            shape((images, ROWS, C), f32),
            shape((images, ROWS, HID), bf16),
            shape((images, ROWS, HID), bf16),
        ],
        [
            pltpu.VMEM((PAIR * ROWS, C), bf16),
            pltpu.VMEM((2, PAIR * ROWS, BLOCK), f32),
            pltpu.VMEM((2, C, HID), bf16),
            pltpu.SemaphoreType.DMA((8, 4, 2)),
        ],
        22,
        prefetch=1,
    )(place, *weight, *after, mid, vec)


def mlp_both_body(stacks, waits, place, *refs):
    arrays, refs = refs[:stacks], refs[stacks + waits :]
    grad, mid, vec, result, grad_mid, pieces, small = refs[:7]
    all_grad, all_act, all_inner, all_normed, inners, pulls, wide, kept, sems = refs[7:]
    first, second = kept.at[0], kept.at[1]
    i = pl.program_id(0)

    @pl.when(i == 0)
    def _():
        fetch(weight_copies(place, arrays, kept, sems, 1))
        small[...] = jnp.zeros_like(small)

    rows = PAIR * ROWS
    start = pl.multiple_of(i * rows, 32)
    here = pl.ds(start, rows)
    sums = jnp.zeros((8, C), f32)
    for n in range(PAIR):
        for r in range(0, ROWS, CHUNK):
            part = grad[n, r : r + CHUNK, :]
            all_grad[pl.ds(start + n * ROWS + r, CHUNK), :] = part.astype(bf16)
            sums = sums + fold(part)
        norm_chunks(mid.at[n], vec, 5, all_normed, start + n * ROWS)
    small[7:8, :] += column_sum(sums)

    def dots(c):
        cols = slice(256 * c, 256 * c + 256)
        inners[c % 2] = mm(all_normed[here, :], first[:, cols])
        pulls[c % 2] = mm(all_grad[here, :], second[:, cols])

    dots(0)
    for c in range(8):
        cols = slice(256 * c, 256 * c + 256)
        if c < 7:
            dots(c + 1)
        row, lane = 8 + c // 2, 256 * (c % 2)
        bias = vec[row : row + 1, lane : lane + 256]
        sums = jnp.zeros((8, BLOCK), f32)
        for r in range(0, rows, CHUNK):
            value, pull = gelu_pair(inners[c % 2, r : r + CHUNK] + bias)
            all_act[pl.ds(start + r, CHUNK), cols] = value.astype(bf16)
            inner = (pulls[c % 2, r : r + CHUNK] * pull).astype(bf16)
            all_inner[pl.ds(start + r, CHUNK), cols] = inner
            sums = sums + fold(inner.astype(f32))
        small[row : row + 1, lane : lane + 256] += column_sum(sums)
    wide[...] = mm(all_inner[here, :], first[...], NT)
    for n in range(PAIR):
        gains, offsets = norm_back_chunks(
            mid.at[n], wide.at[n * ROWS : n * ROWS + ROWS], grad.at[n], vec, 5, grad_mid.at[n], ROWS
        )
        small[5:6, :] += column_sum(gains)
        small[6:7, :] += column_sum(offsets)
    wide[...] = mm(all_act[here, :], second[...], NT)
    for n in range(PAIR):
        alive = (i * PAIR + n < place[2]).astype(f32)
        for r in range(0, ROWS, CHUNK):
            total = mid[n, r : r + CHUNK, :] + vec[7:8, :] + wide[n * ROWS + r : n * ROWS + r + CHUNK, :]
            size = min(CHUNK, TOKENS - r)
            result[n, r : r + size, :] = (total * alive)[:size].astype(bf16)

    @pl.when(i == pl.num_programs(0) - 1)
    def _():
        mlp_weight_grads(place, all_grad, all_act, all_inner, all_normed, pieces)


def mlp_weight_grads(place, all_grad, all_act, all_inner, all_normed, *outs):
    grad_across = all_grad[...].T
    normed_across = all_normed[...].T
    for m in range(8):
        block = m if len(outs) == 1 else place[0] ^ m
        cols = pl.ds(pl.multiple_of(block * BLOCK, BLOCK), BLOCK)
        for p, total in enumerate(
            (mm(normed_across, all_inner[:, cols]), mm(grad_across, all_act[:, cols]))
        ):
            total = total.astype(bf16)
            for z in range(4):
                if len(outs) == 1:
                    outs[0][m, z, p] = total[128 * z : 128 * z + 128]
                else:
                    to = (z + 4 - place[1]) & 3
                    outs[m % 2][m // 2, to, p] = total[128 * z : 128 * z + 128]


def mlp_both(place, grad, mid, weight, vec, after):
    images = mid.shape[0]
    total = images * ROWS
    pieces = (8, 4, 2, 128, BLOCK)
    return call(
        partial(mlp_both_body, len(weight), len(after)),
        "mlp_both",
        (images // PAIR,),
        [HBM] * (len(weight) + len(after)) + [per_pair(ROWS, C), per_pair(ROWS, C), whole(vec.shape)],
        [per_pair(TOKENS, C), per_pair(ROWS, C), whole(pieces), whole((16, C))],
        [
            shape((images, TOKENS, C), bf16),
            shape((images, ROWS, C), f32),
            shape(pieces, bf16),
            shape((16, C), f32),
        ],
        [
            pltpu.VMEM((total, C), bf16),
            pltpu.VMEM((total, HID), bf16),
            pltpu.VMEM((total, HID), bf16),
            pltpu.VMEM((total, C), bf16),
            pltpu.VMEM((2, PAIR * ROWS, BLOCK), f32),
            pltpu.VMEM((2, PAIR * ROWS, BLOCK), f32),
            pltpu.VMEM((PAIR * ROWS, C), f32),
            pltpu.VMEM((2, C, HID), bf16),
            pltpu.SemaphoreType.DMA((8, 4, 2)),
        ],
        45,
        prefetch=1,
    )(place, *weight, *after, grad, mid, vec)


def mlp_backward_body(stacks, waits, place, *refs):
    arrays, refs = refs[:stacks], refs[stacks + waits :]
    grad, act, slope, mid, vec, grad_mid, own, other, small = refs[:9]
    all_grad, all_act, all_inner, all_normed, pulls, wide, kept, sems = refs[9:]
    first, second = kept.at[0], kept.at[1]
    i = pl.program_id(0)

    @pl.when(i == 0)
    def _():
        fetch(weight_copies(place, arrays, kept, sems))
        small[...] = jnp.zeros_like(small)

    rows = PAIR * ROWS
    start = pl.multiple_of(i * rows, 32)
    here = pl.ds(start, rows)
    sums = jnp.zeros((8, C), f32)
    for n in range(PAIR):
        for r in range(0, ROWS, CHUNK):
            low = grad[n, r : r + CHUNK, :].astype(bf16)
            all_grad[pl.ds(start + n * ROWS + r, CHUNK), :] = low
            sums = sums + fold(low.astype(f32))
        norm_chunks(mid.at[n], vec, 5, all_normed, start + n * ROWS)
    small[7:8, :] += column_sum(sums)
    pulls[0] = mm(all_grad[here, :], second[:, 0:BLOCK])
    for c in range(8):
        cols = slice(256 * c, 256 * c + 256)
        if c < 7:
            pulls[(c + 1) % 2] = mm(all_grad[here, :], second[:, 256 * c + 256 : 256 * c + 512])
        row, lane = 8 + c // 2, 256 * (c % 2)
        sums = jnp.zeros((8, BLOCK), f32)
        for n in range(PAIR):
            for r in range(0, ROWS, CHUNK):
                at = n * ROWS + r
                pull = slope[n, r : r + CHUNK, cols].astype(f32)
                inner = (pulls[c % 2, at : at + CHUNK] * pull).astype(bf16)
                all_inner[pl.ds(start + at, CHUNK), cols] = inner
                sums = sums + fold(inner.astype(f32))
        small[row : row + 1, lane : lane + 256] += column_sum(sums)
    all_act[here, :] = act[...].reshape(rows, HID)
    wide[...] = mm(all_inner[here, :], first[...], NT)
    for n in range(PAIR):
        gains, offsets = norm_back_chunks(
            mid.at[n], wide.at[n * ROWS : n * ROWS + ROWS], grad.at[n], vec, 5, grad_mid.at[n], ROWS
        )
        small[5:6, :] += column_sum(gains)
        small[6:7, :] += column_sum(offsets)

    @pl.when(i == pl.num_programs(0) - 1)
    def _():
        mlp_weight_grads(place, all_grad, all_act, all_inner, all_normed, own, other)


def mlp_backward(layer, place, grad, act, slope, mid, weight, vec, after):
    images = mid.shape[0]
    total = images * ROWS
    pieces = (4, 4, 2, 128, BLOCK)
    return call(
        partial(mlp_backward_body, len(weight), len(after)),
        f"mlp_backward_{layer}",
        (images // PAIR,),
        [HBM] * (len(weight) + len(after))
        + [
            per_pair(grad.shape[1], C),
            per_pair(ROWS, HID),
            per_pair(ROWS, HID),
            per_pair(ROWS, C),
            whole(vec.shape),
        ],
        [per_pair(ROWS, C), whole(pieces), whole(pieces), whole((16, C))],
        [
            shape((images, ROWS, C), f32),
            shape(pieces, bf16),
            shape(pieces, bf16),
            shape((16, C), f32),
        ],
        [
            pltpu.VMEM((total, C), bf16),
            pltpu.VMEM((total, HID), bf16),
            pltpu.VMEM((total, HID), bf16),
            pltpu.VMEM((total, C), bf16),
            pltpu.VMEM((2, PAIR * ROWS, BLOCK), f32),
            pltpu.VMEM((PAIR * ROWS, C), f32),
            pltpu.VMEM((2, C, HID), bf16),
            pltpu.SemaphoreType.DMA((8, 4, 2)),
        ],
        30,
        prefetch=1,
    )(place, *weight, *after, grad, act, slope, mid, vec)


def attention_backward_body(layer, stacks, waits, resumed, ends, place, *refs):
    arrays, refs = refs[:stacks], refs[stacks + waits :]
    if resumed:
        (own_before, other_before, pairs_before), refs = refs[1:4], refs[4:]
    grad, x, qkv, merged, totals, table, vec, before = refs[:8]
    perm, perm_back, heads, rel, spread, result = refs[8:14]
    outs, refs = (refs[14:15], refs[15:]) if layer else (refs[14:16], refs[16:])
    pairs, small, framed, grad_framed, all_normed, all_packed, all_merged = refs[:7]
    across, hits, beside, wide, kept, sems = refs[7:]
    weight = kept.at[0]
    i = pl.program_id(0)

    @pl.when(i == 0)
    def _():
        fetch(weight_copies(place, arrays, kept, sems))
        small[...] = before[...]
        pairs[...] = pairs_before[...] if resumed else jnp.zeros_like(pairs)

    start = pl.multiple_of(i * ROWS, 16)
    here = pl.ds(start, ROWS)
    norm_chunks(x.at[0], vec, 0, all_normed, start)
    sums = jnp.zeros((8, C), f32)
    for r in range(0, ROWS, CHUNK):
        low = grad[0, r : r + CHUNK, :].astype(bf16)
        all_packed[pl.ds(start + r, CHUNK), 3 * C :] = low
        sums = sums + fold(low.astype(f32))
    small[4:5, :] += column_sum(sums)
    all_merged[here, :] = merged[0]
    moved = mm(perm[...], all_packed[here, 3 * C :]).astype(bf16)
    framed[...] = mm(moved, weight[:, 3 * C :], NT).astype(bf16)
    lane_head = lane_heads()
    for w in range(4):
        rows = slice(CELL * w, CELL * w + CELL)
        at = [128 * g for g in range(4)]
        keys = [qkv[0, rows, C + c : C + c + 128] for c in at]
        query = [quad_rows(qkv[0, rows, c : c + 128], heads[...]) for c in at]
        pull = [quad_rows(framed[rows, c : c + 128], heads[...]) for c in at]
        scores = [mm(keys[g], query[g], NT) for g in range(4)]
        grad_probs = [
            mm(qkv[0, rows, 2 * C + at[g] : 2 * C + at[g] + 128], pull[g], NT) for g in range(4)
        ]
        probs, grad_scores = [], []
        for g in range(4):
            shifted = scores[g] * scale + table[w % table.shape[0], g]
            prob = jnp.exp(shifted - totals[0, 4 * w + g : 4 * w + g + 1, :])
            mean = jnp.sum(prob * grad_probs[g], 0, keepdims=True)
            grad_score = (prob * (grad_probs[g] - mean)).astype(bf16)
            pairs[g] += grad_score.astype(f32)
            probs.append(prob.astype(bf16))
            grad_scores.append(grad_score)
        for g in range(4):
            grad_value = mm(probs[g], pull[g])
            grad_framed[rows, 2 * C + at[g] : 2 * C + at[g] + 128] = grad_value.astype(bf16)
        for g in range(4):
            grad_key = mm(grad_scores[g], query[g]) * scale
            grad_framed[rows, C + at[g] : C + at[g] + 128] = grad_key.astype(bf16)
        for g in range(4):
            grad_query = pick_heads(mm(grad_scores[g], keys[g], TN), lane_head) * scale
            grad_framed[rows, at[g] : at[g] + 128] = grad_query.astype(bf16)
    for c in range(6):
        cols = slice(256 * c, 256 * c + 256)
        part = mm(perm_back[...], grad_framed[:, cols])
        all_packed[here, cols] = part.astype(bf16)
        if c < 2:
            small[2:3, cols] += column_sum(part)
        if c >= 4:
            small[3:4, 256 * (c - 4) : 256 * (c - 4) + 256] += column_sum(part)
    wide[...] = mm(all_packed[here, : 3 * C], weight[:, : 3 * C], NT)
    gains, offsets = norm_back_chunks(
        x.at[0], wide, grad.at[0], vec, 0, result.at[0], result.shape[1]
    )
    small[0:1, :] += column_sum(gains)
    small[1:2, :] += column_sum(offsets)

    @pl.when(i == pl.num_programs(0) - 1)
    def _():
        across[0] = all_normed[...].T
        across[1] = all_merged[...].T
        beside[...] = jnp.zeros_like(beside)
        if ends:
            hits[...] = jnp.zeros_like(hits)

            def step(r, carry):
                same = rel[...] == r
                for g in range(4):
                    kept_pairs = jnp.where(same, pairs[g], 0.0)
                    hits[pl.ds(r, 1), 256 * g : 256 * g + 256] = column_sum(kept_pairs)
                return carry

            lax.fori_loop(0, NREL, step, 0)
            for z in range(4):
                beside[0, z] = lax.dot_general(
                    spread[...],
                    hits[:, 256 * z : 256 * z + 256],
                    NT,
                    precision=lax.Precision.HIGHEST,
                    preferred_element_type=f32,
                ).astype(bf16)
                beside[1, z, :, 0:128] = small[:, 128 * z : 128 * z + 128].astype(bf16)
        for m in range(8):
            b = m if layer else place[0] ^ m
            left = across[jnp.where(b < 6, 0, 1)]
            right = all_packed[:, pl.ds(pl.multiple_of(b * BLOCK, BLOCK), BLOCK)]
            block = mm(left, right)
            for z in range(4):
                if layer:
                    out = outs[0].at[m, z, 0]
                else:
                    to = (z + 4 - place[1]) & 3
                    out = outs[m % 2].at[m // 2, to, 0]
                new = block[128 * z : 128 * z + 128]
                if resumed:
                    old = other_before if m % 2 else own_before
                    new = new + old[m // 2, to, 0, 0:128, :].astype(f32)
                out[0:128, :] = new.astype(bf16)
                out[128:144, :] = beside[jnp.minimum(b, 2), z]


def attention_backward(
    layer, place, grad, x, qkv, merged, totals, table, weight, vec, small, perm, rel, after,
    first=0, count=None, resume=None,
):
    images = grad.shape[0]
    count = count or images
    pieces = (8 if layer else 4, 4, 1, 128 + SMALL, BLOCK)
    pairs = (4, CELL, QUAD * CELL)
    total = count * ROWS
    out_rows = TOKENS if layer == 0 else ROWS

    def image(rows, cols):
        return pl.BlockSpec((1, rows, cols), lambda i, *_: (i + first, 0, 0))

    resumed = list(resume or [])
    return call(
        partial(
            attention_backward_body, layer, len(weight), len(after), bool(resumed),
            first + count == images,
        ),
        f"attention_backward_{layer}_{first}",
        (count,),
        [HBM] * (len(weight) + len(after))
        + ([HBM, whole(pieces), whole(pieces), whole(pairs)] if resumed else [])
        + [
            image(ROWS, C),
            image(x.shape[1], C),
            image(FRAME, 3 * C),
            image(ROWS, C),
            image(16, QUAD * CELL),
            whole(table.shape),
            whole(vec.shape),
            whole((16, C)),
            whole((FRAME, ROWS)),
            whole((ROWS, FRAME)),
            whole((QUAD * CELL, 128)),
            whole(rel.shape),
            whole((SMALL, QUAD * CELL)),
        ],
        [image(out_rows, C)]
        + [whole(pieces)] * (1 if layer else 2)
        + [whole(pairs), whole((16, C))],
        [shape((images, out_rows, C), f32)]
        + [shape(pieces, bf16)] * (1 if layer else 2)
        + [shape(pairs, f32), shape((16, C), f32)],
        [
            pltpu.VMEM((FRAME, C), bf16),
            pltpu.VMEM((FRAME, 3 * C), bf16),
            pltpu.VMEM((total, C), bf16),
            pltpu.VMEM((total, 4 * C), bf16),
            pltpu.VMEM((total, C), bf16),
            pltpu.VMEM((2, C, total), bf16),
            pltpu.VMEM((256, 4 * QUAD * CELL), f32),
            pltpu.VMEM((3, 4, SMALL, BLOCK), bf16),
            pltpu.VMEM((ROWS, C), f32),
            pltpu.VMEM((1, C, HID), bf16),
            pltpu.SemaphoreType.DMA((8, 4, 1)),
        ],
        6 * count,
        prefetch=1,
        aliases={1 + len(weight) + len(after): 0} if resumed else None,
    )(
        place,
        *weight,
        *after,
        *resumed,
        grad,
        x,
        qkv,
        merged,
        totals,
        table,
        vec,
        small,
        jnp.asarray(perm, bf16),
        jnp.asarray(perm.T, bf16),
        jnp.asarray(head_rows(), bf16),
        rel,
        jnp.asarray(head_spread(SMALL), f32),
    )


def adam_step(weight, first, second, gradient, rate, decay):
    first_new = beta_one * first + (1.0 - beta_one) * gradient
    second_new = beta_two * second + (1.0 - beta_two) * gradient * gradient
    first_hat = first_new / (1.0 - beta_one**STEP)
    second_hat = second_new / (1.0 - beta_two**STEP)
    weight_new = weight - rate * (first_hat / (jnp.sqrt(second_hat) + adam_eps) + decay * weight)
    return (weight_new, first_new, second_new)


def adam_block(grad, weight, first, second, outs, cols):
    for r in range(0, 128, 32):
        rows = slice(r, r + 32)
        part = grad[rows].astype(f32)
        first_new = beta_one * first[0, rows, cols] + (1.0 - beta_one) * part
        second_new = beta_two * second[0, rows, cols] + (1.0 - beta_two) * part * part
        spread = second_new * (1.0 / (1.0 - beta_two**STEP))
        inverse = pltpu.reciprocal(spread * lax.rsqrt(spread) + adam_eps, approx=True)
        step = first_new * (rate_matrix / (1.0 - beta_one**STEP)) * inverse
        outs[0][0, rows, cols] = weight[0, rows, cols] * (1.0 - rate_matrix * weight_decay) - step
        outs[1][0, rows, cols] = first_new
        outs[2][0, rows, cols] = second_new


def adam_body(place, near, far, weight, first, second, *refs):
    for j in range(2):
        for k in range(2):
            block = (((place[0] // 2) & 1) ^ j) * 2 + ((place[0] & 1) ^ k)
            cols = pl.ds(pl.multiple_of(block * BLOCK, BLOCK), BLOCK)
            adam_block((far if k else near).at[j, 0], weight, first, second, refs[-3:], cols)


def adam_body_plain(place, sums, weight, first, second, *refs):
    for k in range(4):
        cols = slice(BLOCK * k, BLOCK * k + BLOCK)
        adam_block(sums.at[k], weight, first, second, refs[-3:], cols)


def adam(layer, part, place, sums, state, done, after):
    kept = [] if done is None else list(done)
    if len(sums) == 2:
        parts = sums[0].shape[1]
        body = adam_body
        spec = pl.BlockSpec(
            (1, 128, 4 * BLOCK),
            lambda p, j, place: (layer, 0, (part + p) % 3 * 2 + ((place[0] // 4) ^ j)),
        )
        piece = pl.BlockSpec((2, 1, 128, BLOCK), lambda p, j, place: (j, p, 0, 0))
    else:
        parts = sums[0].shape[1] // 128
        body = adam_body_plain
        spec = pl.BlockSpec(
            (1, 128, 4 * BLOCK), lambda p, j, place: (layer, 0, (part + p) % 3 * 2 + j)
        )
        piece = pl.BlockSpec((4, 128, BLOCK), lambda p, j, place: (j, p, 0))
    return call(
        body,
        f"adam_{layer}_{part}",
        (parts, 2),
        [piece] * len(sums) + [spec] * 3 + [HBM] * (len(kept) + len(after)),
        [spec] * 3,
        [shape(state[0].shape, f32)] * 3,
        [],
        3 * parts,
        prefetch=1,
        aliases={4 + len(sums) + k: k for k in range(len(kept))},
    )(place, *sums, *state, *kept, *after)


def swap(value, bits):
    return lax.ppermute(value, "dp", [(i, i ^ bits) for i in range(8)])


def shift(value, steps):
    return lax.ppermute(value, "zero", [(i, (i + steps) % 4) for i in range(4)])


def tie(values, after):
    values = list(values)
    return list(lax.optimization_barrier((*values, *after))[: len(values)])


def stack(values, after=()):
    return jnp.stack(tie(values, after) if after else values)


def add_body(count, *refs):
    total = refs[0][...].astype(f32)
    for k in range(1, count):
        total = total + refs[k][...].astype(f32)
    refs[-1][...] = total.astype(bf16)


def add(values, after=()):
    dims = values[0].shape
    return call(
        partial(add_body, len(values)),
        "add",
        (1,),
        [whole(dims)] * len(values) + [HBM] * len(after),
        whole(dims),
        shape(dims, bf16),
        [],
        10,
    )(*values, *after)


def add_split_body(count, lead, *refs):
    for k in range(4):
        if count == 2:
            refs[len(refs) - 4 + k][...] = refs[0][k] + refs[1][k]
            continue
        total = refs[0][k].astype(f32)
        for v in range(1, count):
            total = total + refs[v][k].astype(f32)
        refs[len(refs) - 4 + k][...] = total.astype(bf16)


def add_split(values, after=()):
    dims = values[0].shape
    steps = dims[1] if len(dims) == 5 else 1
    ins = (4, dims[1] // steps, *dims[2:])
    outs = dims[1:]
    zeros = (0,) * (len(dims) - 2)
    return call(
        partial(add_split_body, len(values), True),
        "add_split",
        (steps,),
        [pl.BlockSpec(ins, lambda i: (0, i, *zeros))] * len(values) + [HBM] * len(after),
        [pl.BlockSpec((outs[0] // steps, *outs[1:]), lambda i: (i, *zeros))] * 4,
        [shape(outs, bf16)] * 4,
        [],
        10,
    )(*values, *after)


def join_body(*refs):
    out = refs[-1]
    at = 0
    for ref in refs[:2]:
        parts, rows = ref.shape[1:3]
        for p in range(parts):
            out[0, at : at + rows, :] = ref[0, p]
            at += rows


def join(first, second, after):
    rows = sum(value.shape[1] * value.shape[2] for value in (first, second))

    def spec(value):
        return pl.BlockSpec((1, *value.shape[1:]), lambda i: (i, 0, 0, 0))

    return call(
        join_body,
        "join",
        (4,),
        [spec(first), spec(second)] + [HBM] * len(after),
        pl.BlockSpec((1, rows, BLOCK), lambda i: (i, 0, 0)),
        shape((4, rows, BLOCK), bf16),
        [],
        5,
    )(first, second, *after)


def hold_body(*refs):
    refs[-1][...] = refs[0][...]


def hold(value, after):
    return call(
        hold_body,
        "hold",
        (1,),
        [whole(value.shape)] + [HBM] * len(after),
        whole(value.shape),
        shape(value.shape, value.dtype),
        [],
        2,
    )(value, *after)


def send_z(piece):
    return [piece] + [shift(piece, s) for s in range(1, 4)]


def send_plane(piece):
    return [piece] + [swap(piece, 2 * j) for j in range(1, 4)]


def give_plane(parts):
    return [parts[0]] + [swap(parts[j], 2 * j) for j in range(1, 4)]


def give_z(parts):
    return [parts[0]] + [shift(parts[s], s) for s in range(1, 4)]


def gather_wide(piece, dp, extra):
    fine = dp // 8
    parts, rows = piece.shape[0], piece.shape[1] - extra
    out = lax.all_gather(piece, ("dp", "zero"), axis=0, tiled=False)
    out = out.reshape(8, fine, 4, *piece.shape)
    main = out[..., :rows, :].transpose(0, 2, 3, 1, 4, 5).reshape(8, 4, parts, 128, BLOCK)
    return [jnp.concatenate([main, out[:, 0, ..., rows:, :]], 3)]


def reduce_wide(blocks, dp, extra):
    fine = dp // 8
    blocks = blocks.reshape(8, 4, *blocks.shape[-3:])
    parts, rows = blocks.shape[2], 128 // fine
    main = blocks[..., :128, :].reshape(8, 4, parts, fine, rows, BLOCK).transpose(0, 3, 1, 2, 4, 5)
    beside = jnp.broadcast_to(
        blocks[:, None, ..., 128:, :], (8, fine, 4, parts, extra, BLOCK)
    )
    flat = jnp.concatenate([main, beside], 4).reshape(dp * 4, parts, rows + extra, BLOCK)
    mine = lax.psum_scatter(flat, ("dp", "zero"), scatter_dimension=0, tiled=True)
    out = lax.all_gather(mine[0], "dp", axis=0, tiled=False)
    out = out.reshape(8, fine, parts, rows + extra, BLOCK)
    main = out[..., :rows, :].transpose(0, 2, 1, 3, 4).reshape(8, parts, 128, BLOCK)
    out = jnp.concatenate([main, out[:, 0, :, rows:]], 2)
    return out.reshape(8, -1, BLOCK)


def shards(
    dp, images, cotangent, counts, rel_index, regions,
    mat_w, mat_m, mat_v, vec_w, vec_m, vec_v, tab_w, tab_m, tab_v,
):
    near = dp == 8
    fine = dp // 8
    rows = 128 // fine
    me = lax.axis_index("dp")
    taken_from = jnp.stack([me // fine, me % fine]).astype(jnp.int32)
    spot = [me, lax.axis_index("zero")] if near else [0 * me, 0 * me]
    place = jnp.stack(spot + [counts[0]]).astype(jnp.int32)

    inside = np.arange(CELL) < WIN * WIN
    zones = regions.reshape(2, WIN, 2, WIN).transpose(0, 2, 1, 3).reshape(4, WIN * WIN)
    zones = jnp.pad(zones, ((0, 0), (0, 15)))
    differ = (zones[:, :, None] != zones[:, None, :]) & inside[None, None, :]
    outside = jnp.asarray(np.where(inside, 0.0, -1e30), f32)[None, :, None]
    mask_shifted = jnp.tile(jnp.where(differ, mask_value, 0.0) + outside, (1, 1, QUAD)).astype(f32)
    mask_plain = jnp.broadcast_to(outside, (1, CELL, QUAD * CELL))
    masks = (mask_plain, mask_shifted)
    perms = (frames(False), frames(True))

    packed, cut_mlp0, cut_all1, rel = pack(
        taken_from, rows, mat_w, rel_index, tab_w, vec_w
    )
    alive = (jnp.arange(images.shape[0]) < counts[0]).astype(f32)[:, None, None]
    pad = ((0, 0), (0, ROWS - TOKENS), (0, 0))
    images = jnp.pad(images.astype(f32), pad)
    cotangent = jnp.pad(cotangent.astype(f32) * alive, pad)

    def attention(layer, stream, weight, after):
        return attention_forward(
            layer, place, stream, weight, heads0, masks[layer], perms[layer], after
        )

    half = images.shape[0] // 2
    if near:
        sent_heads0 = send_z(packed)
        *sent_heads0, images = tie([*sent_heads0, images], [])
        z_heads0 = stack(sent_heads0)
        all1 = gather_wide(tie([cut_all1], [z_heads0])[0], dp, 0)
        sent_heads0 = send_plane(z_heads0)
        sent_mlp0 = send_z(tie([cut_mlp0], [z_heads0])[0])
        cotangent, mask_shifted = tie([cotangent, mask_shifted], [z_heads0])
        *sent_heads0, cotangent, mask_shifted = tie(
            [*sent_heads0, cotangent, mask_shifted], sent_mlp0
        )
        masks = (mask_plain, mask_shifted)
        p_heads0 = stack(sent_heads0)
        heads0 = [p_heads0, swap(p_heads0, 1)]
        z_mlp0 = stack(sent_mlp0, [p_heads0])
        sent_mlp0 = send_plane(z_mlp0)
        kept0 = attention(0, images, heads0, [z_mlp0])
        p_mlp0 = stack(sent_mlp0, [kept0[0]])
        mlp0 = [p_mlp0, swap(p_mlp0, 1)]
    else:
        heads0 = gather_wide(packed, dp, EXTRA)
        mlp0 = gather_wide(cut_mlp0, dp, 0)
        all1 = gather_wide(cut_all1, dp, 0)
        kept0 = attention(0, images, heads0, [])
    stream, act, slope = mlp_forward(0, place, kept0[0], mlp0, kept0[5], [])
    kept1 = attention(1, stream, all1, [])
    kept = (kept0, kept1)
    inputs = (images, stream)
    attention_w = (heads0, all1)

    def backward_attention(layer, gradient, small, after, *span):
        mid, qkv, merged, totals, table, vec = kept[layer]
        return attention_backward(
            layer, place, gradient, inputs[layer], qkv, merged, totals, table, attention_w[layer],
            vec, small, perms[layer], rel, after, *span,
        )

    activations, grad_mid, parts_mlp1, small = mlp_both(
        place, cotangent, kept1[0], all1, kept1[5], []
    )

    def backward_mlp0(gradient, after):
        return mlp_backward(0, place, gradient, act, slope, kept0[0], mlp0, kept0[5], after)

    state = (mat_w, mat_m, mat_v)
    def exchange(parts):
        return [parts[0], swap(parts[1], 1)]

    gradient, parts_heads1, _, small1 = backward_attention(1, grad_mid, small, [])
    grad_mid, *parts_mlp0, small = backward_mlp0(gradient, [])
    if near:
        t_mlp1 = lax.psum_scatter(parts_mlp1, "dp", scatter_dimension=0, tiled=True)[0]
        parts_heads1 = tie([parts_heads1], [t_mlp1])[0]
        t_heads1 = lax.psum_scatter(parts_heads1, "dp", scatter_dimension=0, tiled=True)[0]
        gone_mlp0 = exchange(parts_mlp0)
        gradient, *parts_heads0, pairs, small = backward_attention(0, grad_mid, small, [], 0, half)

        s_mlp0 = add_split(gone_mlp0, [gradient])
        gone_mlp0 = give_plane(s_mlp0)
        t_all1 = join(t_mlp1, t_heads1, [s_mlp0[0]])
        g_all1 = lax.psum_scatter(t_all1, "zero", scatter_dimension=0, tiled=True)
        gradient, *parts_heads0, _, small = backward_attention(
            0, grad_mid, small, [t_all1], half, half, [gradient, *parts_heads0, pairs]
        )

        t_mlp0 = add_split(gone_mlp0, [small])
        gone_heads0 = exchange(tie(parts_heads0, [t_mlp0[0]]))
        gone_mlp0 = give_z(t_mlp0)
        g_all1 = tie([g_all1], [t_mlp0[0]])[0]
        n_all1 = lax.all_gather(g_all1[0], "dp", axis=0, tiled=False)
        s_heads0 = add_split(gone_heads0, [t_mlp0[0]])
        gone_heads0 = give_plane(s_heads0)
        g_mlp0 = add(gone_mlp0, [s_heads0[0]])
        gone_mlp0 = send_plane(g_mlp0)
        t_heads0 = add_split(gone_heads0, [g_mlp0])
        gone_heads0 = give_z(t_heads0)
        n_mlp0 = stack(gone_mlp0, [t_heads0[0]])
        sums_mlp0 = [n_mlp0, swap(n_mlp0, 1)]
        g_heads0 = add(gone_heads0, [n_mlp0])
        done = adam(1, 1, place, [n_all1], state, None, [g_heads0])
        n_heads0 = stack(send_plane(g_heads0), [done[0]])
        sums_heads0 = [n_heads0, swap(n_heads0, 1)]
        done = adam(0, 1, place, sums_mlp0, state, done, [n_heads0])
        m = place[0] ^ np.arange(2)
        both = jnp.concatenate([half[:, 0, 128:] for half in sums_heads0])
        beside0 = [
            lax.dynamic_index_in_dim(both, (m[b] % 2) * 4 + m[b] // 2, 0, False) for b in range(2)
        ]
    else:
        gradient, *parts_heads0, _, _ = backward_attention(0, grad_mid, small, [])
        n_mlp1 = reduce_wide(parts_mlp1, dp, 0)
        n_heads1 = reduce_wide(parts_heads1, dp, SMALL)
        n_all1 = jnp.concatenate([n_mlp1, n_heads1], 1)
        done = adam(1, 1, place, [n_all1], state, None, [])
        done = adam(0, 1, place, [reduce_wide(jnp.stack(parts_mlp0, 1), dp, 0)], state, done, [])
        sums_heads0 = [reduce_wide(jnp.stack(parts_heads0, 1), dp, SMALL)]
        beside0 = sums_heads0[0][:2, 128:]
    done = adam(0, 0, place, sums_heads0, state, done, [])

    def beside(block):
        return jnp.stack([beside0[block], n_all1[block, 384:]]).astype(f32)

    new_vec = adam_step(vec_w, vec_m, vec_v, beside(1)[:, 0:12, 0:128], rate_vector, 0.0)
    new_tab = adam_step(tab_w, tab_m, tab_v, beside(0)[:, 0:4, 0:NREL], rate_table, 0.0)
    return (activations, gradient, *done, *new_vec, *new_tab)


def solution(mesh):
    images = P(("dp", "zero"), None, None)
    rows = P(None, "zero", None)
    lanes = P(None, None, "zero")
    return jax.shard_map(
        partial(shards, mesh.shape["dp"]),
        mesh=mesh,
        in_specs=(images, images, P(("dp", "zero")), P(), P())
        + (rows,) * 3 + (lanes,) * 3 + (rows,) * 3,
        out_specs=(images, images) + (rows,) * 3 + (lanes,) * 3 + (rows,) * 3,
        check_vma=False,
    )
```

```python
from functools import partial

import jax
import jax.numpy as jnp
import numpy as np
from jax import lax
from jax.experimental import pallas as pl
from jax.experimental.pallas import tpu as pltpu
from jax.sharding import PartitionSpec as P

WIN = 7
SIDE = 14
STEP = 10
NREL = 169
C = 512
HID = 2048
TOKENS = SIDE * SIDE
PAIR = 2
ROWS = 208
FRAME = 256
CELL = 64
QUAD = 4
BLOCK = 256
EXTRA = 32
SMALL = 16

norm_eps = 1e-05
mask_value = -100.0
beta_one = 0.9
beta_two = 0.999
adam_eps = 1e-08
weight_decay = 0.05
rate_matrix = 0.1
rate_vector = 0.5
rate_table = 1.0
scale = 32 ** (-0.5)

bf16 = jnp.bfloat16
f32 = jnp.float32
NN = (((1,), (0,)), ((), ()))
NT = (((1,), (1,)), ((), ()))
TN = (((0,), (0,)), ((), ()))


def mm(left, right, dims=NN):
    return lax.dot_general(left, right, dims, preferred_element_type=f32)


def frames(shifted):
    move = WIN // 2 if shifted else 0
    placed = np.zeros((FRAME, ROWS), np.float32)
    for wy in range(2):
        for wx in range(2):
            for iy in range(WIN):
                for ix in range(WIN):
                    y = (wy * WIN + iy + move) % SIDE
                    x = (wx * WIN + ix + move) % SIDE
                    placed[(wy * 2 + wx) * CELL + iy * WIN + ix, y * SIDE + x] = 1
    return placed


def head_rows():
    rows = np.zeros((QUAD * CELL, 128), np.float32)
    for h in range(QUAD):
        rows[h * CELL : (h + 1) * CELL, h * 32 : (h + 1) * 32] = 1
    return rows


def head_spread(rows):
    out = np.zeros((rows, QUAD * CELL), np.float32)
    for h in range(QUAD):
        out[h, h * CELL : (h + 1) * CELL] = 1
    return out


def norm(rows):
    centred = rows - jnp.mean(rows, -1, keepdims=True)
    spread = lax.rsqrt(jnp.mean(centred * centred, -1, keepdims=True) + norm_eps)
    return centred * spread, spread


def norm_back(grad_unit, unit, spread):
    return spread * (
        grad_unit
        - jnp.mean(grad_unit, -1, keepdims=True)
        - unit * jnp.mean(grad_unit * unit, -1, keepdims=True)
    )


def column_sum(rows):
    return jnp.sum(rows, 0, keepdims=True)


def gelu_pair(u):
    size = jnp.abs(u)
    below = 1.0 + (0.3275911 * 0.5**0.5) * size
    t = pltpu.reciprocal(below, approx=True)
    bell = jnp.exp2(u * u * (-0.5 * 1.4426950408889634))
    poly = t * (
        0.127414796 + t * (-0.142248368 + t * (0.710706871 + t * (-0.726576013 + t * 0.530702714)))
    )
    tail = poly * bell
    phi = jnp.where(u >= 0, 1.0 - tail, tail)
    return u * phi, phi + u * bell * 0.3989422804014327


def quad_rows(part, heads):
    return jnp.concatenate([part] * QUAD, 0) * heads


def pick_heads(stacked, lane_head):
    low = jnp.where(lane_head == 0, stacked[:CELL], stacked[CELL : 2 * CELL])
    high = jnp.where(lane_head == 2, stacked[2 * CELL : 3 * CELL], stacked[3 * CELL :])
    return jnp.where(lane_head < 2, low, high)


def lane_heads():
    return lax.broadcasted_iota(jnp.int32, (CELL, 128), 1) // 32


def whole(shape):
    zero = (0,) * len(shape)
    return pl.BlockSpec(shape, lambda *_: zero, pipeline_mode=pl.Buffered(1))


def per_image(rows, cols):
    return pl.BlockSpec((1, rows, cols), lambda i, *_: (i, 0, 0))


def per_pair(rows, cols):
    return pl.BlockSpec((PAIR, rows, cols), lambda i, *_: (i, 0, 0))


HBM = pl.BlockSpec(memory_space=pl.ANY)


def weight_copies(place, stacks, kept, sems, part=0):
    copies = []
    for m in range(8):
        for s in range(4):
            for p in range(kept.shape[0]):
                if len(stacks) == 1:
                    source, block, owner = stacks[0].at[m, s, part + p], m, s
                else:
                    source = stacks[m % 2].at[m // 2, s, p]
                    block, owner = place[0] ^ m, (place[1] + 4 - s) & 3
                rows = pl.ds(pl.multiple_of(owner * 128, 128), 128)
                cols = pl.ds(pl.multiple_of(block * BLOCK, BLOCK), BLOCK)
                copies.append(
                    pltpu.make_async_copy(
                        source.at[pl.ds(0, 128), :], kept.at[p, rows, cols], sems.at[m, s, p]
                    )
                )
    return copies


def extra_copies(place, stacks, kept, sems):
    copies = []
    for m in range(8):
        for s in range(4):
            if len(stacks) == 1:
                source, block, owner = stacks[0].at[m, s, 0], m, s
            else:
                source = stacks[m % 2].at[m // 2, s, 0]
                block, owner = place[0] ^ m, (place[1] + 4 - s) & 3
            copies.append(
                pltpu.make_async_copy(
                    source.at[pl.ds(128, EXTRA), :], kept.at[block, owner], sems.at[m, s, 0]
                )
            )
    return copies


def fetch(copies):
    for copy in copies:
        copy.start()
    for copy in copies:
        copy.wait()


def call(body, name, grid, ins, outs, out_shapes, scratch, cost_us, prefetch=0, aliases=None):
    return pl.pallas_call(
        body,
        name=name,
        grid_spec=pltpu.PrefetchScalarGridSpec(
            num_scalar_prefetch=prefetch,
            grid=grid,
            in_specs=ins,
            out_specs=outs,
            scratch_shapes=scratch,
        ),
        out_shape=out_shapes,
        input_output_aliases=aliases or {},
        compiler_params=pltpu.CompilerParams(
            dimension_semantics=("arbitrary",) * len(grid), vmem_limit_bytes=58 * 1024 * 1024
        ),
        cost_estimate=pl.CostEstimate(
            flops=0, bytes_accessed=int(cost_us * 3.69e4), transcendentals=0
        ),
    )


def shape(dims, kind):
    return jax.ShapeDtypeStruct(dims, kind)


def pack_body(place, *refs):
    mats, (pair_index, tab, vec, spread) = refs[:6], refs[6:10]
    out, mlp0, all1, rel, spread_tab, small = refs[10:]
    rows = mats[0].shape[1]
    out[0, 0:rows, :] = mats[0][0].astype(bf16)
    for ref, at, n in ((mlp0, 0, 1), (mlp0, 1, 2), (all1, 0, 3), (all1, 1, 4), (all1, 2, 5)):
        ref[at] = mats[n][0].astype(bf16)
    rel[...] = jnp.full(rel.shape, -1, jnp.int32)
    across = pair_index[...].astype(f32).T.astype(jnp.int32)
    for h in range(QUAD):
        rel[0 : WIN * WIN, CELL * h : CELL * h + WIN * WIN] = across
    for layer in range(2):
        spread_tab[layer, 0:NREL, :] = mm(tab[layer].astype(bf16), spread[...], TN)
    pairs = rel[pl.ds(pl.multiple_of(place[0] * 8, 8), 8), :]

    def step(r, sums):
        hit = pairs == r
        return tuple(
            jnp.where(hit, spread_tab[layer, pl.ds(r, 1), :], sums[layer]) for layer in range(2)
        )

    start = jnp.zeros((8, QUAD * CELL), f32)
    first, second = lax.fori_loop(0, NREL, step, (start, start), unroll=13)
    out[0, rows : rows + 16, :] = jnp.concatenate([first, second], 0).astype(bf16)
    small[...] = jnp.zeros_like(small)
    row = jnp.minimum(place[0] * 2, 10)
    for layer in range(2):
        for k in range(2):
            small[k : k + 1, layer * 128 : (layer + 1) * 128] = vec[row + k, layer : layer + 1, :]
    out[0, rows + 16 : rows + 32, :] = small[...].astype(bf16)


def pack(place, rows, mat_w, rel_index, tab_w, vec_w):
    vec_w = vec_w.transpose(1, 0, 2)

    def block(layer, part):
        return pl.BlockSpec(
            (1, rows, BLOCK), lambda i, place: (layer, place[1], part * 8 + place[0])
        )

    dims = [(1, rows + EXTRA, BLOCK), (2, rows, BLOCK), (3, rows, BLOCK)]
    return call(
        pack_body,
        "pack",
        (1,),
        [block(layer, part) for layer in range(2) for part in range(3)]
        + [
            whole(rel_index.shape),
            whole(tab_w.shape),
            whole(vec_w.shape),
            whole((QUAD, QUAD * CELL)),
        ],
        [whole(d) for d in dims] + [whole((CELL, QUAD * CELL))],
        [shape(d, bf16) for d in dims] + [shape((CELL, QUAD * CELL), jnp.int32)],
        [pltpu.VMEM((2, 176, QUAD * CELL), f32), pltpu.VMEM((16, 256), f32)],
        4,
        prefetch=1,
    )(place, *[mat_w] * 6, rel_index, tab_w, vec_w, jnp.asarray(head_spread(QUAD), bf16))


def attention_forward_body(layer, stacks, waits, place, *refs):
    arrays, refs = refs[: stacks[0]], refs[stacks[0] :]
    extras, refs = refs[: stacks[1]], refs[stacks[1] + waits :]
    x, mask, perm, perm_back, heads = refs[:5]
    mid, qkv, merged, totals, table, vec, framed, kept, extra_kept, sems, more_sems = refs[5:]
    weight, extra = kept.at[0], extra_kept

    @pl.when(pl.program_id(0) == 0)
    def _():
        fetch(
            weight_copies(place, arrays, kept, sems)
            + extra_copies(place, extras, extra_kept, more_sems)
        )
        vec[...] = jnp.zeros_like(vec)
        for z in range(4):
            for d in range(8):
                pair = extra[d, z, 0:16, :].astype(f32)
                bias = pair[8 * layer : 8 * layer + 8]
                for w in range(table.shape[0]):
                    table[w, z, 8 * d : 8 * d + 8, :] = bias + mask[w, 8 * d : 8 * d + 8, :]
                if d < 6:
                    rows = extra[d, z, 16:32, 128 * layer : 128 * layer + 128].astype(f32)
                    vec[2 * d : 2 * d + 2, 128 * z : 128 * z + 128] = rows[0:2]

    stream = x[0]
    unit, _ = norm(stream)
    normed = (unit * vec[0:1, :] + vec[1:2, :]).astype(bf16)
    normed = mm(perm[...], normed).astype(bf16)
    for c in range(6):
        part = mm(normed, weight[:, 256 * c : 256 * c + 256])
        if c < 2:
            part = part + vec[2:3, 256 * c : 256 * c + 256]
        if c >= 4:
            part = part + vec[3:4, 256 * (c - 4) : 256 * (c - 4) + 256]
        qkv[0, :, 256 * c : 256 * c + 256] = part.astype(bf16)
    lane_head = lane_heads()

    def score(unit):
        rows, at = slice(CELL * (unit // 4), CELL * (unit // 4) + CELL), 128 * (unit % 4)
        query = quad_rows(qkv[0, rows, at : at + 128], heads[...])
        return mm(qkv[0, rows, C + at : C + at + 128], query, NT)

    ahead = score(0)
    for n in range(16):
        w, g = n // 4, n % 4
        rows, at = slice(CELL * w, CELL * w + CELL), 128 * g
        scores = ahead * scale + table[w % table.shape[0], g]
        if n < 15:
            ahead = score(n + 1)
        top = jnp.max(scores, 0, keepdims=True)
        raised = jnp.exp(scores - top)
        total = jnp.sum(raised, 0, keepdims=True)
        totals[0, n : n + 1, :] = top + jnp.log(total)
        probs = (raised * (1.0 / total)).astype(bf16)
        stacked = mm(probs, qkv[0, rows, 2 * C + at : 2 * C + at + 128], TN)
        framed[rows, at : at + 128] = pick_heads(stacked, lane_head).astype(bf16)
    gathered = mm(perm_back[...], framed[...]).astype(bf16)
    merged[0] = gathered
    mid[0] = stream + mm(gathered, weight[:, 3 * C :]) + vec[4:5, :]


def attention_forward(layer, place, x, weight, extra, mask, perm, after):
    images = x.shape[0]
    tables = mask.shape[0]
    return call(
        partial(attention_forward_body, layer, (len(weight), len(extra)), len(after)),
        f"attention_forward_{layer}",
        (images,),
        [HBM] * (len(weight) + len(extra) + len(after))
        + [
            per_image(x.shape[1], C),
            whole(mask.shape),
            whole((FRAME, ROWS)),
            whole((ROWS, FRAME)),
            whole((QUAD * CELL, 128)),
        ],
        [
            per_image(ROWS, C),
            per_image(FRAME, 3 * C),
            per_image(ROWS, C),
            per_image(16, QUAD * CELL),
            pl.BlockSpec((tables, 4, CELL, QUAD * CELL), lambda i, *_: (0, 0, 0, 0)),
            pl.BlockSpec((16, C), lambda i, *_: (0, 0)),
        ],
        [
            shape((images, ROWS, C), f32),
            shape((images, FRAME, 3 * C), bf16),
            shape((images, ROWS, C), bf16),
            shape((images, 16, QUAD * CELL), f32),
            shape((tables, 4, CELL, QUAD * CELL), f32),
            shape((16, C), f32),
        ],
        [
            pltpu.VMEM((FRAME, C), bf16),
            pltpu.VMEM((1, C, HID), bf16),
            pltpu.VMEM((8, 4, EXTRA, BLOCK), bf16),
            pltpu.SemaphoreType.DMA((8, 4, 1)),
            pltpu.SemaphoreType.DMA((8, 4, 1)),
        ],
        20,
        prefetch=1,
    )(
        place,
        *weight,
        *extra,
        *after,
        x,
        mask,
        jnp.asarray(perm, bf16),
        jnp.asarray(perm.T, bf16),
        jnp.asarray(head_rows(), bf16),
    )


def mlp_forward_body(stacks, waits, place, *refs):
    arrays, refs = refs[:stacks], refs[stacks + waits :]
    mid, vec, result, act, slope, across, kept, sems = refs
    first, second = kept.at[0], kept.at[1]

    @pl.when(pl.program_id(0) == 0)
    def _():
        fetch(weight_copies(place, arrays, kept, sems))
        across[...] = second[...].T

    rows = PAIR * ROWS
    stream = mid[...].reshape(rows, C)
    unit, _ = norm(stream)
    normed = (unit * vec[5:6, :] + vec[6:7, :]).astype(bf16)
    for c in range(8):
        cols = slice(256 * c, 256 * c + 256)
        bias = vec[8 + c // 2 : 9 + c // 2, 256 * (c % 2) : 256 * (c % 2) + 256]
        value, pull = gelu_pair(mm(normed, first[:, cols]) + bias)
        act[:, :, cols] = value.astype(bf16).reshape(PAIR, ROWS, BLOCK)
        slope[:, :, cols] = pull.astype(bf16).reshape(PAIR, ROWS, BLOCK)
    total = stream + vec[7:8, :] + mm(act[...].reshape(rows, HID), across[...])
    result[...] = total.reshape(PAIR, ROWS, C)


def mlp_forward(layer, place, mid, weight, vec, after):
    images = mid.shape[0]
    return call(
        partial(mlp_forward_body, len(weight), len(after)),
        f"mlp_forward_{layer}",
        (images // PAIR,),
        [HBM] * (len(weight) + len(after)) + [per_pair(ROWS, C), whole(vec.shape)],
        [per_pair(ROWS, C), per_pair(ROWS, HID), per_pair(ROWS, HID)],
        [
            shape((images, ROWS, C), f32),
            shape((images, ROWS, HID), bf16),
            shape((images, ROWS, HID), bf16),
        ],
        [
            pltpu.VMEM((HID, C), bf16),
            pltpu.VMEM((2, C, HID), bf16),
            pltpu.SemaphoreType.DMA((8, 4, 2)),
        ],
        22,
        prefetch=1,
    )(place, *weight, *after, mid, vec)


def mlp_both_body(stacks, waits, place, *refs):
    arrays, refs = refs[:stacks], refs[stacks + waits :]
    grad, mid, vec, result, grad_mid, pieces, small = refs[:7]
    all_grad, all_act, all_inner, all_normed, across, kept, sems = refs[7:]
    first, second = kept.at[0], kept.at[1]
    i = pl.program_id(0)

    @pl.when(i == 0)
    def _():
        fetch(weight_copies(place, arrays, kept, sems, 1))
        for p in range(2):
            across[p] = kept[p].T
        small[...] = jnp.zeros_like(small)

    rows = PAIR * ROWS
    grad_out = grad[...].reshape(rows, C)
    here = pl.ds(pl.multiple_of(i * rows, 32), rows)
    low = grad_out.astype(bf16)
    all_grad[here, :] = low
    small[7:8, :] += column_sum(grad_out)
    stream = mid[...].reshape(rows, C)
    unit, spread = norm(stream)
    normed = (unit * vec[5:6, :] + vec[6:7, :]).astype(bf16)
    all_normed[here, :] = normed
    for c in range(8):
        cols = slice(256 * c, 256 * c + 256)
        row, lane = 8 + c // 2, 256 * (c % 2)
        bias = vec[row : row + 1, lane : lane + 256]
        value, pull = gelu_pair(mm(normed, first[:, cols]) + bias)
        all_act[here, cols] = value.astype(bf16)
        inner = (mm(low, second[:, cols]) * pull).astype(bf16)
        all_inner[here, cols] = inner
        small[row : row + 1, lane : lane + 256] += column_sum(inner.astype(f32))
    back = mm(all_inner[here, :], across[0])
    small[5:6, :] += column_sum(back * unit)
    small[6:7, :] += column_sum(back)
    grad_mid[...] = (grad_out + norm_back(back * vec[5:6, :], unit, spread)).reshape(PAIR, ROWS, C)
    total = stream + vec[7:8, :] + mm(all_act[here, :], across[1])
    for n in range(PAIR):
        alive = (i * PAIR + n < place[2]).astype(f32)
        result[n] = (total[n * ROWS : n * ROWS + TOKENS] * alive).astype(bf16)

    @pl.when(i == pl.num_programs(0) - 1)
    def _():
        mlp_weight_grads(place, all_grad, all_act, all_inner, all_normed, pieces)


def mlp_weight_grads(place, all_grad, all_act, all_inner, all_normed, *outs):
    grad_across = all_grad[...].T
    normed_across = all_normed[...].T
    for m in range(8):
        block = m if len(outs) == 1 else place[0] ^ m
        cols = pl.ds(pl.multiple_of(block * BLOCK, BLOCK), BLOCK)
        for p, total in enumerate(
            (mm(normed_across, all_inner[:, cols]), mm(grad_across, all_act[:, cols]))
        ):
            total = total.astype(bf16)
            for z in range(4):
                if len(outs) == 1:
                    outs[0][m, z, p] = total[128 * z : 128 * z + 128]
                else:
                    to = (z + 4 - place[1]) & 3
                    outs[m % 2][m // 2, to, p] = total[128 * z : 128 * z + 128]


def mlp_both(place, grad, mid, weight, vec, after):
    images = mid.shape[0]
    total = images * ROWS
    pieces = (8, 4, 2, 128, BLOCK)
    return call(
        partial(mlp_both_body, len(weight), len(after)),
        "mlp_both",
        (images // PAIR,),
        [HBM] * (len(weight) + len(after)) + [per_pair(ROWS, C), per_pair(ROWS, C), whole(vec.shape)],
        [per_pair(TOKENS, C), per_pair(ROWS, C), whole(pieces), whole((16, C))],
        [
            shape((images, TOKENS, C), bf16),
            shape((images, ROWS, C), f32),
            shape(pieces, bf16),
            shape((16, C), f32),
        ],
        [
            pltpu.VMEM((total, C), bf16),
            pltpu.VMEM((total, HID), bf16),
            pltpu.VMEM((total, HID), bf16),
            pltpu.VMEM((total, C), bf16),
            pltpu.VMEM((2, HID, C), bf16),
            pltpu.VMEM((2, C, HID), bf16),
            pltpu.SemaphoreType.DMA((8, 4, 2)),
        ],
        45,
        prefetch=1,
    )(place, *weight, *after, grad, mid, vec)


def mlp_backward_body(stacks, waits, place, *refs):
    arrays, refs = refs[:stacks], refs[stacks + waits :]
    grad, act, slope, mid, vec, grad_mid, own, other, small = refs[:9]
    all_grad, all_act, all_inner, all_normed, across, kept, sems = refs[9:]
    first, second = kept.at[0], kept.at[1]
    i = pl.program_id(0)

    @pl.when(i == 0)
    def _():
        fetch(weight_copies(place, arrays, kept, sems))
        across[...] = first[...].T
        small[...] = jnp.zeros_like(small)

    rows = PAIR * ROWS
    grad_out = grad[...].reshape(rows, C)
    here = pl.ds(pl.multiple_of(i * rows, 32), rows)
    low = grad_out.astype(bf16)
    all_grad[here, :] = low
    small[7:8, :] += column_sum(low.astype(f32))
    all_act[here, :] = act[...].reshape(rows, HID)
    unit, spread = norm(mid[...].reshape(rows, C))
    all_normed[here, :] = (unit * vec[5:6, :] + vec[6:7, :]).astype(bf16)
    for c in range(8):
        cols = slice(256 * c, 256 * c + 256)
        pull = slope[:, :, cols].reshape(rows, BLOCK).astype(f32)
        inner = (mm(low, second[:, cols]) * pull).astype(bf16)
        all_inner[here, cols] = inner
        row, lane = 8 + c // 2, 256 * (c % 2)
        small[row : row + 1, lane : lane + 256] += column_sum(inner.astype(f32))
    back = mm(all_inner[here, :], across[...])
    small[5:6, :] += column_sum(back * unit)
    small[6:7, :] += column_sum(back)
    grad_mid[...] = (grad_out + norm_back(back * vec[5:6, :], unit, spread)).reshape(PAIR, ROWS, C)

    @pl.when(i == pl.num_programs(0) - 1)
    def _():
        mlp_weight_grads(place, all_grad, all_act, all_inner, all_normed, own, other)


def mlp_backward(layer, place, grad, act, slope, mid, weight, vec, after):
    images = mid.shape[0]
    total = images * ROWS
    pieces = (4, 4, 2, 128, BLOCK)
    return call(
        partial(mlp_backward_body, len(weight), len(after)),
        f"mlp_backward_{layer}",
        (images // PAIR,),
        [HBM] * (len(weight) + len(after))
        + [
            per_pair(grad.shape[1], C),
            per_pair(ROWS, HID),
            per_pair(ROWS, HID),
            per_pair(ROWS, C),
            whole(vec.shape),
        ],
        [per_pair(ROWS, C), whole(pieces), whole(pieces), whole((16, C))],
        [
            shape((images, ROWS, C), f32),
            shape(pieces, bf16),
            shape(pieces, bf16),
            shape((16, C), f32),
        ],
        [
            pltpu.VMEM((total, C), bf16),
            pltpu.VMEM((total, HID), bf16),
            pltpu.VMEM((total, HID), bf16),
            pltpu.VMEM((total, C), bf16),
            pltpu.VMEM((HID, C), bf16),
            pltpu.VMEM((2, C, HID), bf16),
            pltpu.SemaphoreType.DMA((8, 4, 2)),
        ],
        30,
        prefetch=1,
    )(place, *weight, *after, grad, act, slope, mid, vec)


def attention_backward_body(layer, stacks, waits, resumed, ends, place, *refs):
    arrays, refs = refs[:stacks], refs[stacks + waits :]
    if resumed:
        (own_before, other_before, pairs_before), refs = refs[1:4], refs[4:]
    grad, x, qkv, merged, totals, table, vec, before = refs[:8]
    perm, perm_back, heads, rel, spread, result = refs[8:14]
    outs, refs = (refs[14:15], refs[15:]) if layer else (refs[14:16], refs[16:])
    pairs, small, framed, grad_framed, all_normed, all_packed, all_merged = refs[:7]
    across, hits, beside, weight_across, kept, sems = refs[7:]
    weight = kept.at[0]
    i = pl.program_id(0)

    @pl.when(i == 0)
    def _():
        fetch(weight_copies(place, arrays, kept, sems))
        weight_across[...] = weight[...].T
        small[...] = before[...]
        pairs[...] = pairs_before[...] if resumed else jnp.zeros_like(pairs)

    stream = x[0]
    here = pl.ds(pl.multiple_of(i * ROWS, 16), ROWS)
    unit, spread_one = norm(stream)
    all_normed[here, :] = (unit * vec[0:1, :] + vec[1:2, :]).astype(bf16)
    low = grad[0].astype(bf16)
    all_packed[here, 3 * C :] = low
    all_merged[here, :] = merged[0]
    small[4:5, :] += column_sum(low.astype(f32))
    moved = mm(perm[...], low).astype(bf16)
    framed[...] = mm(moved, weight_across[3 * C :, :]).astype(bf16)
    lane_head = lane_heads()
    for w in range(4):
        rows = slice(CELL * w, CELL * w + CELL)
        at = [128 * g for g in range(4)]
        keys = [qkv[0, rows, C + c : C + c + 128] for c in at]
        query = [quad_rows(qkv[0, rows, c : c + 128], heads[...]) for c in at]
        pull = [quad_rows(framed[rows, c : c + 128], heads[...]) for c in at]
        scores = [mm(keys[g], query[g], NT) for g in range(4)]
        grad_probs = [
            mm(qkv[0, rows, 2 * C + at[g] : 2 * C + at[g] + 128], pull[g], NT) for g in range(4)
        ]
        probs, grad_scores = [], []
        for g in range(4):
            shifted = scores[g] * scale + table[w % table.shape[0], g]
            prob = jnp.exp(shifted - totals[0, 4 * w + g : 4 * w + g + 1, :])
            mean = jnp.sum(prob * grad_probs[g], 0, keepdims=True)
            grad_score = (prob * (grad_probs[g] - mean)).astype(bf16)
            pairs[g] += grad_score.astype(f32)
            probs.append(prob.astype(bf16))
            grad_scores.append(grad_score)
        for g in range(4):
            grad_value = mm(probs[g], pull[g])
            grad_framed[rows, 2 * C + at[g] : 2 * C + at[g] + 128] = grad_value.astype(bf16)
        for g in range(4):
            grad_key = mm(grad_scores[g], query[g]) * scale
            grad_framed[rows, C + at[g] : C + at[g] + 128] = grad_key.astype(bf16)
        for g in range(4):
            grad_query = pick_heads(mm(grad_scores[g], keys[g], TN), lane_head) * scale
            grad_framed[rows, at[g] : at[g] + 128] = grad_query.astype(bf16)
    for c in range(6):
        cols = slice(256 * c, 256 * c + 256)
        part = mm(perm_back[...], grad_framed[:, cols])
        all_packed[here, cols] = part.astype(bf16)
        if c < 2:
            small[2:3, cols] += column_sum(part)
        if c >= 4:
            small[3:4, 256 * (c - 4) : 256 * (c - 4) + 256] += column_sum(part)
    back = mm(all_packed[here, : 3 * C], weight_across[: 3 * C, :])
    small[0:1, :] += column_sum(back * unit)
    small[1:2, :] += column_sum(back)
    total = grad[0] + norm_back(back * vec[0:1, :], unit, spread_one)
    result[0] = total[: result.shape[1]]

    @pl.when(i == pl.num_programs(0) - 1)
    def _():
        across[0] = all_normed[...].T
        across[1] = all_merged[...].T
        beside[...] = jnp.zeros_like(beside)
        if ends:
            hits[...] = jnp.zeros_like(hits)

            def step(r, carry):
                same = rel[...] == r
                for g in range(4):
                    kept_pairs = jnp.where(same, pairs[g], 0.0)
                    hits[pl.ds(r, 1), 256 * g : 256 * g + 256] = column_sum(kept_pairs)
                return carry

            lax.fori_loop(0, NREL, step, 0)
            for z in range(4):
                beside[0, z] = lax.dot_general(
                    spread[...],
                    hits[:, 256 * z : 256 * z + 256],
                    NT,
                    precision=lax.Precision.HIGHEST,
                    preferred_element_type=f32,
                ).astype(bf16)
                beside[1, z, :, 0:128] = small[:, 128 * z : 128 * z + 128].astype(bf16)
        for m in range(8):
            b = m if layer else place[0] ^ m
            left = across[jnp.where(b < 6, 0, 1)]
            right = all_packed[:, pl.ds(pl.multiple_of(b * BLOCK, BLOCK), BLOCK)]
            block = mm(left, right)
            for z in range(4):
                if layer:
                    out = outs[0].at[m, z, 0]
                else:
                    to = (z + 4 - place[1]) & 3
                    out = outs[m % 2].at[m // 2, to, 0]
                new = block[128 * z : 128 * z + 128]
                if resumed:
                    old = other_before if m % 2 else own_before
                    new = new + old[m // 2, to, 0, 0:128, :].astype(f32)
                out[0:128, :] = new.astype(bf16)
                out[128:144, :] = beside[jnp.minimum(b, 2), z]


def attention_backward(
    layer, place, grad, x, qkv, merged, totals, table, weight, vec, small, perm, rel, after,
    first=0, count=None, resume=None,
):
    images = grad.shape[0]
    count = count or images
    pieces = (8 if layer else 4, 4, 1, 128 + SMALL, BLOCK)
    pairs = (4, CELL, QUAD * CELL)
    total = count * ROWS
    out_rows = TOKENS if layer == 0 else ROWS

    def image(rows, cols):
        return pl.BlockSpec((1, rows, cols), lambda i, *_: (i + first, 0, 0))

    resumed = list(resume or [])
    return call(
        partial(
            attention_backward_body, layer, len(weight), len(after), bool(resumed),
            first + count == images,
        ),
        f"attention_backward_{layer}_{first}",
        (count,),
        [HBM] * (len(weight) + len(after))
        + ([HBM, whole(pieces), whole(pieces), whole(pairs)] if resumed else [])
        + [
            image(ROWS, C),
            image(x.shape[1], C),
            image(FRAME, 3 * C),
            image(ROWS, C),
            image(16, QUAD * CELL),
            whole(table.shape),
            whole(vec.shape),
            whole((16, C)),
            whole((FRAME, ROWS)),
            whole((ROWS, FRAME)),
            whole((QUAD * CELL, 128)),
            whole(rel.shape),
            whole((SMALL, QUAD * CELL)),
        ],
        [image(out_rows, C)]
        + [whole(pieces)] * (1 if layer else 2)
        + [whole(pairs), whole((16, C))],
        [shape((images, out_rows, C), f32)]
        + [shape(pieces, bf16)] * (1 if layer else 2)
        + [shape(pairs, f32), shape((16, C), f32)],
        [
            pltpu.VMEM((FRAME, C), bf16),
            pltpu.VMEM((FRAME, 3 * C), bf16),
            pltpu.VMEM((total, C), bf16),
            pltpu.VMEM((total, 4 * C), bf16),
            pltpu.VMEM((total, C), bf16),
            pltpu.VMEM((2, C, total), bf16),
            pltpu.VMEM((256, 4 * QUAD * CELL), f32),
            pltpu.VMEM((3, 4, SMALL, BLOCK), bf16),
            pltpu.VMEM((HID, C), bf16),
            pltpu.VMEM((1, C, HID), bf16),
            pltpu.SemaphoreType.DMA((8, 4, 1)),
        ],
        6 * count,
        prefetch=1,
        aliases={1 + len(weight) + len(after): 0} if resumed else None,
    )(
        place,
        *weight,
        *after,
        *resumed,
        grad,
        x,
        qkv,
        merged,
        totals,
        table,
        vec,
        small,
        jnp.asarray(perm, bf16),
        jnp.asarray(perm.T, bf16),
        jnp.asarray(head_rows(), bf16),
        rel,
        jnp.asarray(head_spread(SMALL), f32),
    )


def adam_step(weight, first, second, gradient, rate, decay):
    first_new = beta_one * first + (1.0 - beta_one) * gradient
    second_new = beta_two * second + (1.0 - beta_two) * gradient * gradient
    first_hat = first_new / (1.0 - beta_one**STEP)
    second_hat = second_new / (1.0 - beta_two**STEP)
    weight_new = weight - rate * (first_hat / (jnp.sqrt(second_hat) + adam_eps) + decay * weight)
    return (weight_new, first_new, second_new)


def adam_block(grad, weight, first, second, outs, cols):
    part = grad.astype(f32)
    first_new = beta_one * first[0, :, cols] + (1.0 - beta_one) * part
    second_new = beta_two * second[0, :, cols] + (1.0 - beta_two) * part * part
    spread = second_new * (1.0 / (1.0 - beta_two**STEP))
    inverse = pltpu.reciprocal(spread * lax.rsqrt(spread) + adam_eps, approx=True)
    step = first_new * (rate_matrix / (1.0 - beta_one**STEP)) * inverse
    outs[0][0, :, cols] = weight[0, :, cols] * (1.0 - rate_matrix * weight_decay) - step
    outs[1][0, :, cols] = first_new
    outs[2][0, :, cols] = second_new


def adam_body(place, near, far, weight, first, second, *refs):
    for j in range(2):
        for k in range(2):
            block = (((place[0] // 2) & 1) ^ j) * 2 + ((place[0] & 1) ^ k)
            cols = pl.ds(pl.multiple_of(block * BLOCK, BLOCK), BLOCK)
            adam_block((far if k else near)[j], weight, first, second, refs[-3:], cols)


def adam_body_plain(place, sums, weight, first, second, *refs):
    for k in range(4):
        cols = slice(BLOCK * k, BLOCK * k + BLOCK)
        adam_block(sums[k], weight, first, second, refs[-3:], cols)


def adam(layer, part, place, sums, state, done, after):
    kept = [] if done is None else list(done)
    if len(sums) == 2:
        parts = sums[0].shape[1] // 128
        body = adam_body
        spec = pl.BlockSpec(
            (1, 128, 4 * BLOCK),
            lambda p, j, place: (layer, 0, (part + p) % 3 * 2 + ((place[0] // 4) ^ j)),
        )
        piece = pl.BlockSpec((2, 128, BLOCK), lambda p, j, place: (j, p, 0))
    else:
        parts = sums[0].shape[1] // 128
        body = adam_body_plain
        spec = pl.BlockSpec(
            (1, 128, 4 * BLOCK), lambda p, j, place: (layer, 0, (part + p) % 3 * 2 + j)
        )
        piece = pl.BlockSpec((4, 128, BLOCK), lambda p, j, place: (j, p, 0))
    return call(
        body,
        f"adam_{layer}_{part}",
        (parts, 2),
        [piece] * len(sums) + [spec] * 3 + [HBM] * (len(kept) + len(after)),
        [spec] * 3,
        [shape(state[0].shape, f32)] * 3,
        [],
        3 * parts,
        prefetch=1,
        aliases={4 + len(sums) + k: k for k in range(len(kept))},
    )(place, *sums, *state, *kept, *after)


def swap(value, bits):
    return lax.ppermute(value, "dp", [(i, i ^ bits) for i in range(8)])


def shift(value, steps):
    return lax.ppermute(value, "zero", [(i, (i + steps) % 4) for i in range(4)])


def tie(values, after):
    values = list(values)
    return list(lax.optimization_barrier((*values, *after))[: len(values)])


def stack(values, after=()):
    return jnp.stack(tie(values, after) if after else values)


def add_body(count, *refs):
    total = refs[0][...].astype(f32)
    for k in range(1, count):
        total = total + refs[k][...].astype(f32)
    refs[-1][...] = total.astype(bf16)


def add(values, after=()):
    dims = values[0].shape
    return call(
        partial(add_body, len(values)),
        "add",
        (1,),
        [whole(dims)] * len(values) + [HBM] * len(after),
        whole(dims),
        shape(dims, bf16),
        [],
        10,
    )(*values, *after)


def add_split_body(count, lead, *refs):
    for k in range(4):
        if count == 2:
            refs[len(refs) - 4 + k][...] = refs[0][k] + refs[1][k]
            continue
        total = refs[0][k].astype(f32)
        for v in range(1, count):
            total = total + refs[v][k].astype(f32)
        refs[len(refs) - 4 + k][...] = total.astype(bf16)


def add_split(values, after=()):
    dims = values[0].shape
    steps = dims[1] if len(dims) == 5 else 1
    ins = (4, dims[1] // steps, *dims[2:])
    outs = dims[1:]
    zeros = (0,) * (len(dims) - 2)
    return call(
        partial(add_split_body, len(values), True),
        "add_split",
        (steps,),
        [pl.BlockSpec(ins, lambda i: (0, i, *zeros))] * len(values) + [HBM] * len(after),
        [pl.BlockSpec((outs[0] // steps, *outs[1:]), lambda i: (i, *zeros))] * 4,
        [shape(outs, bf16)] * 4,
        [],
        10,
    )(*values, *after)


def join_body(*refs):
    out = refs[-1]
    at = 0
    for ref in refs[:2]:
        parts, rows = ref.shape[1:3]
        for p in range(parts):
            out[0, at : at + rows, :] = ref[0, p]
            at += rows


def join(first, second, after):
    rows = sum(value.shape[1] * value.shape[2] for value in (first, second))

    def spec(value):
        return pl.BlockSpec((1, *value.shape[1:]), lambda i: (i, 0, 0, 0))

    return call(
        join_body,
        "join",
        (4,),
        [spec(first), spec(second)] + [HBM] * len(after),
        pl.BlockSpec((1, rows, BLOCK), lambda i: (i, 0, 0)),
        shape((4, rows, BLOCK), bf16),
        [],
        5,
    )(first, second, *after)


def add_last_body(*refs):
    done, out = refs[0], refs[-1]
    rows = done.shape[0] * done.shape[1]
    for p in range(done.shape[0]):
        out[128 * p : 128 * p + 128, :] = done[p]
    total = refs[1][0].astype(f32)
    for ref in refs[2:5]:
        total = total + ref[0].astype(f32)
    out[rows : rows + total.shape[0], :] = total.astype(bf16)


def add_last(done, values, after):
    rows = done.shape[0] * done.shape[1] + values[0].shape[1]
    return call(
        add_last_body,
        "add_last",
        (1,),
        [whole(done.shape)] + [whole(v.shape) for v in values] + [HBM] * len(after),
        whole((rows, BLOCK)),
        shape((rows, BLOCK), bf16),
        [],
        10,
    )(done, *values, *after)


def send_z(piece):
    return [piece] + [shift(piece, s) for s in range(1, 4)]


def send_plane(piece):
    return [piece] + [swap(piece, 2 * j) for j in range(1, 4)]


def give_plane(parts):
    return [parts[0]] + [swap(parts[j], 2 * j) for j in range(1, 4)]


def give_z(parts):
    return [parts[0]] + [shift(parts[s], s) for s in range(1, 4)]


def gather_wide(piece, dp, extra):
    fine = dp // 8
    parts, rows = piece.shape[0], piece.shape[1] - extra
    out = lax.all_gather(piece, ("dp", "zero"), axis=0, tiled=False)
    out = out.reshape(8, fine, 4, *piece.shape)
    main = out[..., :rows, :].transpose(0, 2, 3, 1, 4, 5).reshape(8, 4, parts, 128, BLOCK)
    return [jnp.concatenate([main, out[:, 0, ..., rows:, :]], 3)]


def reduce_wide(blocks, dp, extra):
    fine = dp // 8
    blocks = blocks.reshape(8, 4, *blocks.shape[-3:])
    parts, rows = blocks.shape[2], 128 // fine
    main = blocks[..., :128, :].reshape(8, 4, parts, fine, rows, BLOCK).transpose(0, 3, 1, 2, 4, 5)
    beside = jnp.broadcast_to(
        blocks[:, None, ..., 128:, :], (8, fine, 4, parts, extra, BLOCK)
    )
    flat = jnp.concatenate([main, beside], 4).reshape(dp * 4, parts, rows + extra, BLOCK)
    mine = lax.psum_scatter(flat, ("dp", "zero"), scatter_dimension=0, tiled=True)
    out = lax.all_gather(mine[0], "dp", axis=0, tiled=False)
    out = out.reshape(8, fine, parts, rows + extra, BLOCK)
    main = out[..., :rows, :].transpose(0, 2, 1, 3, 4).reshape(8, parts, 128, BLOCK)
    out = jnp.concatenate([main, out[:, 0, :, rows:]], 2)
    return out.reshape(8, -1, BLOCK)


def shards(
    dp, images, cotangent, counts, rel_index, regions,
    mat_w, mat_m, mat_v, vec_w, vec_m, vec_v, tab_w, tab_m, tab_v,
):
    near = dp == 8
    fine = dp // 8
    rows = 128 // fine
    me = lax.axis_index("dp")
    taken_from = jnp.stack([me // fine, me % fine]).astype(jnp.int32)
    spot = [me, lax.axis_index("zero")] if near else [0 * me, 0 * me]
    place = jnp.stack(spot + [counts[0]]).astype(jnp.int32)

    inside = np.arange(CELL) < WIN * WIN
    zones = regions.reshape(2, WIN, 2, WIN).transpose(0, 2, 1, 3).reshape(4, WIN * WIN)
    zones = jnp.pad(zones, ((0, 0), (0, 15)))
    differ = (zones[:, :, None] != zones[:, None, :]) & inside[None, None, :]
    outside = jnp.asarray(np.where(inside, 0.0, -1e30), f32)[None, :, None]
    mask_shifted = jnp.tile(jnp.where(differ, mask_value, 0.0) + outside, (1, 1, QUAD)).astype(f32)
    mask_plain = jnp.broadcast_to(outside, (1, CELL, QUAD * CELL))
    masks = (mask_plain, mask_shifted)
    perms = (frames(False), frames(True))

    packed, cut_mlp0, cut_all1, rel = pack(
        taken_from, rows, mat_w, rel_index, tab_w, vec_w
    )
    alive = (jnp.arange(images.shape[0]) < counts[0]).astype(f32)[:, None, None]
    pad = ((0, 0), (0, ROWS - TOKENS), (0, 0))
    images = jnp.pad(images.astype(f32), pad)
    cotangent = jnp.pad(cotangent.astype(f32) * alive, pad)

    def attention(layer, stream, weight, after):
        return attention_forward(
            layer, place, stream, weight, heads0, masks[layer], perms[layer], after
        )

    half = images.shape[0] // 2
    if near:
        sent_heads0 = send_z(packed)
        *sent_heads0, images = tie([*sent_heads0, images], [])
        z_heads0 = stack(sent_heads0)
        all1 = gather_wide(tie([cut_all1], [z_heads0])[0], dp, 0)
        sent_heads0 = send_plane(z_heads0)
        sent_mlp0 = send_z(tie([cut_mlp0], [z_heads0])[0])
        cotangent, mask_shifted = tie([cotangent, mask_shifted], [z_heads0])
        *sent_heads0, cotangent, mask_shifted = tie(
            [*sent_heads0, cotangent, mask_shifted], sent_mlp0
        )
        masks = (mask_plain, mask_shifted)
        p_heads0 = stack(sent_heads0)
        heads0 = [p_heads0, swap(p_heads0, 1)]
        z_mlp0 = stack(sent_mlp0, [p_heads0])
        sent_mlp0 = send_plane(z_mlp0)
        kept0 = attention(0, images, heads0, [z_mlp0])
        p_mlp0 = stack(sent_mlp0, [kept0[0]])
        mlp0 = [p_mlp0, swap(p_mlp0, 1)]
    else:
        heads0 = gather_wide(packed, dp, EXTRA)
        mlp0 = gather_wide(cut_mlp0, dp, 0)
        all1 = gather_wide(cut_all1, dp, 0)
        kept0 = attention(0, images, heads0, [])
    stream, act, slope = mlp_forward(0, place, kept0[0], mlp0, kept0[5], [])
    kept1 = attention(1, stream, all1, [])
    kept = (kept0, kept1)
    inputs = (images, stream)
    attention_w = (heads0, all1)

    def backward_attention(layer, gradient, small, after, *span):
        mid, qkv, merged, totals, table, vec = kept[layer]
        return attention_backward(
            layer, place, gradient, inputs[layer], qkv, merged, totals, table, attention_w[layer],
            vec, small, perms[layer], rel, after, *span,
        )

    activations, grad_mid, parts_mlp1, small = mlp_both(
        place, cotangent, kept1[0], all1, kept1[5], []
    )

    def backward_mlp0(gradient, after):
        return mlp_backward(0, place, gradient, act, slope, kept0[0], mlp0, kept0[5], after)

    state = (mat_w, mat_m, mat_v)
    def exchange(parts):
        return [parts[0], swap(parts[1], 1)]

    gradient, parts_heads1, _, _ = backward_attention(1, grad_mid, small, [])
    grad_mid, *parts_mlp0, small = backward_mlp0(gradient, [])
    if near:
        t_mlp1 = lax.psum_scatter(parts_mlp1, "dp", scatter_dimension=0, tiled=True)[0]
        parts_heads1 = tie([parts_heads1], [t_mlp1, small])[0]
        t_heads1 = lax.psum_scatter(parts_heads1, "dp", scatter_dimension=0, tiled=True)[0]
        gone_mlp0 = exchange(parts_mlp0)
        gradient, *parts_heads0, pairs, small = backward_attention(0, grad_mid, small, [], 0, half)

        s_mlp0 = add_split(gone_mlp0, [gradient])
        gone_mlp0 = give_plane(s_mlp0)
        gradient, *parts_heads0, _, small = backward_attention(
            0, grad_mid, small, [s_mlp0[0]], half, half, [gradient, *parts_heads0, pairs]
        )

        t_mlp0 = add_split(gone_mlp0, [small])
        gone_heads0 = exchange(tie(parts_heads0, [t_mlp0[0]]))
        gone_mlp0 = give_z(t_mlp0)
        t_all1 = join(t_mlp1, t_heads1, [t_mlp0[0]])
        g_all1 = lax.psum_scatter(t_all1, "zero", scatter_dimension=0, tiled=True)
        s_heads0 = add_split(gone_heads0, [t_all1])
        gone_heads0 = give_plane(s_heads0)
        g_mlp0 = add(gone_mlp0, [s_heads0[0]])
        t_heads0 = add_split(gone_heads0, [g_mlp0])
        g_all1 = tie([g_all1], [t_heads0[0]])[0]
        n_all1 = lax.all_gather(g_all1[0], "dp", axis=0, tiled=False)
        gone_heads0 = give_z(t_heads0)
        g_all0 = add_last(g_mlp0, gone_heads0, [])
        n_all0 = stack(send_plane(g_all0))
        sums0 = [n_all0, swap(n_all0, 1)]
        m = place[0] ^ np.arange(2)
        both = jnp.concatenate([half[:, 384:] for half in sums0])
        beside0 = [
            lax.dynamic_index_in_dim(both, (m[b] % 2) * 4 + m[b] // 2, 0, False) for b in range(2)
        ]
    else:
        gradient, *parts_heads0, _, _ = backward_attention(0, grad_mid, small, [])
        n_mlp1 = reduce_wide(parts_mlp1, dp, 0)
        n_heads1 = reduce_wide(parts_heads1, dp, SMALL)
        n_all1 = jnp.concatenate([n_mlp1, n_heads1], 1)
        n_mlp0 = reduce_wide(jnp.stack(parts_mlp0, 1), dp, 0)
        n_heads0 = reduce_wide(jnp.stack(parts_heads0, 1), dp, SMALL)
        sums0 = [jnp.concatenate([n_mlp0, n_heads0], 1)]
        beside0 = sums0[0][:2, 384:]
    done = adam(0, 1, place, sums0, state, None, [])
    done = adam(1, 1, place, [n_all1], state, done, [])

    def beside(block):
        return jnp.stack([beside0[block], n_all1[block, 384:]]).astype(f32)

    new_vec = adam_step(vec_w, vec_m, vec_v, beside(1)[:, 0:12, 0:128], rate_vector, 0.0)
    new_tab = adam_step(tab_w, tab_m, tab_v, beside(0)[:, 0:4, 0:NREL], rate_table, 0.0)
    return (activations, gradient, *done, *new_vec, *new_tab)


def solution(mesh):
    images = P(("dp", "zero"), None, None)
    rows = P(None, "zero", None)
    lanes = P(None, None, "zero")
    return jax.shard_map(
        partial(shards, mesh.shape["dp"]),
        mesh=mesh,
        in_specs=(images, images, P(("dp", "zero")), P(), P())
        + (rows,) * 3 + (lanes,) * 3 + (rows,) * 3,
        out_specs=(images, images) + (rows,) * 3 + (lanes,) * 3 + (rows,) * 3,
        check_vma=False,
    )
```

```python
from functools import partial

import jax
import jax.numpy as jnp
import numpy as np
from jax import lax
from jax.experimental import pallas as pl
from jax.experimental.pallas import tpu as pltpu
from jax.sharding import PartitionSpec as P

WIN = 7
SIDE = 14
STEP = 10
NREL = 169
C = 512
HID = 2048
TOKENS = SIDE * SIDE
PAIR = 2
ROWS = 208
FRAME = 256
CELL = 64
QUAD = 4
BLOCK = 256
EXTRA = 32
SMALL = 16

norm_eps = 1e-05
mask_value = -100.0
beta_one = 0.9
beta_two = 0.999
adam_eps = 1e-08
weight_decay = 0.05
rate_matrix = 0.1
rate_vector = 0.5
rate_table = 1.0
scale = 32 ** (-0.5)

bf16 = jnp.bfloat16
f32 = jnp.float32
NN = (((1,), (0,)), ((), ()))
NT = (((1,), (1,)), ((), ()))
TN = (((0,), (0,)), ((), ()))


def mm(left, right, dims=NN):
    return lax.dot_general(left, right, dims, preferred_element_type=f32)


def frames(shifted):
    move = WIN // 2 if shifted else 0
    placed = np.zeros((FRAME, ROWS), np.float32)
    for wy in range(2):
        for wx in range(2):
            for iy in range(WIN):
                for ix in range(WIN):
                    y = (wy * WIN + iy + move) % SIDE
                    x = (wx * WIN + ix + move) % SIDE
                    placed[(wy * 2 + wx) * CELL + iy * WIN + ix, y * SIDE + x] = 1
    return placed


def head_rows():
    rows = np.zeros((QUAD * CELL, 128), np.float32)
    for h in range(QUAD):
        rows[h * CELL : (h + 1) * CELL, h * 32 : (h + 1) * 32] = 1
    return rows


def head_spread(rows):
    out = np.zeros((rows, QUAD * CELL), np.float32)
    for h in range(QUAD):
        out[h, h * CELL : (h + 1) * CELL] = 1
    return out


def norm(rows):
    centred = rows - jnp.mean(rows, -1, keepdims=True)
    spread = lax.rsqrt(jnp.mean(centred * centred, -1, keepdims=True) + norm_eps)
    return centred * spread, spread


def norm_back(grad_unit, unit, spread):
    return spread * (
        grad_unit
        - jnp.mean(grad_unit, -1, keepdims=True)
        - unit * jnp.mean(grad_unit * unit, -1, keepdims=True)
    )


def column_sum(rows):
    return jnp.sum(rows, 0, keepdims=True)


def gelu_pair(u):
    size = jnp.abs(u)
    below = 1.0 + (0.3275911 * 0.5**0.5) * size
    t = pltpu.reciprocal(below, approx=True)
    bell = jnp.exp2(u * u * (-0.5 * 1.4426950408889634))
    poly = t * (
        0.127414796 + t * (-0.142248368 + t * (0.710706871 + t * (-0.726576013 + t * 0.530702714)))
    )
    tail = poly * bell
    phi = jnp.where(u >= 0, 1.0 - tail, tail)
    return u * phi, phi + u * bell * 0.3989422804014327


def quad_rows(part, heads):
    return jnp.concatenate([part] * QUAD, 0) * heads


def pick_heads(stacked, lane_head):
    low = jnp.where(lane_head == 0, stacked[:CELL], stacked[CELL : 2 * CELL])
    high = jnp.where(lane_head == 2, stacked[2 * CELL : 3 * CELL], stacked[3 * CELL :])
    return jnp.where(lane_head < 2, low, high)


def lane_heads():
    return lax.broadcasted_iota(jnp.int32, (CELL, 128), 1) // 32


def whole(shape):
    zero = (0,) * len(shape)
    return pl.BlockSpec(shape, lambda *_: zero, pipeline_mode=pl.Buffered(1))


def per_image(rows, cols):
    return pl.BlockSpec((1, rows, cols), lambda i, *_: (i, 0, 0))


def per_pair(rows, cols):
    return pl.BlockSpec((PAIR, rows, cols), lambda i, *_: (i, 0, 0))


HBM = pl.BlockSpec(memory_space=pl.ANY)


def weight_copies(place, stacks, kept, sems, part=0):
    copies = []
    for m in range(8):
        for s in range(4):
            for p in range(kept.shape[0]):
                if len(stacks) == 1:
                    source, block, owner = stacks[0].at[m, s, part + p], m, s
                else:
                    source = stacks[m % 2].at[m // 2, s, p]
                    block, owner = place[0] ^ m, (place[1] + 4 - s) & 3
                rows = pl.ds(pl.multiple_of(owner * 128, 128), 128)
                cols = pl.ds(pl.multiple_of(block * BLOCK, BLOCK), BLOCK)
                copies.append(
                    pltpu.make_async_copy(
                        source.at[pl.ds(0, 128), :], kept.at[p, rows, cols], sems.at[m, s, p]
                    )
                )
    return copies


def extra_copies(place, stacks, kept, sems):
    copies = []
    for m in range(8):
        for s in range(4):
            if len(stacks) == 1:
                source, block, owner = stacks[0].at[m, s, 0], m, s
            else:
                source = stacks[m % 2].at[m // 2, s, 0]
                block, owner = place[0] ^ m, (place[1] + 4 - s) & 3
            copies.append(
                pltpu.make_async_copy(
                    source.at[pl.ds(128, EXTRA), :], kept.at[block, owner], sems.at[m, s, 0]
                )
            )
    return copies


def fetch(copies):
    for copy in copies:
        copy.start()
    for copy in copies:
        copy.wait()


def call(body, name, grid, ins, outs, out_shapes, scratch, cost_us, prefetch=0, aliases=None):
    return pl.pallas_call(
        body,
        name=name,
        grid_spec=pltpu.PrefetchScalarGridSpec(
            num_scalar_prefetch=prefetch,
            grid=grid,
            in_specs=ins,
            out_specs=outs,
            scratch_shapes=scratch,
        ),
        out_shape=out_shapes,
        input_output_aliases=aliases or {},
        compiler_params=pltpu.CompilerParams(
            dimension_semantics=("arbitrary",) * len(grid), vmem_limit_bytes=58 * 1024 * 1024
        ),
        cost_estimate=pl.CostEstimate(
            flops=0, bytes_accessed=int(cost_us * 3.69e4), transcendentals=0
        ),
    )


def shape(dims, kind):
    return jax.ShapeDtypeStruct(dims, kind)


def pack_body(place, *refs):
    mats, (pair_index, tab, vec, spread) = refs[:6], refs[6:10]
    out, mlp0, all1, rel, spread_tab, small = refs[10:]
    rows = mats[0].shape[1]
    out[0, 0:rows, :] = mats[0][0].astype(bf16)
    for ref, at, n in ((mlp0, 0, 1), (mlp0, 1, 2), (all1, 0, 3), (all1, 1, 4), (all1, 2, 5)):
        ref[at] = mats[n][0].astype(bf16)
    rel[...] = jnp.full(rel.shape, -1, jnp.int32)
    across = pair_index[...].astype(f32).T.astype(jnp.int32)
    for h in range(QUAD):
        rel[0 : WIN * WIN, CELL * h : CELL * h + WIN * WIN] = across
    for layer in range(2):
        spread_tab[layer, 0:NREL, :] = mm(tab[layer].astype(bf16), spread[...], TN)
    pairs = rel[pl.ds(pl.multiple_of(place[0] * 8, 8), 8), :]

    def step(r, sums):
        hit = pairs == r
        return tuple(
            jnp.where(hit, spread_tab[layer, pl.ds(r, 1), :], sums[layer]) for layer in range(2)
        )

    start = jnp.zeros((8, QUAD * CELL), f32)
    first, second = lax.fori_loop(0, NREL, step, (start, start), unroll=13)
    out[0, rows : rows + 16, :] = jnp.concatenate([first, second], 0).astype(bf16)
    small[...] = jnp.zeros_like(small)
    row = jnp.minimum(place[0] * 2, 10)
    for layer in range(2):
        for k in range(2):
            small[k : k + 1, layer * 128 : (layer + 1) * 128] = vec[row + k, layer : layer + 1, :]
    out[0, rows + 16 : rows + 32, :] = small[...].astype(bf16)


def pack(place, rows, mat_w, rel_index, tab_w, vec_w):
    vec_w = vec_w.transpose(1, 0, 2)

    def block(layer, part):
        return pl.BlockSpec(
            (1, rows, BLOCK), lambda i, place: (layer, place[1], part * 8 + place[0])
        )

    dims = [(1, rows + EXTRA, BLOCK), (2, rows, BLOCK), (3, rows, BLOCK)]
    return call(
        pack_body,
        "pack",
        (1,),
        [block(layer, part) for layer in range(2) for part in range(3)]
        + [
            whole(rel_index.shape),
            whole(tab_w.shape),
            whole(vec_w.shape),
            whole((QUAD, QUAD * CELL)),
        ],
        [whole(d) for d in dims] + [whole((CELL, QUAD * CELL))],
        [shape(d, bf16) for d in dims] + [shape((CELL, QUAD * CELL), jnp.int32)],
        [pltpu.VMEM((2, 176, QUAD * CELL), f32), pltpu.VMEM((16, 256), f32)],
        4,
        prefetch=1,
    )(place, *[mat_w] * 6, rel_index, tab_w, vec_w, jnp.asarray(head_spread(QUAD), bf16))


def attention_forward_body(layer, stacks, waits, place, *refs):
    arrays, refs = refs[: stacks[0]], refs[stacks[0] :]
    extras, refs = refs[: stacks[1]], refs[stacks[1] + waits :]
    x, mask, perm, perm_back, heads = refs[:5]
    mid, qkv, merged, totals, table, vec, framed, kept, extra_kept, sems, more_sems = refs[5:]
    weight, extra = kept.at[0], extra_kept

    @pl.when(pl.program_id(0) == 0)
    def _():
        fetch(
            weight_copies(place, arrays, kept, sems)
            + extra_copies(place, extras, extra_kept, more_sems)
        )
        vec[...] = jnp.zeros_like(vec)
        for z in range(4):
            for d in range(8):
                pair = extra[d, z, 0:16, :].astype(f32)
                bias = pair[8 * layer : 8 * layer + 8]
                for w in range(table.shape[0]):
                    table[w, z, 8 * d : 8 * d + 8, :] = bias + mask[w, 8 * d : 8 * d + 8, :]
                if d < 6:
                    rows = extra[d, z, 16:32, 128 * layer : 128 * layer + 128].astype(f32)
                    vec[2 * d : 2 * d + 2, 128 * z : 128 * z + 128] = rows[0:2]

    stream = x[0]
    unit, _ = norm(stream)
    normed = (unit * vec[0:1, :] + vec[1:2, :]).astype(bf16)
    normed = mm(perm[...], normed).astype(bf16)
    for c in range(6):
        part = mm(normed, weight[:, 256 * c : 256 * c + 256])
        if c < 2:
            part = part + vec[2:3, 256 * c : 256 * c + 256]
        if c >= 4:
            part = part + vec[3:4, 256 * (c - 4) : 256 * (c - 4) + 256]
        qkv[0, :, 256 * c : 256 * c + 256] = part.astype(bf16)
    lane_head = lane_heads()

    def score(unit):
        rows, at = slice(CELL * (unit // 4), CELL * (unit // 4) + CELL), 128 * (unit % 4)
        query = quad_rows(qkv[0, rows, at : at + 128], heads[...])
        return mm(qkv[0, rows, C + at : C + at + 128], query, NT)

    ahead = score(0)
    for n in range(16):
        w, g = n // 4, n % 4
        rows, at = slice(CELL * w, CELL * w + CELL), 128 * g
        scores = ahead * scale + table[w % table.shape[0], g]
        if n < 15:
            ahead = score(n + 1)
        top = jnp.max(scores, 0, keepdims=True)
        raised = jnp.exp(scores - top)
        total = jnp.sum(raised, 0, keepdims=True)
        totals[0, n : n + 1, :] = top + jnp.log(total)
        probs = (raised * (1.0 / total)).astype(bf16)
        stacked = mm(probs, qkv[0, rows, 2 * C + at : 2 * C + at + 128], TN)
        framed[rows, at : at + 128] = pick_heads(stacked, lane_head).astype(bf16)
    gathered = mm(perm_back[...], framed[...]).astype(bf16)
    merged[0] = gathered
    mid[0] = stream + mm(gathered, weight[:, 3 * C :]) + vec[4:5, :]


def attention_forward(layer, place, x, weight, extra, mask, perm, after):
    images = x.shape[0]
    tables = mask.shape[0]
    return call(
        partial(attention_forward_body, layer, (len(weight), len(extra)), len(after)),
        f"attention_forward_{layer}",
        (images,),
        [HBM] * (len(weight) + len(extra) + len(after))
        + [
            per_image(x.shape[1], C),
            whole(mask.shape),
            whole((FRAME, ROWS)),
            whole((ROWS, FRAME)),
            whole((QUAD * CELL, 128)),
        ],
        [
            per_image(ROWS, C),
            per_image(FRAME, 3 * C),
            per_image(ROWS, C),
            per_image(16, QUAD * CELL),
            pl.BlockSpec((tables, 4, CELL, QUAD * CELL), lambda i, *_: (0, 0, 0, 0)),
            pl.BlockSpec((16, C), lambda i, *_: (0, 0)),
        ],
        [
            shape((images, ROWS, C), f32),
            shape((images, FRAME, 3 * C), bf16),
            shape((images, ROWS, C), bf16),
            shape((images, 16, QUAD * CELL), f32),
            shape((tables, 4, CELL, QUAD * CELL), f32),
            shape((16, C), f32),
        ],
        [
            pltpu.VMEM((FRAME, C), bf16),
            pltpu.VMEM((1, C, HID), bf16),
            pltpu.VMEM((8, 4, EXTRA, BLOCK), bf16),
            pltpu.SemaphoreType.DMA((8, 4, 1)),
            pltpu.SemaphoreType.DMA((8, 4, 1)),
        ],
        20,
        prefetch=1,
    )(
        place,
        *weight,
        *extra,
        *after,
        x,
        mask,
        jnp.asarray(perm, bf16),
        jnp.asarray(perm.T, bf16),
        jnp.asarray(head_rows(), bf16),
    )


def mlp_forward_body(stacks, waits, place, *refs):
    arrays, refs = refs[:stacks], refs[stacks + waits :]
    mid, vec, result, act, slope, kept, sems = refs
    first, second = kept.at[0], kept.at[1]

    @pl.when(pl.program_id(0) == 0)
    def _():
        fetch(weight_copies(place, arrays, kept, sems))

    rows = PAIR * ROWS
    stream = mid[...].reshape(rows, C)
    unit, _ = norm(stream)
    normed = (unit * vec[5:6, :] + vec[6:7, :]).astype(bf16)
    ahead = mm(normed, first[:, 0:BLOCK])
    for c in range(8):
        cols = slice(256 * c, 256 * c + 256)
        bias = vec[8 + c // 2 : 9 + c // 2, 256 * (c % 2) : 256 * (c % 2) + 256]
        inner = ahead + bias
        if c < 7:
            ahead = mm(normed, first[:, 256 * c + 256 : 256 * c + 512])
        value, pull = gelu_pair(inner)
        act[:, :, cols] = value.astype(bf16).reshape(PAIR, ROWS, BLOCK)
        slope[:, :, cols] = pull.astype(bf16).reshape(PAIR, ROWS, BLOCK)
    total = stream + vec[7:8, :] + mm(act[...].reshape(rows, HID), second[...], NT)
    result[...] = total.reshape(PAIR, ROWS, C)


def mlp_forward(layer, place, mid, weight, vec, after):
    images = mid.shape[0]
    return call(
        partial(mlp_forward_body, len(weight), len(after)),
        f"mlp_forward_{layer}",
        (images // PAIR,),
        [HBM] * (len(weight) + len(after)) + [per_pair(ROWS, C), whole(vec.shape)],
        [per_pair(ROWS, C), per_pair(ROWS, HID), per_pair(ROWS, HID)],
        [
            shape((images, ROWS, C), f32),
            shape((images, ROWS, HID), bf16),
            shape((images, ROWS, HID), bf16),
        ],
        [
            pltpu.VMEM((2, C, HID), bf16),
            pltpu.SemaphoreType.DMA((8, 4, 2)),
        ],
        22,
        prefetch=1,
    )(place, *weight, *after, mid, vec)


def mlp_both_body(stacks, waits, place, *refs):
    arrays, refs = refs[:stacks], refs[stacks + waits :]
    grad, mid, vec, result, grad_mid, pieces, small = refs[:7]
    all_grad, all_act, all_inner, all_normed, kept, sems = refs[7:]
    first, second = kept.at[0], kept.at[1]
    i = pl.program_id(0)

    @pl.when(i == 0)
    def _():
        fetch(weight_copies(place, arrays, kept, sems, 1))
        small[...] = jnp.zeros_like(small)

    rows = PAIR * ROWS
    grad_out = grad[...].reshape(rows, C)
    here = pl.ds(pl.multiple_of(i * rows, 32), rows)
    low = grad_out.astype(bf16)
    all_grad[here, :] = low
    small[7:8, :] += column_sum(grad_out)
    stream = mid[...].reshape(rows, C)
    unit, spread = norm(stream)
    normed = (unit * vec[5:6, :] + vec[6:7, :]).astype(bf16)
    all_normed[here, :] = normed
    ahead = mm(normed, first[:, 0:BLOCK]), mm(low, second[:, 0:BLOCK])
    for c in range(8):
        cols = slice(256 * c, 256 * c + 256)
        row, lane = 8 + c // 2, 256 * (c % 2)
        bias = vec[row : row + 1, lane : lane + 256]
        inner, grad_act = ahead
        if c < 7:
            later = slice(256 * c + 256, 256 * c + 512)
            ahead = mm(normed, first[:, later]), mm(low, second[:, later])
        value, pull = gelu_pair(inner + bias)
        all_act[here, cols] = value.astype(bf16)
        inner = (grad_act * pull).astype(bf16)
        all_inner[here, cols] = inner
        small[row : row + 1, lane : lane + 256] += column_sum(inner.astype(f32))
    back = mm(all_inner[here, :], first[...], NT)
    small[5:6, :] += column_sum(back * unit)
    small[6:7, :] += column_sum(back)
    grad_mid[...] = (grad_out + norm_back(back * vec[5:6, :], unit, spread)).reshape(PAIR, ROWS, C)
    total = stream + vec[7:8, :] + mm(all_act[here, :], second[...], NT)
    for n in range(PAIR):
        alive = (i * PAIR + n < place[2]).astype(f32)
        result[n] = (total[n * ROWS : n * ROWS + TOKENS] * alive).astype(bf16)

    @pl.when(i == pl.num_programs(0) - 1)
    def _():
        mlp_weight_grads(place, all_grad, all_act, all_inner, all_normed, pieces)


def mlp_weight_grads(place, all_grad, all_act, all_inner, all_normed, *outs):
    grad_across = all_grad[...].T
    normed_across = all_normed[...].T
    for m in range(8):
        block = m if len(outs) == 1 else place[0] ^ m
        cols = pl.ds(pl.multiple_of(block * BLOCK, BLOCK), BLOCK)
        for p, total in enumerate(
            (mm(normed_across, all_inner[:, cols]), mm(grad_across, all_act[:, cols]))
        ):
            total = total.astype(bf16)
            for z in range(4):
                if len(outs) == 1:
                    outs[0][m, z, p] = total[128 * z : 128 * z + 128]
                else:
                    outs[m % 2][m // 2, z, p] = total[128 * z : 128 * z + 128]


def mlp_both(place, grad, mid, weight, vec, after):
    images = mid.shape[0]
    total = images * ROWS
    pieces = (8, 4, 2, 128, BLOCK)
    return call(
        partial(mlp_both_body, len(weight), len(after)),
        "mlp_both",
        (images // PAIR,),
        [HBM] * (len(weight) + len(after)) + [per_pair(ROWS, C), per_pair(ROWS, C), whole(vec.shape)],
        [per_pair(TOKENS, C), per_pair(ROWS, C), whole(pieces), whole((16, C))],
        [
            shape((images, TOKENS, C), bf16),
            shape((images, ROWS, C), f32),
            shape(pieces, bf16),
            shape((16, C), f32),
        ],
        [
            pltpu.VMEM((total, C), bf16),
            pltpu.VMEM((total, HID), bf16),
            pltpu.VMEM((total, HID), bf16),
            pltpu.VMEM((total, C), bf16),
            pltpu.VMEM((2, C, HID), bf16),
            pltpu.SemaphoreType.DMA((8, 4, 2)),
        ],
        45,
        prefetch=1,
    )(place, *weight, *after, grad, mid, vec)


def mlp_backward_body(stacks, waits, place, *refs):
    arrays, refs = refs[:stacks], refs[stacks + waits :]
    grad, act, slope, mid, vec, grad_mid, own, other, small = refs[:9]
    all_grad, all_act, all_inner, all_normed, kept, sems = refs[9:]
    first, second = kept.at[0], kept.at[1]
    i = pl.program_id(0)

    @pl.when(i == 0)
    def _():
        fetch(weight_copies(place, arrays, kept, sems))
        small[...] = jnp.zeros_like(small)

    rows = PAIR * ROWS
    grad_out = grad[...].reshape(rows, C)
    here = pl.ds(pl.multiple_of(i * rows, 32), rows)
    low = grad_out.astype(bf16)
    all_grad[here, :] = low
    small[7:8, :] += column_sum(low.astype(f32))
    all_act[here, :] = act[...].reshape(rows, HID)
    unit, spread = norm(mid[...].reshape(rows, C))
    all_normed[here, :] = (unit * vec[5:6, :] + vec[6:7, :]).astype(bf16)
    ahead = mm(low, second[:, 0:BLOCK])
    for c in range(8):
        cols = slice(256 * c, 256 * c + 256)
        pull = slope[:, :, cols].reshape(rows, BLOCK).astype(f32)
        grad_act = ahead
        if c < 7:
            ahead = mm(low, second[:, 256 * c + 256 : 256 * c + 512])
        inner = (grad_act * pull).astype(bf16)
        all_inner[here, cols] = inner
        row, lane = 8 + c // 2, 256 * (c % 2)
        small[row : row + 1, lane : lane + 256] += column_sum(inner.astype(f32))
    back = mm(all_inner[here, :], first[...], NT)
    small[5:6, :] += column_sum(back * unit)
    small[6:7, :] += column_sum(back)
    grad_mid[...] = (grad_out + norm_back(back * vec[5:6, :], unit, spread)).reshape(PAIR, ROWS, C)

    @pl.when(i == pl.num_programs(0) - 1)
    def _():
        mlp_weight_grads(place, all_grad, all_act, all_inner, all_normed, own, other)


def mlp_backward(layer, place, grad, act, slope, mid, weight, vec, after):
    images = mid.shape[0]
    total = images * ROWS
    pieces = (4, 4, 2, 128, BLOCK)
    return call(
        partial(mlp_backward_body, len(weight), len(after)),
        f"mlp_backward_{layer}",
        (images // PAIR,),
        [HBM] * (len(weight) + len(after))
        + [
            per_pair(grad.shape[1], C),
            per_pair(ROWS, HID),
            per_pair(ROWS, HID),
            per_pair(ROWS, C),
            whole(vec.shape),
        ],
        [per_pair(ROWS, C), whole(pieces), whole(pieces), whole((16, C))],
        [
            shape((images, ROWS, C), f32),
            shape(pieces, bf16),
            shape(pieces, bf16),
            shape((16, C), f32),
        ],
        [
            pltpu.VMEM((total, C), bf16),
            pltpu.VMEM((total, HID), bf16),
            pltpu.VMEM((total, HID), bf16),
            pltpu.VMEM((total, C), bf16),
            pltpu.VMEM((2, C, HID), bf16),
            pltpu.SemaphoreType.DMA((8, 4, 2)),
        ],
        30,
        prefetch=1,
    )(place, *weight, *after, grad, act, slope, mid, vec)


def attention_backward_body(layer, stacks, waits, resumed, ends, place, *refs):
    arrays, refs = refs[:stacks], refs[stacks + waits :]
    if resumed:
        (own_before, other_before, pairs_before), refs = refs[1:4], refs[4:]
    grad, x, qkv, merged, totals, table, vec, before = refs[:8]
    perm, perm_back, heads, rel, spread, result = refs[8:14]
    outs, refs = (refs[14:15], refs[15:]) if layer else (refs[14:16], refs[16:])
    pairs, small, framed, grad_framed, all_normed, all_packed, all_merged = refs[:7]
    across, hits, beside, kept, sems = refs[7:]
    weight = kept.at[0]
    i = pl.program_id(0)

    @pl.when(i == 0)
    def _():
        fetch(weight_copies(place, arrays, kept, sems))
        small[...] = before[...]
        pairs[...] = pairs_before[...] if resumed else jnp.zeros_like(pairs)

    stream = x[0]
    here = pl.ds(pl.multiple_of(i * ROWS, 16), ROWS)
    unit, spread_one = norm(stream)
    all_normed[here, :] = (unit * vec[0:1, :] + vec[1:2, :]).astype(bf16)
    low = grad[0].astype(bf16)
    all_packed[here, 3 * C :] = low
    all_merged[here, :] = merged[0]
    small[4:5, :] += column_sum(low.astype(f32))
    moved = mm(perm[...], low).astype(bf16)
    framed[...] = mm(moved, weight[:, 3 * C :], NT).astype(bf16)
    lane_head = lane_heads()
    at = [128 * g for g in range(4)]

    def window(w):
        rows = slice(CELL * w, CELL * w + CELL)
        keys = [qkv[0, rows, C + c : C + c + 128] for c in at]
        query = [quad_rows(qkv[0, rows, c : c + 128], heads[...]) for c in at]
        pull = [quad_rows(framed[rows, c : c + 128], heads[...]) for c in at]
        scores = [mm(keys[g], query[g], NT) for g in range(4)]
        grad_probs = [
            mm(qkv[0, rows, 2 * C + at[g] : 2 * C + at[g] + 128], pull[g], NT) for g in range(4)
        ]
        return keys, query, pull, scores, grad_probs

    ahead = window(0)
    for w in range(4):
        rows = slice(CELL * w, CELL * w + CELL)
        keys, query, pull, scores, grad_probs = ahead
        if w < 3:
            ahead = window(w + 1)
        probs, grad_scores = [], []
        for g in range(4):
            shifted = scores[g] * scale + table[w % table.shape[0], g]
            prob = jnp.exp(shifted - totals[0, 4 * w + g : 4 * w + g + 1, :])
            mean = jnp.sum(prob * grad_probs[g], 0, keepdims=True)
            grad_score = (prob * (grad_probs[g] - mean)).astype(bf16)
            pairs[g] += grad_score.astype(f32)
            probs.append(prob.astype(bf16))
            grad_scores.append(grad_score)
        for g in range(4):
            grad_value = mm(probs[g], pull[g])
            grad_framed[rows, 2 * C + at[g] : 2 * C + at[g] + 128] = grad_value.astype(bf16)
        for g in range(4):
            grad_key = mm(grad_scores[g], query[g]) * scale
            grad_framed[rows, C + at[g] : C + at[g] + 128] = grad_key.astype(bf16)
        for g in range(4):
            grad_query = pick_heads(mm(grad_scores[g], keys[g], TN), lane_head) * scale
            grad_framed[rows, at[g] : at[g] + 128] = grad_query.astype(bf16)
    for c in range(6):
        cols = slice(256 * c, 256 * c + 256)
        part = mm(perm_back[...], grad_framed[:, cols])
        all_packed[here, cols] = part.astype(bf16)
        if c < 2:
            small[2:3, cols] += column_sum(part)
        if c >= 4:
            small[3:4, 256 * (c - 4) : 256 * (c - 4) + 256] += column_sum(part)
    back = mm(all_packed[here, : 3 * C], weight[:, : 3 * C], NT)
    small[0:1, :] += column_sum(back * unit)
    small[1:2, :] += column_sum(back)
    total = grad[0] + norm_back(back * vec[0:1, :], unit, spread_one)
    result[0] = total[: result.shape[1]]

    @pl.when(i == pl.num_programs(0) - 1)
    def _():
        across[0] = all_normed[...].T
        across[1] = all_merged[...].T
        beside[...] = jnp.zeros_like(beside)
        if ends:
            hits[...] = jnp.zeros_like(hits)

            def step(r, carry):
                same = rel[...] == r
                for g in range(4):
                    kept_pairs = jnp.where(same, pairs[g], 0.0)
                    hits[pl.ds(r, 1), 256 * g : 256 * g + 256] = column_sum(kept_pairs)
                return carry

            lax.fori_loop(0, NREL, step, 0)
            for z in range(4):
                beside[0, z] = lax.dot_general(
                    spread[...],
                    hits[:, 256 * z : 256 * z + 256],
                    NT,
                    precision=lax.Precision.HIGHEST,
                    preferred_element_type=f32,
                ).astype(bf16)
                beside[1, z, :, 0:128] = small[:, 128 * z : 128 * z + 128].astype(bf16)
        for m in range(8):
            b = m if layer else place[0] ^ m
            left = across[jnp.where(b < 6, 0, 1)]
            right = all_packed[:, pl.ds(pl.multiple_of(b * BLOCK, BLOCK), BLOCK)]
            block = mm(left, right)
            for z in range(4):
                if layer:
                    out = outs[0].at[m, z, 0]
                else:
                    to = (z + 4 - place[1]) & 3
                    out = outs[m % 2].at[m // 2, to, 0]
                new = block[128 * z : 128 * z + 128]
                if resumed:
                    old = other_before if m % 2 else own_before
                    new = new + old[m // 2, to, 0, 0:128, :].astype(f32)
                out[0:128, :] = new.astype(bf16)
                out[128:144, :] = beside[jnp.minimum(b, 2), z]


def attention_backward(
    layer, place, grad, x, qkv, merged, totals, table, weight, vec, small, perm, rel, after,
    first=0, count=None, resume=None,
):
    images = grad.shape[0]
    count = count or images
    pieces = (8 if layer else 4, 4, 1, 128 + SMALL, BLOCK)
    pairs = (4, CELL, QUAD * CELL)
    total = count * ROWS
    out_rows = TOKENS if layer == 0 else ROWS

    def image(rows, cols):
        return pl.BlockSpec((1, rows, cols), lambda i, *_: (i + first, 0, 0))

    resumed = list(resume or [])
    return call(
        partial(
            attention_backward_body, layer, len(weight), len(after), bool(resumed),
            first + count == images,
        ),
        f"attention_backward_{layer}_{first}",
        (count,),
        [HBM] * (len(weight) + len(after))
        + ([HBM, whole(pieces), whole(pieces), whole(pairs)] if resumed else [])
        + [
            image(ROWS, C),
            image(x.shape[1], C),
            image(FRAME, 3 * C),
            image(ROWS, C),
            image(16, QUAD * CELL),
            whole(table.shape),
            whole(vec.shape),
            whole((16, C)),
            whole((FRAME, ROWS)),
            whole((ROWS, FRAME)),
            whole((QUAD * CELL, 128)),
            whole(rel.shape),
            whole((SMALL, QUAD * CELL)),
        ],
        [image(out_rows, C)]
        + [whole(pieces)] * (1 if layer else 2)
        + [whole(pairs), whole((16, C))],
        [shape((images, out_rows, C), f32)]
        + [shape(pieces, bf16)] * (1 if layer else 2)
        + [shape(pairs, f32), shape((16, C), f32)],
        [
            pltpu.VMEM((FRAME, C), bf16),
            pltpu.VMEM((FRAME, 3 * C), bf16),
            pltpu.VMEM((total, C), bf16),
            pltpu.VMEM((total, 4 * C), bf16),
            pltpu.VMEM((total, C), bf16),
            pltpu.VMEM((2, C, total), bf16),
            pltpu.VMEM((256, 4 * QUAD * CELL), f32),
            pltpu.VMEM((3, 4, SMALL, BLOCK), bf16),
            pltpu.VMEM((1, C, HID), bf16),
            pltpu.SemaphoreType.DMA((8, 4, 1)),
        ],
        6 * count,
        prefetch=1,
        aliases={1 + len(weight) + len(after): 0} if resumed else None,
    )(
        place,
        *weight,
        *after,
        *resumed,
        grad,
        x,
        qkv,
        merged,
        totals,
        table,
        vec,
        small,
        jnp.asarray(perm, bf16),
        jnp.asarray(perm.T, bf16),
        jnp.asarray(head_rows(), bf16),
        rel,
        jnp.asarray(head_spread(SMALL), f32),
    )


def adam_step(weight, first, second, gradient, rate, decay):
    first_new = beta_one * first + (1.0 - beta_one) * gradient
    second_new = beta_two * second + (1.0 - beta_two) * gradient * gradient
    first_hat = first_new / (1.0 - beta_one**STEP)
    second_hat = second_new / (1.0 - beta_two**STEP)
    weight_new = weight - rate * (first_hat / (jnp.sqrt(second_hat) + adam_eps) + decay * weight)
    return (weight_new, first_new, second_new)


def adam_block(grad, weight, first, second, outs, cols):
    part = grad.astype(f32)
    first_new = beta_one * first[0, :, cols] + (1.0 - beta_one) * part
    second_new = beta_two * second[0, :, cols] + (1.0 - beta_two) * part * part
    spread = second_new * (1.0 / (1.0 - beta_two**STEP))
    inverse = pltpu.reciprocal(spread * lax.rsqrt(spread) + adam_eps, approx=True)
    step = first_new * (rate_matrix / (1.0 - beta_one**STEP)) * inverse
    outs[0][0, :, cols] = weight[0, :, cols] * (1.0 - rate_matrix * weight_decay) - step
    outs[1][0, :, cols] = first_new
    outs[2][0, :, cols] = second_new


def adam_body(place, near, far, weight, first, second, *refs):
    for j in range(2):
        for k in range(2):
            block = (((place[0] // 2) & 1) ^ j) * 2 + ((place[0] & 1) ^ k)
            cols = pl.ds(pl.multiple_of(block * BLOCK, BLOCK), BLOCK)
            adam_block((far if k else near)[j], weight, first, second, refs[-3:], cols)


def adam_body_plain(place, sums, weight, first, second, *refs):
    for k in range(4):
        cols = slice(BLOCK * k, BLOCK * k + BLOCK)
        adam_block(sums[k], weight, first, second, refs[-3:], cols)


def adam(layer, part, place, sums, state, done, after):
    kept = [] if done is None else list(done)
    if len(sums) == 2:
        parts = sums[0].shape[1] // 128
        body = adam_body
        spec = pl.BlockSpec(
            (1, 128, 4 * BLOCK),
            lambda p, j, place: (layer, 0, (part + p) % 3 * 2 + ((place[0] // 4) ^ j)),
        )
        piece = pl.BlockSpec((2, 128, BLOCK), lambda p, j, place: (j, p, 0))
    else:
        parts = sums[0].shape[1] // 128
        body = adam_body_plain
        spec = pl.BlockSpec(
            (1, 128, 4 * BLOCK), lambda p, j, place: (layer, 0, (part + p) % 3 * 2 + j)
        )
        piece = pl.BlockSpec((4, 128, BLOCK), lambda p, j, place: (j, p, 0))
    return call(
        body,
        f"adam_{layer}_{part}",
        (parts, 2),
        [piece] * len(sums) + [spec] * 3 + [HBM] * (len(kept) + len(after)),
        [spec] * 3,
        [shape(state[0].shape, f32)] * 3,
        [],
        3 * parts,
        prefetch=1,
        aliases={4 + len(sums) + k: k for k in range(len(kept))},
    )(place, *sums, *state, *kept, *after)


def swap(value, bits):
    return lax.ppermute(value, "dp", [(i, i ^ bits) for i in range(8)])


def shift(value, steps):
    return lax.ppermute(value, "zero", [(i, (i + steps) % 4) for i in range(4)])


def tie(values, after):
    values = list(values)
    return list(lax.optimization_barrier((*values, *after))[: len(values)])


def stack(values, after=()):
    return jnp.stack(tie(values, after) if after else values)


def add_body(count, *refs):
    total = refs[0][...].astype(f32)
    for k in range(1, count):
        total = total + refs[k][...].astype(f32)
    refs[-1][...] = total.astype(bf16)


def add(values, after=()):
    dims = values[0].shape
    return call(
        partial(add_body, len(values)),
        "add",
        (1,),
        [whole(dims)] * len(values) + [HBM] * len(after),
        whole(dims),
        shape(dims, bf16),
        [],
        10,
    )(*values, *after)


def add_split_body(count, lead, *refs):
    for k in range(4):
        if count == 2:
            refs[len(refs) - 4 + k][...] = refs[0][k] + refs[1][k]
            continue
        total = refs[0][k].astype(f32)
        for v in range(1, count):
            total = total + refs[v][k].astype(f32)
        refs[len(refs) - 4 + k][...] = total.astype(bf16)


def add_split(values, after=()):
    dims = values[0].shape
    steps = dims[1] if len(dims) == 5 else 1
    ins = (4, dims[1] // steps, *dims[2:])
    outs = dims[1:]
    zeros = (0,) * (len(dims) - 2)
    return call(
        partial(add_split_body, len(values), True),
        "add_split",
        (steps,),
        [pl.BlockSpec(ins, lambda i: (0, i, *zeros))] * len(values) + [HBM] * len(after),
        [pl.BlockSpec((outs[0] // steps, *outs[1:]), lambda i: (i, *zeros))] * 4,
        [shape(outs, bf16)] * 4,
        [],
        10,
    )(*values, *after)


def join_body(*refs):
    out = refs[-1]
    at = 0
    for group in (refs[:1], refs[1:2], refs[2:6]):
        parts, rows = group[0].shape[1:3]
        for p in range(parts):
            total = group[0][0, p]
            if len(group) > 1:
                total = total.astype(f32)
                for ref in group[1:]:
                    total = total + ref[0, p].astype(f32)
            out[0, at : at + rows, :] = total.astype(bf16)
            at += rows


def join(first, second, summed, after):
    rows = sum(value.shape[1] * value.shape[2] for value in (first, second, summed[0]))

    def spec(value):
        return pl.BlockSpec((1, *value.shape[1:]), lambda i: (i, 0, 0, 0))

    ins = [first, second, *summed]
    return call(
        join_body,
        "join",
        (4,),
        [spec(v) for v in ins] + [HBM] * len(after),
        pl.BlockSpec((1, rows, BLOCK), lambda i: (i, 0, 0)),
        shape((4, rows, BLOCK), bf16),
        [],
        5,
    )(*ins, *after)


def add_last_body(*refs):
    done, out = refs[0], refs[-1]
    rows = done.shape[0]
    out[0:rows, :] = done[...]
    total = refs[1][0].astype(f32)
    for ref in refs[2:5]:
        total = total + ref[0].astype(f32)
    out[rows : rows + total.shape[0], :] = total.astype(bf16)


def add_last(done, values, after):
    rows = done.shape[0] + values[0].shape[1]
    return call(
        add_last_body,
        "add_last",
        (1,),
        [whole(done.shape)] + [whole(v.shape) for v in values] + [HBM] * len(after),
        whole((rows, BLOCK)),
        shape((rows, BLOCK), bf16),
        [],
        10,
    )(done, *values, *after)


def send_z(piece):
    return [piece] + [shift(piece, s) for s in range(1, 4)]


def send_plane(piece):
    return [piece] + [swap(piece, 2 * j) for j in range(1, 4)]


def give_plane(parts):
    return [parts[0]] + [swap(parts[j], 2 * j) for j in range(1, 4)]


def give_z(parts):
    return [parts[0]] + [shift(parts[s], s) for s in range(1, 4)]


def gather_wide(piece, dp, extra):
    fine = dp // 8
    parts, rows = piece.shape[0], piece.shape[1] - extra
    out = lax.all_gather(piece, ("dp", "zero"), axis=0, tiled=False)
    out = out.reshape(8, fine, 4, *piece.shape)
    main = out[..., :rows, :].transpose(0, 2, 3, 1, 4, 5).reshape(8, 4, parts, 128, BLOCK)
    return [jnp.concatenate([main, out[:, 0, ..., rows:, :]], 3)]


def reduce_wide(blocks, dp, extra):
    fine = dp // 8
    blocks = blocks.reshape(8, 4, *blocks.shape[-3:])
    parts, rows = blocks.shape[2], 128 // fine
    main = blocks[..., :128, :].reshape(8, 4, parts, fine, rows, BLOCK).transpose(0, 3, 1, 2, 4, 5)
    beside = jnp.broadcast_to(
        blocks[:, None, ..., 128:, :], (8, fine, 4, parts, extra, BLOCK)
    )
    flat = jnp.concatenate([main, beside], 4).reshape(dp * 4, parts, rows + extra, BLOCK)
    mine = lax.psum_scatter(flat, ("dp", "zero"), scatter_dimension=0, tiled=True)
    out = lax.all_gather(mine[0], "dp", axis=0, tiled=False)
    out = out.reshape(8, fine, parts, rows + extra, BLOCK)
    main = out[..., :rows, :].transpose(0, 2, 1, 3, 4).reshape(8, parts, 128, BLOCK)
    out = jnp.concatenate([main, out[:, 0, :, rows:]], 2)
    return out.reshape(8, -1, BLOCK)


def shards(
    dp, images, cotangent, counts, rel_index, regions,
    mat_w, mat_m, mat_v, vec_w, vec_m, vec_v, tab_w, tab_m, tab_v,
):
    near = dp == 8
    fine = dp // 8
    rows = 128 // fine
    me = lax.axis_index("dp")
    taken_from = jnp.stack([me // fine, me % fine]).astype(jnp.int32)
    spot = [me, lax.axis_index("zero")] if near else [0 * me, 0 * me]
    place = jnp.stack(spot + [counts[0]]).astype(jnp.int32)

    inside = np.arange(CELL) < WIN * WIN
    zones = regions.reshape(2, WIN, 2, WIN).transpose(0, 2, 1, 3).reshape(4, WIN * WIN)
    zones = jnp.pad(zones, ((0, 0), (0, 15)))
    differ = (zones[:, :, None] != zones[:, None, :]) & inside[None, None, :]
    outside = jnp.asarray(np.where(inside, 0.0, -1e30), f32)[None, :, None]
    mask_shifted = jnp.tile(jnp.where(differ, mask_value, 0.0) + outside, (1, 1, QUAD)).astype(f32)
    mask_plain = jnp.broadcast_to(outside, (1, CELL, QUAD * CELL))
    masks = (mask_plain, mask_shifted)
    perms = (frames(False), frames(True))

    packed, cut_mlp0, cut_all1, rel = pack(
        taken_from, rows, mat_w, rel_index, tab_w, vec_w
    )
    alive = (jnp.arange(images.shape[0]) < counts[0]).astype(f32)[:, None, None]
    pad = ((0, 0), (0, ROWS - TOKENS), (0, 0))
    images = jnp.pad(images.astype(f32), pad)
    cotangent = jnp.pad(cotangent.astype(f32) * alive, pad)

    def attention(layer, stream, weight, after):
        return attention_forward(
            layer, place, stream, weight, heads0, masks[layer], perms[layer], after
        )

    half = images.shape[0] // 2
    if near:
        sent_heads0 = send_z(packed)
        *sent_heads0, images = tie([*sent_heads0, images], [])
        z_heads0 = stack(sent_heads0)
        all1 = gather_wide(tie([cut_all1], [z_heads0])[0], dp, 0)
        sent_heads0 = send_plane(z_heads0)
        sent_mlp0 = send_z(tie([cut_mlp0], [z_heads0])[0])
        cotangent, mask_shifted = tie([cotangent, mask_shifted], [z_heads0])
        *sent_heads0, cotangent, mask_shifted = tie(
            [*sent_heads0, cotangent, mask_shifted], sent_mlp0
        )
        masks = (mask_plain, mask_shifted)
        p_heads0 = stack(sent_heads0)
        heads0 = [p_heads0, swap(p_heads0, 1)]
        z_mlp0 = stack(sent_mlp0, [p_heads0])
        sent_mlp0 = send_plane(z_mlp0)
        kept0 = attention(0, images, heads0, [z_mlp0])
        p_mlp0 = stack(sent_mlp0, [kept0[0]])
        mlp0 = [p_mlp0, swap(p_mlp0, 1)]
    else:
        heads0 = gather_wide(packed, dp, EXTRA)
        mlp0 = gather_wide(cut_mlp0, dp, 0)
        all1 = gather_wide(cut_all1, dp, 0)
        kept0 = attention(0, images, heads0, [])
    stream, act, slope = mlp_forward(0, place, kept0[0], mlp0, kept0[5], [])
    kept1 = attention(1, stream, all1, [])
    kept = (kept0, kept1)
    inputs = (images, stream)
    attention_w = (heads0, all1)

    def backward_attention(layer, gradient, small, after, *span):
        mid, qkv, merged, totals, table, vec = kept[layer]
        return attention_backward(
            layer, place, gradient, inputs[layer], qkv, merged, totals, table, attention_w[layer],
            vec, small, perms[layer], rel, after, *span,
        )

    activations, grad_mid, parts_mlp1, small = mlp_both(
        place, cotangent, kept1[0], all1, kept1[5], []
    )

    def backward_mlp0(gradient, after):
        return mlp_backward(0, place, gradient, act, slope, kept0[0], mlp0, kept0[5], after)

    state = (mat_w, mat_m, mat_v)
    def exchange(parts):
        return [parts[0], swap(parts[1], 1)]

    gradient, parts_heads1, _, _ = backward_attention(1, grad_mid, small, [])
    grad_mid, *parts_mlp0, small = backward_mlp0(gradient, [])
    if near:
        t_mlp1 = lax.psum_scatter(parts_mlp1, "dp", scatter_dimension=0, tiled=True)[0]
        parts_heads1 = tie([parts_heads1], [t_mlp1, small])[0]
        t_heads1 = lax.psum_scatter(parts_heads1, "dp", scatter_dimension=0, tiled=True)[0]
        gone_mlp0 = exchange(parts_mlp0)
        gradient, *parts_heads0, pairs, small = backward_attention(0, grad_mid, small, [], 0, half)

        s_mlp0 = add_split(gone_mlp0, [gradient])
        gone_mlp0 = give_plane(s_mlp0)
        gradient, *parts_heads0, _, small = backward_attention(
            0, grad_mid, small, [s_mlp0[0]], half, half, [gradient, *parts_heads0, pairs]
        )

        t_all = join(t_mlp1, t_heads1, gone_mlp0, [small])
        gone_heads0 = exchange(tie(parts_heads0, [t_all]))
        g_all = lax.psum_scatter(t_all, "zero", scatter_dimension=0, tiled=True)[0]
        s_heads0 = add_split(gone_heads0, [t_all])
        gone_heads0 = give_plane(s_heads0)
        t_heads0 = add_split(gone_heads0, [])
        g_all = tie([g_all], [t_heads0[0]])[0]
        n_all1 = lax.all_gather(g_all[:400], "dp", axis=0, tiled=False)
        gone_heads0 = give_z(t_heads0)
        g_all0 = add_last(g_all[400:], gone_heads0, [])
        n_all0 = stack(send_plane(g_all0))
        sums0 = [n_all0, swap(n_all0, 1)]
        m = place[0] ^ np.arange(2)
        both = jnp.concatenate([half[:, 384:] for half in sums0])
        beside0 = [
            lax.dynamic_index_in_dim(both, (m[b] % 2) * 4 + m[b] // 2, 0, False) for b in range(2)
        ]
    else:
        gradient, *parts_heads0, _, _ = backward_attention(0, grad_mid, small, [])
        n_mlp1 = reduce_wide(parts_mlp1, dp, 0)
        n_heads1 = reduce_wide(parts_heads1, dp, SMALL)
        n_all1 = jnp.concatenate([n_mlp1, n_heads1], 1)
        n_mlp0 = reduce_wide(jnp.stack(parts_mlp0, 1), dp, 0)
        n_heads0 = reduce_wide(jnp.stack(parts_heads0, 1), dp, SMALL)
        sums0 = [jnp.concatenate([n_mlp0, n_heads0], 1)]
        beside0 = sums0[0][:2, 384:]
    done = adam(0, 1, place, sums0, state, None, [])
    done = adam(1, 1, place, [n_all1], state, done, [])

    def beside(block):
        return jnp.stack([beside0[block], n_all1[block, 384:]]).astype(f32)

    new_vec = adam_step(vec_w, vec_m, vec_v, beside(1)[:, 0:12, 0:128], rate_vector, 0.0)
    new_tab = adam_step(tab_w, tab_m, tab_v, beside(0)[:, 0:4, 0:NREL], rate_table, 0.0)
    return (activations, gradient, *done, *new_vec, *new_tab)


def solution(mesh):
    images = P(("dp", "zero"), None, None)
    rows = P(None, "zero", None)
    lanes = P(None, None, "zero")
    return jax.shard_map(
        partial(shards, mesh.shape["dp"]),
        mesh=mesh,
        in_specs=(images, images, P(("dp", "zero")), P(), P())
        + (rows,) * 3 + (lanes,) * 3 + (rows,) * 3,
        out_specs=(images, images) + (rows,) * 3 + (lanes,) * 3 + (rows,) * 3,
        check_vma=False,
    )
```

```python
from functools import partial

import jax
import jax.numpy as jnp
import numpy as np
from jax import lax
from jax.experimental import pallas as pl
from jax.experimental.pallas import tpu as pltpu
from jax.sharding import PartitionSpec as P

WIN = 7
SIDE = 14
STEP = 10
NREL = 169
C = 512
HID = 2048
TOKENS = SIDE * SIDE
PAIR = 2
ROWS = 208
FRAME = 256
CELL = 64
QUAD = 4
BLOCK = 256
EXTRA = 32
SMALL = 16

norm_eps = 1e-05
mask_value = -100.0
beta_one = 0.9
beta_two = 0.999
adam_eps = 1e-08
weight_decay = 0.05
rate_matrix = 0.1
rate_vector = 0.5
rate_table = 1.0
scale = 32 ** (-0.5)

bf16 = jnp.bfloat16
f32 = jnp.float32
NN = (((1,), (0,)), ((), ()))
NT = (((1,), (1,)), ((), ()))
TN = (((0,), (0,)), ((), ()))


def mm(left, right, dims=NN):
    return lax.dot_general(left, right, dims, preferred_element_type=f32)


def frames(shifted):
    move = WIN // 2 if shifted else 0
    placed = np.zeros((FRAME, ROWS), np.float32)
    for wy in range(2):
        for wx in range(2):
            for iy in range(WIN):
                for ix in range(WIN):
                    y = (wy * WIN + iy + move) % SIDE
                    x = (wx * WIN + ix + move) % SIDE
                    placed[(wy * 2 + wx) * CELL + iy * WIN + ix, y * SIDE + x] = 1
    return placed


def head_rows():
    rows = np.zeros((QUAD * CELL, 128), np.float32)
    for h in range(QUAD):
        rows[h * CELL : (h + 1) * CELL, h * 32 : (h + 1) * 32] = 1
    return rows


def head_spread(rows):
    out = np.zeros((rows, QUAD * CELL), np.float32)
    for h in range(QUAD):
        out[h, h * CELL : (h + 1) * CELL] = 1
    return out


def norm(rows):
    centred = rows - jnp.mean(rows, -1, keepdims=True)
    spread = lax.rsqrt(jnp.mean(centred * centred, -1, keepdims=True) + norm_eps)
    return centred * spread, spread


def norm_back(grad_unit, unit, spread):
    return spread * (
        grad_unit
        - jnp.mean(grad_unit, -1, keepdims=True)
        - unit * jnp.mean(grad_unit * unit, -1, keepdims=True)
    )


def column_sum(rows):
    return jnp.sum(rows, 0, keepdims=True)


def gelu_pair(u):
    size = jnp.abs(u)
    below = 1.0 + (0.3275911 * 0.5**0.5) * size
    t = pltpu.reciprocal(below, approx=True)
    bell = jnp.exp2(u * u * (-0.5 * 1.4426950408889634))
    poly = t * (
        0.127414796 + t * (-0.142248368 + t * (0.710706871 + t * (-0.726576013 + t * 0.530702714)))
    )
    tail = poly * bell
    phi = jnp.where(u >= 0, 1.0 - tail, tail)
    return u * phi, phi + u * bell * 0.3989422804014327


def quad_rows(part, heads):
    return jnp.concatenate([part] * QUAD, 0) * heads


def pick_heads(stacked, lane_head):
    low = jnp.where(lane_head == 0, stacked[:CELL], stacked[CELL : 2 * CELL])
    high = jnp.where(lane_head == 2, stacked[2 * CELL : 3 * CELL], stacked[3 * CELL :])
    return jnp.where(lane_head < 2, low, high)


def lane_heads():
    return lax.broadcasted_iota(jnp.int32, (CELL, 128), 1) // 32


def whole(shape):
    zero = (0,) * len(shape)
    return pl.BlockSpec(shape, lambda *_: zero, pipeline_mode=pl.Buffered(1))


def per_image(rows, cols):
    return pl.BlockSpec((1, rows, cols), lambda i, *_: (i, 0, 0))


def per_pair(rows, cols):
    return pl.BlockSpec((PAIR, rows, cols), lambda i, *_: (i, 0, 0))


HBM = pl.BlockSpec(memory_space=pl.ANY)


def weight_copies(place, stacks, kept, sems, part=0):
    copies = []
    for m in range(8):
        for s in range(4):
            for p in range(kept.shape[0]):
                if len(stacks) == 1:
                    source, block, owner = stacks[0].at[m, s, part + p], m, s
                else:
                    source = stacks[m % 2].at[m // 2, s, p]
                    block, owner = place[0] ^ m, (place[1] + 4 - s) & 3
                rows = pl.ds(pl.multiple_of(owner * 128, 128), 128)
                cols = pl.ds(pl.multiple_of(block * BLOCK, BLOCK), BLOCK)
                copies.append(
                    pltpu.make_async_copy(
                        source.at[pl.ds(0, 128), :], kept.at[p, rows, cols], sems.at[m, s, p]
                    )
                )
    return copies


def extra_copies(place, stacks, kept, sems):
    copies = []
    for m in range(8):
        for s in range(4):
            if len(stacks) == 1:
                source, block, owner = stacks[0].at[m, s, 0], m, s
            else:
                source = stacks[m % 2].at[m // 2, s, 0]
                block, owner = place[0] ^ m, (place[1] + 4 - s) & 3
            copies.append(
                pltpu.make_async_copy(
                    source.at[pl.ds(128, EXTRA), :], kept.at[block, owner], sems.at[m, s, 0]
                )
            )
    return copies


def fetch(copies):
    for copy in copies:
        copy.start()
    for copy in copies:
        copy.wait()


def call(body, name, grid, ins, outs, out_shapes, scratch, cost_us, prefetch=0, aliases=None):
    return pl.pallas_call(
        body,
        name=name,
        grid_spec=pltpu.PrefetchScalarGridSpec(
            num_scalar_prefetch=prefetch,
            grid=grid,
            in_specs=ins,
            out_specs=outs,
            scratch_shapes=scratch,
        ),
        out_shape=out_shapes,
        input_output_aliases=aliases or {},
        compiler_params=pltpu.CompilerParams(
            dimension_semantics=("arbitrary",) * len(grid), vmem_limit_bytes=58 * 1024 * 1024
        ),
        cost_estimate=pl.CostEstimate(
            flops=0, bytes_accessed=int(cost_us * 3.69e4), transcendentals=0
        ),
    )


def shape(dims, kind):
    return jax.ShapeDtypeStruct(dims, kind)


def pack_body(place, *refs):
    mats, (pair_index, tab, vec, spread) = refs[:6], refs[6:10]
    out, mlp0, all1, rel, spread_tab, small = refs[10:]
    rows = mats[0].shape[1]
    out[0, 0:rows, :] = mats[0][0].astype(bf16)
    for ref, at, n in ((mlp0, 0, 1), (mlp0, 1, 2), (all1, 0, 3), (all1, 1, 4), (all1, 2, 5)):
        ref[at] = mats[n][0].astype(bf16)
    rel[...] = jnp.full(rel.shape, -1, jnp.int32)
    across = pair_index[...].astype(f32).T.astype(jnp.int32)
    for h in range(QUAD):
        rel[0 : WIN * WIN, CELL * h : CELL * h + WIN * WIN] = across
    for layer in range(2):
        spread_tab[layer, 0:NREL, :] = mm(tab[layer].astype(bf16), spread[...], TN)
    pairs = rel[pl.ds(pl.multiple_of(place[0] * 8, 8), 8), :]

    def step(r, sums):
        hit = pairs == r
        return tuple(
            jnp.where(hit, spread_tab[layer, pl.ds(r, 1), :], sums[layer]) for layer in range(2)
        )

    start = jnp.zeros((8, QUAD * CELL), f32)
    first, second = lax.fori_loop(0, NREL, step, (start, start), unroll=13)
    out[0, rows : rows + 16, :] = jnp.concatenate([first, second], 0).astype(bf16)
    small[...] = jnp.zeros_like(small)
    row = jnp.minimum(place[0] * 2, 10)
    for layer in range(2):
        for k in range(2):
            small[k : k + 1, layer * 128 : (layer + 1) * 128] = vec[row + k, layer : layer + 1, :]
    out[0, rows + 16 : rows + 32, :] = small[...].astype(bf16)


def pack(place, rows, mat_w, rel_index, tab_w, vec_w):
    vec_w = vec_w.transpose(1, 0, 2)

    def block(layer, part):
        return pl.BlockSpec(
            (1, rows, BLOCK), lambda i, place: (layer, place[1], part * 8 + place[0])
        )

    dims = [(1, rows + EXTRA, BLOCK), (2, rows, BLOCK), (3, rows, BLOCK)]
    return call(
        pack_body,
        "pack",
        (1,),
        [block(layer, part) for layer in range(2) for part in range(3)]
        + [
            whole(rel_index.shape),
            whole(tab_w.shape),
            whole(vec_w.shape),
            whole((QUAD, QUAD * CELL)),
        ],
        [whole(d) for d in dims] + [whole((CELL, QUAD * CELL))],
        [shape(d, bf16) for d in dims] + [shape((CELL, QUAD * CELL), jnp.int32)],
        [pltpu.VMEM((2, 176, QUAD * CELL), f32), pltpu.VMEM((16, 256), f32)],
        4,
        prefetch=1,
    )(place, *[mat_w] * 6, rel_index, tab_w, vec_w, jnp.asarray(head_spread(QUAD), bf16))


def attention_forward_body(layer, stacks, waits, place, *refs):
    arrays, refs = refs[: stacks[0]], refs[stacks[0] :]
    extras, refs = refs[: stacks[1]], refs[stacks[1] + waits :]
    x, mask, perm, perm_back, heads = refs[:5]
    mid, qkv, merged, totals, table, vec, framed, kept, extra_kept, sems, more_sems = refs[5:]
    weight, extra = kept.at[0], extra_kept

    @pl.when(pl.program_id(0) == 0)
    def _():
        fetch(
            weight_copies(place, arrays, kept, sems)
            + extra_copies(place, extras, extra_kept, more_sems)
        )
        vec[...] = jnp.zeros_like(vec)
        for z in range(4):
            for d in range(8):
                pair = extra[d, z, 0:16, :].astype(f32)
                bias = pair[8 * layer : 8 * layer + 8]
                for w in range(table.shape[0]):
                    table[w, z, 8 * d : 8 * d + 8, :] = bias + mask[w, 8 * d : 8 * d + 8, :]
                if d < 6:
                    rows = extra[d, z, 16:32, 128 * layer : 128 * layer + 128].astype(f32)
                    vec[2 * d : 2 * d + 2, 128 * z : 128 * z + 128] = rows[0:2]

    stream = x[0]
    unit, _ = norm(stream)
    normed = (unit * vec[0:1, :] + vec[1:2, :]).astype(bf16)
    normed = mm(perm[...], normed).astype(bf16)
    for c in range(6):
        part = mm(normed, weight[:, 256 * c : 256 * c + 256])
        if c < 2:
            part = part + vec[2:3, 256 * c : 256 * c + 256]
        if c >= 4:
            part = part + vec[3:4, 256 * (c - 4) : 256 * (c - 4) + 256]
        qkv[0, :, 256 * c : 256 * c + 256] = part.astype(bf16)
    lane_head = lane_heads()

    at = [128 * g for g in range(4)]

    def window(w):
        rows = slice(CELL * w, CELL * w + CELL)
        query = [quad_rows(qkv[0, rows, c : c + 128], heads[...]) for c in at]
        return [mm(qkv[0, rows, C + at[g] : C + at[g] + 128], query[g], NT) for g in range(4)]

    ahead = window(0)
    for w in range(4):
        rows = slice(CELL * w, CELL * w + CELL)
        scores = ahead
        if w < 3:
            ahead = window(w + 1)
        probs = []
        for g in range(4):
            shifted = scores[g] * scale + table[w % table.shape[0], g]
            top = jnp.max(shifted, 0, keepdims=True)
            raised = jnp.exp(shifted - top)
            total = jnp.sum(raised, 0, keepdims=True)
            totals[0, 4 * w + g : 4 * w + g + 1, :] = top + jnp.log(total)
            probs.append((raised * (1.0 / total)).astype(bf16))
        stacked = [mm(probs[g], qkv[0, rows, 2 * C + at[g] : 2 * C + at[g] + 128], TN) for g in range(4)]
        for g in range(4):
            framed[rows, at[g] : at[g] + 128] = pick_heads(stacked[g], lane_head).astype(bf16)
    gathered = mm(perm_back[...], framed[...]).astype(bf16)
    merged[0] = gathered
    mid[0] = stream + mm(gathered, weight[:, 3 * C :]) + vec[4:5, :]


def attention_forward(layer, place, x, weight, extra, mask, perm, after):
    images = x.shape[0]
    tables = mask.shape[0]
    return call(
        partial(attention_forward_body, layer, (len(weight), len(extra)), len(after)),
        f"attention_forward_{layer}",
        (images,),
        [HBM] * (len(weight) + len(extra) + len(after))
        + [
            per_image(x.shape[1], C),
            whole(mask.shape),
            whole((FRAME, ROWS)),
            whole((ROWS, FRAME)),
            whole((QUAD * CELL, 128)),
        ],
        [
            per_image(ROWS, C),
            per_image(FRAME, 3 * C),
            per_image(ROWS, C),
            per_image(16, QUAD * CELL),
            pl.BlockSpec((tables, 4, CELL, QUAD * CELL), lambda i, *_: (0, 0, 0, 0)),
            pl.BlockSpec((16, C), lambda i, *_: (0, 0)),
        ],
        [
            shape((images, ROWS, C), f32),
            shape((images, FRAME, 3 * C), bf16),
            shape((images, ROWS, C), bf16),
            shape((images, 16, QUAD * CELL), f32),
            shape((tables, 4, CELL, QUAD * CELL), f32),
            shape((16, C), f32),
        ],
        [
            pltpu.VMEM((FRAME, C), bf16),
            pltpu.VMEM((1, C, HID), bf16),
            pltpu.VMEM((8, 4, EXTRA, BLOCK), bf16),
            pltpu.SemaphoreType.DMA((8, 4, 1)),
            pltpu.SemaphoreType.DMA((8, 4, 1)),
        ],
        20,
        prefetch=1,
    )(
        place,
        *weight,
        *extra,
        *after,
        x,
        mask,
        jnp.asarray(perm, bf16),
        jnp.asarray(perm.T, bf16),
        jnp.asarray(head_rows(), bf16),
    )


def mlp_forward_body(stacks, waits, place, *refs):
    arrays, refs = refs[:stacks], refs[stacks + waits :]
    mid, vec, result, act, slope, kept, sems = refs
    first, second = kept.at[0], kept.at[1]

    @pl.when(pl.program_id(0) == 0)
    def _():
        fetch(weight_copies(place, arrays, kept, sems))

    rows = PAIR * ROWS
    stream = mid[...].reshape(rows, C)
    unit, _ = norm(stream)
    normed = (unit * vec[5:6, :] + vec[6:7, :]).astype(bf16)
    ahead = mm(normed, first[:, 0:BLOCK])
    for c in range(8):
        cols = slice(256 * c, 256 * c + 256)
        bias = vec[8 + c // 2 : 9 + c // 2, 256 * (c % 2) : 256 * (c % 2) + 256]
        inner = ahead + bias
        if c < 7:
            ahead = mm(normed, first[:, 256 * c + 256 : 256 * c + 512])
        value, pull = gelu_pair(inner)
        act[:, :, cols] = value.astype(bf16).reshape(PAIR, ROWS, BLOCK)
        slope[:, :, cols] = pull.astype(bf16).reshape(PAIR, ROWS, BLOCK)
    total = stream + vec[7:8, :] + mm(act[...].reshape(rows, HID), second[...], NT)
    result[...] = total.reshape(PAIR, ROWS, C)


def mlp_forward(layer, place, mid, weight, vec, after):
    images = mid.shape[0]
    return call(
        partial(mlp_forward_body, len(weight), len(after)),
        f"mlp_forward_{layer}",
        (images // PAIR,),
        [HBM] * (len(weight) + len(after)) + [per_pair(ROWS, C), whole(vec.shape)],
        [per_pair(ROWS, C), per_pair(ROWS, HID), per_pair(ROWS, HID)],
        [
            shape((images, ROWS, C), f32),
            shape((images, ROWS, HID), bf16),
            shape((images, ROWS, HID), bf16),
        ],
        [
            pltpu.VMEM((2, C, HID), bf16),
            pltpu.SemaphoreType.DMA((8, 4, 2)),
        ],
        22,
        prefetch=1,
    )(place, *weight, *after, mid, vec)


def mlp_both_body(stacks, waits, place, *refs):
    arrays, refs = refs[:stacks], refs[stacks + waits :]
    grad, mid, vec, result, grad_mid, pieces, small = refs[:7]
    all_grad, all_act, all_inner, all_normed, kept, sems = refs[7:]
    first, second = kept.at[0], kept.at[1]
    i = pl.program_id(0)

    @pl.when(i == 0)
    def _():
        fetch(weight_copies(place, arrays, kept, sems, 1))
        small[...] = jnp.zeros_like(small)

    rows = PAIR * ROWS
    grad_out = grad[...].reshape(rows, C)
    here = pl.ds(pl.multiple_of(i * rows, 32), rows)
    low = grad_out.astype(bf16)
    all_grad[here, :] = low
    small[7:8, :] += column_sum(grad_out)
    stream = mid[...].reshape(rows, C)
    unit, spread = norm(stream)
    normed = (unit * vec[5:6, :] + vec[6:7, :]).astype(bf16)
    all_normed[here, :] = normed
    ahead = mm(normed, first[:, 0:BLOCK]), mm(low, second[:, 0:BLOCK])
    for c in range(8):
        cols = slice(256 * c, 256 * c + 256)
        row, lane = 8 + c // 2, 256 * (c % 2)
        bias = vec[row : row + 1, lane : lane + 256]
        inner, grad_act = ahead
        if c < 7:
            later = slice(256 * c + 256, 256 * c + 512)
            ahead = mm(normed, first[:, later]), mm(low, second[:, later])
        value, pull = gelu_pair(inner + bias)
        all_act[here, cols] = value.astype(bf16)
        inner = (grad_act * pull).astype(bf16)
        all_inner[here, cols] = inner
        small[row : row + 1, lane : lane + 256] += column_sum(inner.astype(f32))
    back = mm(all_inner[here, :], first[...], NT)
    small[5:6, :] += column_sum(back * unit)
    small[6:7, :] += column_sum(back)
    grad_mid[...] = (grad_out + norm_back(back * vec[5:6, :], unit, spread)).reshape(PAIR, ROWS, C)
    total = stream + vec[7:8, :] + mm(all_act[here, :], second[...], NT)
    for n in range(PAIR):
        alive = (i * PAIR + n < place[2]).astype(f32)
        result[n] = (total[n * ROWS : n * ROWS + TOKENS] * alive).astype(bf16)

    @pl.when(i == pl.num_programs(0) - 1)
    def _():
        mlp_weight_grads(place, all_grad, all_act, all_inner, all_normed, pieces)


def mlp_weight_grads(place, all_grad, all_act, all_inner, all_normed, *outs):
    grad_across = all_grad[...].T
    normed_across = all_normed[...].T
    for m in range(8):
        block = m if len(outs) == 1 else place[0] ^ m
        cols = pl.ds(pl.multiple_of(block * BLOCK, BLOCK), BLOCK)
        for p, total in enumerate(
            (mm(normed_across, all_inner[:, cols]), mm(grad_across, all_act[:, cols]))
        ):
            total = total.astype(bf16)
            for z in range(4):
                if len(outs) == 1:
                    outs[0][m, z, p] = total[128 * z : 128 * z + 128]
                else:
                    outs[m % 2][m // 2, z, p] = total[128 * z : 128 * z + 128]


def mlp_both(place, grad, mid, weight, vec, after):
    images = mid.shape[0]
    total = images * ROWS
    pieces = (8, 4, 2, 128, BLOCK)
    return call(
        partial(mlp_both_body, len(weight), len(after)),
        "mlp_both",
        (images // PAIR,),
        [HBM] * (len(weight) + len(after)) + [per_pair(ROWS, C), per_pair(ROWS, C), whole(vec.shape)],
        [per_pair(TOKENS, C), per_pair(ROWS, C), whole(pieces), whole((16, C))],
        [
            shape((images, TOKENS, C), bf16),
            shape((images, ROWS, C), f32),
            shape(pieces, bf16),
            shape((16, C), f32),
        ],
        [
            pltpu.VMEM((total, C), bf16),
            pltpu.VMEM((total, HID), bf16),
            pltpu.VMEM((total, HID), bf16),
            pltpu.VMEM((total, C), bf16),
            pltpu.VMEM((2, C, HID), bf16),
            pltpu.SemaphoreType.DMA((8, 4, 2)),
        ],
        45,
        prefetch=1,
    )(place, *weight, *after, grad, mid, vec)


def mlp_backward_body(stacks, waits, place, *refs):
    arrays, refs = refs[:stacks], refs[stacks + waits :]
    grad, act, slope, mid, vec, grad_mid, own, other, small = refs[:9]
    all_grad, all_act, all_inner, all_normed, kept, sems = refs[9:]
    first, second = kept.at[0], kept.at[1]
    i = pl.program_id(0)

    @pl.when(i == 0)
    def _():
        fetch(weight_copies(place, arrays, kept, sems))
        small[...] = jnp.zeros_like(small)

    rows = PAIR * ROWS
    grad_out = grad[...].reshape(rows, C)
    here = pl.ds(pl.multiple_of(i * rows, 32), rows)
    low = grad_out.astype(bf16)
    all_grad[here, :] = low
    small[7:8, :] += column_sum(low.astype(f32))
    all_act[here, :] = act[...].reshape(rows, HID)
    unit, spread = norm(mid[...].reshape(rows, C))
    all_normed[here, :] = (unit * vec[5:6, :] + vec[6:7, :]).astype(bf16)
    ahead = mm(low, second[:, 0:BLOCK])
    for c in range(8):
        cols = slice(256 * c, 256 * c + 256)
        pull = slope[:, :, cols].reshape(rows, BLOCK).astype(f32)
        grad_act = ahead
        if c < 7:
            ahead = mm(low, second[:, 256 * c + 256 : 256 * c + 512])
        inner = (grad_act * pull).astype(bf16)
        all_inner[here, cols] = inner
        row, lane = 8 + c // 2, 256 * (c % 2)
        small[row : row + 1, lane : lane + 256] += column_sum(inner.astype(f32))
    back = mm(all_inner[here, :], first[...], NT)
    small[5:6, :] += column_sum(back * unit)
    small[6:7, :] += column_sum(back)
    grad_mid[...] = (grad_out + norm_back(back * vec[5:6, :], unit, spread)).reshape(PAIR, ROWS, C)

    @pl.when(i == pl.num_programs(0) - 1)
    def _():
        mlp_weight_grads(place, all_grad, all_act, all_inner, all_normed, own, other)


def mlp_backward(layer, place, grad, act, slope, mid, weight, vec, after):
    images = mid.shape[0]
    total = images * ROWS
    pieces = (4, 4, 2, 128, BLOCK)
    return call(
        partial(mlp_backward_body, len(weight), len(after)),
        f"mlp_backward_{layer}",
        (images // PAIR,),
        [HBM] * (len(weight) + len(after))
        + [
            per_pair(grad.shape[1], C),
            per_pair(ROWS, HID),
            per_pair(ROWS, HID),
            per_pair(ROWS, C),
            whole(vec.shape),
        ],
        [per_pair(ROWS, C), whole(pieces), whole(pieces), whole((16, C))],
        [
            shape((images, ROWS, C), f32),
            shape(pieces, bf16),
            shape(pieces, bf16),
            shape((16, C), f32),
        ],
        [
            pltpu.VMEM((total, C), bf16),
            pltpu.VMEM((total, HID), bf16),
            pltpu.VMEM((total, HID), bf16),
            pltpu.VMEM((total, C), bf16),
            pltpu.VMEM((2, C, HID), bf16),
            pltpu.SemaphoreType.DMA((8, 4, 2)),
        ],
        30,
        prefetch=1,
    )(place, *weight, *after, grad, act, slope, mid, vec)


def attention_backward_body(layer, stacks, waits, resumed, ends, place, *refs):
    arrays, refs = refs[:stacks], refs[stacks + waits :]
    if resumed:
        (own_before, other_before, pairs_before), refs = refs[1:4], refs[4:]
    grad, x, qkv, merged, totals, table, vec, before = refs[:8]
    perm, perm_back, heads, rel, spread, result = refs[8:14]
    outs, refs = (refs[14:15], refs[15:]) if layer else (refs[14:16], refs[16:])
    pairs, small, framed, grad_framed, all_normed, all_packed, all_merged = refs[:7]
    across, hits, beside, kept, sems = refs[7:]
    weight = kept.at[0]
    i = pl.program_id(0)

    @pl.when(i == 0)
    def _():
        fetch(weight_copies(place, arrays, kept, sems))
        small[...] = before[...]
        pairs[...] = pairs_before[...] if resumed else jnp.zeros_like(pairs)

    stream = x[0]
    here = pl.ds(pl.multiple_of(i * ROWS, 16), ROWS)
    unit, spread_one = norm(stream)
    all_normed[here, :] = (unit * vec[0:1, :] + vec[1:2, :]).astype(bf16)
    low = grad[0].astype(bf16)
    all_packed[here, 3 * C :] = low
    all_merged[here, :] = merged[0]
    small[4:5, :] += column_sum(low.astype(f32))
    moved = mm(perm[...], low).astype(bf16)
    framed[...] = mm(moved, weight[:, 3 * C :], NT).astype(bf16)
    lane_head = lane_heads()
    at = [128 * g for g in range(4)]

    def window(w):
        rows = slice(CELL * w, CELL * w + CELL)
        keys = [qkv[0, rows, C + c : C + c + 128] for c in at]
        query = [quad_rows(qkv[0, rows, c : c + 128], heads[...]) for c in at]
        pull = [quad_rows(framed[rows, c : c + 128], heads[...]) for c in at]
        scores = [mm(keys[g], query[g], NT) for g in range(4)]
        grad_probs = [
            mm(qkv[0, rows, 2 * C + at[g] : 2 * C + at[g] + 128], pull[g], NT) for g in range(4)
        ]
        return keys, query, pull, scores, grad_probs

    ahead = window(0)
    for w in range(4):
        rows = slice(CELL * w, CELL * w + CELL)
        keys, query, pull, scores, grad_probs = ahead
        if w < 3:
            ahead = window(w + 1)
        probs, grad_scores = [], []
        for g in range(4):
            shifted = scores[g] * scale + table[w % table.shape[0], g]
            prob = jnp.exp(shifted - totals[0, 4 * w + g : 4 * w + g + 1, :])
            mean = jnp.sum(prob * grad_probs[g], 0, keepdims=True)
            grad_score = (prob * (grad_probs[g] - mean)).astype(bf16)
            pairs[g] += grad_score.astype(f32)
            probs.append(prob.astype(bf16))
            grad_scores.append(grad_score)
        for g in range(4):
            grad_value = mm(probs[g], pull[g])
            grad_framed[rows, 2 * C + at[g] : 2 * C + at[g] + 128] = grad_value.astype(bf16)
        for g in range(4):
            grad_key = mm(grad_scores[g], query[g]) * scale
            grad_framed[rows, C + at[g] : C + at[g] + 128] = grad_key.astype(bf16)
        for g in range(4):
            grad_query = pick_heads(mm(grad_scores[g], keys[g], TN), lane_head) * scale
            grad_framed[rows, at[g] : at[g] + 128] = grad_query.astype(bf16)
    for c in range(6):
        cols = slice(256 * c, 256 * c + 256)
        part = mm(perm_back[...], grad_framed[:, cols])
        all_packed[here, cols] = part.astype(bf16)
        if c < 2:
            small[2:3, cols] += column_sum(part)
        if c >= 4:
            small[3:4, 256 * (c - 4) : 256 * (c - 4) + 256] += column_sum(part)
    back = mm(all_packed[here, : 3 * C], weight[:, : 3 * C], NT)
    small[0:1, :] += column_sum(back * unit)
    small[1:2, :] += column_sum(back)
    total = grad[0] + norm_back(back * vec[0:1, :], unit, spread_one)
    result[0] = total[: result.shape[1]]

    @pl.when(i == pl.num_programs(0) - 1)
    def _():
        across[0] = all_normed[...].T
        across[1] = all_merged[...].T
        beside[...] = jnp.zeros_like(beside)
        if ends:
            hits[...] = jnp.zeros_like(hits)

            def step(r, carry):
                same = rel[...] == r
                for g in range(4):
                    kept_pairs = jnp.where(same, pairs[g], 0.0)
                    hits[pl.ds(r, 1), 256 * g : 256 * g + 256] = column_sum(kept_pairs)
                return carry

            lax.fori_loop(0, NREL, step, 0)
            for z in range(4):
                beside[0, z] = lax.dot_general(
                    spread[...],
                    hits[:, 256 * z : 256 * z + 256],
                    NT,
                    precision=lax.Precision.HIGHEST,
                    preferred_element_type=f32,
                ).astype(bf16)
                beside[1, z, :, 0:128] = small[:, 128 * z : 128 * z + 128].astype(bf16)
        for m in range(8):
            b = m if layer else place[0] ^ m
            left = across[jnp.where(b < 6, 0, 1)]
            right = all_packed[:, pl.ds(pl.multiple_of(b * BLOCK, BLOCK), BLOCK)]
            block = mm(left, right)
            for z in range(4):
                if layer:
                    out = outs[0].at[m, z, 0]
                else:
                    to = (z + 4 - place[1]) & 3
                    out = outs[m % 2].at[m // 2, to, 0]
                new = block[128 * z : 128 * z + 128]
                if resumed:
                    old = other_before if m % 2 else own_before
                    new = new + old[m // 2, to, 0, 0:128, :].astype(f32)
                out[0:128, :] = new.astype(bf16)
                out[128:144, :] = beside[jnp.minimum(b, 2), z]


def attention_backward(
    layer, place, grad, x, qkv, merged, totals, table, weight, vec, small, perm, rel, after,
    first=0, count=None, resume=None,
):
    images = grad.shape[0]
    count = count or images
    pieces = (8 if layer else 4, 4, 1, 128 + SMALL, BLOCK)
    pairs = (4, CELL, QUAD * CELL)
    total = count * ROWS
    out_rows = TOKENS if layer == 0 else ROWS

    def image(rows, cols):
        return pl.BlockSpec((1, rows, cols), lambda i, *_: (i + first, 0, 0))

    resumed = list(resume or [])
    return call(
        partial(
            attention_backward_body, layer, len(weight), len(after), bool(resumed),
            first + count == images,
        ),
        f"attention_backward_{layer}_{first}",
        (count,),
        [HBM] * (len(weight) + len(after))
        + ([HBM, whole(pieces), whole(pieces), whole(pairs)] if resumed else [])
        + [
            image(ROWS, C),
            image(x.shape[1], C),
            image(FRAME, 3 * C),
            image(ROWS, C),
            image(16, QUAD * CELL),
            whole(table.shape),
            whole(vec.shape),
            whole((16, C)),
            whole((FRAME, ROWS)),
            whole((ROWS, FRAME)),
            whole((QUAD * CELL, 128)),
            whole(rel.shape),
            whole((SMALL, QUAD * CELL)),
        ],
        [image(out_rows, C)]
        + [whole(pieces)] * (1 if layer else 2)
        + [whole(pairs), whole((16, C))],
        [shape((images, out_rows, C), f32)]
        + [shape(pieces, bf16)] * (1 if layer else 2)
        + [shape(pairs, f32), shape((16, C), f32)],
        [
            pltpu.VMEM((FRAME, C), bf16),
            pltpu.VMEM((FRAME, 3 * C), bf16),
            pltpu.VMEM((total, C), bf16),
            pltpu.VMEM((total, 4 * C), bf16),
            pltpu.VMEM((total, C), bf16),
            pltpu.VMEM((2, C, total), bf16),
            pltpu.VMEM((256, 4 * QUAD * CELL), f32),
            pltpu.VMEM((3, 4, SMALL, BLOCK), bf16),
            pltpu.VMEM((1, C, HID), bf16),
            pltpu.SemaphoreType.DMA((8, 4, 1)),
        ],
        6 * count,
        prefetch=1,
        aliases={1 + len(weight) + len(after): 0} if resumed else None,
    )(
        place,
        *weight,
        *after,
        *resumed,
        grad,
        x,
        qkv,
        merged,
        totals,
        table,
        vec,
        small,
        jnp.asarray(perm, bf16),
        jnp.asarray(perm.T, bf16),
        jnp.asarray(head_rows(), bf16),
        rel,
        jnp.asarray(head_spread(SMALL), f32),
    )


def adam_step(weight, first, second, gradient, rate, decay):
    first_new = beta_one * first + (1.0 - beta_one) * gradient
    second_new = beta_two * second + (1.0 - beta_two) * gradient * gradient
    first_hat = first_new / (1.0 - beta_one**STEP)
    second_hat = second_new / (1.0 - beta_two**STEP)
    weight_new = weight - rate * (first_hat / (jnp.sqrt(second_hat) + adam_eps) + decay * weight)
    return (weight_new, first_new, second_new)


def adam_block(grad, weight, first, second, outs, cols):
    part = grad.astype(f32)
    first_new = beta_one * first[0, :, cols] + (1.0 - beta_one) * part
    second_new = beta_two * second[0, :, cols] + (1.0 - beta_two) * part * part
    spread = second_new * (1.0 / (1.0 - beta_two**STEP))
    inverse = pltpu.reciprocal(spread * lax.rsqrt(spread) + adam_eps, approx=True)
    step = first_new * (rate_matrix / (1.0 - beta_one**STEP)) * inverse
    outs[0][0, :, cols] = weight[0, :, cols] * (1.0 - rate_matrix * weight_decay) - step
    outs[1][0, :, cols] = first_new
    outs[2][0, :, cols] = second_new


def adam_body(place, near, far, weight, first, second, *refs):
    for j in range(2):
        for k in range(2):
            block = (((place[0] // 2) & 1) ^ j) * 2 + ((place[0] & 1) ^ k)
            cols = pl.ds(pl.multiple_of(block * BLOCK, BLOCK), BLOCK)
            adam_block((far if k else near)[j], weight, first, second, refs[-3:], cols)


def adam_body_plain(place, sums, weight, first, second, *refs):
    for k in range(4):
        cols = slice(BLOCK * k, BLOCK * k + BLOCK)
        adam_block(sums[k], weight, first, second, refs[-3:], cols)


def adam(layer, part, place, sums, state, done, after):
    kept = [] if done is None else list(done)
    if len(sums) == 2:
        parts = sums[0].shape[1] // 128
        body = adam_body
        spec = pl.BlockSpec(
            (1, 128, 4 * BLOCK),
            lambda p, j, place: (layer, 0, (part + p) % 3 * 2 + ((place[0] // 4) ^ j)),
        )
        piece = pl.BlockSpec((2, 128, BLOCK), lambda p, j, place: (j, p, 0))
    else:
        parts = sums[0].shape[1] // 128
        body = adam_body_plain
        spec = pl.BlockSpec(
            (1, 128, 4 * BLOCK), lambda p, j, place: (layer, 0, (part + p) % 3 * 2 + j)
        )
        piece = pl.BlockSpec((4, 128, BLOCK), lambda p, j, place: (j, p, 0))
    return call(
        body,
        f"adam_{layer}_{part}",
        (parts, 2),
        [piece] * len(sums) + [spec] * 3 + [HBM] * (len(kept) + len(after)),
        [spec] * 3,
        [shape(state[0].shape, f32)] * 3,
        [],
        3 * parts,
        prefetch=1,
        aliases={4 + len(sums) + k: k for k in range(len(kept))},
    )(place, *sums, *state, *kept, *after)


def swap(value, bits):
    return lax.ppermute(value, "dp", [(i, i ^ bits) for i in range(8)])


def shift(value, steps):
    return lax.ppermute(value, "zero", [(i, (i + steps) % 4) for i in range(4)])


def tie(values, after):
    values = list(values)
    return list(lax.optimization_barrier((*values, *after))[: len(values)])


def stack(values, after=()):
    return jnp.stack(tie(values, after) if after else values)


def add_body(count, *refs):
    total = refs[0][...].astype(f32)
    for k in range(1, count):
        total = total + refs[k][...].astype(f32)
    refs[-1][...] = total.astype(bf16)


def add(values, after=()):
    dims = values[0].shape
    return call(
        partial(add_body, len(values)),
        "add",
        (1,),
        [whole(dims)] * len(values) + [HBM] * len(after),
        whole(dims),
        shape(dims, bf16),
        [],
        10,
    )(*values, *after)


def add_split_body(count, lead, *refs):
    for k in range(4):
        if count == 2:
            refs[len(refs) - 4 + k][...] = refs[0][k] + refs[1][k]
            continue
        total = refs[0][k].astype(f32)
        for v in range(1, count):
            total = total + refs[v][k].astype(f32)
        refs[len(refs) - 4 + k][...] = total.astype(bf16)


def add_split(values, after=()):
    dims = values[0].shape
    steps = dims[1] if len(dims) == 5 else 1
    ins = (4, dims[1] // steps, *dims[2:])
    outs = dims[1:]
    zeros = (0,) * (len(dims) - 2)
    return call(
        partial(add_split_body, len(values), True),
        "add_split",
        (steps,),
        [pl.BlockSpec(ins, lambda i: (0, i, *zeros))] * len(values) + [HBM] * len(after),
        [pl.BlockSpec((outs[0] // steps, *outs[1:]), lambda i: (i, *zeros))] * 4,
        [shape(outs, bf16)] * 4,
        [],
        10,
    )(*values, *after)


def join_body(*refs):
    out = refs[-1]
    at = 0
    for group in (refs[:1], refs[1:2], refs[2:6]):
        parts, rows = group[0].shape[1:3]
        for p in range(parts):
            total = group[0][0, p]
            if len(group) > 1:
                total = total.astype(f32)
                for ref in group[1:]:
                    total = total + ref[0, p].astype(f32)
            out[0, at : at + rows, :] = total.astype(bf16)
            at += rows


def join(first, second, summed, after):
    rows = sum(value.shape[1] * value.shape[2] for value in (first, second, summed[0]))

    def spec(value):
        return pl.BlockSpec((1, *value.shape[1:]), lambda i: (i, 0, 0, 0))

    ins = [first, second, *summed]
    return call(
        join_body,
        "join",
        (4,),
        [spec(v) for v in ins] + [HBM] * len(after),
        pl.BlockSpec((1, rows, BLOCK), lambda i: (i, 0, 0)),
        shape((4, rows, BLOCK), bf16),
        [],
        5,
    )(*ins, *after)


def add_last_body(*refs):
    done, out = refs[0], refs[-1]
    rows = 256
    out[0:rows, :] = done[done.shape[0] - rows :, :]
    total = refs[1][0].astype(f32)
    for ref in refs[2:5]:
        total = total + ref[0].astype(f32)
    out[rows : rows + total.shape[0], :] = total.astype(bf16)


def add_last(done, values, after):
    rows = 256 + values[0].shape[1]
    return call(
        add_last_body,
        "add_last",
        (1,),
        [whole(done.shape)] + [whole(v.shape) for v in values] + [HBM] * len(after),
        whole((rows, BLOCK)),
        shape((rows, BLOCK), bf16),
        [],
        10,
    )(done, *values, *after)


def send_z(piece):
    return [piece] + [shift(piece, s) for s in range(1, 4)]


def send_plane(piece):
    return [piece] + [swap(piece, 2 * j) for j in range(1, 4)]


def give_plane(parts):
    return [parts[0]] + [swap(parts[j], 2 * j) for j in range(1, 4)]


def give_z(parts):
    return [parts[0]] + [shift(parts[s], s) for s in range(1, 4)]


def gather_wide(piece, dp, extra):
    fine = dp // 8
    parts, rows = piece.shape[0], piece.shape[1] - extra
    out = lax.all_gather(piece, ("dp", "zero"), axis=0, tiled=False)
    out = out.reshape(8, fine, 4, *piece.shape)
    main = out[..., :rows, :].transpose(0, 2, 3, 1, 4, 5).reshape(8, 4, parts, 128, BLOCK)
    return [jnp.concatenate([main, out[:, 0, ..., rows:, :]], 3)]


def reduce_wide(blocks, dp, extra):
    fine = dp // 8
    blocks = blocks.reshape(8, 4, *blocks.shape[-3:])
    parts, rows = blocks.shape[2], 128 // fine
    main = blocks[..., :128, :].reshape(8, 4, parts, fine, rows, BLOCK).transpose(0, 3, 1, 2, 4, 5)
    beside = jnp.broadcast_to(
        blocks[:, None, ..., 128:, :], (8, fine, 4, parts, extra, BLOCK)
    )
    flat = jnp.concatenate([main, beside], 4).reshape(dp * 4, parts, rows + extra, BLOCK)
    mine = lax.psum_scatter(flat, ("dp", "zero"), scatter_dimension=0, tiled=True)
    out = lax.all_gather(mine[0], "dp", axis=0, tiled=False)
    out = out.reshape(8, fine, parts, rows + extra, BLOCK)
    main = out[..., :rows, :].transpose(0, 2, 1, 3, 4).reshape(8, parts, 128, BLOCK)
    out = jnp.concatenate([main, out[:, 0, :, rows:]], 2)
    return out.reshape(8, -1, BLOCK)


def shards(
    dp, images, cotangent, counts, rel_index, regions,
    mat_w, mat_m, mat_v, vec_w, vec_m, vec_v, tab_w, tab_m, tab_v,
):
    near = dp == 8
    fine = dp // 8
    rows = 128 // fine
    me = lax.axis_index("dp")
    taken_from = jnp.stack([me // fine, me % fine]).astype(jnp.int32)
    spot = [me, lax.axis_index("zero")] if near else [0 * me, 0 * me]
    place = jnp.stack(spot + [counts[0]]).astype(jnp.int32)

    inside = np.arange(CELL) < WIN * WIN
    zones = regions.reshape(2, WIN, 2, WIN).transpose(0, 2, 1, 3).reshape(4, WIN * WIN)
    zones = jnp.pad(zones, ((0, 0), (0, 15)))
    differ = (zones[:, :, None] != zones[:, None, :]) & inside[None, None, :]
    outside = jnp.asarray(np.where(inside, 0.0, -1e30), f32)[None, :, None]
    mask_shifted = jnp.tile(jnp.where(differ, mask_value, 0.0) + outside, (1, 1, QUAD)).astype(f32)
    mask_plain = jnp.broadcast_to(outside, (1, CELL, QUAD * CELL))
    masks = (mask_plain, mask_shifted)
    perms = (frames(False), frames(True))

    packed, cut_mlp0, cut_all1, rel = pack(
        taken_from, rows, mat_w, rel_index, tab_w, vec_w
    )
    alive = (jnp.arange(images.shape[0]) < counts[0]).astype(f32)[:, None, None]
    pad = ((0, 0), (0, ROWS - TOKENS), (0, 0))
    images = jnp.pad(images.astype(f32), pad)
    cotangent = jnp.pad(cotangent.astype(f32) * alive, pad)

    def attention(layer, stream, weight, after):
        return attention_forward(
            layer, place, stream, weight, heads0, masks[layer], perms[layer], after
        )

    half = images.shape[0] // 2
    if near:
        sent_heads0 = send_z(packed)
        *sent_heads0, images = tie([*sent_heads0, images], [])
        z_heads0 = stack(sent_heads0)
        all1 = gather_wide(tie([cut_all1], [z_heads0])[0], dp, 0)
        sent_heads0 = send_plane(z_heads0)
        sent_mlp0 = send_z(tie([cut_mlp0], [z_heads0])[0])
        cotangent, mask_shifted = tie([cotangent, mask_shifted], [z_heads0])
        *sent_heads0, cotangent, mask_shifted = tie(
            [*sent_heads0, cotangent, mask_shifted], sent_mlp0
        )
        masks = (mask_plain, mask_shifted)
        p_heads0 = stack(sent_heads0)
        heads0 = [p_heads0, swap(p_heads0, 1)]
        z_mlp0 = stack(sent_mlp0, [p_heads0])
        sent_mlp0 = send_plane(z_mlp0)
        kept0 = attention(0, images, heads0, [z_mlp0])
        p_mlp0 = stack(sent_mlp0, [kept0[0]])
        mlp0 = [p_mlp0, swap(p_mlp0, 1)]
    else:
        heads0 = gather_wide(packed, dp, EXTRA)
        mlp0 = gather_wide(cut_mlp0, dp, 0)
        all1 = gather_wide(cut_all1, dp, 0)
        kept0 = attention(0, images, heads0, [])
    stream, act, slope = mlp_forward(0, place, kept0[0], mlp0, kept0[5], [])
    kept1 = attention(1, stream, all1, [])
    kept = (kept0, kept1)
    inputs = (images, stream)
    attention_w = (heads0, all1)

    def backward_attention(layer, gradient, small, after, *span):
        mid, qkv, merged, totals, table, vec = kept[layer]
        return attention_backward(
            layer, place, gradient, inputs[layer], qkv, merged, totals, table, attention_w[layer],
            vec, small, perms[layer], rel, after, *span,
        )

    activations, grad_mid, parts_mlp1, small = mlp_both(
        place, cotangent, kept1[0], all1, kept1[5], []
    )

    def backward_mlp0(gradient, after):
        return mlp_backward(0, place, gradient, act, slope, kept0[0], mlp0, kept0[5], after)

    state = (mat_w, mat_m, mat_v)
    def exchange(parts):
        return [parts[0], swap(parts[1], 1)]

    gradient, parts_heads1, _, _ = backward_attention(1, grad_mid, small, [])
    grad_mid, *parts_mlp0, small = backward_mlp0(gradient, [])
    if near:
        t_mlp1 = lax.psum_scatter(parts_mlp1, "dp", scatter_dimension=0, tiled=True)[0]
        parts_heads1 = tie([parts_heads1], [t_mlp1, small])[0]
        t_heads1 = lax.psum_scatter(parts_heads1, "dp", scatter_dimension=0, tiled=True)[0]
        gone_mlp0 = exchange(parts_mlp0)
        gradient, *parts_heads0, pairs, small = backward_attention(0, grad_mid, small, [], 0, half)

        s_mlp0 = add_split(gone_mlp0, [gradient])
        gone_mlp0 = give_plane(s_mlp0)
        gradient, *parts_heads0, _, small = backward_attention(
            0, grad_mid, small, [s_mlp0[0]], half, half, [gradient, *parts_heads0, pairs]
        )

        t_all = join(t_mlp1, t_heads1, gone_mlp0, [small])
        gone_heads0 = exchange(tie(parts_heads0, [t_all]))
        g_all = lax.psum_scatter(t_all, "zero", scatter_dimension=0, tiled=True)[0]
        s_heads0 = add_split(gone_heads0, [t_all])
        gone_heads0 = give_plane(s_heads0)
        across = [activations.transpose(1, 0, 2), gradient.transpose(1, 0, 2)]
        t_heads0 = add_split(gone_heads0, across)
        activations, gradient = [value.transpose(1, 0, 2) for value in across]
        gone_heads0 = give_z(t_heads0)
        g_all, *gone_heads0 = tie([g_all, *gone_heads0], [])
        n_all1 = lax.all_gather(g_all[:400], "dp", axis=0, tiled=False)
        g_all0 = add_last(g_all, gone_heads0, [])
        n_all0 = stack(send_plane(g_all0))
        sums0 = [n_all0, swap(n_all0, 1)]
        m = place[0] ^ np.arange(2)
        both = jnp.concatenate([half[:, 384:] for half in sums0])
        beside0 = [
            lax.dynamic_index_in_dim(both, (m[b] % 2) * 4 + m[b] // 2, 0, False) for b in range(2)
        ]
    else:
        gradient, *parts_heads0, _, _ = backward_attention(0, grad_mid, small, [])
        n_mlp1 = reduce_wide(parts_mlp1, dp, 0)
        n_heads1 = reduce_wide(parts_heads1, dp, SMALL)
        n_all1 = jnp.concatenate([n_mlp1, n_heads1], 1)
        n_mlp0 = reduce_wide(jnp.stack(parts_mlp0, 1), dp, 0)
        n_heads0 = reduce_wide(jnp.stack(parts_heads0, 1), dp, SMALL)
        sums0 = [jnp.concatenate([n_mlp0, n_heads0], 1)]
        beside0 = sums0[0][:2, 384:]
    done = adam(0, 1, place, sums0, state, None, [])
    done = adam(1, 1, place, [n_all1], state, done, [])

    def beside(block):
        return jnp.stack([beside0[block], n_all1[block, 384:]]).astype(f32)

    new_vec = adam_step(vec_w, vec_m, vec_v, beside(1)[:, 0:12, 0:128], rate_vector, 0.0)
    new_tab = adam_step(tab_w, tab_m, tab_v, beside(0)[:, 0:4, 0:NREL], rate_table, 0.0)
    return (activations, gradient, *done, *new_vec, *new_tab)


def solution(mesh):
    images = P(("dp", "zero"), None, None)
    rows = P(None, "zero", None)
    lanes = P(None, None, "zero")
    return jax.shard_map(
        partial(shards, mesh.shape["dp"]),
        mesh=mesh,
        in_specs=(images, images, P(("dp", "zero")), P(), P())
        + (rows,) * 3 + (lanes,) * 3 + (rows,) * 3,
        out_specs=(images, images) + (rows,) * 3 + (lanes,) * 3 + (rows,) * 3,
        check_vma=False,
    )
```

```python
from functools import partial

import jax
import jax.numpy as jnp
import numpy as np
from jax import lax
from jax.experimental import pallas as pl
from jax.experimental.pallas import tpu as pltpu
from jax.sharding import PartitionSpec as P

WIN = 7
SIDE = 14
STEP = 10
NREL = 169
C = 512
HID = 2048
TOKENS = SIDE * SIDE
PAIR = 2
ROWS = 208
FRAME = 256
CELL = 64
QUAD = 4
BLOCK = 256
EXTRA = 32
SMALL = 16

norm_eps = 1e-05
mask_value = -100.0
beta_one = 0.9
beta_two = 0.999
adam_eps = 1e-08
weight_decay = 0.05
rate_matrix = 0.1
rate_vector = 0.5
rate_table = 1.0
scale = 32 ** (-0.5)

bf16 = jnp.bfloat16
f32 = jnp.float32
NN = (((1,), (0,)), ((), ()))
NT = (((1,), (1,)), ((), ()))
TN = (((0,), (0,)), ((), ()))


def mm(left, right, dims=NN):
    return lax.dot_general(left, right, dims, preferred_element_type=f32)


def frames(shifted):
    move = WIN // 2 if shifted else 0
    placed = np.zeros((FRAME, ROWS), np.float32)
    for wy in range(2):
        for wx in range(2):
            for iy in range(WIN):
                for ix in range(WIN):
                    y = (wy * WIN + iy + move) % SIDE
                    x = (wx * WIN + ix + move) % SIDE
                    placed[(wy * 2 + wx) * CELL + iy * WIN + ix, y * SIDE + x] = 1
    return placed


def head_rows():
    rows = np.zeros((QUAD * CELL, 128), np.float32)
    for h in range(QUAD):
        rows[h * CELL : (h + 1) * CELL, h * 32 : (h + 1) * 32] = 1
    return rows


def head_spread(rows):
    out = np.zeros((rows, QUAD * CELL), np.float32)
    for h in range(QUAD):
        out[h, h * CELL : (h + 1) * CELL] = 1
    return out


def norm(rows):
    centred = rows - jnp.mean(rows, -1, keepdims=True)
    spread = lax.rsqrt(jnp.mean(centred * centred, -1, keepdims=True) + norm_eps)
    return centred * spread, spread


def norm_back(grad_unit, unit, spread):
    return spread * (
        grad_unit
        - jnp.mean(grad_unit, -1, keepdims=True)
        - unit * jnp.mean(grad_unit * unit, -1, keepdims=True)
    )


def column_sum(rows):
    return jnp.sum(rows, 0, keepdims=True)


def gelu_pair(u):
    size = jnp.abs(u)
    below = 1.0 + (0.3275911 * 0.5**0.5) * size
    t = pltpu.reciprocal(below, approx=True)
    bell = jnp.exp2(u * u * (-0.5 * 1.4426950408889634))
    poly = t * (
        0.127414796 + t * (-0.142248368 + t * (0.710706871 + t * (-0.726576013 + t * 0.530702714)))
    )
    tail = poly * bell
    phi = jnp.where(u >= 0, 1.0 - tail, tail)
    return u * phi, phi + u * bell * 0.3989422804014327


def quad_rows(part, heads):
    return jnp.concatenate([part] * QUAD, 0) * heads


def pick_heads(stacked, lane_head):
    low = jnp.where(lane_head == 0, stacked[:CELL], stacked[CELL : 2 * CELL])
    high = jnp.where(lane_head == 2, stacked[2 * CELL : 3 * CELL], stacked[3 * CELL :])
    return jnp.where(lane_head < 2, low, high)


def lane_heads():
    return lax.broadcasted_iota(jnp.int32, (CELL, 128), 1) // 32


def whole(shape):
    zero = (0,) * len(shape)
    return pl.BlockSpec(shape, lambda *_: zero, pipeline_mode=pl.Buffered(1))


def per_image(rows, cols):
    return pl.BlockSpec((1, rows, cols), lambda i, *_: (i, 0, 0))


def per_pair(rows, cols):
    return pl.BlockSpec((PAIR, rows, cols), lambda i, *_: (i, 0, 0))


HBM = pl.BlockSpec(memory_space=pl.ANY)


def weight_copies(place, stacks, kept, sems, part=0):
    copies = []
    for m in range(8):
        for s in range(4):
            for p in range(kept.shape[0]):
                if len(stacks) == 1:
                    source, block, owner = stacks[0].at[m, s, part + p], m, s
                else:
                    source = stacks[m % 2].at[m // 2, s, p]
                    block, owner = place[0] ^ m, (place[1] + 4 - s) & 3
                rows = pl.ds(pl.multiple_of(owner * 128, 128), 128)
                cols = pl.ds(pl.multiple_of(block * BLOCK, BLOCK), BLOCK)
                copies.append(
                    pltpu.make_async_copy(
                        source.at[pl.ds(0, 128), :], kept.at[p, rows, cols], sems.at[m, s, p]
                    )
                )
    return copies


def extra_copies(place, stacks, kept, sems):
    copies = []
    for m in range(8):
        for s in range(4):
            if len(stacks) == 1:
                source, block, owner = stacks[0].at[m, s, 0], m, s
            else:
                source = stacks[m % 2].at[m // 2, s, 0]
                block, owner = place[0] ^ m, (place[1] + 4 - s) & 3
            copies.append(
                pltpu.make_async_copy(
                    source.at[pl.ds(128, EXTRA), :], kept.at[block, owner], sems.at[m, s, 0]
                )
            )
    return copies


def start(copies):
    for copy in copies:
        copy.start()


def wait(copies):
    for copy in copies:
        copy.wait()


def call(body, name, grid, ins, outs, out_shapes, scratch, cost_us, prefetch=0, aliases=None):
    return pl.pallas_call(
        body,
        name=name,
        grid_spec=pltpu.PrefetchScalarGridSpec(
            num_scalar_prefetch=prefetch,
            grid=grid,
            in_specs=ins,
            out_specs=outs,
            scratch_shapes=scratch,
        ),
        out_shape=out_shapes,
        input_output_aliases=aliases or {},
        compiler_params=pltpu.CompilerParams(
            dimension_semantics=("arbitrary",) * len(grid), vmem_limit_bytes=58 * 1024 * 1024
        ),
        cost_estimate=pl.CostEstimate(
            flops=0, bytes_accessed=int(cost_us * 3.69e4), transcendentals=0
        ),
    )


def shape(dims, kind):
    return jax.ShapeDtypeStruct(dims, kind)


def pack_body(place, *refs):
    mats, (pair_index, tab, vec, spread) = refs[:6], refs[6:10]
    out, mlp0, all1, rel, spread_tab, small = refs[10:]
    rows = mats[0].shape[1]
    out[0, 0:rows, :] = mats[0][0].astype(bf16)
    for ref, at, n in ((mlp0, 0, 1), (mlp0, 1, 2), (all1, 0, 3), (all1, 1, 4), (all1, 2, 5)):
        ref[at] = mats[n][0].astype(bf16)
    rel[...] = jnp.full(rel.shape, -1, jnp.int32)
    across = pair_index[...].astype(f32).T.astype(jnp.int32)
    for h in range(QUAD):
        rel[0 : WIN * WIN, CELL * h : CELL * h + WIN * WIN] = across
    for layer in range(2):
        spread_tab[layer, 0:NREL, :] = mm(tab[layer].astype(bf16), spread[...], TN)
    pairs = rel[pl.ds(pl.multiple_of(place[0] * 8, 8), 8), :]

    def step(r, sums):
        hit = pairs == r
        return tuple(
            jnp.where(hit, spread_tab[layer, pl.ds(r, 1), :], sums[layer]) for layer in range(2)
        )

    start = jnp.zeros((8, QUAD * CELL), f32)
    first, second = lax.fori_loop(0, NREL, step, (start, start), unroll=13)
    out[0, rows : rows + 16, :] = jnp.concatenate([first, second], 0).astype(bf16)
    small[...] = jnp.zeros_like(small)
    row = jnp.minimum(place[0] * 2, 10)
    for layer in range(2):
        for k in range(2):
            small[k : k + 1, layer * 128 : (layer + 1) * 128] = vec[row + k, layer : layer + 1, :]
    out[0, rows + 16 : rows + 32, :] = small[...].astype(bf16)


def pack(place, rows, mat_w, rel_index, tab_w, vec_w):
    vec_w = vec_w.transpose(1, 0, 2)

    def block(layer, part):
        return pl.BlockSpec(
            (1, rows, BLOCK), lambda i, place: (layer, place[1], part * 8 + place[0])
        )

    dims = [(1, rows + EXTRA, BLOCK), (2, rows, BLOCK), (3, rows, BLOCK)]
    return call(
        pack_body,
        "pack",
        (1,),
        [block(layer, part) for layer in range(2) for part in range(3)]
        + [
            whole(rel_index.shape),
            whole(tab_w.shape),
            whole(vec_w.shape),
            whole((QUAD, QUAD * CELL)),
        ],
        [whole(d) for d in dims] + [whole((CELL, QUAD * CELL))],
        [shape(d, bf16) for d in dims] + [shape((CELL, QUAD * CELL), jnp.int32)],
        [pltpu.VMEM((2, 176, QUAD * CELL), f32), pltpu.VMEM((16, 256), f32)],
        4,
        prefetch=1,
    )(place, *[mat_w] * 6, rel_index, tab_w, vec_w, jnp.asarray(head_spread(QUAD), bf16))


def attention_forward_body(layer, stacks, waits, place, *refs):
    arrays, refs = refs[: stacks[0]], refs[stacks[0] :]
    extras, refs = refs[: stacks[1]], refs[stacks[1] + waits :]
    x, mask, perm, perm_back, heads = refs[:5]
    mid, qkv, merged, totals, table, vec, framed, kept, extra_kept, sems, more_sems = refs[5:]
    weight, extra = kept.at[0], extra_kept

    @pl.when(pl.program_id(0) == 0)
    def _():
        start(extra_copies(place, extras, extra_kept, more_sems))
        start(weight_copies(place, arrays, kept, sems))
        wait(extra_copies(place, extras, extra_kept, more_sems))
        vec[...] = jnp.zeros_like(vec)
        for z in range(4):
            for d in range(8):
                pair = extra[d, z, 0:16, :].astype(f32)
                bias = pair[8 * layer : 8 * layer + 8]
                for w in range(table.shape[0]):
                    table[w, z, 8 * d : 8 * d + 8, :] = bias + mask[w, 8 * d : 8 * d + 8, :]
                if d < 6:
                    rows = extra[d, z, 16:32, 128 * layer : 128 * layer + 128].astype(f32)
                    vec[2 * d : 2 * d + 2, 128 * z : 128 * z + 128] = rows[0:2]

    stream = x[0]
    unit, _ = norm(stream)
    normed = (unit * vec[0:1, :] + vec[1:2, :]).astype(bf16)
    normed = mm(perm[...], normed).astype(bf16)

    @pl.when(pl.program_id(0) == 0)
    def _():
        wait(weight_copies(place, arrays, kept, sems))

    for c in range(6):
        part = mm(normed, weight[:, 256 * c : 256 * c + 256])
        if c < 2:
            part = part + vec[2:3, 256 * c : 256 * c + 256]
        if c >= 4:
            part = part + vec[3:4, 256 * (c - 4) : 256 * (c - 4) + 256]
        qkv[0, :, 256 * c : 256 * c + 256] = part.astype(bf16)
    lane_head = lane_heads()

    at = [128 * g for g in range(4)]

    def window(w):
        rows = slice(CELL * w, CELL * w + CELL)
        query = [quad_rows(qkv[0, rows, c : c + 128], heads[...]) for c in at]
        return [mm(qkv[0, rows, C + at[g] : C + at[g] + 128], query[g], NT) for g in range(4)]

    ahead = window(0)
    for w in range(4):
        rows = slice(CELL * w, CELL * w + CELL)
        scores = ahead
        if w < 3:
            ahead = window(w + 1)
        probs = []
        for g in range(4):
            shifted = scores[g] * scale + table[w % table.shape[0], g]
            top = jnp.max(shifted, 0, keepdims=True)
            raised = jnp.exp(shifted - top)
            total = jnp.sum(raised, 0, keepdims=True)
            totals[0, 4 * w + g : 4 * w + g + 1, :] = top + jnp.log(total)
            probs.append((raised * (1.0 / total)).astype(bf16))
        stacked = [mm(probs[g], qkv[0, rows, 2 * C + at[g] : 2 * C + at[g] + 128], TN) for g in range(4)]
        for g in range(4):
            framed[rows, at[g] : at[g] + 128] = pick_heads(stacked[g], lane_head).astype(bf16)
    gathered = mm(perm_back[...], framed[...]).astype(bf16)
    merged[0] = gathered
    mid[0] = stream + mm(gathered, weight[:, 3 * C :]) + vec[4:5, :]


def attention_forward(layer, place, x, weight, extra, mask, perm, after):
    images = x.shape[0]
    tables = mask.shape[0]
    return call(
        partial(attention_forward_body, layer, (len(weight), len(extra)), len(after)),
        f"attention_forward_{layer}",
        (images,),
        [HBM] * (len(weight) + len(extra) + len(after))
        + [
            per_image(x.shape[1], C),
            whole(mask.shape),
            whole((FRAME, ROWS)),
            whole((ROWS, FRAME)),
            whole((QUAD * CELL, 128)),
        ],
        [
            per_image(ROWS, C),
            per_image(FRAME, 3 * C),
            per_image(ROWS, C),
            per_image(16, QUAD * CELL),
            pl.BlockSpec((tables, 4, CELL, QUAD * CELL), lambda i, *_: (0, 0, 0, 0)),
            pl.BlockSpec((16, C), lambda i, *_: (0, 0)),
        ],
        [
            shape((images, ROWS, C), f32),
            shape((images, FRAME, 3 * C), bf16),
            shape((images, ROWS, C), bf16),
            shape((images, 16, QUAD * CELL), f32),
            shape((tables, 4, CELL, QUAD * CELL), f32),
            shape((16, C), f32),
        ],
        [
            pltpu.VMEM((FRAME, C), bf16),
            pltpu.VMEM((1, C, HID), bf16),
            pltpu.VMEM((8, 4, EXTRA, BLOCK), bf16),
            pltpu.SemaphoreType.DMA((8, 4, 1)),
            pltpu.SemaphoreType.DMA((8, 4, 1)),
        ],
        20,
        prefetch=1,
    )(
        place,
        *weight,
        *extra,
        *after,
        x,
        mask,
        jnp.asarray(perm, bf16),
        jnp.asarray(perm.T, bf16),
        jnp.asarray(head_rows(), bf16),
    )


def mlp_forward_body(stacks, waits, place, *refs):
    arrays, refs = refs[:stacks], refs[stacks + waits :]
    mid, vec, result, act, slope, kept, sems = refs
    first, second = kept.at[0], kept.at[1]

    @pl.when(pl.program_id(0) == 0)
    def _():
        start(weight_copies(place, arrays, kept, sems))

    rows = PAIR * ROWS
    stream = mid[...].reshape(rows, C)
    unit, _ = norm(stream)
    normed = (unit * vec[5:6, :] + vec[6:7, :]).astype(bf16)

    @pl.when(pl.program_id(0) == 0)
    def _():
        wait(weight_copies(place, arrays, kept, sems))

    ahead = mm(normed, first[:, 0:BLOCK])
    for c in range(8):
        cols = slice(256 * c, 256 * c + 256)
        bias = vec[8 + c // 2 : 9 + c // 2, 256 * (c % 2) : 256 * (c % 2) + 256]
        inner = ahead + bias
        if c < 7:
            ahead = mm(normed, first[:, 256 * c + 256 : 256 * c + 512])
        value, pull = gelu_pair(inner)
        act[:, :, cols] = value.astype(bf16).reshape(PAIR, ROWS, BLOCK)
        slope[:, :, cols] = pull.astype(bf16).reshape(PAIR, ROWS, BLOCK)
    total = stream + vec[7:8, :] + mm(act[...].reshape(rows, HID), second[...], NT)
    result[...] = total.reshape(PAIR, ROWS, C)


def mlp_forward(layer, place, mid, weight, vec, after):
    images = mid.shape[0]
    return call(
        partial(mlp_forward_body, len(weight), len(after)),
        f"mlp_forward_{layer}",
        (images // PAIR,),
        [HBM] * (len(weight) + len(after)) + [per_pair(ROWS, C), whole(vec.shape)],
        [per_pair(ROWS, C), per_pair(ROWS, HID), per_pair(ROWS, HID)],
        [
            shape((images, ROWS, C), f32),
            shape((images, ROWS, HID), bf16),
            shape((images, ROWS, HID), bf16),
        ],
        [
            pltpu.VMEM((2, C, HID), bf16),
            pltpu.SemaphoreType.DMA((8, 4, 2)),
        ],
        22,
        prefetch=1,
    )(place, *weight, *after, mid, vec)


def mlp_both_body(stacks, waits, place, *refs):
    arrays, refs = refs[:stacks], refs[stacks + waits :]
    grad, mid, vec, result, grad_mid, pieces, small = refs[:7]
    all_grad, all_act, all_inner, all_normed, kept, sems = refs[7:]
    first, second = kept.at[0], kept.at[1]
    i = pl.program_id(0)

    @pl.when(i == 0)
    def _():
        start(weight_copies(place, arrays, kept, sems, 1))
        small[...] = jnp.zeros_like(small)

    rows = PAIR * ROWS
    grad_out = grad[...].reshape(rows, C)
    here = pl.ds(pl.multiple_of(i * rows, 32), rows)
    low = grad_out.astype(bf16)
    all_grad[here, :] = low
    small[7:8, :] += column_sum(grad_out)
    stream = mid[...].reshape(rows, C)
    unit, spread = norm(stream)
    normed = (unit * vec[5:6, :] + vec[6:7, :]).astype(bf16)
    all_normed[here, :] = normed

    @pl.when(i == 0)
    def _():
        wait(weight_copies(place, arrays, kept, sems, 1))

    ahead = mm(normed, first[:, 0:BLOCK]), mm(low, second[:, 0:BLOCK])
    for c in range(8):
        cols = slice(256 * c, 256 * c + 256)
        row, lane = 8 + c // 2, 256 * (c % 2)
        bias = vec[row : row + 1, lane : lane + 256]
        inner, grad_act = ahead
        if c < 7:
            later = slice(256 * c + 256, 256 * c + 512)
            ahead = mm(normed, first[:, later]), mm(low, second[:, later])
        value, pull = gelu_pair(inner + bias)
        all_act[here, cols] = value.astype(bf16)
        inner = (grad_act * pull).astype(bf16)
        all_inner[here, cols] = inner
        small[row : row + 1, lane : lane + 256] += column_sum(inner.astype(f32))
    back = mm(all_inner[here, :], first[...], NT)
    small[5:6, :] += column_sum(back * unit)
    small[6:7, :] += column_sum(back)
    grad_mid[...] = (grad_out + norm_back(back * vec[5:6, :], unit, spread)).reshape(PAIR, ROWS, C)
    total = stream + vec[7:8, :] + mm(all_act[here, :], second[...], NT)
    for n in range(PAIR):
        alive = (i * PAIR + n < place[2]).astype(f32)
        result[n] = (total[n * ROWS : n * ROWS + TOKENS] * alive).astype(bf16)

    @pl.when(i == pl.num_programs(0) - 1)
    def _():
        mlp_weight_grads(place, all_grad, all_act, all_inner, all_normed, pieces)


def mlp_weight_grads(place, all_grad, all_act, all_inner, all_normed, *outs):
    grad_across = all_grad[...].T
    normed_across = all_normed[...].T
    for m in range(8):
        block = m if len(outs) == 1 else place[0] ^ m
        cols = pl.ds(pl.multiple_of(block * BLOCK, BLOCK), BLOCK)
        for p, total in enumerate(
            (mm(normed_across, all_inner[:, cols]), mm(grad_across, all_act[:, cols]))
        ):
            total = total.astype(bf16)
            for z in range(4):
                if len(outs) == 1:
                    outs[0][m, z, p] = total[128 * z : 128 * z + 128]
                else:
                    outs[m % 2][m // 2, z, p] = total[128 * z : 128 * z + 128]


def mlp_both(place, grad, mid, weight, vec, after):
    images = mid.shape[0]
    total = images * ROWS
    pieces = (8, 4, 2, 128, BLOCK)
    return call(
        partial(mlp_both_body, len(weight), len(after)),
        "mlp_both",
        (images // PAIR,),
        [HBM] * (len(weight) + len(after)) + [per_pair(ROWS, C), per_pair(ROWS, C), whole(vec.shape)],
        [per_pair(TOKENS, C), per_pair(ROWS, C), whole(pieces), whole((16, C))],
        [
            shape((images, TOKENS, C), bf16),
            shape((images, ROWS, C), f32),
            shape(pieces, bf16),
            shape((16, C), f32),
        ],
        [
            pltpu.VMEM((total, C), bf16),
            pltpu.VMEM((total, HID), bf16),
            pltpu.VMEM((total, HID), bf16),
            pltpu.VMEM((total, C), bf16),
            pltpu.VMEM((2, C, HID), bf16),
            pltpu.SemaphoreType.DMA((8, 4, 2)),
        ],
        45,
        prefetch=1,
    )(place, *weight, *after, grad, mid, vec)


def mlp_backward_body(stacks, waits, place, *refs):
    arrays, refs = refs[:stacks], refs[stacks + waits :]
    grad, act, slope, mid, vec, grad_mid, own, other, small = refs[:9]
    all_grad, all_act, all_inner, all_normed, kept, sems = refs[9:]
    first, second = kept.at[0], kept.at[1]
    i = pl.program_id(0)

    @pl.when(i == 0)
    def _():
        start(weight_copies(place, arrays, kept, sems))
        small[...] = jnp.zeros_like(small)

    rows = PAIR * ROWS
    grad_out = grad[...].reshape(rows, C)
    here = pl.ds(pl.multiple_of(i * rows, 32), rows)
    low = grad_out.astype(bf16)
    all_grad[here, :] = low
    small[7:8, :] += column_sum(low.astype(f32))
    all_act[here, :] = act[...].reshape(rows, HID)
    unit, spread = norm(mid[...].reshape(rows, C))
    all_normed[here, :] = (unit * vec[5:6, :] + vec[6:7, :]).astype(bf16)

    @pl.when(i == 0)
    def _():
        wait(weight_copies(place, arrays, kept, sems))

    ahead = mm(low, second[:, 0:BLOCK])
    for c in range(8):
        cols = slice(256 * c, 256 * c + 256)
        pull = slope[:, :, cols].reshape(rows, BLOCK).astype(f32)
        grad_act = ahead
        if c < 7:
            ahead = mm(low, second[:, 256 * c + 256 : 256 * c + 512])
        inner = (grad_act * pull).astype(bf16)
        all_inner[here, cols] = inner
        row, lane = 8 + c // 2, 256 * (c % 2)
        small[row : row + 1, lane : lane + 256] += column_sum(inner.astype(f32))
    back = mm(all_inner[here, :], first[...], NT)
    small[5:6, :] += column_sum(back * unit)
    small[6:7, :] += column_sum(back)
    grad_mid[...] = (grad_out + norm_back(back * vec[5:6, :], unit, spread)).reshape(PAIR, ROWS, C)

    @pl.when(i == pl.num_programs(0) - 1)
    def _():
        mlp_weight_grads(place, all_grad, all_act, all_inner, all_normed, own, other)


def mlp_backward(layer, place, grad, act, slope, mid, weight, vec, after):
    images = mid.shape[0]
    total = images * ROWS
    pieces = (4, 4, 2, 128, BLOCK)
    return call(
        partial(mlp_backward_body, len(weight), len(after)),
        f"mlp_backward_{layer}",
        (images // PAIR,),
        [HBM] * (len(weight) + len(after))
        + [
            per_pair(grad.shape[1], C),
            per_pair(ROWS, HID),
            per_pair(ROWS, HID),
            per_pair(ROWS, C),
            whole(vec.shape),
        ],
        [per_pair(ROWS, C), whole(pieces), whole(pieces), whole((16, C))],
        [
            shape((images, ROWS, C), f32),
            shape(pieces, bf16),
            shape(pieces, bf16),
            shape((16, C), f32),
        ],
        [
            pltpu.VMEM((total, C), bf16),
            pltpu.VMEM((total, HID), bf16),
            pltpu.VMEM((total, HID), bf16),
            pltpu.VMEM((total, C), bf16),
            pltpu.VMEM((2, C, HID), bf16),
            pltpu.SemaphoreType.DMA((8, 4, 2)),
        ],
        30,
        prefetch=1,
    )(place, *weight, *after, grad, act, slope, mid, vec)


def attention_backward_body(layer, stacks, waits, resumed, ends, place, *refs):
    arrays, refs = refs[:stacks], refs[stacks + waits :]
    if resumed:
        (own_before, other_before, pairs_before), refs = refs[1:4], refs[4:]
    grad, x, qkv, merged, totals, table, vec, before = refs[:8]
    perm, perm_back, heads, rel, spread, result = refs[8:14]
    outs, refs = (refs[14:15], refs[15:]) if layer else (refs[14:16], refs[16:])
    pairs, small, framed, grad_framed, all_normed, all_packed, all_merged = refs[:7]
    across, hits, beside, kept, sems = refs[7:]
    weight = kept.at[0]
    i = pl.program_id(0)

    @pl.when(i == 0)
    def _():
        start(weight_copies(place, arrays, kept, sems))
        small[...] = before[...]
        pairs[...] = pairs_before[...] if resumed else jnp.zeros_like(pairs)

    stream = x[0]
    here = pl.ds(pl.multiple_of(i * ROWS, 16), ROWS)
    unit, spread_one = norm(stream)
    all_normed[here, :] = (unit * vec[0:1, :] + vec[1:2, :]).astype(bf16)
    low = grad[0].astype(bf16)
    all_packed[here, 3 * C :] = low
    all_merged[here, :] = merged[0]
    small[4:5, :] += column_sum(low.astype(f32))
    moved = mm(perm[...], low).astype(bf16)

    @pl.when(i == 0)
    def _():
        wait(weight_copies(place, arrays, kept, sems))

    framed[...] = mm(moved, weight[:, 3 * C :], NT).astype(bf16)
    lane_head = lane_heads()
    at = [128 * g for g in range(4)]

    def window(w):
        rows = slice(CELL * w, CELL * w + CELL)
        keys = [qkv[0, rows, C + c : C + c + 128] for c in at]
        query = [quad_rows(qkv[0, rows, c : c + 128], heads[...]) for c in at]
        pull = [quad_rows(framed[rows, c : c + 128], heads[...]) for c in at]
        scores = [mm(keys[g], query[g], NT) for g in range(4)]
        grad_probs = [
            mm(qkv[0, rows, 2 * C + at[g] : 2 * C + at[g] + 128], pull[g], NT) for g in range(4)
        ]
        return keys, query, pull, scores, grad_probs

    ahead = window(0)
    for w in range(4):
        rows = slice(CELL * w, CELL * w + CELL)
        keys, query, pull, scores, grad_probs = ahead
        if w < 3:
            ahead = window(w + 1)
        probs, grad_scores = [], []
        for g in range(4):
            shifted = scores[g] * scale + table[w % table.shape[0], g]
            prob = jnp.exp(shifted - totals[0, 4 * w + g : 4 * w + g + 1, :])
            mean = jnp.sum(prob * grad_probs[g], 0, keepdims=True)
            grad_score = (prob * (grad_probs[g] - mean)).astype(bf16)
            pairs[g] += grad_score.astype(f32)
            probs.append(prob.astype(bf16))
            grad_scores.append(grad_score)
        for g in range(4):
            grad_value = mm(probs[g], pull[g])
            grad_framed[rows, 2 * C + at[g] : 2 * C + at[g] + 128] = grad_value.astype(bf16)
        for g in range(4):
            grad_key = mm(grad_scores[g], query[g]) * scale
            grad_framed[rows, C + at[g] : C + at[g] + 128] = grad_key.astype(bf16)
        for g in range(4):
            grad_query = pick_heads(mm(grad_scores[g], keys[g], TN), lane_head) * scale
            grad_framed[rows, at[g] : at[g] + 128] = grad_query.astype(bf16)
    for c in range(6):
        cols = slice(256 * c, 256 * c + 256)
        part = mm(perm_back[...], grad_framed[:, cols])
        all_packed[here, cols] = part.astype(bf16)
        if c < 2:
            small[2:3, cols] += column_sum(part)
        if c >= 4:
            small[3:4, 256 * (c - 4) : 256 * (c - 4) + 256] += column_sum(part)
    back = mm(all_packed[here, : 3 * C], weight[:, : 3 * C], NT)
    small[0:1, :] += column_sum(back * unit)
    small[1:2, :] += column_sum(back)
    total = grad[0] + norm_back(back * vec[0:1, :], unit, spread_one)
    result[0] = total[: result.shape[1]]

    @pl.when(i == pl.num_programs(0) - 1)
    def _():
        across[0] = all_normed[...].T
        across[1] = all_merged[...].T
        beside[...] = jnp.zeros_like(beside)
        if ends:
            hits[...] = jnp.zeros_like(hits)

            def step(r, carry):
                same = rel[...] == r
                for g in range(4):
                    kept_pairs = jnp.where(same, pairs[g], 0.0)
                    hits[pl.ds(r, 1), 256 * g : 256 * g + 256] = column_sum(kept_pairs)
                return carry

            lax.fori_loop(0, NREL, step, 0)
            for z in range(4):
                beside[0, z] = lax.dot_general(
                    spread[...],
                    hits[:, 256 * z : 256 * z + 256],
                    NT,
                    precision=lax.Precision.HIGHEST,
                    preferred_element_type=f32,
                ).astype(bf16)
                beside[1, z, :, 0:128] = small[:, 128 * z : 128 * z + 128].astype(bf16)
        for m in range(8):
            b = m if layer else place[0] ^ m
            left = across[jnp.where(b < 6, 0, 1)]
            right = all_packed[:, pl.ds(pl.multiple_of(b * BLOCK, BLOCK), BLOCK)]
            block = mm(left, right)
            for z in range(4):
                if layer:
                    out = outs[0].at[m, z, 0]
                else:
                    to = (z + 4 - place[1]) & 3
                    out = outs[m % 2].at[m // 2, to, 0]
                new = block[128 * z : 128 * z + 128]
                if resumed:
                    old = other_before if m % 2 else own_before
                    new = new + old[m // 2, to, 0, 0:128, :].astype(f32)
                out[0:128, :] = new.astype(bf16)
                out[128:144, :] = beside[jnp.minimum(b, 2), z]


def attention_backward(
    layer, place, grad, x, qkv, merged, totals, table, weight, vec, small, perm, rel, after,
    first=0, count=None, resume=None,
):
    images = grad.shape[0]
    count = count or images
    pieces = (8 if layer else 4, 4, 1, 128 + SMALL, BLOCK)
    pairs = (4, CELL, QUAD * CELL)
    total = count * ROWS
    out_rows = TOKENS if layer == 0 else ROWS

    def image(rows, cols):
        return pl.BlockSpec((1, rows, cols), lambda i, *_: (i + first, 0, 0))

    resumed = list(resume or [])
    return call(
        partial(
            attention_backward_body, layer, len(weight), len(after), bool(resumed),
            first + count == images,
        ),
        f"attention_backward_{layer}_{first}",
        (count,),
        [HBM] * (len(weight) + len(after))
        + ([HBM, whole(pieces), whole(pieces), whole(pairs)] if resumed else [])
        + [
            image(ROWS, C),
            image(x.shape[1], C),
            image(FRAME, 3 * C),
            image(ROWS, C),
            image(16, QUAD * CELL),
            whole(table.shape),
            whole(vec.shape),
            whole((16, C)),
            whole((FRAME, ROWS)),
            whole((ROWS, FRAME)),
            whole((QUAD * CELL, 128)),
            whole(rel.shape),
            whole((SMALL, QUAD * CELL)),
        ],
        [image(out_rows, C)]
        + [whole(pieces)] * (1 if layer else 2)
        + [whole(pairs), whole((16, C))],
        [shape((images, out_rows, C), f32)]
        + [shape(pieces, bf16)] * (1 if layer else 2)
        + [shape(pairs, f32), shape((16, C), f32)],
        [
            pltpu.VMEM((FRAME, C), bf16),
            pltpu.VMEM((FRAME, 3 * C), bf16),
            pltpu.VMEM((total, C), bf16),
            pltpu.VMEM((total, 4 * C), bf16),
            pltpu.VMEM((total, C), bf16),
            pltpu.VMEM((2, C, total), bf16),
            pltpu.VMEM((256, 4 * QUAD * CELL), f32),
            pltpu.VMEM((3, 4, SMALL, BLOCK), bf16),
            pltpu.VMEM((1, C, HID), bf16),
            pltpu.SemaphoreType.DMA((8, 4, 1)),
        ],
        6 * count,
        prefetch=1,
        aliases={1 + len(weight) + len(after): 0} if resumed else None,
    )(
        place,
        *weight,
        *after,
        *resumed,
        grad,
        x,
        qkv,
        merged,
        totals,
        table,
        vec,
        small,
        jnp.asarray(perm, bf16),
        jnp.asarray(perm.T, bf16),
        jnp.asarray(head_rows(), bf16),
        rel,
        jnp.asarray(head_spread(SMALL), f32),
    )


def adam_step(weight, first, second, gradient, rate, decay):
    first_new = beta_one * first + (1.0 - beta_one) * gradient
    second_new = beta_two * second + (1.0 - beta_two) * gradient * gradient
    first_hat = first_new / (1.0 - beta_one**STEP)
    second_hat = second_new / (1.0 - beta_two**STEP)
    weight_new = weight - rate * (first_hat / (jnp.sqrt(second_hat) + adam_eps) + decay * weight)
    return (weight_new, first_new, second_new)


def adam_block(grad, weight, first, second, outs, cols):
    part = grad.astype(f32)
    first_new = beta_one * first[0, :, cols] + (1.0 - beta_one) * part
    second_new = beta_two * second[0, :, cols] + (1.0 - beta_two) * part * part
    spread = second_new * (1.0 / (1.0 - beta_two**STEP))
    inverse = pltpu.reciprocal(spread * lax.rsqrt(spread) + adam_eps, approx=True)
    step = first_new * (rate_matrix / (1.0 - beta_one**STEP)) * inverse
    outs[0][0, :, cols] = weight[0, :, cols] * (1.0 - rate_matrix * weight_decay) - step
    outs[1][0, :, cols] = first_new
    outs[2][0, :, cols] = second_new


def adam_body(place, near, far, weight, first, second, *refs):
    for j in range(2):
        for k in range(2):
            block = (((place[0] // 2) & 1) ^ j) * 2 + ((place[0] & 1) ^ k)
            cols = pl.ds(pl.multiple_of(block * BLOCK, BLOCK), BLOCK)
            adam_block((far if k else near)[j], weight, first, second, refs[-3:], cols)


def adam_body_plain(place, sums, weight, first, second, *refs):
    for k in range(4):
        cols = slice(BLOCK * k, BLOCK * k + BLOCK)
        adam_block(sums[k], weight, first, second, refs[-3:], cols)


def adam(layer, part, place, sums, state, done, after):
    kept = [] if done is None else list(done)
    if len(sums) == 2:
        parts = sums[0].shape[1] // 128
        body = adam_body
        spec = pl.BlockSpec(
            (1, 128, 4 * BLOCK),
            lambda p, j, place: (layer, 0, (part + p) % 3 * 2 + ((place[0] // 4) ^ j)),
        )
        piece = pl.BlockSpec((2, 128, BLOCK), lambda p, j, place: (j, p, 0))
    else:
        parts = sums[0].shape[1] // 128
        body = adam_body_plain
        spec = pl.BlockSpec(
            (1, 128, 4 * BLOCK), lambda p, j, place: (layer, 0, (part + p) % 3 * 2 + j)
        )
        piece = pl.BlockSpec((4, 128, BLOCK), lambda p, j, place: (j, p, 0))
    return call(
        body,
        f"adam_{layer}_{part}",
        (parts, 2),
        [piece] * len(sums) + [spec] * 3 + [HBM] * (len(kept) + len(after)),
        [spec] * 3,
        [shape(state[0].shape, f32)] * 3,
        [],
        3 * parts,
        prefetch=1,
        aliases={4 + len(sums) + k: k for k in range(len(kept))},
    )(place, *sums, *state, *kept, *after)


def swap(value, bits):
    return lax.ppermute(value, "dp", [(i, i ^ bits) for i in range(8)])


def shift(value, steps):
    return lax.ppermute(value, "zero", [(i, (i + steps) % 4) for i in range(4)])


def tie(values, after):
    values = list(values)
    return list(lax.optimization_barrier((*values, *after))[: len(values)])


def stack(values, after=()):
    return jnp.stack(tie(values, after) if after else values)


def add_body(count, *refs):
    total = refs[0][...].astype(f32)
    for k in range(1, count):
        total = total + refs[k][...].astype(f32)
    refs[-1][...] = total.astype(bf16)


def add(values, after=()):
    dims = values[0].shape
    return call(
        partial(add_body, len(values)),
        "add",
        (1,),
        [whole(dims)] * len(values) + [HBM] * len(after),
        whole(dims),
        shape(dims, bf16),
        [],
        10,
    )(*values, *after)


def add_split_body(count, lead, *refs):
    for k in range(4):
        if count == 2:
            refs[len(refs) - 4 + k][...] = refs[0][k] + refs[1][k]
            continue
        total = refs[0][k].astype(f32)
        for v in range(1, count):
            total = total + refs[v][k].astype(f32)
        refs[len(refs) - 4 + k][...] = total.astype(bf16)


def add_split(values, after=()):
    dims = values[0].shape
    steps = dims[1] if len(dims) == 5 else 1
    ins = (4, dims[1] // steps, *dims[2:])
    outs = dims[1:]
    zeros = (0,) * (len(dims) - 2)
    return call(
        partial(add_split_body, len(values), True),
        "add_split",
        (steps,),
        [pl.BlockSpec(ins, lambda i: (0, i, *zeros))] * len(values) + [HBM] * len(after),
        [pl.BlockSpec((outs[0] // steps, *outs[1:]), lambda i: (i, *zeros))] * 4,
        [shape(outs, bf16)] * 4,
        [],
        10,
    )(*values, *after)


def join_body(*refs):
    out = refs[-1]
    at = 0
    for group in (refs[:1], refs[1:2], refs[2:6]):
        parts, rows = group[0].shape[1:3]
        for p in range(parts):
            total = group[0][0, p]
            if len(group) > 1:
                total = total.astype(f32)
                for ref in group[1:]:
                    total = total + ref[0, p].astype(f32)
            out[0, at : at + rows, :] = total.astype(bf16)
            at += rows


def join(first, second, summed, after):
    rows = sum(value.shape[1] * value.shape[2] for value in (first, second, summed[0]))

    def spec(value):
        return pl.BlockSpec((1, *value.shape[1:]), lambda i: (i, 0, 0, 0))

    ins = [first, second, *summed]
    return call(
        join_body,
        "join",
        (4,),
        [spec(v) for v in ins] + [HBM] * len(after),
        pl.BlockSpec((1, rows, BLOCK), lambda i: (i, 0, 0)),
        shape((4, rows, BLOCK), bf16),
        [],
        5,
    )(*ins, *after)


def add_last_body(*refs):
    done, out = refs[0], refs[-1]
    rows = 256
    out[0:rows, :] = done[done.shape[0] - rows :, :]
    total = refs[1][0].astype(f32)
    for ref in refs[2:5]:
        total = total + ref[0].astype(f32)
    out[rows : rows + total.shape[0], :] = total.astype(bf16)


def add_last(done, values, after):
    rows = 256 + values[0].shape[1]
    return call(
        add_last_body,
        "add_last",
        (1,),
        [whole(done.shape)] + [whole(v.shape) for v in values] + [HBM] * len(after),
        whole((rows, BLOCK)),
        shape((rows, BLOCK), bf16),
        [],
        10,
    )(done, *values, *after)


def send_z(piece):
    return [piece] + [shift(piece, s) for s in range(1, 4)]


def send_plane(piece):
    return [piece] + [swap(piece, 2 * j) for j in range(1, 4)]


def give_plane(parts):
    return [parts[0]] + [swap(parts[j], 2 * j) for j in range(1, 4)]


def give_z(parts):
    return [parts[0]] + [shift(parts[s], s) for s in range(1, 4)]


def gather_wide(piece, dp, extra):
    fine = dp // 8
    parts, rows = piece.shape[0], piece.shape[1] - extra
    out = lax.all_gather(piece, ("dp", "zero"), axis=0, tiled=False)
    out = out.reshape(8, fine, 4, *piece.shape)
    main = out[..., :rows, :].transpose(0, 2, 3, 1, 4, 5).reshape(8, 4, parts, 128, BLOCK)
    return [jnp.concatenate([main, out[:, 0, ..., rows:, :]], 3)]


def reduce_wide(blocks, dp, extra):
    fine = dp // 8
    blocks = blocks.reshape(8, 4, *blocks.shape[-3:])
    parts, rows = blocks.shape[2], 128 // fine
    main = blocks[..., :128, :].reshape(8, 4, parts, fine, rows, BLOCK).transpose(0, 3, 1, 2, 4, 5)
    beside = jnp.broadcast_to(
        blocks[:, None, ..., 128:, :], (8, fine, 4, parts, extra, BLOCK)
    )
    flat = jnp.concatenate([main, beside], 4).reshape(dp * 4, parts, rows + extra, BLOCK)
    mine = lax.psum_scatter(flat, ("dp", "zero"), scatter_dimension=0, tiled=True)
    out = lax.all_gather(mine[0], "dp", axis=0, tiled=False)
    out = out.reshape(8, fine, parts, rows + extra, BLOCK)
    main = out[..., :rows, :].transpose(0, 2, 1, 3, 4).reshape(8, parts, 128, BLOCK)
    out = jnp.concatenate([main, out[:, 0, :, rows:]], 2)
    return out.reshape(8, -1, BLOCK)


def shards(
    dp, images, cotangent, counts, rel_index, regions,
    mat_w, mat_m, mat_v, vec_w, vec_m, vec_v, tab_w, tab_m, tab_v,
):
    near = dp == 8
    fine = dp // 8
    rows = 128 // fine
    me = lax.axis_index("dp")
    taken_from = jnp.stack([me // fine, me % fine]).astype(jnp.int32)
    spot = [me, lax.axis_index("zero")] if near else [0 * me, 0 * me]
    place = jnp.stack(spot + [counts[0]]).astype(jnp.int32)

    inside = np.arange(CELL) < WIN * WIN
    zones = regions.reshape(2, WIN, 2, WIN).transpose(0, 2, 1, 3).reshape(4, WIN * WIN)
    zones = jnp.pad(zones, ((0, 0), (0, 15)))
    differ = (zones[:, :, None] != zones[:, None, :]) & inside[None, None, :]
    outside = jnp.asarray(np.where(inside, 0.0, -1e30), f32)[None, :, None]
    mask_shifted = jnp.tile(jnp.where(differ, mask_value, 0.0) + outside, (1, 1, QUAD)).astype(f32)
    mask_plain = jnp.broadcast_to(outside, (1, CELL, QUAD * CELL))
    masks = (mask_plain, mask_shifted)
    perms = (frames(False), frames(True))

    packed, cut_mlp0, cut_all1, rel = pack(
        taken_from, rows, mat_w, rel_index, tab_w, vec_w
    )
    alive = (jnp.arange(images.shape[0]) < counts[0]).astype(f32)[:, None, None]
    pad = ((0, 0), (0, ROWS - TOKENS), (0, 0))
    images = jnp.pad(images.astype(f32), pad)
    cotangent = jnp.pad(cotangent.astype(f32) * alive, pad)

    def attention(layer, stream, weight, after):
        return attention_forward(
            layer, place, stream, weight, heads0, masks[layer], perms[layer], after
        )

    half = images.shape[0] // 2
    if near:
        sent_heads0 = send_z(packed)
        *sent_heads0, images = tie([*sent_heads0, images], [])
        z_heads0 = stack(sent_heads0)
        all1 = gather_wide(tie([cut_all1], [z_heads0])[0], dp, 0)
        sent_heads0 = send_plane(z_heads0)
        sent_mlp0 = send_z(tie([cut_mlp0], [z_heads0])[0])
        cotangent, mask_shifted = tie([cotangent, mask_shifted], [z_heads0])
        *sent_heads0, cotangent, mask_shifted = tie(
            [*sent_heads0, cotangent, mask_shifted], sent_mlp0
        )
        masks = (mask_plain, mask_shifted)
        p_heads0 = stack(sent_heads0)
        heads0 = [p_heads0, swap(p_heads0, 1)]
        z_mlp0 = stack(sent_mlp0, [p_heads0])
        sent_mlp0 = send_plane(z_mlp0)
        kept0 = attention(0, images, heads0, [z_mlp0])
        p_mlp0 = stack(sent_mlp0, [kept0[0]])
        mlp0 = [p_mlp0, swap(p_mlp0, 1)]
    else:
        heads0 = gather_wide(packed, dp, EXTRA)
        mlp0 = gather_wide(cut_mlp0, dp, 0)
        all1 = gather_wide(cut_all1, dp, 0)
        kept0 = attention(0, images, heads0, [])
    stream, act, slope = mlp_forward(0, place, kept0[0], mlp0, kept0[5], [])
    kept1 = attention(1, stream, all1, [])
    kept = (kept0, kept1)
    inputs = (images, stream)
    attention_w = (heads0, all1)

    def backward_attention(layer, gradient, small, after, *span):
        mid, qkv, merged, totals, table, vec = kept[layer]
        return attention_backward(
            layer, place, gradient, inputs[layer], qkv, merged, totals, table, attention_w[layer],
            vec, small, perms[layer], rel, after, *span,
        )

    activations, grad_mid, parts_mlp1, small = mlp_both(
        place, cotangent, kept1[0], all1, kept1[5], []
    )

    def backward_mlp0(gradient, after):
        return mlp_backward(0, place, gradient, act, slope, kept0[0], mlp0, kept0[5], after)

    state = (mat_w, mat_m, mat_v)
    def exchange(parts):
        return [parts[0], swap(parts[1], 1)]

    gradient, parts_heads1, _, _ = backward_attention(1, grad_mid, small, [])
    grad_mid, *parts_mlp0, small = backward_mlp0(gradient, [])
    if near:
        t_mlp1 = lax.psum_scatter(parts_mlp1, "dp", scatter_dimension=0, tiled=True)[0]
        parts_heads1 = tie([parts_heads1], [t_mlp1, small])[0]
        t_heads1 = lax.psum_scatter(parts_heads1, "dp", scatter_dimension=0, tiled=True)[0]
        gone_mlp0 = exchange(parts_mlp0)
        gradient, *parts_heads0, pairs, small = backward_attention(0, grad_mid, small, [], 0, half)

        s_mlp0 = add_split(gone_mlp0, [gradient])
        gone_mlp0 = give_plane(s_mlp0)
        gradient, *parts_heads0, _, small = backward_attention(
            0, grad_mid, small, [s_mlp0[0]], half, half, [gradient, *parts_heads0, pairs]
        )

        t_all = join(t_mlp1, t_heads1, gone_mlp0, [small])
        gone_heads0 = exchange(tie(parts_heads0, gone_mlp0))
        g_all = lax.psum_scatter(t_all, "zero", scatter_dimension=0, tiled=True)[0]
        s_heads0 = add_split(gone_heads0, [t_all])
        gone_heads0 = give_plane(s_heads0)
        across = tie([activations.transpose(1, 0, 2), gradient.transpose(1, 0, 2)], [])
        t_heads0 = add_split(gone_heads0, across)
        activations, gradient = [value.transpose(1, 0, 2) for value in across]
        gone_heads0 = give_z(t_heads0)
        g_all, *gone_heads0 = tie([g_all, *gone_heads0], [])
        n_all1 = lax.all_gather(g_all[:400], "dp", axis=0, tiled=False)
        g_all0 = add_last(g_all, gone_heads0, [])
        n_all0 = stack(send_plane(g_all0))
        sums0 = [n_all0, swap(n_all0, 1)]
        m = place[0] ^ np.arange(2)
        both = jnp.concatenate([half[:, 384:] for half in sums0])
        beside0 = [
            lax.dynamic_index_in_dim(both, (m[b] % 2) * 4 + m[b] // 2, 0, False) for b in range(2)
        ]
    else:
        gradient, *parts_heads0, _, _ = backward_attention(0, grad_mid, small, [])
        n_mlp1 = reduce_wide(parts_mlp1, dp, 0)
        n_heads1 = reduce_wide(parts_heads1, dp, SMALL)
        n_all1 = jnp.concatenate([n_mlp1, n_heads1], 1)
        n_mlp0 = reduce_wide(jnp.stack(parts_mlp0, 1), dp, 0)
        n_heads0 = reduce_wide(jnp.stack(parts_heads0, 1), dp, SMALL)
        sums0 = [jnp.concatenate([n_mlp0, n_heads0], 1)]
        beside0 = sums0[0][:2, 384:]
    done = adam(0, 1, place, sums0, state, None, [])
    done = adam(1, 1, place, [n_all1], state, done, [])

    def beside(block):
        return jnp.stack([beside0[block], n_all1[block, 384:]]).astype(f32)

    new_vec = adam_step(vec_w, vec_m, vec_v, beside(1)[:, 0:12, 0:128], rate_vector, 0.0)
    new_tab = adam_step(tab_w, tab_m, tab_v, beside(0)[:, 0:4, 0:NREL], rate_table, 0.0)
    return (activations, gradient, *done, *new_vec, *new_tab)


def solution(mesh):
    images = P(("dp", "zero"), None, None)
    rows = P(None, "zero", None)
    lanes = P(None, None, "zero")
    return jax.shard_map(
        partial(shards, mesh.shape["dp"]),
        mesh=mesh,
        in_specs=(images, images, P(("dp", "zero")), P(), P())
        + (rows,) * 3 + (lanes,) * 3 + (rows,) * 3,
        out_specs=(images, images) + (rows,) * 3 + (lanes,) * 3 + (rows,) * 3,
        check_vma=False,
    )
```

```python
from functools import partial

import jax
import jax.numpy as jnp
import numpy as np
from jax import lax
from jax.experimental import pallas as pl
from jax.experimental.pallas import tpu as pltpu
from jax.sharding import PartitionSpec as P

WIN = 7
SIDE = 14
STEP = 10
NREL = 169
C = 512
HID = 2048
TOKENS = SIDE * SIDE
PAIR = 2
ROWS = 208
FRAME = 256
CELL = 64
QUAD = 4
BLOCK = 256
EXTRA = 32
SMALL = 16

norm_eps = 1e-05
mask_value = -100.0
beta_one = 0.9
beta_two = 0.999
adam_eps = 1e-08
weight_decay = 0.05
rate_matrix = 0.1
rate_vector = 0.5
rate_table = 1.0
scale = 32 ** (-0.5)

bf16 = jnp.bfloat16
f32 = jnp.float32
NN = (((1,), (0,)), ((), ()))
NT = (((1,), (1,)), ((), ()))
TN = (((0,), (0,)), ((), ()))


def mm(left, right, dims=NN):
    return lax.dot_general(left, right, dims, preferred_element_type=f32)


def frames(shifted):
    move = WIN // 2 if shifted else 0
    placed = np.zeros((FRAME, ROWS), np.float32)
    for wy in range(2):
        for wx in range(2):
            for iy in range(WIN):
                for ix in range(WIN):
                    y = (wy * WIN + iy + move) % SIDE
                    x = (wx * WIN + ix + move) % SIDE
                    placed[(wy * 2 + wx) * CELL + iy * WIN + ix, y * SIDE + x] = 1
    return placed


def head_rows():
    rows = np.zeros((QUAD * CELL, 128), np.float32)
    for h in range(QUAD):
        rows[h * CELL : (h + 1) * CELL, h * 32 : (h + 1) * 32] = 1
    return rows


def head_spread(rows):
    out = np.zeros((rows, QUAD * CELL), np.float32)
    for h in range(QUAD):
        out[h, h * CELL : (h + 1) * CELL] = 1
    return out


def norm(rows):
    centred = rows - jnp.mean(rows, -1, keepdims=True)
    spread = lax.rsqrt(jnp.mean(centred * centred, -1, keepdims=True) + norm_eps)
    return centred * spread, spread


def norm_back(grad_unit, unit, spread):
    return spread * (
        grad_unit
        - jnp.mean(grad_unit, -1, keepdims=True)
        - unit * jnp.mean(grad_unit * unit, -1, keepdims=True)
    )


def column_sum(rows):
    return jnp.sum(rows, 0, keepdims=True)


def gelu_pair(u):
    size = jnp.abs(u)
    below = 1.0 + (0.3275911 * 0.5**0.5) * size
    t = pltpu.reciprocal(below, approx=True)
    bell = jnp.exp2(u * u * (-0.5 * 1.4426950408889634))
    poly = t * (
        0.127414796 + t * (-0.142248368 + t * (0.710706871 + t * (-0.726576013 + t * 0.530702714)))
    )
    tail = poly * bell
    phi = jnp.where(u >= 0, 1.0 - tail, tail)
    return u * phi, phi + u * bell * 0.3989422804014327


def quad_rows(part, heads):
    return jnp.concatenate([part] * QUAD, 0) * heads


def pick_heads(stacked, lane_head):
    low = jnp.where(lane_head == 0, stacked[:CELL], stacked[CELL : 2 * CELL])
    high = jnp.where(lane_head == 2, stacked[2 * CELL : 3 * CELL], stacked[3 * CELL :])
    return jnp.where(lane_head < 2, low, high)


def lane_heads():
    return lax.broadcasted_iota(jnp.int32, (CELL, 128), 1) // 32


def whole(shape):
    zero = (0,) * len(shape)
    return pl.BlockSpec(shape, lambda *_: zero, pipeline_mode=pl.Buffered(1))


def per_image(rows, cols):
    return pl.BlockSpec((1, rows, cols), lambda i, *_: (i, 0, 0))


def per_pair(rows, cols):
    return pl.BlockSpec((PAIR, rows, cols), lambda i, *_: (i, 0, 0))


HBM = pl.BlockSpec(memory_space=pl.ANY)


def weight_copies(place, stacks, kept, sems, part=0):
    copies = []
    for m in range(8):
        for s in range(4):
            for p in range(kept.shape[0]):
                if len(stacks) == 1:
                    source, block, owner = stacks[0].at[m, s, part + p], m, s
                else:
                    source = stacks[m % 2].at[m // 2, s, p]
                    block, owner = place[0] ^ m, (place[1] + 4 - s) & 3
                rows = pl.ds(pl.multiple_of(owner * 128, 128), 128)
                cols = pl.ds(pl.multiple_of(block * BLOCK, BLOCK), BLOCK)
                copies.append(
                    pltpu.make_async_copy(
                        source.at[pl.ds(0, 128), :], kept.at[p, rows, cols], sems.at[m, s, p]
                    )
                )
    return copies


def extra_copies(place, stacks, kept, sems):
    copies = []
    for m in range(8):
        for s in range(4):
            if len(stacks) == 1:
                source, block, owner = stacks[0].at[m, s, 0], m, s
            else:
                source = stacks[m % 2].at[m // 2, s, 0]
                block, owner = place[0] ^ m, (place[1] + 4 - s) & 3
            copies.append(
                pltpu.make_async_copy(
                    source.at[pl.ds(128, EXTRA), :], kept.at[block, owner], sems.at[m, s, 0]
                )
            )
    return copies


def fetch(copies):
    for copy in copies:
        copy.start()
    for copy in copies:
        copy.wait()


def call(body, name, grid, ins, outs, out_shapes, scratch, cost_us, prefetch=0, aliases=None):
    return pl.pallas_call(
        body,
        name=name,
        grid_spec=pltpu.PrefetchScalarGridSpec(
            num_scalar_prefetch=prefetch,
            grid=grid,
            in_specs=ins,
            out_specs=outs,
            scratch_shapes=scratch,
        ),
        out_shape=out_shapes,
        input_output_aliases=aliases or {},
        compiler_params=pltpu.CompilerParams(
            dimension_semantics=("arbitrary",) * len(grid), vmem_limit_bytes=58 * 1024 * 1024
        ),
        cost_estimate=pl.CostEstimate(
            flops=0, bytes_accessed=int(cost_us * 3.69e4), transcendentals=0
        ),
    )


def shape(dims, kind):
    return jax.ShapeDtypeStruct(dims, kind)


def pack_body(place, *refs):
    mats, (pair_index, tab, vec, spread) = refs[:6], refs[6:10]
    out, mlp0, all1, rel, spread_tab, small = refs[10:]
    rows = mats[0].shape[1]
    out[0, 0:rows, :] = mats[0][0].astype(bf16)
    for ref, at, n in ((mlp0, 0, 1), (mlp0, 1, 2), (all1, 0, 3), (all1, 1, 4), (all1, 2, 5)):
        ref[at] = mats[n][0].astype(bf16)
    rel[...] = jnp.full(rel.shape, -1, jnp.int32)
    across = pair_index[...].astype(f32).T.astype(jnp.int32)
    for h in range(QUAD):
        rel[0 : WIN * WIN, CELL * h : CELL * h + WIN * WIN] = across
    for layer in range(2):
        spread_tab[layer, 0:NREL, :] = mm(tab[layer].astype(bf16), spread[...], TN)
    pairs = rel[pl.ds(pl.multiple_of(place[0] * 8, 8), 8), :]

    def step(r, sums):
        hit = pairs == r
        return tuple(
            jnp.where(hit, spread_tab[layer, pl.ds(r, 1), :], sums[layer]) for layer in range(2)
        )

    start = jnp.zeros((8, QUAD * CELL), f32)
    first, second = lax.fori_loop(0, NREL, step, (start, start), unroll=13)
    out[0, rows : rows + 16, :] = jnp.concatenate([first, second], 0).astype(bf16)
    small[...] = jnp.zeros_like(small)
    row = jnp.minimum(place[0] * 2, 10)
    for layer in range(2):
        for k in range(2):
            small[k : k + 1, layer * 128 : (layer + 1) * 128] = vec[row + k, layer : layer + 1, :]
    out[0, rows + 16 : rows + 32, :] = small[...].astype(bf16)


def pack(place, rows, mat_w, rel_index, tab_w, vec_w):
    vec_w = vec_w.transpose(1, 0, 2)

    def block(layer, part):
        return pl.BlockSpec(
            (1, rows, BLOCK), lambda i, place: (layer, place[1], part * 8 + place[0])
        )

    dims = [(1, rows + EXTRA, BLOCK), (2, rows, BLOCK), (3, rows, BLOCK)]
    return call(
        pack_body,
        "pack",
        (1,),
        [block(layer, part) for layer in range(2) for part in range(3)]
        + [
            whole(rel_index.shape),
            whole(tab_w.shape),
            whole(vec_w.shape),
            whole((QUAD, QUAD * CELL)),
        ],
        [whole(d) for d in dims] + [whole((CELL, QUAD * CELL))],
        [shape(d, bf16) for d in dims] + [shape((CELL, QUAD * CELL), jnp.int32)],
        [pltpu.VMEM((2, 176, QUAD * CELL), f32), pltpu.VMEM((16, 256), f32)],
        4,
        prefetch=1,
    )(place, *[mat_w] * 6, rel_index, tab_w, vec_w, jnp.asarray(head_spread(QUAD), bf16))


def attention_forward_body(layer, stacks, waits, place, *refs):
    arrays, refs = refs[: stacks[0]], refs[stacks[0] :]
    extras, refs = refs[: stacks[1]], refs[stacks[1] + waits :]
    x, mask, perm, perm_back, heads = refs[:5]
    mid, qkv, merged, totals, table, vec, framed, kept, extra_kept, sems, more_sems = refs[5:]
    weight, extra = kept.at[0], extra_kept

    @pl.when(pl.program_id(0) == 0)
    def _():
        fetch(
            weight_copies(place, arrays, kept, sems)
            + extra_copies(place, extras, extra_kept, more_sems)
        )
        vec[...] = jnp.zeros_like(vec)
        for z in range(4):
            for d in range(8):
                pair = extra[d, z, 0:16, :].astype(f32)
                bias = pair[8 * layer : 8 * layer + 8]
                for w in range(table.shape[0]):
                    table[w, z, 8 * d : 8 * d + 8, :] = bias + mask[w, 8 * d : 8 * d + 8, :]
                if d < 6:
                    rows = extra[d, z, 16:32, 128 * layer : 128 * layer + 128].astype(f32)
                    vec[2 * d : 2 * d + 2, 128 * z : 128 * z + 128] = rows[0:2]

    stream = x[0]
    unit, _ = norm(stream)
    normed = (unit * vec[0:1, :] + vec[1:2, :]).astype(bf16)
    normed = mm(perm[...], normed).astype(bf16)
    for c in range(6):
        part = mm(normed, weight[:, 256 * c : 256 * c + 256])
        if c < 2:
            part = part + vec[2:3, 256 * c : 256 * c + 256]
        if c >= 4:
            part = part + vec[3:4, 256 * (c - 4) : 256 * (c - 4) + 256]
        qkv[0, :, 256 * c : 256 * c + 256] = part.astype(bf16)
    lane_head = lane_heads()

    def score(unit):
        rows, at = slice(CELL * (unit // 4), CELL * (unit // 4) + CELL), 128 * (unit % 4)
        query = quad_rows(qkv[0, rows, at : at + 128], heads[...])
        return mm(qkv[0, rows, C + at : C + at + 128], query, NT)

    ahead = score(0)
    for n in range(16):
        w, g = n // 4, n % 4
        rows, at = slice(CELL * w, CELL * w + CELL), 128 * g
        scores = ahead * scale + table[w % table.shape[0], g]
        if n < 15:
            ahead = score(n + 1)
        top = jnp.max(scores, 0, keepdims=True)
        raised = jnp.exp(scores - top)
        total = jnp.sum(raised, 0, keepdims=True)
        totals[0, n : n + 1, :] = top + jnp.log(total)
        probs = (raised * (1.0 / total)).astype(bf16)
        stacked = mm(probs, qkv[0, rows, 2 * C + at : 2 * C + at + 128], TN)
        framed[rows, at : at + 128] = pick_heads(stacked, lane_head).astype(bf16)
    gathered = mm(perm_back[...], framed[...]).astype(bf16)
    merged[0] = gathered
    mid[0] = stream + mm(gathered, weight[:, 3 * C :]) + vec[4:5, :]


def attention_forward(layer, place, x, weight, extra, mask, perm, after):
    images = x.shape[0]
    tables = mask.shape[0]
    return call(
        partial(attention_forward_body, layer, (len(weight), len(extra)), len(after)),
        f"attention_forward_{layer}",
        (images,),
        [HBM] * (len(weight) + len(extra) + len(after))
        + [
            per_image(x.shape[1], C),
            whole(mask.shape),
            whole((FRAME, ROWS)),
            whole((ROWS, FRAME)),
            whole((QUAD * CELL, 128)),
        ],
        [
            per_image(ROWS, C),
            per_image(FRAME, 3 * C),
            per_image(ROWS, C),
            per_image(16, QUAD * CELL),
            pl.BlockSpec((tables, 4, CELL, QUAD * CELL), lambda i, *_: (0, 0, 0, 0)),
            pl.BlockSpec((16, C), lambda i, *_: (0, 0)),
        ],
        [
            shape((images, ROWS, C), f32),
            shape((images, FRAME, 3 * C), bf16),
            shape((images, ROWS, C), bf16),
            shape((images, 16, QUAD * CELL), f32),
            shape((tables, 4, CELL, QUAD * CELL), f32),
            shape((16, C), f32),
        ],
        [
            pltpu.VMEM((FRAME, C), bf16),
            pltpu.VMEM((1, C, HID), bf16),
            pltpu.VMEM((8, 4, EXTRA, BLOCK), bf16),
            pltpu.SemaphoreType.DMA((8, 4, 1)),
            pltpu.SemaphoreType.DMA((8, 4, 1)),
        ],
        20,
        prefetch=1,
    )(
        place,
        *weight,
        *extra,
        *after,
        x,
        mask,
        jnp.asarray(perm, bf16),
        jnp.asarray(perm.T, bf16),
        jnp.asarray(head_rows(), bf16),
    )


def mlp_forward_body(stacks, waits, place, *refs):
    arrays, refs = refs[:stacks], refs[stacks + waits :]
    mid, vec, result, act, slope, kept, sems = refs
    first, second = kept.at[0], kept.at[1]

    @pl.when(pl.program_id(0) == 0)
    def _():
        fetch(weight_copies(place, arrays, kept, sems))

    rows = PAIR * ROWS
    stream = mid[...].reshape(rows, C)
    unit, _ = norm(stream)
    normed = (unit * vec[5:6, :] + vec[6:7, :]).astype(bf16)
    ahead = mm(normed, first[:, 0:BLOCK])
    for c in range(8):
        cols = slice(256 * c, 256 * c + 256)
        bias = vec[8 + c // 2 : 9 + c // 2, 256 * (c % 2) : 256 * (c % 2) + 256]
        inner = ahead + bias
        if c < 7:
            ahead = mm(normed, first[:, 256 * c + 256 : 256 * c + 512])
        value, pull = gelu_pair(inner)
        act[:, :, cols] = value.astype(bf16).reshape(PAIR, ROWS, BLOCK)
        slope[:, :, cols] = pull.astype(bf16).reshape(PAIR, ROWS, BLOCK)
    total = stream + vec[7:8, :] + mm(act[...].reshape(rows, HID), second[...], NT)
    result[...] = total.reshape(PAIR, ROWS, C)


def mlp_forward(layer, place, mid, weight, vec, after):
    images = mid.shape[0]
    return call(
        partial(mlp_forward_body, len(weight), len(after)),
        f"mlp_forward_{layer}",
        (images // PAIR,),
        [HBM] * (len(weight) + len(after)) + [per_pair(ROWS, C), whole(vec.shape)],
        [per_pair(ROWS, C), per_pair(ROWS, HID), per_pair(ROWS, HID)],
        [
            shape((images, ROWS, C), f32),
            shape((images, ROWS, HID), bf16),
            shape((images, ROWS, HID), bf16),
        ],
        [
            pltpu.VMEM((2, C, HID), bf16),
            pltpu.SemaphoreType.DMA((8, 4, 2)),
        ],
        22,
        prefetch=1,
    )(place, *weight, *after, mid, vec)


def mlp_both_body(stacks, waits, place, *refs):
    arrays, refs = refs[:stacks], refs[stacks + waits :]
    grad, mid, vec, result, grad_mid, pieces, small = refs[:7]
    all_grad, all_act, all_inner, all_normed, kept, sems = refs[7:]
    first, second = kept.at[0], kept.at[1]
    i = pl.program_id(0)

    @pl.when(i == 0)
    def _():
        fetch(weight_copies(place, arrays, kept, sems, 1))
        small[...] = jnp.zeros_like(small)

    rows = PAIR * ROWS
    grad_out = grad[...].reshape(rows, C)
    here = pl.ds(pl.multiple_of(i * rows, 32), rows)
    low = grad_out.astype(bf16)
    all_grad[here, :] = low
    small[7:8, :] += column_sum(grad_out)
    stream = mid[...].reshape(rows, C)
    unit, spread = norm(stream)
    normed = (unit * vec[5:6, :] + vec[6:7, :]).astype(bf16)
    all_normed[here, :] = normed
    ahead = mm(normed, first[:, 0:BLOCK]), mm(low, second[:, 0:BLOCK])
    for c in range(8):
        cols = slice(256 * c, 256 * c + 256)
        row, lane = 8 + c // 2, 256 * (c % 2)
        bias = vec[row : row + 1, lane : lane + 256]
        inner, grad_act = ahead
        if c < 7:
            later = slice(256 * c + 256, 256 * c + 512)
            ahead = mm(normed, first[:, later]), mm(low, second[:, later])
        value, pull = gelu_pair(inner + bias)
        all_act[here, cols] = value.astype(bf16)
        inner = (grad_act * pull).astype(bf16)
        all_inner[here, cols] = inner
        small[row : row + 1, lane : lane + 256] += column_sum(inner.astype(f32))
    back = mm(all_inner[here, :], first[...], NT)
    small[5:6, :] += column_sum(back * unit)
    small[6:7, :] += column_sum(back)
    grad_mid[...] = (grad_out + norm_back(back * vec[5:6, :], unit, spread)).reshape(PAIR, ROWS, C)
    total = stream + vec[7:8, :] + mm(all_act[here, :], second[...], NT)
    for n in range(PAIR):
        alive = (i * PAIR + n < place[2]).astype(f32)
        result[n] = (total[n * ROWS : n * ROWS + TOKENS] * alive).astype(bf16)

    @pl.when(i == pl.num_programs(0) - 1)
    def _():
        mlp_weight_grads(place, all_grad, all_act, all_inner, all_normed, pieces)


def mlp_weight_grads(place, all_grad, all_act, all_inner, all_normed, *outs):
    grad_across = all_grad[...].T
    normed_across = all_normed[...].T
    for m in range(8):
        block = m if len(outs) == 1 else place[0] ^ m
        cols = pl.ds(pl.multiple_of(block * BLOCK, BLOCK), BLOCK)
        for p, total in enumerate(
            (mm(normed_across, all_inner[:, cols]), mm(grad_across, all_act[:, cols]))
        ):
            total = total.astype(bf16)
            for z in range(4):
                if len(outs) == 1:
                    outs[0][m, z, p] = total[128 * z : 128 * z + 128]
                else:
                    outs[m % 2][m // 2, z, p] = total[128 * z : 128 * z + 128]


def mlp_both(place, grad, mid, weight, vec, after):
    images = mid.shape[0]
    total = images * ROWS
    pieces = (8, 4, 2, 128, BLOCK)
    return call(
        partial(mlp_both_body, len(weight), len(after)),
        "mlp_both",
        (images // PAIR,),
        [HBM] * (len(weight) + len(after)) + [per_pair(ROWS, C), per_pair(ROWS, C), whole(vec.shape)],
        [per_pair(TOKENS, C), per_pair(ROWS, C), whole(pieces), whole((16, C))],
        [
            shape((images, TOKENS, C), bf16),
            shape((images, ROWS, C), f32),
            shape(pieces, bf16),
            shape((16, C), f32),
        ],
        [
            pltpu.VMEM((total, C), bf16),
            pltpu.VMEM((total, HID), bf16),
            pltpu.VMEM((total, HID), bf16),
            pltpu.VMEM((total, C), bf16),
            pltpu.VMEM((2, C, HID), bf16),
            pltpu.SemaphoreType.DMA((8, 4, 2)),
        ],
        45,
        prefetch=1,
    )(place, *weight, *after, grad, mid, vec)


def mlp_backward_body(stacks, waits, place, *refs):
    arrays, refs = refs[:stacks], refs[stacks + waits :]
    grad, act, slope, mid, vec, grad_mid, own, other, small = refs[:9]
    all_grad, all_act, all_inner, all_normed, kept, sems = refs[9:]
    first, second = kept.at[0], kept.at[1]
    i = pl.program_id(0)

    @pl.when(i == 0)
    def _():
        fetch(weight_copies(place, arrays, kept, sems))
        small[...] = jnp.zeros_like(small)

    rows = PAIR * ROWS
    grad_out = grad[...].reshape(rows, C)
    here = pl.ds(pl.multiple_of(i * rows, 32), rows)
    low = grad_out.astype(bf16)
    all_grad[here, :] = low
    small[7:8, :] += column_sum(low.astype(f32))
    all_act[here, :] = act[...].reshape(rows, HID)
    unit, spread = norm(mid[...].reshape(rows, C))
    all_normed[here, :] = (unit * vec[5:6, :] + vec[6:7, :]).astype(bf16)
    ahead = mm(low, second[:, 0:BLOCK])
    for c in range(8):
        cols = slice(256 * c, 256 * c + 256)
        pull = slope[:, :, cols].reshape(rows, BLOCK).astype(f32)
        grad_act = ahead
        if c < 7:
            ahead = mm(low, second[:, 256 * c + 256 : 256 * c + 512])
        inner = (grad_act * pull).astype(bf16)
        all_inner[here, cols] = inner
        row, lane = 8 + c // 2, 256 * (c % 2)
        small[row : row + 1, lane : lane + 256] += column_sum(inner.astype(f32))
    back = mm(all_inner[here, :], first[...], NT)
    small[5:6, :] += column_sum(back * unit)
    small[6:7, :] += column_sum(back)
    grad_mid[...] = (grad_out + norm_back(back * vec[5:6, :], unit, spread)).reshape(PAIR, ROWS, C)

    @pl.when(i == pl.num_programs(0) - 1)
    def _():
        mlp_weight_grads(place, all_grad, all_act, all_inner, all_normed, own, other)


def mlp_backward(layer, place, grad, act, slope, mid, weight, vec, after):
    images = mid.shape[0]
    total = images * ROWS
    pieces = (4, 4, 2, 128, BLOCK)
    return call(
        partial(mlp_backward_body, len(weight), len(after)),
        f"mlp_backward_{layer}",
        (images // PAIR,),
        [HBM] * (len(weight) + len(after))
        + [
            per_pair(grad.shape[1], C),
            per_pair(ROWS, HID),
            per_pair(ROWS, HID),
            per_pair(ROWS, C),
            whole(vec.shape),
        ],
        [per_pair(ROWS, C), whole(pieces), whole(pieces), whole((16, C))],
        [
            shape((images, ROWS, C), f32),
            shape(pieces, bf16),
            shape(pieces, bf16),
            shape((16, C), f32),
        ],
        [
            pltpu.VMEM((total, C), bf16),
            pltpu.VMEM((total, HID), bf16),
            pltpu.VMEM((total, HID), bf16),
            pltpu.VMEM((total, C), bf16),
            pltpu.VMEM((2, C, HID), bf16),
            pltpu.SemaphoreType.DMA((8, 4, 2)),
        ],
        30,
        prefetch=1,
    )(place, *weight, *after, grad, act, slope, mid, vec)


def attention_backward_body(layer, stacks, waits, resumed, ends, place, *refs):
    arrays, refs = refs[:stacks], refs[stacks + waits :]
    if resumed:
        (own_before, other_before, pairs_before), refs = refs[1:4], refs[4:]
    grad, x, qkv, merged, totals, table, vec, before = refs[:8]
    perm, perm_back, heads, rel, spread, result = refs[8:14]
    outs, refs = (refs[14:15], refs[15:]) if layer else (refs[14:16], refs[16:])
    pairs, small, framed, grad_framed, all_normed, all_packed, all_merged = refs[:7]
    across, hits, beside, kept, sems = refs[7:]
    weight = kept.at[0]
    i = pl.program_id(0)

    @pl.when(i == 0)
    def _():
        fetch(weight_copies(place, arrays, kept, sems))
        small[...] = before[...]
        pairs[...] = pairs_before[...] if resumed else jnp.zeros_like(pairs)

    stream = x[0]
    here = pl.ds(pl.multiple_of(i * ROWS, 16), ROWS)
    unit, spread_one = norm(stream)
    all_normed[here, :] = (unit * vec[0:1, :] + vec[1:2, :]).astype(bf16)
    low = grad[0].astype(bf16)
    all_packed[here, 3 * C :] = low
    all_merged[here, :] = merged[0]
    small[4:5, :] += column_sum(low.astype(f32))
    moved = mm(perm[...], low).astype(bf16)
    framed[...] = mm(moved, weight[:, 3 * C :], NT).astype(bf16)
    lane_head = lane_heads()
    at = [128 * g for g in range(4)]

    def window(w):
        rows = slice(CELL * w, CELL * w + CELL)
        keys = [qkv[0, rows, C + c : C + c + 128] for c in at]
        query = [quad_rows(qkv[0, rows, c : c + 128], heads[...]) for c in at]
        pull = [quad_rows(framed[rows, c : c + 128], heads[...]) for c in at]
        scores = [mm(keys[g], query[g], NT) for g in range(4)]
        grad_probs = [
            mm(qkv[0, rows, 2 * C + at[g] : 2 * C + at[g] + 128], pull[g], NT) for g in range(4)
        ]
        return keys, query, pull, scores, grad_probs

    ahead = window(0)
    for w in range(4):
        rows = slice(CELL * w, CELL * w + CELL)
        keys, query, pull, scores, grad_probs = ahead
        if w < 3:
            ahead = window(w + 1)
        probs, grad_scores = [], []
        for g in range(4):
            shifted = scores[g] * scale + table[w % table.shape[0], g]
            prob = jnp.exp(shifted - totals[0, 4 * w + g : 4 * w + g + 1, :])
            mean = jnp.sum(prob * grad_probs[g], 0, keepdims=True)
            grad_score = (prob * (grad_probs[g] - mean)).astype(bf16)
            pairs[g] += grad_score.astype(f32)
            probs.append(prob.astype(bf16))
            grad_scores.append(grad_score)
        for g in range(4):
            grad_value = mm(probs[g], pull[g])
            grad_framed[rows, 2 * C + at[g] : 2 * C + at[g] + 128] = grad_value.astype(bf16)
        for g in range(4):
            grad_key = mm(grad_scores[g], query[g]) * scale
            grad_framed[rows, C + at[g] : C + at[g] + 128] = grad_key.astype(bf16)
        for g in range(4):
            grad_query = pick_heads(mm(grad_scores[g], keys[g], TN), lane_head) * scale
            grad_framed[rows, at[g] : at[g] + 128] = grad_query.astype(bf16)
    for c in range(6):
        cols = slice(256 * c, 256 * c + 256)
        part = mm(perm_back[...], grad_framed[:, cols])
        all_packed[here, cols] = part.astype(bf16)
        if c < 2:
            small[2:3, cols] += column_sum(part)
        if c >= 4:
            small[3:4, 256 * (c - 4) : 256 * (c - 4) + 256] += column_sum(part)
    back = mm(all_packed[here, : 3 * C], weight[:, : 3 * C], NT)
    small[0:1, :] += column_sum(back * unit)
    small[1:2, :] += column_sum(back)
    total = grad[0] + norm_back(back * vec[0:1, :], unit, spread_one)
    result[0] = total[: result.shape[1]]

    @pl.when(i == pl.num_programs(0) - 1)
    def _():
        across[0] = all_normed[...].T
        across[1] = all_merged[...].T
        beside[...] = jnp.zeros_like(beside)
        if ends:
            hits[...] = jnp.zeros_like(hits)

            def step(r, carry):
                same = rel[...] == r
                for g in range(4):
                    kept_pairs = jnp.where(same, pairs[g], 0.0)
                    hits[pl.ds(r, 1), 256 * g : 256 * g + 256] = column_sum(kept_pairs)
                return carry

            lax.fori_loop(0, NREL, step, 0)
            for z in range(4):
                beside[0, z] = lax.dot_general(
                    spread[...],
                    hits[:, 256 * z : 256 * z + 256],
                    NT,
                    precision=lax.Precision.HIGHEST,
                    preferred_element_type=f32,
                ).astype(bf16)
                beside[1, z, :, 0:128] = small[:, 128 * z : 128 * z + 128].astype(bf16)
        for m in range(8):
            b = m if layer else place[0] ^ m
            left = across[jnp.where(b < 6, 0, 1)]
            right = all_packed[:, pl.ds(pl.multiple_of(b * BLOCK, BLOCK), BLOCK)]
            block = mm(left, right)
            for z in range(4):
                if layer:
                    out = outs[0].at[m, z, 0]
                else:
                    to = (z + 4 - place[1]) & 3
                    out = outs[m % 2].at[m // 2, to, 0]
                new = block[128 * z : 128 * z + 128]
                if resumed:
                    old = other_before if m % 2 else own_before
                    new = new + old[m // 2, to, 0, 0:128, :].astype(f32)
                out[0:128, :] = new.astype(bf16)
                out[128:144, :] = beside[jnp.minimum(b, 2), z]


def attention_backward(
    layer, place, grad, x, qkv, merged, totals, table, weight, vec, small, perm, rel, after,
    first=0, count=None, resume=None,
):
    images = grad.shape[0]
    count = count or images
    pieces = (8 if layer else 4, 4, 1, 128 + SMALL, BLOCK)
    pairs = (4, CELL, QUAD * CELL)
    total = count * ROWS
    out_rows = TOKENS if layer == 0 else ROWS

    def image(rows, cols):
        return pl.BlockSpec((1, rows, cols), lambda i, *_: (i + first, 0, 0))

    resumed = list(resume or [])
    return call(
        partial(
            attention_backward_body, layer, len(weight), len(after), bool(resumed),
            first + count == images,
        ),
        f"attention_backward_{layer}_{first}",
        (count,),
        [HBM] * (len(weight) + len(after))
        + ([HBM, whole(pieces), whole(pieces), whole(pairs)] if resumed else [])
        + [
            image(ROWS, C),
            image(x.shape[1], C),
            image(FRAME, 3 * C),
            image(ROWS, C),
            image(16, QUAD * CELL),
            whole(table.shape),
            whole(vec.shape),
            whole((16, C)),
            whole((FRAME, ROWS)),
            whole((ROWS, FRAME)),
            whole((QUAD * CELL, 128)),
            whole(rel.shape),
            whole((SMALL, QUAD * CELL)),
        ],
        [image(out_rows, C)]
        + [whole(pieces)] * (1 if layer else 2)
        + [whole(pairs), whole((16, C))],
        [shape((images, out_rows, C), f32)]
        + [shape(pieces, bf16)] * (1 if layer else 2)
        + [shape(pairs, f32), shape((16, C), f32)],
        [
            pltpu.VMEM((FRAME, C), bf16),
            pltpu.VMEM((FRAME, 3 * C), bf16),
            pltpu.VMEM((total, C), bf16),
            pltpu.VMEM((total, 4 * C), bf16),
            pltpu.VMEM((total, C), bf16),
            pltpu.VMEM((2, C, total), bf16),
            pltpu.VMEM((256, 4 * QUAD * CELL), f32),
            pltpu.VMEM((3, 4, SMALL, BLOCK), bf16),
            pltpu.VMEM((1, C, HID), bf16),
            pltpu.SemaphoreType.DMA((8, 4, 1)),
        ],
        6 * count,
        prefetch=1,
        aliases={1 + len(weight) + len(after): 0} if resumed else None,
    )(
        place,
        *weight,
        *after,
        *resumed,
        grad,
        x,
        qkv,
        merged,
        totals,
        table,
        vec,
        small,
        jnp.asarray(perm, bf16),
        jnp.asarray(perm.T, bf16),
        jnp.asarray(head_rows(), bf16),
        rel,
        jnp.asarray(head_spread(SMALL), f32),
    )


def adam_step(weight, first, second, gradient, rate, decay):
    first_new = beta_one * first + (1.0 - beta_one) * gradient
    second_new = beta_two * second + (1.0 - beta_two) * gradient * gradient
    first_hat = first_new / (1.0 - beta_one**STEP)
    second_hat = second_new / (1.0 - beta_two**STEP)
    weight_new = weight - rate * (first_hat / (jnp.sqrt(second_hat) + adam_eps) + decay * weight)
    return (weight_new, first_new, second_new)


def adam_block(grad, weight, first, second, outs, cols):
    part = grad.astype(f32)
    first_new = beta_one * first[0, :, cols] + (1.0 - beta_one) * part
    second_new = beta_two * second[0, :, cols] + (1.0 - beta_two) * part * part
    spread = second_new * (1.0 / (1.0 - beta_two**STEP))
    inverse = pltpu.reciprocal(spread * lax.rsqrt(spread) + adam_eps, approx=True)
    step = first_new * (rate_matrix / (1.0 - beta_one**STEP)) * inverse
    outs[0][0, :, cols] = weight[0, :, cols] * (1.0 - rate_matrix * weight_decay) - step
    outs[1][0, :, cols] = first_new
    outs[2][0, :, cols] = second_new


def adam_body(place, near, far, weight, first, second, *refs):
    for j in range(2):
        for k in range(2):
            block = (((place[0] // 2) & 1) ^ j) * 2 + ((place[0] & 1) ^ k)
            cols = pl.ds(pl.multiple_of(block * BLOCK, BLOCK), BLOCK)
            adam_block((far if k else near)[j], weight, first, second, refs[-3:], cols)


def adam_body_plain(place, sums, weight, first, second, *refs):
    for k in range(4):
        cols = slice(BLOCK * k, BLOCK * k + BLOCK)
        adam_block(sums[k], weight, first, second, refs[-3:], cols)


def adam(layer, part, place, sums, state, done, after):
    kept = [] if done is None else list(done)
    if len(sums) == 2:
        parts = sums[0].shape[1] // 128
        body = adam_body
        spec = pl.BlockSpec(
            (1, 128, 4 * BLOCK),
            lambda p, j, place: (layer, 0, (part + p) % 3 * 2 + ((place[0] // 4) ^ j)),
        )
        piece = pl.BlockSpec((2, 128, BLOCK), lambda p, j, place: (j, p, 0))
    else:
        parts = sums[0].shape[1] // 128
        body = adam_body_plain
        spec = pl.BlockSpec(
            (1, 128, 4 * BLOCK), lambda p, j, place: (layer, 0, (part + p) % 3 * 2 + j)
        )
        piece = pl.BlockSpec((4, 128, BLOCK), lambda p, j, place: (j, p, 0))
    return call(
        body,
        f"adam_{layer}_{part}",
        (parts, 2),
        [piece] * len(sums) + [spec] * 3 + [HBM] * (len(kept) + len(after)),
        [spec] * 3,
        [shape(state[0].shape, f32)] * 3,
        [],
        3 * parts,
        prefetch=1,
        aliases={4 + len(sums) + k: k for k in range(len(kept))},
    )(place, *sums, *state, *kept, *after)


def swap(value, bits):
    return lax.ppermute(value, "dp", [(i, i ^ bits) for i in range(8)])


def shift(value, steps):
    return lax.ppermute(value, "zero", [(i, (i + steps) % 4) for i in range(4)])


def tie(values, after):
    values = list(values)
    return list(lax.optimization_barrier((*values, *after))[: len(values)])


def stack(values, after=()):
    return jnp.stack(tie(values, after) if after else values)


def add_body(count, *refs):
    total = refs[0][...].astype(f32)
    for k in range(1, count):
        total = total + refs[k][...].astype(f32)
    refs[-1][...] = total.astype(bf16)


def add(values, after=()):
    dims = values[0].shape
    return call(
        partial(add_body, len(values)),
        "add",
        (1,),
        [whole(dims)] * len(values) + [HBM] * len(after),
        whole(dims),
        shape(dims, bf16),
        [],
        10,
    )(*values, *after)


def add_split_body(count, lead, *refs):
    for k in range(4):
        if count == 2:
            refs[len(refs) - 4 + k][...] = refs[0][k] + refs[1][k]
            continue
        total = refs[0][k].astype(f32)
        for v in range(1, count):
            total = total + refs[v][k].astype(f32)
        refs[len(refs) - 4 + k][...] = total.astype(bf16)


def add_split(values, after=()):
    dims = values[0].shape
    steps = 1
    ins = (4, dims[1] // steps, *dims[2:])
    outs = dims[1:]
    zeros = (0,) * (len(dims) - 2)
    return call(
        partial(add_split_body, len(values), True),
        "add_split",
        (steps,),
        [pl.BlockSpec(ins, lambda i: (0, i, *zeros))] * len(values) + [HBM] * len(after),
        [pl.BlockSpec((outs[0] // steps, *outs[1:]), lambda i: (i, *zeros))] * 4,
        [shape(outs, bf16)] * 4,
        [],
        10,
    )(*values, *after)


def join_body(*refs):
    out = refs[-1]
    at = 0
    for group in (refs[:1], refs[1:2], refs[2:6]):
        parts, rows = group[0].shape[1:3]
        for p in range(parts):
            total = group[0][:, p]
            if len(group) > 1:
                total = total.astype(f32)
                for ref in group[1:]:
                    total = total + ref[:, p].astype(f32)
            out[:, at : at + rows, :] = total.astype(bf16)
            at += rows


def join(first, second, summed, after):
    rows = sum(value.shape[1] * value.shape[2] for value in (first, second, summed[0]))
    ins = [first, second, *summed]
    return call(
        join_body,
        "join",
        (1,),
        [whole(v.shape) for v in ins] + [HBM] * len(after),
        whole((4, rows, BLOCK)),
        shape((4, rows, BLOCK), bf16),
        [],
        5,
    )(*ins, *after)


def add_last_body(*refs):
    done, out = refs[0], refs[-1]
    rows = 256
    out[0:rows, :] = done[done.shape[0] - rows :, :]
    total = refs[1][0].astype(f32)
    for ref in refs[2:5]:
        total = total + ref[0].astype(f32)
    out[rows : rows + total.shape[0], :] = total.astype(bf16)


def add_last(done, values, after):
    rows = 256 + values[0].shape[1]
    return call(
        add_last_body,
        "add_last",
        (1,),
        [whole(done.shape)] + [whole(v.shape) for v in values] + [HBM] * len(after),
        whole((rows, BLOCK)),
        shape((rows, BLOCK), bf16),
        [],
        10,
    )(done, *values, *after)


def send_z(piece):
    return [piece] + [shift(piece, s) for s in range(1, 4)]


def send_plane(piece):
    return [piece] + [swap(piece, 2 * j) for j in range(1, 4)]


def give_plane(parts):
    return [parts[0]] + [swap(parts[j], 2 * j) for j in range(1, 4)]


def give_z(parts):
    return [parts[0]] + [shift(parts[s], s) for s in range(1, 4)]


def gather_wide(piece, dp, extra):
    fine = dp // 8
    parts, rows = piece.shape[0], piece.shape[1] - extra
    out = lax.all_gather(piece, ("dp", "zero"), axis=0, tiled=False)
    out = out.reshape(8, fine, 4, *piece.shape)
    main = out[..., :rows, :].transpose(0, 2, 3, 1, 4, 5).reshape(8, 4, parts, 128, BLOCK)
    return [jnp.concatenate([main, out[:, 0, ..., rows:, :]], 3)]


def reduce_wide(blocks, dp, extra):
    fine = dp // 8
    blocks = blocks.reshape(8, 4, *blocks.shape[-3:])
    parts, rows = blocks.shape[2], 128 // fine
    main = blocks[..., :128, :].reshape(8, 4, parts, fine, rows, BLOCK).transpose(0, 3, 1, 2, 4, 5)
    beside = jnp.broadcast_to(
        blocks[:, None, ..., 128:, :], (8, fine, 4, parts, extra, BLOCK)
    )
    flat = jnp.concatenate([main, beside], 4).reshape(dp * 4, parts, rows + extra, BLOCK)
    mine = lax.psum_scatter(flat, ("dp", "zero"), scatter_dimension=0, tiled=True)
    out = lax.all_gather(mine[0], "dp", axis=0, tiled=False)
    out = out.reshape(8, fine, parts, rows + extra, BLOCK)
    main = out[..., :rows, :].transpose(0, 2, 1, 3, 4).reshape(8, parts, 128, BLOCK)
    out = jnp.concatenate([main, out[:, 0, :, rows:]], 2)
    return out.reshape(8, -1, BLOCK)


def shards(
    dp, images, cotangent, counts, rel_index, regions,
    mat_w, mat_m, mat_v, vec_w, vec_m, vec_v, tab_w, tab_m, tab_v,
):
    near = dp == 8
    fine = dp // 8
    rows = 128 // fine
    me = lax.axis_index("dp")
    taken_from = jnp.stack([me // fine, me % fine]).astype(jnp.int32)
    spot = [me, lax.axis_index("zero")] if near else [0 * me, 0 * me]
    place = jnp.stack(spot + [counts[0]]).astype(jnp.int32)

    inside = np.arange(CELL) < WIN * WIN
    zones = regions.reshape(2, WIN, 2, WIN).transpose(0, 2, 1, 3).reshape(4, WIN * WIN)
    zones = jnp.pad(zones, ((0, 0), (0, 15)))
    differ = (zones[:, :, None] != zones[:, None, :]) & inside[None, None, :]
    outside = jnp.asarray(np.where(inside, 0.0, -1e30), f32)[None, :, None]
    mask_shifted = jnp.tile(jnp.where(differ, mask_value, 0.0) + outside, (1, 1, QUAD)).astype(f32)
    mask_plain = jnp.broadcast_to(outside, (1, CELL, QUAD * CELL))
    masks = (mask_plain, mask_shifted)
    perms = (frames(False), frames(True))

    packed, cut_mlp0, cut_all1, rel = pack(
        taken_from, rows, mat_w, rel_index, tab_w, vec_w
    )
    alive = (jnp.arange(images.shape[0]) < counts[0]).astype(f32)[:, None, None]
    pad = ((0, 0), (0, ROWS - TOKENS), (0, 0))
    images = jnp.pad(images.astype(f32), pad)
    cotangent = jnp.pad(cotangent.astype(f32) * alive, pad)

    def attention(layer, stream, weight, after):
        return attention_forward(
            layer, place, stream, weight, heads0, masks[layer], perms[layer], after
        )

    half = images.shape[0] // 2
    if near:
        sent_heads0 = send_z(packed)
        *sent_heads0, images = tie([*sent_heads0, images], [])
        z_heads0 = stack(sent_heads0)
        all1 = gather_wide(tie([cut_all1], [z_heads0])[0], dp, 0)
        sent_heads0 = send_plane(z_heads0)
        sent_mlp0 = send_z(tie([cut_mlp0], [z_heads0])[0])
        cotangent, mask_shifted = tie([cotangent, mask_shifted], [z_heads0])
        *sent_heads0, cotangent, mask_shifted = tie(
            [*sent_heads0, cotangent, mask_shifted], sent_mlp0
        )
        masks = (mask_plain, mask_shifted)
        p_heads0 = stack(sent_heads0)
        heads0 = [p_heads0, swap(p_heads0, 1)]
        z_mlp0 = stack(sent_mlp0, [p_heads0])
        sent_mlp0 = send_plane(z_mlp0)
        kept0 = attention(0, images, heads0, [z_mlp0])
        p_mlp0 = stack(sent_mlp0, [kept0[0]])
        mlp0 = [p_mlp0, swap(p_mlp0, 1)]
    else:
        heads0 = gather_wide(packed, dp, EXTRA)
        mlp0 = gather_wide(cut_mlp0, dp, 0)
        all1 = gather_wide(cut_all1, dp, 0)
        kept0 = attention(0, images, heads0, [])
    stream, act, slope = mlp_forward(0, place, kept0[0], mlp0, kept0[5], [])
    kept1 = attention(1, stream, all1, [])
    kept = (kept0, kept1)
    inputs = (images, stream)
    attention_w = (heads0, all1)

    def backward_attention(layer, gradient, small, after, *span):
        mid, qkv, merged, totals, table, vec = kept[layer]
        return attention_backward(
            layer, place, gradient, inputs[layer], qkv, merged, totals, table, attention_w[layer],
            vec, small, perms[layer], rel, after, *span,
        )

    activations, grad_mid, parts_mlp1, small = mlp_both(
        place, cotangent, kept1[0], all1, kept1[5], []
    )

    def backward_mlp0(gradient, after):
        return mlp_backward(0, place, gradient, act, slope, kept0[0], mlp0, kept0[5], after)

    state = (mat_w, mat_m, mat_v)
    def exchange(parts):
        return [parts[0], swap(parts[1], 1)]

    gradient, parts_heads1, _, _ = backward_attention(1, grad_mid, small, [])
    grad_mid, *parts_mlp0, small = backward_mlp0(gradient, [])
    if near:
        t_mlp1 = lax.psum_scatter(parts_mlp1, "dp", scatter_dimension=0, tiled=True)[0]
        parts_heads1 = tie([parts_heads1], [t_mlp1, small])[0]
        t_heads1 = lax.psum_scatter(parts_heads1, "dp", scatter_dimension=0, tiled=True)[0]
        gone_mlp0 = exchange(parts_mlp0)
        gradient, *parts_heads0, pairs, small = backward_attention(0, grad_mid, small, [], 0, half)

        s_mlp0 = add_split(gone_mlp0, [gradient])
        gone_mlp0 = give_plane(s_mlp0)
        gradient, *parts_heads0, _, small = backward_attention(
            0, grad_mid, small, [s_mlp0[0]], half, half, [gradient, *parts_heads0, pairs]
        )

        t_all = join(t_mlp1, t_heads1, gone_mlp0, [small])
        gone_heads0 = exchange(tie(parts_heads0, gone_mlp0))
        g_all = lax.psum_scatter(t_all, "zero", scatter_dimension=0, tiled=True)[0]
        s_heads0 = add_split(gone_heads0, [t_all])
        gone_heads0 = give_plane(s_heads0)
        across = tie([activations.transpose(1, 0, 2), gradient.transpose(1, 0, 2)], [])
        t_heads0 = add_split(gone_heads0, across)
        activations, gradient = [value.transpose(1, 0, 2) for value in across]
        gone_heads0 = give_z(t_heads0)
        g_all, *gone_heads0 = tie([g_all, *gone_heads0], [])
        n_all1 = lax.all_gather(g_all[:400], "dp", axis=0, tiled=False)
        g_all0 = add_last(g_all, gone_heads0, [])
        n_all0 = stack(send_plane(g_all0))
        sums0 = [n_all0, swap(n_all0, 1)]
        m = place[0] ^ np.arange(2)
        both = jnp.concatenate([half[:, 384:] for half in sums0])
        beside0 = [
            lax.dynamic_index_in_dim(both, (m[b] % 2) * 4 + m[b] // 2, 0, False) for b in range(2)
        ]
    else:
        gradient, *parts_heads0, _, _ = backward_attention(0, grad_mid, small, [])
        n_mlp1 = reduce_wide(parts_mlp1, dp, 0)
        n_heads1 = reduce_wide(parts_heads1, dp, SMALL)
        n_all1 = jnp.concatenate([n_mlp1, n_heads1], 1)
        n_mlp0 = reduce_wide(jnp.stack(parts_mlp0, 1), dp, 0)
        n_heads0 = reduce_wide(jnp.stack(parts_heads0, 1), dp, SMALL)
        sums0 = [jnp.concatenate([n_mlp0, n_heads0], 1)]
        beside0 = sums0[0][:2, 384:]
    done = adam(0, 1, place, sums0, state, None, [])
    done = adam(1, 1, place, [n_all1], state, done, [])

    def beside(block):
        return jnp.stack([beside0[block], n_all1[block, 384:]]).astype(f32)

    new_vec = adam_step(vec_w, vec_m, vec_v, beside(1)[:, 0:12, 0:128], rate_vector, 0.0)
    new_tab = adam_step(tab_w, tab_m, tab_v, beside(0)[:, 0:4, 0:NREL], rate_table, 0.0)
    return (activations, gradient, *done, *new_vec, *new_tab)


def solution(mesh):
    images = P(("dp", "zero"), None, None)
    rows = P(None, "zero", None)
    lanes = P(None, None, "zero")
    return jax.shard_map(
        partial(shards, mesh.shape["dp"]),
        mesh=mesh,
        in_specs=(images, images, P(("dp", "zero")), P(), P())
        + (rows,) * 3 + (lanes,) * 3 + (rows,) * 3,
        out_specs=(images, images) + (rows,) * 3 + (lanes,) * 3 + (rows,) * 3,
        check_vma=False,
    )
```

```python
from functools import partial

import jax
import jax.numpy as jnp
import numpy as np
from jax import lax
from jax.experimental import pallas as pl
from jax.experimental.pallas import tpu as pltpu
from jax.sharding import PartitionSpec as P

WIN = 7
SIDE = 14
STEP = 10
NREL = 169
C = 512
HID = 2048
TOKENS = SIDE * SIDE
PAIR = 2
ROWS = 208
FRAME = 256
CELL = 64
QUAD = 4
BLOCK = 256
EXTRA = 32
SMALL = 16

norm_eps = 1e-05
mask_value = -100.0
beta_one = 0.9
beta_two = 0.999
adam_eps = 1e-08
weight_decay = 0.05
rate_matrix = 0.1
rate_vector = 0.5
rate_table = 1.0
scale = 32 ** (-0.5)

bf16 = jnp.bfloat16
f32 = jnp.float32
NN = (((1,), (0,)), ((), ()))
NT = (((1,), (1,)), ((), ()))
TN = (((0,), (0,)), ((), ()))


def mm(left, right, dims=NN):
    return lax.dot_general(left, right, dims, preferred_element_type=f32)


def frames(shifted):
    move = WIN // 2 if shifted else 0
    placed = np.zeros((FRAME, ROWS), np.float32)
    for wy in range(2):
        for wx in range(2):
            for iy in range(WIN):
                for ix in range(WIN):
                    y = (wy * WIN + iy + move) % SIDE
                    x = (wx * WIN + ix + move) % SIDE
                    placed[(wy * 2 + wx) * CELL + iy * WIN + ix, y * SIDE + x] = 1
    return placed


def head_rows():
    rows = np.zeros((QUAD * CELL, 128), np.float32)
    for h in range(QUAD):
        rows[h * CELL : (h + 1) * CELL, h * 32 : (h + 1) * 32] = 1
    return rows


def head_spread(rows):
    out = np.zeros((rows, QUAD * CELL), np.float32)
    for h in range(QUAD):
        out[h, h * CELL : (h + 1) * CELL] = 1
    return out


def norm(rows):
    centred = rows - jnp.mean(rows, -1, keepdims=True)
    spread = lax.rsqrt(jnp.mean(centred * centred, -1, keepdims=True) + norm_eps)
    return centred * spread, spread


def norm_back(grad_unit, unit, spread):
    return spread * (
        grad_unit
        - jnp.mean(grad_unit, -1, keepdims=True)
        - unit * jnp.mean(grad_unit * unit, -1, keepdims=True)
    )


def column_sum(rows):
    return jnp.sum(rows, 0, keepdims=True)


def gelu_pair(u):
    size = jnp.abs(u)
    below = 1.0 + (0.3275911 * 0.5**0.5) * size
    t = pltpu.reciprocal(below, approx=True)
    bell = jnp.exp2(u * u * (-0.5 * 1.4426950408889634))
    poly = t * (
        0.127414796 + t * (-0.142248368 + t * (0.710706871 + t * (-0.726576013 + t * 0.530702714)))
    )
    tail = poly * bell
    phi = jnp.where(u >= 0, 1.0 - tail, tail)
    return u * phi, phi + u * bell * 0.3989422804014327


def quad_rows(part, heads):
    return jnp.concatenate([part] * QUAD, 0) * heads


def pick_heads(stacked, lane_head):
    low = jnp.where(lane_head == 0, stacked[:CELL], stacked[CELL : 2 * CELL])
    high = jnp.where(lane_head == 2, stacked[2 * CELL : 3 * CELL], stacked[3 * CELL :])
    return jnp.where(lane_head < 2, low, high)


def lane_heads():
    return lax.broadcasted_iota(jnp.int32, (CELL, 128), 1) // 32


def whole(shape):
    zero = (0,) * len(shape)
    return pl.BlockSpec(shape, lambda *_: zero, pipeline_mode=pl.Buffered(1))


def per_image(rows, cols):
    return pl.BlockSpec((1, rows, cols), lambda i, *_: (i, 0, 0))


def per_pair(rows, cols):
    return pl.BlockSpec((PAIR, rows, cols), lambda i, *_: (i, 0, 0))


HBM = pl.BlockSpec(memory_space=pl.ANY)


def weight_copies(place, stacks, kept, sems, part=0):
    copies = []
    for m in range(8):
        for s in range(4):
            for p in range(kept.shape[0]):
                if len(stacks) == 1:
                    source, block, owner = stacks[0].at[m, s, part + p], m, s
                else:
                    source = stacks[m % 2].at[m // 2, s, p]
                    block, owner = place[0] ^ m, (place[1] + 4 - s) & 3
                rows = pl.ds(pl.multiple_of(owner * 128, 128), 128)
                cols = pl.ds(pl.multiple_of(block * BLOCK, BLOCK), BLOCK)
                copies.append(
                    pltpu.make_async_copy(
                        source.at[pl.ds(0, 128), :], kept.at[p, rows, cols], sems.at[m, s, p]
                    )
                )
    return copies


def extra_copies(place, stacks, kept, sems):
    copies = []
    for m in range(8):
        for s in range(4):
            if len(stacks) == 1:
                source, block, owner = stacks[0].at[m, s, 0], m, s
            else:
                source = stacks[m % 2].at[m // 2, s, 0]
                block, owner = place[0] ^ m, (place[1] + 4 - s) & 3
            copies.append(
                pltpu.make_async_copy(
                    source.at[pl.ds(128, EXTRA), :], kept.at[block, owner], sems.at[m, s, 0]
                )
            )
    return copies


def fetch(copies):
    for copy in copies:
        copy.start()
    for copy in copies:
        copy.wait()


def call(
    body, name, grid, ins, outs, out_shapes, scratch, cost_us, prefetch=0, aliases=None, mib=20
):
    return pl.pallas_call(
        body,
        name=name,
        grid_spec=pltpu.PrefetchScalarGridSpec(
            num_scalar_prefetch=prefetch,
            grid=grid,
            in_specs=ins,
            out_specs=outs,
            scratch_shapes=scratch,
        ),
        out_shape=out_shapes,
        input_output_aliases=aliases or {},
        compiler_params=pltpu.CompilerParams(
            dimension_semantics=("arbitrary",) * len(grid), vmem_limit_bytes=mib * 1024 * 1024
        ),
        cost_estimate=pl.CostEstimate(
            flops=0, bytes_accessed=int(cost_us * 3.69e4), transcendentals=0
        ),
    )


def shape(dims, kind):
    return jax.ShapeDtypeStruct(dims, kind)


def pack_body(place, *refs):
    mats, (pair_index, tab, vec, spread) = refs[:6], refs[6:10]
    out, mlp0, all1, rel, spread_tab, small = refs[10:]
    rows = mats[0].shape[1]
    out[0, 0:rows, :] = mats[0][0].astype(bf16)
    for ref, at, n in ((mlp0, 0, 1), (mlp0, 1, 2), (all1, 0, 3), (all1, 1, 4), (all1, 2, 5)):
        ref[at] = mats[n][0].astype(bf16)
    rel[...] = jnp.full(rel.shape, -1, jnp.int32)
    across = pair_index[...].astype(f32).T.astype(jnp.int32)
    for h in range(QUAD):
        rel[0 : WIN * WIN, CELL * h : CELL * h + WIN * WIN] = across
    for layer in range(2):
        spread_tab[layer, 0:NREL, :] = mm(tab[layer].astype(bf16), spread[...], TN)
    pairs = rel[pl.ds(pl.multiple_of(place[3] * 8, 8), 8), :]

    def step(r, sums):
        hit = pairs == r
        return tuple(
            jnp.where(hit, spread_tab[layer, pl.ds(r, 1), :], sums[layer]) for layer in range(2)
        )

    start = jnp.zeros((8, QUAD * CELL), f32)
    first, second = lax.fori_loop(0, NREL, step, (start, start), unroll=13)
    out[0, rows : rows + 16, :] = jnp.concatenate([first, second], 0).astype(bf16)
    small[...] = jnp.zeros_like(small)
    row = jnp.minimum(place[3] * 2, 10)
    for layer in range(2):
        for k in range(2):
            small[k : k + 1, layer * 128 : (layer + 1) * 128] = vec[row + k, layer : layer + 1, :]
    out[0, rows + 16 : rows + 32, :] = small[...].astype(bf16)


def pack(place, rows, mat_w, rel_index, tab_w, vec_w):
    vec_w = vec_w.transpose(1, 0, 2)

    def block(layer, part):
        return pl.BlockSpec(
            (1, rows, BLOCK), lambda i, place: (layer, place[4], part * 8 + place[3])
        )

    dims = [(1, rows + EXTRA, BLOCK), (2, rows, BLOCK), (3, rows, BLOCK)]
    return call(
        pack_body,
        "pack",
        (1,),
        [block(layer, part) for layer in range(2) for part in range(3)]
        + [
            whole(rel_index.shape),
            whole(tab_w.shape),
            whole(vec_w.shape),
            whole((QUAD, QUAD * CELL)),
        ],
        [whole(d) for d in dims] + [whole((CELL, QUAD * CELL))],
        [shape(d, bf16) for d in dims] + [shape((CELL, QUAD * CELL), jnp.int32)],
        [pltpu.VMEM((2, 176, QUAD * CELL), f32), pltpu.VMEM((16, 256), f32)],
        4,
        prefetch=1,
    )(place, *[mat_w] * 6, rel_index, tab_w, vec_w, jnp.asarray(head_spread(QUAD), bf16))


def attention_forward_body(layer, stacks, waits, place, *refs):
    arrays, refs = refs[: stacks[0]], refs[stacks[0] :]
    extras, refs = refs[: stacks[1]], refs[stacks[1] + waits :]
    x, mask, perm, perm_back, heads = refs[:5]
    mid, qkv, merged, totals, table, vec, framed, kept, extra_kept, sems, more_sems = refs[5:]
    weight, extra = kept.at[0], extra_kept

    @pl.when(pl.program_id(0) == 0)
    def _():
        fetch(
            weight_copies(place, arrays, kept, sems)
            + extra_copies(place, extras, extra_kept, more_sems)
        )
        vec[...] = jnp.zeros_like(vec)
        for z in range(4):
            for d in range(8):
                pair = extra[d, z, 0:16, :].astype(f32)
                bias = pair[8 * layer : 8 * layer + 8]
                for w in range(table.shape[0]):
                    table[w, z, 8 * d : 8 * d + 8, :] = bias + mask[w, 8 * d : 8 * d + 8, :]
                if d < 6:
                    rows = extra[d, z, 16:32, 128 * layer : 128 * layer + 128].astype(f32)
                    vec[2 * d : 2 * d + 2, 128 * z : 128 * z + 128] = rows[0:2]

    stream = x[0]
    unit, _ = norm(stream)
    normed = (unit * vec[0:1, :] + vec[1:2, :]).astype(bf16)
    normed = mm(perm[...], normed).astype(bf16)
    for c in range(6):
        part = mm(normed, weight[:, 256 * c : 256 * c + 256])
        if c < 2:
            part = part + vec[2:3, 256 * c : 256 * c + 256]
        if c >= 4:
            part = part + vec[3:4, 256 * (c - 4) : 256 * (c - 4) + 256]
        qkv[0, :, 256 * c : 256 * c + 256] = part.astype(bf16)
    lane_head = lane_heads()

    def score(unit):
        rows, at = slice(CELL * (unit // 4), CELL * (unit // 4) + CELL), 128 * (unit % 4)
        query = quad_rows(qkv[0, rows, at : at + 128], heads[...])
        return mm(qkv[0, rows, C + at : C + at + 128], query, NT)

    ahead = score(0)
    for n in range(16):
        w, g = n // 4, n % 4
        rows, at = slice(CELL * w, CELL * w + CELL), 128 * g
        scores = ahead * scale + table[w % table.shape[0], g]
        if n < 15:
            ahead = score(n + 1)
        top = jnp.max(scores, 0, keepdims=True)
        raised = jnp.exp(scores - top)
        total = jnp.sum(raised, 0, keepdims=True)
        totals[0, n : n + 1, :] = top + jnp.log(total)
        probs = (raised * (1.0 / total)).astype(bf16)
        stacked = mm(probs, qkv[0, rows, 2 * C + at : 2 * C + at + 128], TN)
        framed[rows, at : at + 128] = pick_heads(stacked, lane_head).astype(bf16)
    gathered = mm(perm_back[...], framed[...]).astype(bf16)
    merged[0] = gathered
    mid[0] = stream + mm(gathered, weight[:, 3 * C :]) + vec[4:5, :]


def attention_forward(layer, place, x, weight, extra, mask, perm, after):
    images = x.shape[0]
    tables = mask.shape[0]
    return call(
        partial(attention_forward_body, layer, (len(weight), len(extra)), len(after)),
        f"attention_forward_{layer}",
        (images,),
        [HBM] * (len(weight) + len(extra) + len(after))
        + [
            per_image(x.shape[1], C),
            whole(mask.shape),
            whole((FRAME, ROWS)),
            whole((ROWS, FRAME)),
            whole((QUAD * CELL, 128)),
        ],
        [
            per_image(ROWS, C),
            per_image(FRAME, 3 * C),
            per_image(ROWS, C),
            per_image(16, QUAD * CELL),
            pl.BlockSpec((tables, 4, CELL, QUAD * CELL), lambda i, *_: (0, 0, 0, 0)),
            pl.BlockSpec((16, C), lambda i, *_: (0, 0)),
        ],
        [
            shape((images, ROWS, C), f32),
            shape((images, FRAME, 3 * C), bf16),
            shape((images, ROWS, C), bf16),
            shape((images, 16, QUAD * CELL), f32),
            shape((tables, 4, CELL, QUAD * CELL), f32),
            shape((16, C), f32),
        ],
        [
            pltpu.VMEM((FRAME, C), bf16),
            pltpu.VMEM((1, C, HID), bf16),
            pltpu.VMEM((8, 4, EXTRA, BLOCK), bf16),
            pltpu.SemaphoreType.DMA((8, 4, 1)),
            pltpu.SemaphoreType.DMA((8, 4, 1)),
        ],
        20,
        prefetch=1,
        mib=24,
    )(
        place,
        *weight,
        *extra,
        *after,
        x,
        mask,
        jnp.asarray(perm, bf16),
        jnp.asarray(perm.T, bf16),
        jnp.asarray(head_rows(), bf16),
    )


def mlp_forward_body(stacks, waits, place, *refs):
    arrays, refs = refs[:stacks], refs[stacks + waits :]
    mid, vec, result, act, slope, kept, sems = refs
    first, second = kept.at[0], kept.at[1]

    @pl.when(pl.program_id(0) == 0)
    def _():
        fetch(weight_copies(place, arrays, kept, sems))

    rows = PAIR * ROWS
    stream = mid[...].reshape(rows, C)
    unit, _ = norm(stream)
    normed = (unit * vec[5:6, :] + vec[6:7, :]).astype(bf16)
    ahead = mm(normed, first[:, 0:BLOCK])
    for c in range(8):
        cols = slice(256 * c, 256 * c + 256)
        bias = vec[8 + c // 2 : 9 + c // 2, 256 * (c % 2) : 256 * (c % 2) + 256]
        inner = ahead + bias
        if c < 7:
            ahead = mm(normed, first[:, 256 * c + 256 : 256 * c + 512])
        value, pull = gelu_pair(inner)
        act[:, :, cols] = value.astype(bf16).reshape(PAIR, ROWS, BLOCK)
        slope[:, :, cols] = pull.astype(bf16).reshape(PAIR, ROWS, BLOCK)
    total = stream + vec[7:8, :] + mm(act[...].reshape(rows, HID), second[...], NT)
    result[...] = total.reshape(PAIR, ROWS, C)


def mlp_forward(layer, place, mid, weight, vec, after):
    images = mid.shape[0]
    return call(
        partial(mlp_forward_body, len(weight), len(after)),
        f"mlp_forward_{layer}",
        (images // PAIR,),
        [HBM] * (len(weight) + len(after)) + [per_pair(ROWS, C), whole(vec.shape)],
        [per_pair(ROWS, C), per_pair(ROWS, HID), per_pair(ROWS, HID)],
        [
            shape((images, ROWS, C), f32),
            shape((images, ROWS, HID), bf16),
            shape((images, ROWS, HID), bf16),
        ],
        [
            pltpu.VMEM((2, C, HID), bf16),
            pltpu.SemaphoreType.DMA((8, 4, 2)),
        ],
        22,
        prefetch=1,
        mib=32,
    )(place, *weight, *after, mid, vec)


def mlp_both_body(stacks, waits, place, *refs):
    arrays, refs = refs[:stacks], refs[stacks + waits :]
    grad, mid, vec, result, grad_mid, pieces, small = refs[:7]
    all_grad, all_act, all_inner, all_normed, kept, sems = refs[7:]
    first, second = kept.at[0], kept.at[1]
    i = pl.program_id(0)

    @pl.when(i == 0)
    def _():
        fetch(weight_copies(place, arrays, kept, sems, 1))
        small[...] = jnp.zeros_like(small)

    rows = PAIR * ROWS
    grad_out = grad[...].reshape(rows, C)
    here = pl.ds(pl.multiple_of(i * rows, 32), rows)
    low = grad_out.astype(bf16)
    all_grad[here, :] = low
    small[7:8, :] += column_sum(grad_out)
    stream = mid[...].reshape(rows, C)
    unit, spread = norm(stream)
    normed = (unit * vec[5:6, :] + vec[6:7, :]).astype(bf16)
    all_normed[here, :] = normed
    ahead = mm(normed, first[:, 0:BLOCK]), mm(low, second[:, 0:BLOCK])
    for c in range(8):
        cols = slice(256 * c, 256 * c + 256)
        row, lane = 8 + c // 2, 256 * (c % 2)
        bias = vec[row : row + 1, lane : lane + 256]
        inner, grad_act = ahead
        if c < 7:
            later = slice(256 * c + 256, 256 * c + 512)
            ahead = mm(normed, first[:, later]), mm(low, second[:, later])
        value, pull = gelu_pair(inner + bias)
        all_act[here, cols] = value.astype(bf16)
        inner = (grad_act * pull).astype(bf16)
        all_inner[here, cols] = inner
        small[row : row + 1, lane : lane + 256] += column_sum(inner.astype(f32))
    back = mm(all_inner[here, :], first[...], NT)
    small[5:6, :] += column_sum(back * unit)
    small[6:7, :] += column_sum(back)
    grad_mid[...] = (grad_out + norm_back(back * vec[5:6, :], unit, spread)).reshape(PAIR, ROWS, C)
    total = stream + vec[7:8, :] + mm(all_act[here, :], second[...], NT)
    for n in range(PAIR):
        alive = (i * PAIR + n < place[2]).astype(f32)
        result[n] = (total[n * ROWS : n * ROWS + TOKENS] * alive).astype(bf16)

    @pl.when(i == pl.num_programs(0) - 1)
    def _():
        mlp_weight_grads(place, all_grad, all_act, all_inner, all_normed, pieces)


def mlp_weight_grads(place, all_grad, all_act, all_inner, all_normed, *outs):
    grad_across = all_grad[...].T
    normed_across = all_normed[...].T
    for m in range(8):
        block = m if len(outs) == 1 else place[0] ^ m
        cols = pl.ds(pl.multiple_of(block * BLOCK, BLOCK), BLOCK)
        for p, total in enumerate(
            (mm(normed_across, all_inner[:, cols]), mm(grad_across, all_act[:, cols]))
        ):
            total = total.astype(bf16)
            for z in range(4):
                if len(outs) == 1:
                    outs[0][m, z, p] = total[128 * z : 128 * z + 128]
                else:
                    outs[m % 2][m // 2, z, p] = total[128 * z : 128 * z + 128]


def mlp_both(place, grad, mid, weight, vec, after):
    images = mid.shape[0]
    total = images * ROWS
    pieces = (8, 4, 2, 128, BLOCK)
    return call(
        partial(mlp_both_body, len(weight), len(after)),
        "mlp_both",
        (images // PAIR,),
        [HBM] * (len(weight) + len(after)) + [per_pair(ROWS, C), per_pair(ROWS, C), whole(vec.shape)],
        [per_pair(TOKENS, C), per_pair(ROWS, C), whole(pieces), whole((16, C))],
        [
            shape((images, TOKENS, C), bf16),
            shape((images, ROWS, C), f32),
            shape(pieces, bf16),
            shape((16, C), f32),
        ],
        [
            pltpu.VMEM((total, C), bf16),
            pltpu.VMEM((total, HID), bf16),
            pltpu.VMEM((total, HID), bf16),
            pltpu.VMEM((total, C), bf16),
            pltpu.VMEM((2, C, HID), bf16),
            pltpu.SemaphoreType.DMA((8, 4, 2)),
        ],
        45,
        prefetch=1,
        mib=46,
    )(place, *weight, *after, grad, mid, vec)


def mlp_backward_body(stacks, waits, place, *refs):
    arrays, refs = refs[:stacks], refs[stacks + waits :]
    grad, act, slope, mid, vec, grad_mid, own, other, small = refs[:9]
    all_grad, all_act, all_inner, all_normed, kept, sems = refs[9:]
    first, second = kept.at[0], kept.at[1]
    i = pl.program_id(0)

    @pl.when(i == 0)
    def _():
        fetch(weight_copies(place, arrays, kept, sems))
        small[...] = jnp.zeros_like(small)

    rows = PAIR * ROWS
    grad_out = grad[...].reshape(rows, C)
    here = pl.ds(pl.multiple_of(i * rows, 32), rows)
    low = grad_out.astype(bf16)
    all_grad[here, :] = low
    small[7:8, :] += column_sum(low.astype(f32))
    all_act[here, :] = act[...].reshape(rows, HID)
    unit, spread = norm(mid[...].reshape(rows, C))
    all_normed[here, :] = (unit * vec[5:6, :] + vec[6:7, :]).astype(bf16)
    ahead = mm(low, second[:, 0:BLOCK])
    for c in range(8):
        cols = slice(256 * c, 256 * c + 256)
        pull = slope[:, :, cols].reshape(rows, BLOCK).astype(f32)
        grad_act = ahead
        if c < 7:
            ahead = mm(low, second[:, 256 * c + 256 : 256 * c + 512])
        inner = (grad_act * pull).astype(bf16)
        all_inner[here, cols] = inner
        row, lane = 8 + c // 2, 256 * (c % 2)
        small[row : row + 1, lane : lane + 256] += column_sum(inner.astype(f32))
    back = mm(all_inner[here, :], first[...], NT)
    small[5:6, :] += column_sum(back * unit)
    small[6:7, :] += column_sum(back)
    grad_mid[...] = (grad_out + norm_back(back * vec[5:6, :], unit, spread)).reshape(PAIR, ROWS, C)

    @pl.when(i == pl.num_programs(0) - 1)
    def _():
        mlp_weight_grads(place, all_grad, all_act, all_inner, all_normed, own, other)


def mlp_backward(layer, place, grad, act, slope, mid, weight, vec, after):
    images = mid.shape[0]
    total = images * ROWS
    pieces = (4, 4, 2, 128, BLOCK)
    return call(
        partial(mlp_backward_body, len(weight), len(after)),
        f"mlp_backward_{layer}",
        (images // PAIR,),
        [HBM] * (len(weight) + len(after))
        + [
            per_pair(grad.shape[1], C),
            per_pair(ROWS, HID),
            per_pair(ROWS, HID),
            per_pair(ROWS, C),
            whole(vec.shape),
        ],
        [per_pair(ROWS, C), whole(pieces), whole(pieces), whole((16, C))],
        [
            shape((images, ROWS, C), f32),
            shape(pieces, bf16),
            shape(pieces, bf16),
            shape((16, C), f32),
        ],
        [
            pltpu.VMEM((total, C), bf16),
            pltpu.VMEM((total, HID), bf16),
            pltpu.VMEM((total, HID), bf16),
            pltpu.VMEM((total, C), bf16),
            pltpu.VMEM((2, C, HID), bf16),
            pltpu.SemaphoreType.DMA((8, 4, 2)),
        ],
        30,
        prefetch=1,
        mib=52,
    )(place, *weight, *after, grad, act, slope, mid, vec)


def attention_backward_body(layer, stacks, waits, resumed, ends, place, *refs):
    arrays, refs = refs[:stacks], refs[stacks + waits :]
    if resumed:
        (own_before, other_before, pairs_before), refs = refs[1:4], refs[4:]
    grad, x, qkv, merged, totals, table, vec, before = refs[:8]
    perm, perm_back, heads, rel, spread, result = refs[8:14]
    outs, refs = (refs[14:15], refs[15:]) if layer else (refs[14:16], refs[16:])
    pairs, small, framed, grad_framed, all_normed, all_packed, all_merged = refs[:7]
    across, hits, beside, kept, sems = refs[7:]
    weight = kept.at[0]
    i = pl.program_id(0)

    @pl.when(i == 0)
    def _():
        fetch(weight_copies(place, arrays, kept, sems))
        small[...] = before[...]
        pairs[...] = pairs_before[...] if resumed else jnp.zeros_like(pairs)

    stream = x[0]
    here = pl.ds(pl.multiple_of(i * ROWS, 16), ROWS)
    unit, spread_one = norm(stream)
    all_normed[here, :] = (unit * vec[0:1, :] + vec[1:2, :]).astype(bf16)
    low = grad[0].astype(bf16)
    all_packed[here, 3 * C :] = low
    all_merged[here, :] = merged[0]
    small[4:5, :] += column_sum(low.astype(f32))
    moved = mm(perm[...], low).astype(bf16)
    framed[...] = mm(moved, weight[:, 3 * C :], NT).astype(bf16)
    lane_head = lane_heads()
    at = [128 * g for g in range(4)]

    def window(w):
        rows = slice(CELL * w, CELL * w + CELL)
        keys = [qkv[0, rows, C + c : C + c + 128] for c in at]
        query = [quad_rows(qkv[0, rows, c : c + 128], heads[...]) for c in at]
        pull = [quad_rows(framed[rows, c : c + 128], heads[...]) for c in at]
        scores = [mm(keys[g], query[g], NT) for g in range(4)]
        grad_probs = [
            mm(qkv[0, rows, 2 * C + at[g] : 2 * C + at[g] + 128], pull[g], NT) for g in range(4)
        ]
        return keys, query, pull, scores, grad_probs

    ahead = window(0)
    for w in range(4):
        rows = slice(CELL * w, CELL * w + CELL)
        keys, query, pull, scores, grad_probs = ahead
        if w < 3:
            ahead = window(w + 1)
        probs, grad_scores = [], []
        for g in range(4):
            shifted = scores[g] * scale + table[w % table.shape[0], g]
            prob = jnp.exp(shifted - totals[0, 4 * w + g : 4 * w + g + 1, :])
            mean = jnp.sum(prob * grad_probs[g], 0, keepdims=True)
            grad_score = (prob * (grad_probs[g] - mean)).astype(bf16)
            pairs[g] += grad_score.astype(f32)
            probs.append(prob.astype(bf16))
            grad_scores.append(grad_score)
        for g in range(4):
            grad_value = mm(probs[g], pull[g])
            grad_framed[rows, 2 * C + at[g] : 2 * C + at[g] + 128] = grad_value.astype(bf16)
        for g in range(4):
            grad_key = mm(grad_scores[g], query[g]) * scale
            grad_framed[rows, C + at[g] : C + at[g] + 128] = grad_key.astype(bf16)
        for g in range(4):
            grad_query = pick_heads(mm(grad_scores[g], keys[g], TN), lane_head) * scale
            grad_framed[rows, at[g] : at[g] + 128] = grad_query.astype(bf16)
    for c in range(6):
        cols = slice(256 * c, 256 * c + 256)
        part = mm(perm_back[...], grad_framed[:, cols])
        all_packed[here, cols] = part.astype(bf16)
        if c < 2:
            small[2:3, cols] += column_sum(part)
        if c >= 4:
            small[3:4, 256 * (c - 4) : 256 * (c - 4) + 256] += column_sum(part)
    back = mm(all_packed[here, : 3 * C], weight[:, : 3 * C], NT)
    small[0:1, :] += column_sum(back * unit)
    small[1:2, :] += column_sum(back)
    total = grad[0] + norm_back(back * vec[0:1, :], unit, spread_one)
    result[0] = total[: result.shape[1]]

    @pl.when(i == pl.num_programs(0) - 1)
    def _():
        across[0] = all_normed[...].T
        across[1] = all_merged[...].T
        beside[...] = jnp.zeros_like(beside)
        if ends:
            hits[...] = jnp.zeros_like(hits)

            def step(r, carry):
                same = rel[...] == r
                for g in range(4):
                    kept_pairs = jnp.where(same, pairs[g], 0.0)
                    hits[pl.ds(r, 1), 256 * g : 256 * g + 256] = column_sum(kept_pairs)
                return carry

            lax.fori_loop(0, NREL, step, 0)
            for z in range(4):
                beside[0, z] = lax.dot_general(
                    spread[...],
                    hits[:, 256 * z : 256 * z + 256],
                    NT,
                    precision=lax.Precision.HIGHEST,
                    preferred_element_type=f32,
                ).astype(bf16)
                beside[1, z, :, 0:128] = small[:, 128 * z : 128 * z + 128].astype(bf16)
        for m in range(8):
            b = m if layer else place[0] ^ m
            left = across[jnp.where(b < 6, 0, 1)]
            right = all_packed[:, pl.ds(pl.multiple_of(b * BLOCK, BLOCK), BLOCK)]
            block = mm(left, right)
            for z in range(4):
                if layer:
                    out = outs[0].at[m, z, 0]
                else:
                    to = (z + 4 - place[1]) & 3
                    out = outs[m % 2].at[m // 2, to, 0]
                new = block[128 * z : 128 * z + 128]
                if resumed:
                    old = other_before if m % 2 else own_before
                    new = new + old[m // 2, to, 0, 0:128, :].astype(f32)
                out[0:128, :] = new.astype(bf16)
                out[128:144, :] = beside[jnp.minimum(b, 2), z]


def attention_backward(
    layer, place, grad, x, qkv, merged, totals, table, weight, vec, small, perm, rel, after,
    first=0, count=None, resume=None,
):
    images = grad.shape[0]
    count = count or images
    pieces = (8 if layer else 4, 4, 1, 128 + SMALL, BLOCK)
    pairs = (4, CELL, QUAD * CELL)
    total = count * ROWS
    out_rows = TOKENS if layer == 0 else ROWS

    def image(rows, cols):
        return pl.BlockSpec((1, rows, cols), lambda i, *_: (i + first, 0, 0))

    resumed = list(resume or [])
    return call(
        partial(
            attention_backward_body, layer, len(weight), len(after), bool(resumed),
            first + count == images,
        ),
        f"attention_backward_{layer}_{first}",
        (count,),
        [HBM] * (len(weight) + len(after))
        + ([HBM, whole(pieces), whole(pieces), whole(pairs)] if resumed else [])
        + [
            image(ROWS, C),
            image(x.shape[1], C),
            image(FRAME, 3 * C),
            image(ROWS, C),
            image(16, QUAD * CELL),
            whole(table.shape),
            whole(vec.shape),
            whole((16, C)),
            whole((FRAME, ROWS)),
            whole((ROWS, FRAME)),
            whole((QUAD * CELL, 128)),
            whole(rel.shape),
            whole((SMALL, QUAD * CELL)),
        ],
        [image(out_rows, C)]
        + [whole(pieces)] * (1 if layer else 2)
        + [whole(pairs), whole((16, C))],
        [shape((images, out_rows, C), f32)]
        + [shape(pieces, bf16)] * (1 if layer else 2)
        + [shape(pairs, f32), shape((16, C), f32)],
        [
            pltpu.VMEM((FRAME, C), bf16),
            pltpu.VMEM((FRAME, 3 * C), bf16),
            pltpu.VMEM((total, C), bf16),
            pltpu.VMEM((total, 4 * C), bf16),
            pltpu.VMEM((total, C), bf16),
            pltpu.VMEM((2, C, total), bf16),
            pltpu.VMEM((256, 4 * QUAD * CELL), f32),
            pltpu.VMEM((3, 4, SMALL, BLOCK), bf16),
            pltpu.VMEM((1, C, HID), bf16),
            pltpu.SemaphoreType.DMA((8, 4, 1)),
        ],
        6 * count,
        prefetch=1,
        mib=40,
        aliases={1 + len(weight) + len(after): 0} if resumed else None,
    )(
        place,
        *weight,
        *after,
        *resumed,
        grad,
        x,
        qkv,
        merged,
        totals,
        table,
        vec,
        small,
        jnp.asarray(perm, bf16),
        jnp.asarray(perm.T, bf16),
        jnp.asarray(head_rows(), bf16),
        rel,
        jnp.asarray(head_spread(SMALL), f32),
    )


def adam_step(weight, first, second, gradient, rate, decay):
    first_new = beta_one * first + (1.0 - beta_one) * gradient
    second_new = beta_two * second + (1.0 - beta_two) * gradient * gradient
    first_hat = first_new / (1.0 - beta_one**STEP)
    second_hat = second_new / (1.0 - beta_two**STEP)
    weight_new = weight - rate * (first_hat / (jnp.sqrt(second_hat) + adam_eps) + decay * weight)
    return (weight_new, first_new, second_new)


def adam_block(grad, weight, first, second, outs, cols):
    part = grad.astype(f32)
    first_new = beta_one * first[0, :, cols] + (1.0 - beta_one) * part
    second_new = beta_two * second[0, :, cols] + (1.0 - beta_two) * part * part
    spread = second_new * (1.0 / (1.0 - beta_two**STEP))
    inverse = pltpu.reciprocal(spread * lax.rsqrt(spread) + adam_eps, approx=True)
    step = first_new * (rate_matrix / (1.0 - beta_one**STEP)) * inverse
    outs[0][0, :, cols] = weight[0, :, cols] * (1.0 - rate_matrix * weight_decay) - step
    outs[1][0, :, cols] = first_new
    outs[2][0, :, cols] = second_new


def adam_body(place, near, far, weight, first, second, *refs):
    for j in range(2):
        for k in range(2):
            block = (((place[0] // 2) & 1) ^ j) * 2 + ((place[0] & 1) ^ k)
            cols = pl.ds(pl.multiple_of(block * BLOCK, BLOCK), BLOCK)
            adam_block((far if k else near)[j], weight, first, second, refs[-3:], cols)


def adam_body_plain(place, sums, weight, first, second, *refs):
    for k in range(4):
        cols = slice(BLOCK * k, BLOCK * k + BLOCK)
        adam_block(sums[k], weight, first, second, refs[-3:], cols)


def adam(layer, part, place, sums, state, done, after):
    kept = [] if done is None else list(done)
    if len(sums) == 2:
        parts = sums[0].shape[1] // 128
        body = adam_body
        spec = pl.BlockSpec(
            (1, 128, 4 * BLOCK),
            lambda p, j, place: (layer, 0, (part + p) % 3 * 2 + ((place[0] // 4) ^ j)),
        )
        piece = pl.BlockSpec((2, 128, BLOCK), lambda p, j, place: (j, p, 0))
    else:
        parts = sums[0].shape[1] // 128
        body = adam_body_plain
        spec = pl.BlockSpec(
            (1, 128, 4 * BLOCK), lambda p, j, place: (layer, 0, (part + p) % 3 * 2 + j)
        )
        piece = pl.BlockSpec((4, 128, BLOCK), lambda p, j, place: (j, p, 0))
    return call(
        body,
        f"adam_{layer}_{part}",
        (parts, 2),
        [piece] * len(sums) + [spec] * 3 + [HBM] * (len(kept) + len(after)),
        [spec] * 3,
        [shape(state[0].shape, f32)] * 3,
        [],
        3 * parts,
        prefetch=1,
        aliases={4 + len(sums) + k: k for k in range(len(kept))},
    )(place, *sums, *state, *kept, *after)


def swap(value, bits):
    return lax.ppermute(value, "dp", [(i, i ^ bits) for i in range(8)])


def shift(value, steps):
    return lax.ppermute(value, "zero", [(i, (i + steps) % 4) for i in range(4)])


def tie(values, after):
    values = list(values)
    return list(lax.optimization_barrier((*values, *after))[: len(values)])


def stack(values, after=()):
    return jnp.stack(tie(values, after) if after else values)


def add_body(count, *refs):
    total = refs[0][...].astype(f32)
    for k in range(1, count):
        total = total + refs[k][...].astype(f32)
    refs[-1][...] = total.astype(bf16)


def add(values, after=()):
    dims = values[0].shape
    return call(
        partial(add_body, len(values)),
        "add",
        (1,),
        [whole(dims)] * len(values) + [HBM] * len(after),
        whole(dims),
        shape(dims, bf16),
        [],
        10,
    )(*values, *after)


def add_split_body(count, lead, *refs):
    for k in range(4):
        if count == 2:
            refs[len(refs) - 4 + k][...] = refs[0][k] + refs[1][k]
            continue
        total = refs[0][k].astype(f32)
        for v in range(1, count):
            total = total + refs[v][k].astype(f32)
        refs[len(refs) - 4 + k][...] = total.astype(bf16)


def add_split(values, after=()):
    dims = values[0].shape
    steps = 1
    ins = (4, dims[1] // steps, *dims[2:])
    outs = dims[1:]
    zeros = (0,) * (len(dims) - 2)
    return call(
        partial(add_split_body, len(values), True),
        "add_split",
        (steps,),
        [pl.BlockSpec(ins, lambda i: (0, i, *zeros))] * len(values) + [HBM] * len(after),
        [pl.BlockSpec((outs[0] // steps, *outs[1:]), lambda i: (i, *zeros))] * 4,
        [shape(outs, bf16)] * 4,
        [],
        10,
    )(*values, *after)


def join_body(*refs):
    out = refs[-1]
    at = 0
    for group in (refs[:1], refs[1:2], refs[2:6]):
        parts, rows = group[0].shape[1:3]
        for p in range(parts):
            total = group[0][:, p]
            if len(group) > 1:
                total = total.astype(f32)
                for ref in group[1:]:
                    total = total + ref[:, p].astype(f32)
            out[:, at : at + rows, :] = total.astype(bf16)
            at += rows


def join(first, second, summed, after):
    rows = sum(value.shape[1] * value.shape[2] for value in (first, second, summed[0]))
    ins = [first, second, *summed]
    return call(
        join_body,
        "join",
        (1,),
        [whole(v.shape) for v in ins] + [HBM] * len(after),
        whole((4, rows, BLOCK)),
        shape((4, rows, BLOCK), bf16),
        [],
        5,
    )(*ins, *after)


def add_last_body(*refs):
    done, out = refs[0], refs[-1]
    rows = 256
    out[0:rows, :] = done[done.shape[0] - rows :, :]
    total = refs[1][0].astype(f32)
    for ref in refs[2:5]:
        total = total + ref[0].astype(f32)
    out[rows : rows + total.shape[0], :] = total.astype(bf16)


def add_last(done, values, after):
    rows = 256 + values[0].shape[1]
    return call(
        add_last_body,
        "add_last",
        (1,),
        [whole(done.shape)] + [whole(v.shape) for v in values] + [HBM] * len(after),
        whole((rows, BLOCK)),
        shape((rows, BLOCK), bf16),
        [],
        10,
    )(done, *values, *after)


def send_z(piece):
    return [piece] + [shift(piece, s) for s in range(1, 4)]


def send_plane(piece):
    return [piece] + [swap(piece, 2 * j) for j in range(1, 4)]


def give_plane(parts):
    return [parts[0]] + [swap(parts[j], 2 * j) for j in range(1, 4)]


def give_z(parts):
    return [parts[0]] + [shift(parts[s], s) for s in range(1, 4)]


def gather_wide(piece, dp, extra):
    fine = dp // 8
    parts, rows = piece.shape[0], piece.shape[1] - extra
    out = lax.all_gather(piece, ("dp", "zero"), axis=0, tiled=False)
    out = out.reshape(8, fine, 4, *piece.shape)
    main = out[..., :rows, :].transpose(0, 2, 3, 1, 4, 5).reshape(8, 4, parts, 128, BLOCK)
    return [jnp.concatenate([main, out[:, 0, ..., rows:, :]], 3)]


def reduce_wide(blocks, dp, extra):
    fine = dp // 8
    blocks = blocks.reshape(8, 4, *blocks.shape[-3:])
    parts, rows = blocks.shape[2], 128 // fine
    main = blocks[..., :128, :].reshape(8, 4, parts, fine, rows, BLOCK).transpose(0, 3, 1, 2, 4, 5)
    beside = jnp.broadcast_to(
        blocks[:, None, ..., 128:, :], (8, fine, 4, parts, extra, BLOCK)
    )
    flat = jnp.concatenate([main, beside], 4).reshape(dp * 4, parts, rows + extra, BLOCK)
    mine = lax.psum_scatter(flat, ("dp", "zero"), scatter_dimension=0, tiled=True)
    out = lax.all_gather(mine[0], "dp", axis=0, tiled=False)
    out = out.reshape(8, fine, parts, rows + extra, BLOCK)
    main = out[..., :rows, :].transpose(0, 2, 1, 3, 4).reshape(8, parts, 128, BLOCK)
    out = jnp.concatenate([main, out[:, 0, :, rows:]], 2)
    return out.reshape(8, -1, BLOCK)


def shards(
    dp, images, cotangent, counts, rel_index, regions,
    mat_w, mat_m, mat_v, vec_w, vec_m, vec_v, tab_w, tab_m, tab_v,
):
    near = dp == 8
    fine = dp // 8
    rows = 128 // fine
    me = lax.axis_index("dp")
    spot = [me, lax.axis_index("zero")] if near else [0 * me, 0 * me]
    place = jnp.stack(spot + [counts[0], me // fine, me % fine]).astype(jnp.int32)

    inside = np.arange(CELL) < WIN * WIN
    zones = regions.reshape(2, WIN, 2, WIN).transpose(0, 2, 1, 3).reshape(4, WIN * WIN)
    zones = jnp.pad(zones, ((0, 0), (0, 15)))
    differ = (zones[:, :, None] != zones[:, None, :]) & inside[None, None, :]
    outside = np.where(inside, 0.0, -1e30).astype(np.float32)[None, :, None]
    mask_shifted = jnp.tile(jnp.where(differ, mask_value, 0.0) + outside, (1, 1, QUAD)).astype(f32)
    mask_plain = jnp.asarray(np.ascontiguousarray(np.broadcast_to(outside, (1, CELL, QUAD * CELL))))
    masks = (mask_plain, mask_shifted)
    perms = (frames(False), frames(True))

    packed, cut_mlp0, cut_all1, rel = pack(
        place, rows, mat_w, rel_index, tab_w, vec_w
    )
    alive = (jnp.arange(images.shape[0]) < counts[0]).astype(f32)[:, None, None]
    pad = ((0, 0), (0, ROWS - TOKENS), (0, 0))
    images = jnp.pad(images.astype(f32), pad)
    cotangent = jnp.pad(cotangent.astype(f32) * alive, pad)

    def attention(layer, stream, weight, after):
        return attention_forward(
            layer, place, stream, weight, heads0, masks[layer], perms[layer], after
        )

    half = images.shape[0] // 2
    if near:
        sent_heads0 = send_z(packed)
        *sent_heads0, images = tie([*sent_heads0, images], [])
        z_heads0 = stack(sent_heads0)
        all1 = gather_wide(tie([cut_all1], [z_heads0])[0], dp, 0)
        sent_heads0 = send_plane(z_heads0)
        sent_mlp0 = send_z(tie([cut_mlp0], [z_heads0])[0])
        cotangent, mask_shifted = tie([cotangent, mask_shifted], [z_heads0])
        *sent_heads0, cotangent, mask_shifted = tie(
            [*sent_heads0, cotangent, mask_shifted], sent_mlp0
        )
        masks = (mask_plain, mask_shifted)
        p_heads0 = stack(sent_heads0)
        heads0 = [p_heads0, swap(p_heads0, 1)]
        z_mlp0 = stack(sent_mlp0, [p_heads0])
        sent_mlp0 = send_plane(z_mlp0)
        kept0 = attention(0, images, heads0, [z_mlp0])
        p_mlp0 = stack(sent_mlp0, [kept0[0]])
        mlp0 = [p_mlp0, swap(p_mlp0, 1)]
    else:
        heads0 = gather_wide(packed, dp, EXTRA)
        mlp0 = gather_wide(cut_mlp0, dp, 0)
        all1 = gather_wide(cut_all1, dp, 0)
        kept0 = attention(0, images, heads0, [])
    stream, act, slope = mlp_forward(0, place, kept0[0], mlp0, kept0[5], [])
    kept1 = attention(1, stream, all1, [])
    kept = (kept0, kept1)
    inputs = (images, stream)
    attention_w = (heads0, all1)

    def backward_attention(layer, gradient, small, after, *span):
        mid, qkv, merged, totals, table, vec = kept[layer]
        return attention_backward(
            layer, place, gradient, inputs[layer], qkv, merged, totals, table, attention_w[layer],
            vec, small, perms[layer], rel, after, *span,
        )

    activations, grad_mid, parts_mlp1, small = mlp_both(
        place, cotangent, kept1[0], all1, kept1[5], []
    )

    def backward_mlp0(gradient, after):
        return mlp_backward(0, place, gradient, act, slope, kept0[0], mlp0, kept0[5], after)

    state = (mat_w, mat_m, mat_v)
    def exchange(parts):
        return [parts[0], swap(parts[1], 1)]

    gradient, parts_heads1, _, _ = backward_attention(1, grad_mid, small, [])
    grad_mid, *parts_mlp0, small = backward_mlp0(gradient, [])
    if near:
        t_mlp1 = lax.psum_scatter(parts_mlp1, "dp", scatter_dimension=0, tiled=True)[0]
        parts_heads1 = tie([parts_heads1], [t_mlp1, small])[0]
        t_heads1 = lax.psum_scatter(parts_heads1, "dp", scatter_dimension=0, tiled=True)[0]
        gone_mlp0 = exchange(parts_mlp0)
        gradient, *parts_heads0, pairs, small = backward_attention(0, grad_mid, small, [], 0, half)

        s_mlp0 = add_split(gone_mlp0, [gradient])
        gone_mlp0 = give_plane(s_mlp0)
        gradient, *parts_heads0, _, small = backward_attention(
            0, grad_mid, small, [s_mlp0[0]], half, half, [gradient, *parts_heads0, pairs]
        )

        t_all = join(t_mlp1, t_heads1, gone_mlp0, [small])
        gone_heads0 = exchange(tie(parts_heads0, gone_mlp0))
        g_all = lax.psum_scatter(t_all, "zero", scatter_dimension=0, tiled=True)[0]
        s_heads0 = add_split(gone_heads0, [t_all])
        gone_heads0 = give_plane(s_heads0)
        across = tie([activations.transpose(1, 0, 2), gradient.transpose(1, 0, 2)], [])
        t_heads0 = add_split(gone_heads0, across)
        activations, gradient = [value.transpose(1, 0, 2) for value in across]
        gone_heads0 = give_z(t_heads0)
        g_all, *gone_heads0 = tie([g_all, *gone_heads0], [])
        g_all0 = add_last(g_all, gone_heads0, [])
        g_all = tie([g_all], [g_all0])[0]
        n_all1 = lax.all_gather(g_all[:400], "dp", axis=0, tiled=False)
        n_all0 = stack(send_plane(g_all0))
        sums0 = [n_all0, swap(n_all0, 1)]
        m = place[0] ^ np.arange(2)
        both = jnp.concatenate([half[:, 384:] for half in sums0])
        beside0 = [
            lax.dynamic_index_in_dim(both, (m[b] % 2) * 4 + m[b] // 2, 0, False) for b in range(2)
        ]
    else:
        gradient, *parts_heads0, _, _ = backward_attention(0, grad_mid, small, [])
        n_mlp1 = reduce_wide(parts_mlp1, dp, 0)
        n_heads1 = reduce_wide(parts_heads1, dp, SMALL)
        n_all1 = jnp.concatenate([n_mlp1, n_heads1], 1)
        n_mlp0 = reduce_wide(jnp.stack(parts_mlp0, 1), dp, 0)
        n_heads0 = reduce_wide(jnp.stack(parts_heads0, 1), dp, SMALL)
        sums0 = [jnp.concatenate([n_mlp0, n_heads0], 1)]
        beside0 = sums0[0][:2, 384:]
    done = adam(0, 1, place, sums0, state, None, [])
    done = adam(1, 1, place, [n_all1], state, done, [])

    def beside(block):
        return jnp.stack([beside0[block], n_all1[block, 384:]]).astype(f32)

    new_vec = adam_step(vec_w, vec_m, vec_v, beside(1)[:, 0:12, 0:128], rate_vector, 0.0)
    new_tab = adam_step(tab_w, tab_m, tab_v, beside(0)[:, 0:4, 0:NREL], rate_table, 0.0)
    return (activations, gradient, *done, *new_vec, *new_tab)


def solution(mesh):
    images = P(("dp", "zero"), None, None)
    rows = P(None, "zero", None)
    lanes = P(None, None, "zero")
    return jax.shard_map(
        partial(shards, mesh.shape["dp"]),
        mesh=mesh,
        in_specs=(images, images, P(("dp", "zero")), P(), P())
        + (rows,) * 3 + (lanes,) * 3 + (rows,) * 3,
        out_specs=(images, images) + (rows,) * 3 + (lanes,) * 3 + (rows,) * 3,
        check_vma=False,
    )
```

```python
from functools import partial

import jax
import jax.numpy as jnp
import numpy as np
from jax import lax
from jax.experimental import pallas as pl
from jax.experimental.pallas import tpu as pltpu
from jax.sharding import PartitionSpec as P

WIN = 7
SIDE = 14
STEP = 10
NREL = 169
C = 512
HID = 2048
TOKENS = SIDE * SIDE
PAIR = 2
ROWS = 208
FRAME = 256
CELL = 64
QUAD = 4
BLOCK = 256
EXTRA = 32
SMALL = 16

norm_eps = 1e-05
mask_value = -100.0
beta_one = 0.9
beta_two = 0.999
adam_eps = 1e-08
weight_decay = 0.05
rate_matrix = 0.1
rate_vector = 0.5
rate_table = 1.0
scale = 32 ** (-0.5)

bf16 = jnp.bfloat16
f32 = jnp.float32
NN = (((1,), (0,)), ((), ()))
NT = (((1,), (1,)), ((), ()))
TN = (((0,), (0,)), ((), ()))


def mm(left, right, dims=NN):
    return lax.dot_general(left, right, dims, preferred_element_type=f32)


def frames(shifted):
    move = WIN // 2 if shifted else 0
    placed = np.zeros((FRAME, ROWS), np.float32)
    for wy in range(2):
        for wx in range(2):
            for iy in range(WIN):
                for ix in range(WIN):
                    y = (wy * WIN + iy + move) % SIDE
                    x = (wx * WIN + ix + move) % SIDE
                    placed[(wy * 2 + wx) * CELL + iy * WIN + ix, y * SIDE + x] = 1
    return placed


def head_rows():
    rows = np.zeros((QUAD * CELL, 128), np.float32)
    for h in range(QUAD):
        rows[h * CELL : (h + 1) * CELL, h * 32 : (h + 1) * 32] = 1
    return rows


def head_spread(rows):
    out = np.zeros((rows, QUAD * CELL), np.float32)
    for h in range(QUAD):
        out[h, h * CELL : (h + 1) * CELL] = 1
    return out


def norm(rows):
    centred = rows - jnp.mean(rows, -1, keepdims=True)
    spread = lax.rsqrt(jnp.mean(centred * centred, -1, keepdims=True) + norm_eps)
    return centred * spread, spread


def norm_back(grad_unit, unit, spread):
    return spread * (
        grad_unit
        - jnp.mean(grad_unit, -1, keepdims=True)
        - unit * jnp.mean(grad_unit * unit, -1, keepdims=True)
    )


def column_sum(rows):
    return jnp.sum(rows, 0, keepdims=True)


def gelu_pair(u):
    size = jnp.abs(u)
    below = 1.0 + (0.3275911 * 0.5**0.5) * size
    t = pltpu.reciprocal(below, approx=True)
    bell = jnp.exp2(u * u * (-0.5 * 1.4426950408889634))
    poly = t * (
        0.127414796 + t * (-0.142248368 + t * (0.710706871 + t * (-0.726576013 + t * 0.530702714)))
    )
    tail = poly * bell
    phi = jnp.where(u >= 0, 1.0 - tail, tail)
    return u * phi, phi + u * bell * 0.3989422804014327


def quad_rows(part, heads):
    return jnp.concatenate([part] * QUAD, 0) * heads


def pick_heads(stacked, lane_head):
    low = jnp.where(lane_head == 0, stacked[:CELL], stacked[CELL : 2 * CELL])
    high = jnp.where(lane_head == 2, stacked[2 * CELL : 3 * CELL], stacked[3 * CELL :])
    return jnp.where(lane_head < 2, low, high)


def lane_heads():
    return lax.broadcasted_iota(jnp.int32, (CELL, 128), 1) // 32


def whole(shape):
    zero = (0,) * len(shape)
    return pl.BlockSpec(shape, lambda *_: zero, pipeline_mode=pl.Buffered(1))


def per_image(rows, cols):
    return pl.BlockSpec((1, rows, cols), lambda i, *_: (i, 0, 0))


def per_pair(rows, cols):
    return pl.BlockSpec((PAIR, rows, cols), lambda i, *_: (i, 0, 0))


HBM = pl.BlockSpec(memory_space=pl.ANY)


def weight_copies(place, stacks, kept, sems, part=0):
    copies = []
    for m in range(8):
        for s in range(4):
            for p in range(kept.shape[0]):
                if len(stacks) == 1:
                    source, block, owner = stacks[0].at[m, s, part + p], m, s
                else:
                    source = stacks[m % 2].at[m // 2, s, p]
                    block, owner = place[0] ^ m, (place[1] + 4 - s) & 3
                rows = pl.ds(pl.multiple_of(owner * 128, 128), 128)
                cols = pl.ds(pl.multiple_of(block * BLOCK, BLOCK), BLOCK)
                copies.append(
                    pltpu.make_async_copy(
                        source.at[pl.ds(0, 128), :], kept.at[p, rows, cols], sems.at[m, s, p]
                    )
                )
    return copies


def extra_copies(place, stacks, kept, sems):
    copies = []
    for m in range(8):
        for s in range(4):
            if len(stacks) == 1:
                source, block, owner = stacks[0].at[m, s, 0], m, s
            else:
                source = stacks[m % 2].at[m // 2, s, 0]
                block, owner = place[0] ^ m, (place[1] + 4 - s) & 3
            copies.append(
                pltpu.make_async_copy(
                    source.at[pl.ds(128, EXTRA), :], kept.at[block, owner], sems.at[m, s, 0]
                )
            )
    return copies


def fetch(copies):
    for copy in copies:
        copy.start()
    for copy in copies:
        copy.wait()


def call(
    body, name, grid, ins, outs, out_shapes, scratch, cost_us, prefetch=0, aliases=None, mib=58
):
    return pl.pallas_call(
        body,
        name=name,
        grid_spec=pltpu.PrefetchScalarGridSpec(
            num_scalar_prefetch=prefetch,
            grid=grid,
            in_specs=ins,
            out_specs=outs,
            scratch_shapes=scratch,
        ),
        out_shape=out_shapes,
        input_output_aliases=aliases or {},
        compiler_params=pltpu.CompilerParams(
            dimension_semantics=("arbitrary",) * len(grid), vmem_limit_bytes=mib * 1024 * 1024
        ),
        cost_estimate=pl.CostEstimate(
            flops=0, bytes_accessed=int(cost_us * 3.69e4), transcendentals=0
        ),
    )


def shape(dims, kind):
    return jax.ShapeDtypeStruct(dims, kind)


def pack_body(place, *refs):
    mats, (pair_index, tab, vec, spread) = refs[:6], refs[6:10]
    out, mlp0, all1, rel, spread_tab, small = refs[10:]
    rows = mats[0].shape[1]
    out[0, 0:rows, :] = mats[0][0].astype(bf16)
    for ref, at, n in ((mlp0, 0, 1), (mlp0, 1, 2), (all1, 0, 3), (all1, 1, 4), (all1, 2, 5)):
        ref[at] = mats[n][0].astype(bf16)
    rel[...] = jnp.full(rel.shape, -1, jnp.int32)
    across = pair_index[...].astype(f32).T.astype(jnp.int32)
    for h in range(QUAD):
        rel[0 : WIN * WIN, CELL * h : CELL * h + WIN * WIN] = across
    for layer in range(2):
        spread_tab[layer, 0:NREL, :] = mm(tab[layer].astype(bf16), spread[...], TN)
    pairs = rel[pl.ds(pl.multiple_of(place[3] * 8, 8), 8), :]

    def step(r, sums):
        hit = pairs == r
        return tuple(
            jnp.where(hit, spread_tab[layer, pl.ds(r, 1), :], sums[layer]) for layer in range(2)
        )

    start = jnp.zeros((8, QUAD * CELL), f32)
    first, second = lax.fori_loop(0, NREL, step, (start, start), unroll=13)
    out[0, rows : rows + 16, :] = jnp.concatenate([first, second], 0).astype(bf16)
    small[...] = jnp.zeros_like(small)
    row = jnp.minimum(place[3] * 2, 10)
    for layer in range(2):
        for k in range(2):
            small[k : k + 1, layer * 128 : (layer + 1) * 128] = vec[row + k, layer : layer + 1, :]
    out[0, rows + 16 : rows + 32, :] = small[...].astype(bf16)


def pack(place, rows, mat_w, rel_index, tab_w, vec_w):
    vec_w = vec_w.transpose(1, 0, 2)

    def block(layer, part):
        return pl.BlockSpec(
            (1, rows, BLOCK), lambda i, place: (layer, place[4], part * 8 + place[3])
        )

    dims = [(1, rows + EXTRA, BLOCK), (2, rows, BLOCK), (3, rows, BLOCK)]
    return call(
        pack_body,
        "pack",
        (1,),
        [block(layer, part) for layer in range(2) for part in range(3)]
        + [
            whole(rel_index.shape),
            whole(tab_w.shape),
            whole(vec_w.shape),
            whole((QUAD, QUAD * CELL)),
        ],
        [whole(d) for d in dims] + [whole((CELL, QUAD * CELL))],
        [shape(d, bf16) for d in dims] + [shape((CELL, QUAD * CELL), jnp.int32)],
        [pltpu.VMEM((2, 176, QUAD * CELL), f32), pltpu.VMEM((16, 256), f32)],
        4,
        prefetch=1,
    )(place, *[mat_w] * 6, rel_index, tab_w, vec_w, jnp.asarray(head_spread(QUAD), bf16))


def attention_forward_body(layer, stacks, waits, place, *refs):
    arrays, refs = refs[: stacks[0]], refs[stacks[0] :]
    extras, refs = refs[: stacks[1]], refs[stacks[1] + waits :]
    x, mask, perm, perm_back, heads = refs[:5]
    mid, qkv, merged, totals, table, vec, framed, kept, extra_kept, sems, more_sems = refs[5:]
    weight, extra = kept.at[0], extra_kept

    @pl.when(pl.program_id(0) == 0)
    def _():
        fetch(
            weight_copies(place, arrays, kept, sems)
            + extra_copies(place, extras, extra_kept, more_sems)
        )
        vec[...] = jnp.zeros_like(vec)
        for z in range(4):
            for d in range(8):
                pair = extra[d, z, 0:16, :].astype(f32)
                bias = pair[8 * layer : 8 * layer + 8]
                for w in range(table.shape[0]):
                    table[w, z, 8 * d : 8 * d + 8, :] = bias + mask[w, 8 * d : 8 * d + 8, :]
                if d < 6:
                    rows = extra[d, z, 16:32, 128 * layer : 128 * layer + 128].astype(f32)
                    vec[2 * d : 2 * d + 2, 128 * z : 128 * z + 128] = rows[0:2]

    stream = x[0]
    unit, _ = norm(stream)
    normed = (unit * vec[0:1, :] + vec[1:2, :]).astype(bf16)
    normed = mm(perm[...], normed).astype(bf16)
    for c in range(6):
        part = mm(normed, weight[:, 256 * c : 256 * c + 256])
        if c < 2:
            part = part + vec[2:3, 256 * c : 256 * c + 256]
        if c >= 4:
            part = part + vec[3:4, 256 * (c - 4) : 256 * (c - 4) + 256]
        qkv[0, :, 256 * c : 256 * c + 256] = part.astype(bf16)
    lane_head = lane_heads()

    def score(unit):
        rows, at = slice(CELL * (unit // 4), CELL * (unit // 4) + CELL), 128 * (unit % 4)
        query = quad_rows(qkv[0, rows, at : at + 128], heads[...])
        return mm(qkv[0, rows, C + at : C + at + 128], query, NT)

    ahead = score(0)
    for n in range(16):
        w, g = n // 4, n % 4
        rows, at = slice(CELL * w, CELL * w + CELL), 128 * g
        scores = ahead * scale + table[w % table.shape[0], g]
        if n < 15:
            ahead = score(n + 1)
        top = jnp.max(scores, 0, keepdims=True)
        raised = jnp.exp(scores - top)
        total = jnp.sum(raised, 0, keepdims=True)
        totals[0, n : n + 1, :] = top + jnp.log(total)
        probs = (raised * (1.0 / total)).astype(bf16)
        stacked = mm(probs, qkv[0, rows, 2 * C + at : 2 * C + at + 128], TN)
        framed[rows, at : at + 128] = pick_heads(stacked, lane_head).astype(bf16)
    gathered = mm(perm_back[...], framed[...]).astype(bf16)
    merged[0] = gathered
    mid[0] = stream + mm(gathered, weight[:, 3 * C :]) + vec[4:5, :]


def attention_forward(layer, place, x, weight, extra, mask, perm, after):
    images = x.shape[0]
    tables = mask.shape[0]
    return call(
        partial(attention_forward_body, layer, (len(weight), len(extra)), len(after)),
        f"attention_forward_{layer}",
        (images,),
        [HBM] * (len(weight) + len(extra) + len(after))
        + [
            per_image(x.shape[1], C),
            whole(mask.shape),
            whole((FRAME, ROWS)),
            whole((ROWS, FRAME)),
            whole((QUAD * CELL, 128)),
        ],
        [
            per_image(ROWS, C),
            per_image(FRAME, 3 * C),
            per_image(ROWS, C),
            per_image(16, QUAD * CELL),
            pl.BlockSpec((tables, 4, CELL, QUAD * CELL), lambda i, *_: (0, 0, 0, 0)),
            pl.BlockSpec((16, C), lambda i, *_: (0, 0)),
        ],
        [
            shape((images, ROWS, C), f32),
            shape((images, FRAME, 3 * C), bf16),
            shape((images, ROWS, C), bf16),
            shape((images, 16, QUAD * CELL), f32),
            shape((tables, 4, CELL, QUAD * CELL), f32),
            shape((16, C), f32),
        ],
        [
            pltpu.VMEM((FRAME, C), bf16),
            pltpu.VMEM((1, C, HID), bf16),
            pltpu.VMEM((8, 4, EXTRA, BLOCK), bf16),
            pltpu.SemaphoreType.DMA((8, 4, 1)),
            pltpu.SemaphoreType.DMA((8, 4, 1)),
        ],
        20,
        prefetch=1,
    )(
        place,
        *weight,
        *extra,
        *after,
        x,
        mask,
        jnp.asarray(perm, bf16),
        jnp.asarray(perm.T, bf16),
        jnp.asarray(head_rows(), bf16),
    )


def mlp_forward_body(stacks, waits, place, *refs):
    arrays, refs = refs[:stacks], refs[stacks + waits :]
    mid, vec, result, act, slope, kept, sems = refs
    first, second = kept.at[0], kept.at[1]

    @pl.when(pl.program_id(0) == 0)
    def _():
        fetch(weight_copies(place, arrays, kept, sems))

    rows = PAIR * ROWS
    stream = mid[...].reshape(rows, C)
    unit, _ = norm(stream)
    normed = (unit * vec[5:6, :] + vec[6:7, :]).astype(bf16)
    ahead = mm(normed, first[:, 0:BLOCK])
    for c in range(8):
        cols = slice(256 * c, 256 * c + 256)
        bias = vec[8 + c // 2 : 9 + c // 2, 256 * (c % 2) : 256 * (c % 2) + 256]
        inner = ahead + bias
        if c < 7:
            ahead = mm(normed, first[:, 256 * c + 256 : 256 * c + 512])
        value, pull = gelu_pair(inner)
        act[:, :, cols] = value.astype(bf16).reshape(PAIR, ROWS, BLOCK)
        slope[:, :, cols] = pull.astype(bf16).reshape(PAIR, ROWS, BLOCK)
    total = stream + vec[7:8, :] + mm(act[...].reshape(rows, HID), second[...], NT)
    result[...] = total.reshape(PAIR, ROWS, C)


def mlp_forward(layer, place, mid, weight, vec, after):
    images = mid.shape[0]
    return call(
        partial(mlp_forward_body, len(weight), len(after)),
        f"mlp_forward_{layer}",
        (images // PAIR,),
        [HBM] * (len(weight) + len(after)) + [per_pair(ROWS, C), whole(vec.shape)],
        [per_pair(ROWS, C), per_pair(ROWS, HID), per_pair(ROWS, HID)],
        [
            shape((images, ROWS, C), f32),
            shape((images, ROWS, HID), bf16),
            shape((images, ROWS, HID), bf16),
        ],
        [
            pltpu.VMEM((2, C, HID), bf16),
            pltpu.SemaphoreType.DMA((8, 4, 2)),
        ],
        22,
        prefetch=1,
    )(place, *weight, *after, mid, vec)


def mlp_both_body(stacks, waits, place, *refs):
    arrays, refs = refs[:stacks], refs[stacks + waits :]
    grad, mid, vec, result, grad_mid, pieces, small = refs[:7]
    all_grad, all_act, all_inner, all_normed, kept, sems = refs[7:]
    first, second = kept.at[0], kept.at[1]
    i = pl.program_id(0)

    @pl.when(i == 0)
    def _():
        fetch(weight_copies(place, arrays, kept, sems, 1))
        small[...] = jnp.zeros_like(small)

    rows = PAIR * ROWS
    grad_out = grad[...].reshape(rows, C)
    here = pl.ds(pl.multiple_of(i * rows, 32), rows)
    low = grad_out.astype(bf16)
    all_grad[here, :] = low
    small[7:8, :] += column_sum(grad_out)
    stream = mid[...].reshape(rows, C)
    unit, spread = norm(stream)
    normed = (unit * vec[5:6, :] + vec[6:7, :]).astype(bf16)
    all_normed[here, :] = normed
    ahead = mm(normed, first[:, 0:BLOCK]), mm(low, second[:, 0:BLOCK])
    for c in range(8):
        cols = slice(256 * c, 256 * c + 256)
        row, lane = 8 + c // 2, 256 * (c % 2)
        bias = vec[row : row + 1, lane : lane + 256]
        inner, grad_act = ahead
        if c < 7:
            later = slice(256 * c + 256, 256 * c + 512)
            ahead = mm(normed, first[:, later]), mm(low, second[:, later])
        value, pull = gelu_pair(inner + bias)
        all_act[here, cols] = value.astype(bf16)
        inner = (grad_act * pull).astype(bf16)
        all_inner[here, cols] = inner
        small[row : row + 1, lane : lane + 256] += column_sum(inner.astype(f32))
    back = mm(all_inner[here, :], first[...], NT)
    small[5:6, :] += column_sum(back * unit)
    small[6:7, :] += column_sum(back)
    grad_mid[...] = (grad_out + norm_back(back * vec[5:6, :], unit, spread)).reshape(PAIR, ROWS, C)
    total = stream + vec[7:8, :] + mm(all_act[here, :], second[...], NT)
    for n in range(PAIR):
        alive = (i * PAIR + n < place[2]).astype(f32)
        result[n] = (total[n * ROWS : n * ROWS + TOKENS] * alive).astype(bf16)

    @pl.when(i == pl.num_programs(0) - 1)
    def _():
        mlp_weight_grads(place, all_grad, all_act, all_inner, all_normed, pieces)


def mlp_weight_grads(place, all_grad, all_act, all_inner, all_normed, *outs):
    grad_across = all_grad[...].T
    normed_across = all_normed[...].T
    for m in range(8):
        block = m if len(outs) == 1 else place[0] ^ m
        cols = pl.ds(pl.multiple_of(block * BLOCK, BLOCK), BLOCK)
        for p, total in enumerate(
            (mm(normed_across, all_inner[:, cols]), mm(grad_across, all_act[:, cols]))
        ):
            total = total.astype(bf16)
            for z in range(4):
                if len(outs) == 1:
                    outs[0][m, z, p] = total[128 * z : 128 * z + 128]
                else:
                    outs[m % 2][m // 2, z, p] = total[128 * z : 128 * z + 128]


def mlp_both(place, grad, mid, weight, vec, after):
    images = mid.shape[0]
    total = images * ROWS
    pieces = (8, 4, 2, 128, BLOCK)
    return call(
        partial(mlp_both_body, len(weight), len(after)),
        "mlp_both",
        (images // PAIR,),
        [HBM] * (len(weight) + len(after)) + [per_pair(ROWS, C), per_pair(ROWS, C), whole(vec.shape)],
        [per_pair(TOKENS, C), per_pair(ROWS, C), whole(pieces), whole((16, C))],
        [
            shape((images, TOKENS, C), bf16),
            shape((images, ROWS, C), f32),
            shape(pieces, bf16),
            shape((16, C), f32),
        ],
        [
            pltpu.VMEM((total, C), bf16),
            pltpu.VMEM((total, HID), bf16),
            pltpu.VMEM((total, HID), bf16),
            pltpu.VMEM((total, C), bf16),
            pltpu.VMEM((2, C, HID), bf16),
            pltpu.SemaphoreType.DMA((8, 4, 2)),
        ],
        45,
        prefetch=1,
    )(place, *weight, *after, grad, mid, vec)


def mlp_backward_body(stacks, waits, place, *refs):
    arrays, refs = refs[:stacks], refs[stacks + waits :]
    grad, act, slope, mid, vec, grad_mid, own, other, small = refs[:9]
    all_grad, all_act, all_inner, all_normed, kept, sems = refs[9:]
    first, second = kept.at[0], kept.at[1]
    i = pl.program_id(0)

    @pl.when(i == 0)
    def _():
        fetch(weight_copies(place, arrays, kept, sems))
        small[...] = jnp.zeros_like(small)

    rows = PAIR * ROWS
    grad_out = grad[...].reshape(rows, C)
    here = pl.ds(pl.multiple_of(i * rows, 32), rows)
    low = grad_out.astype(bf16)
    all_grad[here, :] = low
    small[7:8, :] += column_sum(low.astype(f32))
    all_act[here, :] = act[...].reshape(rows, HID)
    unit, spread = norm(mid[...].reshape(rows, C))
    all_normed[here, :] = (unit * vec[5:6, :] + vec[6:7, :]).astype(bf16)
    ahead = mm(low, second[:, 0:BLOCK])
    for c in range(8):
        cols = slice(256 * c, 256 * c + 256)
        pull = slope[:, :, cols].reshape(rows, BLOCK).astype(f32)
        grad_act = ahead
        if c < 7:
            ahead = mm(low, second[:, 256 * c + 256 : 256 * c + 512])
        inner = (grad_act * pull).astype(bf16)
        all_inner[here, cols] = inner
        row, lane = 8 + c // 2, 256 * (c % 2)
        small[row : row + 1, lane : lane + 256] += column_sum(inner.astype(f32))
    back = mm(all_inner[here, :], first[...], NT)
    small[5:6, :] += column_sum(back * unit)
    small[6:7, :] += column_sum(back)
    grad_mid[...] = (grad_out + norm_back(back * vec[5:6, :], unit, spread)).reshape(PAIR, ROWS, C)

    @pl.when(i == pl.num_programs(0) - 1)
    def _():
        mlp_weight_grads(place, all_grad, all_act, all_inner, all_normed, own, other)


def mlp_backward(layer, place, grad, act, slope, mid, weight, vec, after):
    images = mid.shape[0]
    total = images * ROWS
    pieces = (4, 4, 2, 128, BLOCK)
    return call(
        partial(mlp_backward_body, len(weight), len(after)),
        f"mlp_backward_{layer}",
        (images // PAIR,),
        [HBM] * (len(weight) + len(after))
        + [
            per_pair(grad.shape[1], C),
            per_pair(ROWS, HID),
            per_pair(ROWS, HID),
            per_pair(ROWS, C),
            whole(vec.shape),
        ],
        [per_pair(ROWS, C), whole(pieces), whole(pieces), whole((16, C))],
        [
            shape((images, ROWS, C), f32),
            shape(pieces, bf16),
            shape(pieces, bf16),
            shape((16, C), f32),
        ],
        [
            pltpu.VMEM((total, C), bf16),
            pltpu.VMEM((total, HID), bf16),
            pltpu.VMEM((total, HID), bf16),
            pltpu.VMEM((total, C), bf16),
            pltpu.VMEM((2, C, HID), bf16),
            pltpu.SemaphoreType.DMA((8, 4, 2)),
        ],
        30,
        prefetch=1,
    )(place, *weight, *after, grad, act, slope, mid, vec)


def attention_backward_body(layer, stacks, waits, resumed, ends, place, *refs):
    arrays, refs = refs[:stacks], refs[stacks + waits :]
    if resumed:
        (own_before, other_before, pairs_before), refs = refs[1:4], refs[4:]
    grad, x, qkv, merged, totals, table, vec, before = refs[:8]
    perm, perm_back, heads, rel, spread, result = refs[8:14]
    outs, refs = (refs[14:15], refs[15:]) if layer else (refs[14:16], refs[16:])
    pairs, small, framed, grad_framed, all_normed, all_packed, all_merged = refs[:7]
    across, hits, beside, kept, sems = refs[7:]
    weight = kept.at[0]
    i = pl.program_id(0)

    @pl.when(i == 0)
    def _():
        fetch(weight_copies(place, arrays, kept, sems))
        small[...] = before[...]
        pairs[...] = pairs_before[...] if resumed else jnp.zeros_like(pairs)

    stream = x[0]
    here = pl.ds(pl.multiple_of(i * ROWS, 16), ROWS)
    unit, spread_one = norm(stream)
    all_normed[here, :] = (unit * vec[0:1, :] + vec[1:2, :]).astype(bf16)
    low = grad[0].astype(bf16)
    all_packed[here, 3 * C :] = low
    all_merged[here, :] = merged[0]
    small[4:5, :] += column_sum(low.astype(f32))
    moved = mm(perm[...], low).astype(bf16)
    framed[...] = mm(moved, weight[:, 3 * C :], NT).astype(bf16)
    lane_head = lane_heads()
    at = [128 * g for g in range(4)]

    def window(w):
        rows = slice(CELL * w, CELL * w + CELL)
        keys = [qkv[0, rows, C + c : C + c + 128] for c in at]
        query = [quad_rows(qkv[0, rows, c : c + 128], heads[...]) for c in at]
        pull = [quad_rows(framed[rows, c : c + 128], heads[...]) for c in at]
        scores = [mm(keys[g], query[g], NT) for g in range(4)]
        grad_probs = [
            mm(qkv[0, rows, 2 * C + at[g] : 2 * C + at[g] + 128], pull[g], NT) for g in range(4)
        ]
        return keys, query, pull, scores, grad_probs

    ahead = window(0)
    for w in range(4):
        rows = slice(CELL * w, CELL * w + CELL)
        keys, query, pull, scores, grad_probs = ahead
        if w < 3:
            ahead = window(w + 1)
        probs, grad_scores = [], []
        for g in range(4):
            shifted = scores[g] * scale + table[w % table.shape[0], g]
            prob = jnp.exp(shifted - totals[0, 4 * w + g : 4 * w + g + 1, :])
            mean = jnp.sum(prob * grad_probs[g], 0, keepdims=True)
            grad_score = (prob * (grad_probs[g] - mean)).astype(bf16)
            pairs[g] += grad_score.astype(f32)
            probs.append(prob.astype(bf16))
            grad_scores.append(grad_score)
        for g in range(4):
            grad_value = mm(probs[g], pull[g])
            grad_framed[rows, 2 * C + at[g] : 2 * C + at[g] + 128] = grad_value.astype(bf16)
        for g in range(4):
            grad_key = mm(grad_scores[g], query[g]) * scale
            grad_framed[rows, C + at[g] : C + at[g] + 128] = grad_key.astype(bf16)
        for g in range(4):
            grad_query = pick_heads(mm(grad_scores[g], keys[g], TN), lane_head) * scale
            grad_framed[rows, at[g] : at[g] + 128] = grad_query.astype(bf16)
    for c in range(6):
        cols = slice(256 * c, 256 * c + 256)
        part = mm(perm_back[...], grad_framed[:, cols])
        all_packed[here, cols] = part.astype(bf16)
        if c < 2:
            small[2:3, cols] += column_sum(part)
        if c >= 4:
            small[3:4, 256 * (c - 4) : 256 * (c - 4) + 256] += column_sum(part)
    back = mm(all_packed[here, : 3 * C], weight[:, : 3 * C], NT)
    small[0:1, :] += column_sum(back * unit)
    small[1:2, :] += column_sum(back)
    total = grad[0] + norm_back(back * vec[0:1, :], unit, spread_one)
    result[0] = total[: result.shape[1]]

    @pl.when(i == pl.num_programs(0) - 1)
    def _():
        across[0] = all_normed[...].T
        across[1] = all_merged[...].T
        beside[...] = jnp.zeros_like(beside)
        if ends:
            hits[...] = jnp.zeros_like(hits)

            def step(r, carry):
                same = rel[...] == r
                for g in range(4):
                    kept_pairs = jnp.where(same, pairs[g], 0.0)
                    hits[pl.ds(r, 1), 256 * g : 256 * g + 256] = column_sum(kept_pairs)
                return carry

            lax.fori_loop(0, NREL, step, 0)
            for z in range(4):
                beside[0, z] = lax.dot_general(
                    spread[...],
                    hits[:, 256 * z : 256 * z + 256],
                    NT,
                    precision=lax.Precision.HIGHEST,
                    preferred_element_type=f32,
                ).astype(bf16)
                beside[1, z, :, 0:128] = small[:, 128 * z : 128 * z + 128].astype(bf16)
        for m in range(8):
            b = m if layer else place[0] ^ m
            left = across[jnp.where(b < 6, 0, 1)]
            right = all_packed[:, pl.ds(pl.multiple_of(b * BLOCK, BLOCK), BLOCK)]
            block = mm(left, right)
            for z in range(4):
                if layer:
                    out = outs[0].at[m, z, 0]
                else:
                    to = (z + 4 - place[1]) & 3
                    out = outs[m % 2].at[m // 2, to, 0]
                new = block[128 * z : 128 * z + 128]
                if resumed:
                    old = other_before if m % 2 else own_before
                    new = new + old[m // 2, to, 0, 0:128, :].astype(f32)
                out[0:128, :] = new.astype(bf16)
                out[128:144, :] = beside[jnp.minimum(b, 2), z]


def attention_backward(
    layer, place, grad, x, qkv, merged, totals, table, weight, vec, small, perm, rel, after,
    first=0, count=None, resume=None,
):
    images = grad.shape[0]
    count = count or images
    pieces = (8 if layer else 4, 4, 1, 128 + SMALL, BLOCK)
    pairs = (4, CELL, QUAD * CELL)
    total = count * ROWS
    out_rows = TOKENS if layer == 0 else ROWS

    def image(rows, cols):
        return pl.BlockSpec((1, rows, cols), lambda i, *_: (i + first, 0, 0))

    resumed = list(resume or [])
    return call(
        partial(
            attention_backward_body, layer, len(weight), len(after), bool(resumed),
            first + count == images,
        ),
        f"attention_backward_{layer}_{first}",
        (count,),
        [HBM] * (len(weight) + len(after))
        + ([HBM, whole(pieces), whole(pieces), whole(pairs)] if resumed else [])
        + [
            image(ROWS, C),
            image(x.shape[1], C),
            image(FRAME, 3 * C),
            image(ROWS, C),
            image(16, QUAD * CELL),
            whole(table.shape),
            whole(vec.shape),
            whole((16, C)),
            whole((FRAME, ROWS)),
            whole((ROWS, FRAME)),
            whole((QUAD * CELL, 128)),
            whole(rel.shape),
            whole((SMALL, QUAD * CELL)),
        ],
        [image(out_rows, C)]
        + [whole(pieces)] * (1 if layer else 2)
        + [whole(pairs), whole((16, C))],
        [shape((images, out_rows, C), f32)]
        + [shape(pieces, bf16)] * (1 if layer else 2)
        + [shape(pairs, f32), shape((16, C), f32)],
        [
            pltpu.VMEM((FRAME, C), bf16),
            pltpu.VMEM((FRAME, 3 * C), bf16),
            pltpu.VMEM((total, C), bf16),
            pltpu.VMEM((total, 4 * C), bf16),
            pltpu.VMEM((total, C), bf16),
            pltpu.VMEM((2, C, total), bf16),
            pltpu.VMEM((256, 4 * QUAD * CELL), f32),
            pltpu.VMEM((3, 4, SMALL, BLOCK), bf16),
            pltpu.VMEM((1, C, HID), bf16),
            pltpu.SemaphoreType.DMA((8, 4, 1)),
        ],
        6 * count,
        prefetch=1,
        aliases={1 + len(weight) + len(after): 0} if resumed else None,
    )(
        place,
        *weight,
        *after,
        *resumed,
        grad,
        x,
        qkv,
        merged,
        totals,
        table,
        vec,
        small,
        jnp.asarray(perm, bf16),
        jnp.asarray(perm.T, bf16),
        jnp.asarray(head_rows(), bf16),
        rel,
        jnp.asarray(head_spread(SMALL), f32),
    )


def adam_step(weight, first, second, gradient, rate, decay):
    first_new = beta_one * first + (1.0 - beta_one) * gradient
    second_new = beta_two * second + (1.0 - beta_two) * gradient * gradient
    first_hat = first_new / (1.0 - beta_one**STEP)
    second_hat = second_new / (1.0 - beta_two**STEP)
    weight_new = weight - rate * (first_hat / (jnp.sqrt(second_hat) + adam_eps) + decay * weight)
    return (weight_new, first_new, second_new)


def adam_block(grad, weight, first, second, outs, cols):
    part = grad.astype(f32)
    first_new = beta_one * first[0, :, cols] + (1.0 - beta_one) * part
    second_new = beta_two * second[0, :, cols] + (1.0 - beta_two) * part * part
    spread = second_new * (1.0 / (1.0 - beta_two**STEP))
    inverse = pltpu.reciprocal(spread * lax.rsqrt(spread) + adam_eps, approx=True)
    step = first_new * (rate_matrix / (1.0 - beta_one**STEP)) * inverse
    outs[0][0, :, cols] = weight[0, :, cols] * (1.0 - rate_matrix * weight_decay) - step
    outs[1][0, :, cols] = first_new
    outs[2][0, :, cols] = second_new


def adam_body(place, near, far, weight, first, second, *refs):
    for j in range(2):
        for k in range(2):
            block = (((place[0] // 2) & 1) ^ j) * 2 + ((place[0] & 1) ^ k)
            cols = pl.ds(pl.multiple_of(block * BLOCK, BLOCK), BLOCK)
            adam_block((far if k else near)[j], weight, first, second, refs[-3:], cols)


def adam_body_plain(place, sums, weight, first, second, *refs):
    for k in range(4):
        cols = slice(BLOCK * k, BLOCK * k + BLOCK)
        adam_block(sums[k], weight, first, second, refs[-3:], cols)


def adam(layer, part, place, sums, state, done, after):
    kept = [] if done is None else list(done)
    if len(sums) == 2:
        parts = sums[0].shape[1] // 128
        body = adam_body
        spec = pl.BlockSpec(
            (1, 128, 4 * BLOCK),
            lambda p, j, place: (layer, 0, (part + p) % 3 * 2 + ((place[0] // 4) ^ j)),
        )
        piece = pl.BlockSpec((2, 128, BLOCK), lambda p, j, place: (j, p, 0))
    else:
        parts = sums[0].shape[1] // 128
        body = adam_body_plain
        spec = pl.BlockSpec(
            (1, 128, 4 * BLOCK), lambda p, j, place: (layer, 0, (part + p) % 3 * 2 + j)
        )
        piece = pl.BlockSpec((4, 128, BLOCK), lambda p, j, place: (j, p, 0))
    return call(
        body,
        f"adam_{layer}_{part}",
        (parts, 2),
        [piece] * len(sums) + [spec] * 3 + [HBM] * (len(kept) + len(after)),
        [spec] * 3,
        [shape(state[0].shape, f32)] * 3,
        [],
        3 * parts,
        prefetch=1,
        aliases={4 + len(sums) + k: k for k in range(len(kept))},
    )(place, *sums, *state, *kept, *after)


def swap(value, bits):
    return lax.ppermute(value, "dp", [(i, i ^ bits) for i in range(8)])


def shift(value, steps):
    return lax.ppermute(value, "zero", [(i, (i + steps) % 4) for i in range(4)])


def tie(values, after):
    values = list(values)
    return list(lax.optimization_barrier((*values, *after))[: len(values)])


def stack(values, after=()):
    return jnp.stack(tie(values, after) if after else values)


def add_body(count, *refs):
    total = refs[0][...].astype(f32)
    for k in range(1, count):
        total = total + refs[k][...].astype(f32)
    refs[-1][...] = total.astype(bf16)


def add(values, after=()):
    dims = values[0].shape
    return call(
        partial(add_body, len(values)),
        "add",
        (1,),
        [whole(dims)] * len(values) + [HBM] * len(after),
        whole(dims),
        shape(dims, bf16),
        [],
        10,
        mib=24,
    )(*values, *after)


def add_split_body(count, lead, *refs):
    for k in range(4):
        if count == 2:
            refs[len(refs) - 4 + k][...] = refs[0][k] + refs[1][k]
            continue
        total = refs[0][k].astype(f32)
        for v in range(1, count):
            total = total + refs[v][k].astype(f32)
        refs[len(refs) - 4 + k][...] = total.astype(bf16)


def add_split(values, after=()):
    dims = values[0].shape
    steps = 1
    ins = (4, dims[1] // steps, *dims[2:])
    outs = dims[1:]
    zeros = (0,) * (len(dims) - 2)
    return call(
        partial(add_split_body, len(values), True),
        "add_split",
        (steps,),
        [pl.BlockSpec(ins, lambda i: (0, i, *zeros))] * len(values) + [HBM] * len(after),
        [pl.BlockSpec((outs[0] // steps, *outs[1:]), lambda i: (i, *zeros))] * 4,
        [shape(outs, bf16)] * 4,
        [],
        10,
        mib=24,
    )(*values, *after)


def join_body(*refs):
    out = refs[-1]
    at = 0
    for group in (refs[:1], refs[1:2], refs[2:6]):
        parts, rows = group[0].shape[1:3]
        for p in range(parts):
            total = group[0][:, p]
            if len(group) > 1:
                total = total.astype(f32)
                for ref in group[1:]:
                    total = total + ref[:, p].astype(f32)
            out[:, at : at + rows, :] = total.astype(bf16)
            at += rows


def join(first, second, summed, after):
    rows = sum(value.shape[1] * value.shape[2] for value in (first, second, summed[0]))
    ins = [first, second, *summed]
    return call(
        join_body,
        "join",
        (1,),
        [whole(v.shape) for v in ins] + [HBM] * len(after),
        whole((4, rows, BLOCK)),
        shape((4, rows, BLOCK), bf16),
        [],
        5,
        mib=24,
    )(*ins, *after)


def add_last_body(*refs):
    done, out = refs[0], refs[-1]
    rows = 256
    out[0:rows, :] = done[done.shape[0] - rows :, :]
    total = refs[1][0].astype(f32)
    for ref in refs[2:5]:
        total = total + ref[0].astype(f32)
    out[rows : rows + total.shape[0], :] = total.astype(bf16)


def add_last(done, values, after):
    rows = 256 + values[0].shape[1]
    return call(
        add_last_body,
        "add_last",
        (1,),
        [whole(done.shape)] + [whole(v.shape) for v in values] + [HBM] * len(after),
        whole((rows, BLOCK)),
        shape((rows, BLOCK), bf16),
        [],
        10,
        mib=24,
    )(done, *values, *after)


def send_z(piece):
    return [piece] + [shift(piece, s) for s in range(1, 4)]


def send_plane(piece):
    return [piece] + [swap(piece, 2 * j) for j in range(1, 4)]


def give_plane(parts):
    return [parts[0]] + [swap(parts[j], 2 * j) for j in range(1, 4)]


def give_z(parts):
    return [parts[0]] + [shift(parts[s], s) for s in range(1, 4)]


def gather_wide(piece, dp, extra):
    fine = dp // 8
    parts, rows = piece.shape[0], piece.shape[1] - extra
    out = lax.all_gather(piece, ("dp", "zero"), axis=0, tiled=False)
    out = out.reshape(8, fine, 4, *piece.shape)
    main = out[..., :rows, :].transpose(0, 2, 3, 1, 4, 5).reshape(8, 4, parts, 128, BLOCK)
    return [jnp.concatenate([main, out[:, 0, ..., rows:, :]], 3)]


def reduce_wide(blocks, dp, extra):
    fine = dp // 8
    blocks = blocks.reshape(8, 4, *blocks.shape[-3:])
    parts, rows = blocks.shape[2], 128 // fine
    main = blocks[..., :128, :].reshape(8, 4, parts, fine, rows, BLOCK).transpose(0, 3, 1, 2, 4, 5)
    beside = jnp.broadcast_to(
        blocks[:, None, ..., 128:, :], (8, fine, 4, parts, extra, BLOCK)
    )
    flat = jnp.concatenate([main, beside], 4).reshape(dp * 4, parts, rows + extra, BLOCK)
    mine = lax.psum_scatter(flat, ("dp", "zero"), scatter_dimension=0, tiled=True)
    out = lax.all_gather(mine[0], "dp", axis=0, tiled=False)
    out = out.reshape(8, fine, parts, rows + extra, BLOCK)
    main = out[..., :rows, :].transpose(0, 2, 1, 3, 4).reshape(8, parts, 128, BLOCK)
    out = jnp.concatenate([main, out[:, 0, :, rows:]], 2)
    return out.reshape(8, -1, BLOCK)


def shards(
    dp, images, cotangent, counts, rel_index, regions,
    mat_w, mat_m, mat_v, vec_w, vec_m, vec_v, tab_w, tab_m, tab_v,
):
    near = dp == 8
    fine = dp // 8
    rows = 128 // fine
    me = lax.axis_index("dp")
    spot = [me, lax.axis_index("zero")] if near else [0 * me, 0 * me]
    place = jnp.stack(spot + [counts[0], me // fine, me % fine]).astype(jnp.int32)

    inside = np.arange(CELL) < WIN * WIN
    zones = regions.reshape(2, WIN, 2, WIN).transpose(0, 2, 1, 3).reshape(4, WIN * WIN)
    zones = jnp.pad(zones, ((0, 0), (0, 15)))
    differ = (zones[:, :, None] != zones[:, None, :]) & inside[None, None, :]
    outside = np.where(inside, 0.0, -1e30).astype(np.float32)[None, :, None]
    mask_shifted = jnp.tile(jnp.where(differ, mask_value, 0.0) + outside, (1, 1, QUAD)).astype(f32)
    mask_plain = jnp.asarray(np.ascontiguousarray(np.broadcast_to(outside, (1, CELL, QUAD * CELL))))
    masks = (mask_plain, mask_shifted)
    perms = (frames(False), frames(True))

    packed, cut_mlp0, cut_all1, rel = pack(
        place, rows, mat_w, rel_index, tab_w, vec_w
    )
    alive = (jnp.arange(images.shape[0]) < counts[0]).astype(f32)[:, None, None]
    pad = ((0, 0), (0, ROWS - TOKENS), (0, 0))
    images = jnp.pad(images.astype(f32), pad)
    cotangent = jnp.pad(cotangent.astype(f32) * alive, pad)

    def attention(layer, stream, weight, after):
        return attention_forward(
            layer, place, stream, weight, heads0, masks[layer], perms[layer], after
        )

    half = images.shape[0] // 2
    if near:
        sent_heads0 = send_z(packed)
        *sent_heads0, images = tie([*sent_heads0, images], [])
        z_heads0 = stack(sent_heads0)
        all1 = gather_wide(tie([cut_all1], [z_heads0])[0], dp, 0)
        sent_heads0 = send_plane(z_heads0)
        sent_mlp0 = send_z(tie([cut_mlp0], [z_heads0])[0])
        cotangent, mask_shifted = tie([cotangent, mask_shifted], [z_heads0])
        *sent_heads0, cotangent, mask_shifted = tie(
            [*sent_heads0, cotangent, mask_shifted], sent_mlp0
        )
        masks = (mask_plain, mask_shifted)
        p_heads0 = stack(sent_heads0)
        heads0 = [p_heads0, swap(p_heads0, 1)]
        z_mlp0 = stack(sent_mlp0, [p_heads0])
        sent_mlp0 = send_plane(z_mlp0)
        kept0 = attention(0, images, heads0, [z_mlp0])
        p_mlp0 = stack(sent_mlp0, [kept0[0]])
        mlp0 = [p_mlp0, swap(p_mlp0, 1)]
    else:
        heads0 = gather_wide(packed, dp, EXTRA)
        mlp0 = gather_wide(cut_mlp0, dp, 0)
        all1 = gather_wide(cut_all1, dp, 0)
        kept0 = attention(0, images, heads0, [])
    stream, act, slope = mlp_forward(0, place, kept0[0], mlp0, kept0[5], [])
    kept1 = attention(1, stream, all1, [])
    kept = (kept0, kept1)
    inputs = (images, stream)
    attention_w = (heads0, all1)

    def backward_attention(layer, gradient, small, after, *span):
        mid, qkv, merged, totals, table, vec = kept[layer]
        return attention_backward(
            layer, place, gradient, inputs[layer], qkv, merged, totals, table, attention_w[layer],
            vec, small, perms[layer], rel, after, *span,
        )

    activations, grad_mid, parts_mlp1, small = mlp_both(
        place, cotangent, kept1[0], all1, kept1[5], []
    )

    def backward_mlp0(gradient, after):
        return mlp_backward(0, place, gradient, act, slope, kept0[0], mlp0, kept0[5], after)

    state = (mat_w, mat_m, mat_v)
    def exchange(parts):
        return [parts[0], swap(parts[1], 1)]

    gradient, parts_heads1, _, _ = backward_attention(1, grad_mid, small, [])
    grad_mid, *parts_mlp0, small = backward_mlp0(gradient, [])
    if near:
        t_mlp1 = lax.psum_scatter(parts_mlp1, "dp", scatter_dimension=0, tiled=True)[0]
        parts_heads1 = tie([parts_heads1], [t_mlp1, small])[0]
        t_heads1 = lax.psum_scatter(parts_heads1, "dp", scatter_dimension=0, tiled=True)[0]
        gone_mlp0 = exchange(parts_mlp0)
        gradient, *parts_heads0, pairs, small = backward_attention(0, grad_mid, small, [], 0, half)

        s_mlp0 = add_split(gone_mlp0, [gradient])
        gone_mlp0 = give_plane(s_mlp0)
        gradient, *parts_heads0, _, small = backward_attention(
            0, grad_mid, small, [s_mlp0[0]], half, half, [gradient, *parts_heads0, pairs]
        )

        t_all = join(t_mlp1, t_heads1, gone_mlp0, [small])
        gone_heads0 = exchange(tie(parts_heads0, gone_mlp0))
        g_all = lax.psum_scatter(t_all, "zero", scatter_dimension=0, tiled=True)[0]
        s_heads0 = add_split(gone_heads0, [t_all])
        gone_heads0 = give_plane(s_heads0)
        across = tie([activations.transpose(1, 0, 2), gradient.transpose(1, 0, 2)], [])
        t_heads0 = add_split(gone_heads0, across)
        activations, gradient = [value.transpose(1, 0, 2) for value in across]
        gone_heads0 = give_z(t_heads0)
        g_all, *gone_heads0 = tie([g_all, *gone_heads0], [])
        g_all0 = add_last(g_all, gone_heads0, [])
        g_all = tie([g_all], [g_all0])[0]
        n_all1 = lax.all_gather(g_all[:400], "dp", axis=0, tiled=False)
        n_all0 = stack(send_plane(g_all0))
        sums0 = [n_all0, swap(n_all0, 1)]
        m = place[0] ^ np.arange(2)
        both = jnp.concatenate([half[:, 384:] for half in sums0])
        beside0 = [
            lax.dynamic_index_in_dim(both, (m[b] % 2) * 4 + m[b] // 2, 0, False) for b in range(2)
        ]
    else:
        gradient, *parts_heads0, _, _ = backward_attention(0, grad_mid, small, [])
        n_mlp1 = reduce_wide(parts_mlp1, dp, 0)
        n_heads1 = reduce_wide(parts_heads1, dp, SMALL)
        n_all1 = jnp.concatenate([n_mlp1, n_heads1], 1)
        n_mlp0 = reduce_wide(jnp.stack(parts_mlp0, 1), dp, 0)
        n_heads0 = reduce_wide(jnp.stack(parts_heads0, 1), dp, SMALL)
        sums0 = [jnp.concatenate([n_mlp0, n_heads0], 1)]
        beside0 = sums0[0][:2, 384:]
    done = adam(0, 1, place, sums0, state, None, [])
    done = adam(1, 1, place, [n_all1], state, done, [])

    def beside(block):
        return jnp.stack([beside0[block], n_all1[block, 384:]]).astype(f32)

    new_vec = adam_step(vec_w, vec_m, vec_v, beside(1)[:, 0:12, 0:128], rate_vector, 0.0)
    new_tab = adam_step(tab_w, tab_m, tab_v, beside(0)[:, 0:4, 0:NREL], rate_table, 0.0)
    return (activations, gradient, *done, *new_vec, *new_tab)


def solution(mesh):
    images = P(("dp", "zero"), None, None)
    rows = P(None, "zero", None)
    lanes = P(None, None, "zero")
    return jax.shard_map(
        partial(shards, mesh.shape["dp"]),
        mesh=mesh,
        in_specs=(images, images, P(("dp", "zero")), P(), P())
        + (rows,) * 3 + (lanes,) * 3 + (rows,) * 3,
        out_specs=(images, images) + (rows,) * 3 + (lanes,) * 3 + (rows,) * 3,
        check_vma=False,
    )
```

```python
from functools import partial

import jax
import jax.numpy as jnp
import numpy as np
from jax import lax
from jax.experimental import pallas as pl
from jax.experimental.pallas import tpu as pltpu
from jax.sharding import PartitionSpec as P

WIN = 7
SIDE = 14
STEP = 10
NREL = 169
C = 512
HID = 2048
TOKENS = SIDE * SIDE
PAIR = 2
ROWS = 208
FRAME = 256
CELL = 64
QUAD = 4
BLOCK = 256
EXTRA = 32
SMALL = 16

norm_eps = 1e-05
mask_value = -100.0
beta_one = 0.9
beta_two = 0.999
adam_eps = 1e-08
weight_decay = 0.05
rate_matrix = 0.1
rate_vector = 0.5
rate_table = 1.0
scale = 32 ** (-0.5)

bf16 = jnp.bfloat16
f32 = jnp.float32
NN = (((1,), (0,)), ((), ()))
NT = (((1,), (1,)), ((), ()))
TN = (((0,), (0,)), ((), ()))


def mm(left, right, dims=NN):
    return lax.dot_general(left, right, dims, preferred_element_type=f32)


def frames(shifted):
    move = WIN // 2 if shifted else 0
    placed = np.zeros((FRAME, ROWS), np.float32)
    for wy in range(2):
        for wx in range(2):
            for iy in range(WIN):
                for ix in range(WIN):
                    y = (wy * WIN + iy + move) % SIDE
                    x = (wx * WIN + ix + move) % SIDE
                    placed[(wy * 2 + wx) * CELL + iy * WIN + ix, y * SIDE + x] = 1
    return placed


def head_rows():
    rows = np.zeros((QUAD * CELL, 128), np.float32)
    for h in range(QUAD):
        rows[h * CELL : (h + 1) * CELL, h * 32 : (h + 1) * 32] = 1
    return rows


def head_spread(rows):
    out = np.zeros((rows, QUAD * CELL), np.float32)
    for h in range(QUAD):
        out[h, h * CELL : (h + 1) * CELL] = 1
    return out


def norm(rows):
    centred = rows - jnp.mean(rows, -1, keepdims=True)
    spread = lax.rsqrt(jnp.mean(centred * centred, -1, keepdims=True) + norm_eps)
    return centred * spread, spread


def norm_back(grad_unit, unit, spread):
    return spread * (
        grad_unit
        - jnp.mean(grad_unit, -1, keepdims=True)
        - unit * jnp.mean(grad_unit * unit, -1, keepdims=True)
    )


def column_sum(rows):
    return jnp.sum(rows, 0, keepdims=True)


def gelu_pair(u):
    size = jnp.abs(u)
    below = 1.0 + (0.3275911 * 0.5**0.5) * size
    t = pltpu.reciprocal(below, approx=True)
    bell = jnp.exp2(u * u * (-0.5 * 1.4426950408889634))
    poly = t * (
        0.127414796 + t * (-0.142248368 + t * (0.710706871 + t * (-0.726576013 + t * 0.530702714)))
    )
    tail = poly * bell
    phi = jnp.where(u >= 0, 1.0 - tail, tail)
    return u * phi, phi + u * bell * 0.3989422804014327


def quad_rows(part, heads):
    return jnp.concatenate([part] * QUAD, 0) * heads


def pick_heads(stacked, lane_head):
    low = jnp.where(lane_head == 0, stacked[:CELL], stacked[CELL : 2 * CELL])
    high = jnp.where(lane_head == 2, stacked[2 * CELL : 3 * CELL], stacked[3 * CELL :])
    return jnp.where(lane_head < 2, low, high)


def lane_heads():
    return lax.broadcasted_iota(jnp.int32, (CELL, 128), 1) // 32


def whole(shape):
    zero = (0,) * len(shape)
    return pl.BlockSpec(shape, lambda *_: zero, pipeline_mode=pl.Buffered(1))


def per_image(rows, cols):
    return pl.BlockSpec((1, rows, cols), lambda i, *_: (i, 0, 0))


def per_pair(rows, cols):
    return pl.BlockSpec((PAIR, rows, cols), lambda i, *_: (i, 0, 0))


HBM = pl.BlockSpec(memory_space=pl.ANY)


def weight_copies(place, stacks, kept, sems, part=0):
    copies = []
    for m in range(8):
        for s in range(4):
            for p in range(kept.shape[0]):
                if len(stacks) == 1:
                    source, block, owner = stacks[0].at[m, s, part + p], m, s
                else:
                    source = stacks[m % 2].at[m // 2, s, p]
                    block, owner = place[0] ^ m, (place[1] + 4 - s) & 3
                rows = pl.ds(pl.multiple_of(owner * 128, 128), 128)
                cols = pl.ds(pl.multiple_of(block * BLOCK, BLOCK), BLOCK)
                copies.append(
                    pltpu.make_async_copy(
                        source.at[pl.ds(0, 128), :], kept.at[p, rows, cols], sems.at[m, s, p]
                    )
                )
    return copies


def extra_copies(place, stacks, kept, sems):
    copies = []
    for m in range(8):
        for s in range(4):
            if len(stacks) == 1:
                source, block, owner = stacks[0].at[m, s, 0], m, s
            else:
                source = stacks[m % 2].at[m // 2, s, 0]
                block, owner = place[0] ^ m, (place[1] + 4 - s) & 3
            copies.append(
                pltpu.make_async_copy(
                    source.at[pl.ds(128, EXTRA), :], kept.at[block, owner], sems.at[m, s, 0]
                )
            )
    return copies


def fetch(copies):
    for copy in copies:
        copy.start()
    for copy in copies:
        copy.wait()


def call(
    body, name, grid, ins, outs, out_shapes, scratch, cost_us, prefetch=0, aliases=None, mib=58
):
    return pl.pallas_call(
        body,
        name=name,
        grid_spec=pltpu.PrefetchScalarGridSpec(
            num_scalar_prefetch=prefetch,
            grid=grid,
            in_specs=ins,
            out_specs=outs,
            scratch_shapes=scratch,
        ),
        out_shape=out_shapes,
        input_output_aliases=aliases or {},
        compiler_params=pltpu.CompilerParams(
            dimension_semantics=("arbitrary",) * len(grid), vmem_limit_bytes=mib * 1024 * 1024
        ),
        cost_estimate=pl.CostEstimate(
            flops=0, bytes_accessed=int(cost_us * 3.69e4), transcendentals=0
        ),
    )


def shape(dims, kind):
    return jax.ShapeDtypeStruct(dims, kind)


def pack_body(place, *refs):
    mats, (pair_index, tab, vec, spread) = refs[:6], refs[6:10]
    out, mlp0, all1, rel, spread_tab, small = refs[10:]
    rows = mats[0].shape[1]
    out[0, 0:rows, :] = mats[0][0].astype(bf16)
    for ref, at, n in ((mlp0, 0, 1), (mlp0, 1, 2), (all1, 0, 3), (all1, 1, 4), (all1, 2, 5)):
        ref[at] = mats[n][0].astype(bf16)
    rel[...] = jnp.full(rel.shape, -1, jnp.int32)
    across = pair_index[...].astype(f32).T.astype(jnp.int32)
    for h in range(QUAD):
        rel[0 : WIN * WIN, CELL * h : CELL * h + WIN * WIN] = across
    for layer in range(2):
        spread_tab[layer, 0:NREL, :] = mm(tab[layer].astype(bf16), spread[...], TN)
    pairs = rel[pl.ds(pl.multiple_of(place[3] * 8, 8), 8), :]

    def step(r, sums):
        hit = pairs == r
        return tuple(
            jnp.where(hit, spread_tab[layer, pl.ds(r, 1), :], sums[layer]) for layer in range(2)
        )

    start = jnp.zeros((8, QUAD * CELL), f32)
    first, second = lax.fori_loop(0, NREL, step, (start, start), unroll=13)
    out[0, rows : rows + 16, :] = jnp.concatenate([first, second], 0).astype(bf16)
    small[...] = jnp.zeros_like(small)
    row = jnp.minimum(place[3] * 2, 10)
    for layer in range(2):
        for k in range(2):
            small[k : k + 1, layer * 128 : (layer + 1) * 128] = vec[row + k, layer : layer + 1, :]
    out[0, rows + 16 : rows + 32, :] = small[...].astype(bf16)


def pack(place, rows, mat_w, rel_index, tab_w, vec_w):
    vec_w = vec_w.transpose(1, 0, 2)

    def block(layer, part):
        return pl.BlockSpec(
            (1, rows, BLOCK), lambda i, place: (layer, place[4], part * 8 + place[3])
        )

    dims = [(1, rows + EXTRA, BLOCK), (2, rows, BLOCK), (3, rows, BLOCK)]
    return call(
        pack_body,
        "pack",
        (1,),
        [block(layer, part) for layer in range(2) for part in range(3)]
        + [
            whole(rel_index.shape),
            whole(tab_w.shape),
            whole(vec_w.shape),
            whole((QUAD, QUAD * CELL)),
        ],
        [whole(d) for d in dims] + [whole((CELL, QUAD * CELL))],
        [shape(d, bf16) for d in dims] + [shape((CELL, QUAD * CELL), jnp.int32)],
        [pltpu.VMEM((2, 176, QUAD * CELL), f32), pltpu.VMEM((16, 256), f32)],
        4,
        prefetch=1,
    )(place, *[mat_w] * 6, rel_index, tab_w, vec_w, jnp.asarray(head_spread(QUAD), bf16))


def attention_forward_body(layer, stacks, waits, place, *refs):
    arrays, refs = refs[: stacks[0]], refs[stacks[0] :]
    extras, refs = refs[: stacks[1]], refs[stacks[1] + waits :]
    x, mask, perm, perm_back, heads = refs[:5]
    mid, qkv, merged, totals, table, vec, framed, kept, extra_kept, sems, more_sems = refs[5:]
    weight, extra = kept.at[0], extra_kept

    @pl.when(pl.program_id(0) == 0)
    def _():
        fetch(
            weight_copies(place, arrays, kept, sems)
            + extra_copies(place, extras, extra_kept, more_sems)
        )
        vec[...] = jnp.zeros_like(vec)
        for z in range(4):
            for d in range(8):
                pair = extra[d, z, 0:16, :].astype(f32)
                bias = pair[8 * layer : 8 * layer + 8]
                for w in range(table.shape[0]):
                    table[w, z, 8 * d : 8 * d + 8, :] = bias + mask[w, 8 * d : 8 * d + 8, :]
                if d < 6:
                    rows = extra[d, z, 16:32, 128 * layer : 128 * layer + 128].astype(f32)
                    vec[2 * d : 2 * d + 2, 128 * z : 128 * z + 128] = rows[0:2]

    stream = x[0]
    unit, _ = norm(stream)
    normed = (unit * vec[0:1, :] + vec[1:2, :]).astype(bf16)
    normed = mm(perm[...], normed).astype(bf16)
    for c in range(6):
        part = mm(normed, weight[:, 256 * c : 256 * c + 256])
        if c < 2:
            part = part + vec[2:3, 256 * c : 256 * c + 256]
        if c >= 4:
            part = part + vec[3:4, 256 * (c - 4) : 256 * (c - 4) + 256]
        qkv[0, :, 256 * c : 256 * c + 256] = part.astype(bf16)
    lane_head = lane_heads()

    def score(unit):
        rows, at = slice(CELL * (unit // 4), CELL * (unit // 4) + CELL), 128 * (unit % 4)
        query = quad_rows(qkv[0, rows, at : at + 128], heads[...])
        return mm(qkv[0, rows, C + at : C + at + 128], query, NT)

    ahead = score(0)
    for n in range(16):
        w, g = n // 4, n % 4
        rows, at = slice(CELL * w, CELL * w + CELL), 128 * g
        scores = ahead * scale + table[w % table.shape[0], g]
        if n < 15:
            ahead = score(n + 1)
        top = jnp.max(scores, 0, keepdims=True)
        raised = jnp.exp(scores - top)
        total = jnp.sum(raised, 0, keepdims=True)
        totals[0, n : n + 1, :] = top + jnp.log(total)
        probs = (raised * (1.0 / total)).astype(bf16)
        stacked = mm(probs, qkv[0, rows, 2 * C + at : 2 * C + at + 128], TN)
        framed[rows, at : at + 128] = pick_heads(stacked, lane_head).astype(bf16)
    gathered = mm(perm_back[...], framed[...]).astype(bf16)
    merged[0] = gathered
    mid[0] = stream + mm(gathered, weight[:, 3 * C :]) + vec[4:5, :]


def attention_forward(layer, place, x, weight, extra, mask, perm, after):
    images = x.shape[0]
    tables = mask.shape[0]
    return call(
        partial(attention_forward_body, layer, (len(weight), len(extra)), len(after)),
        f"attention_forward_{layer}",
        (images,),
        [HBM] * (len(weight) + len(extra) + len(after))
        + [
            per_image(x.shape[1], C),
            whole(mask.shape),
            whole((FRAME, ROWS)),
            whole((ROWS, FRAME)),
            whole((QUAD * CELL, 128)),
        ],
        [
            per_image(ROWS, C),
            per_image(FRAME, 3 * C),
            per_image(ROWS, C),
            per_image(16, QUAD * CELL),
            pl.BlockSpec((tables, 4, CELL, QUAD * CELL), lambda i, *_: (0, 0, 0, 0)),
            pl.BlockSpec((16, C), lambda i, *_: (0, 0)),
        ],
        [
            shape((images, ROWS, C), f32),
            shape((images, FRAME, 3 * C), bf16),
            shape((images, ROWS, C), bf16),
            shape((images, 16, QUAD * CELL), f32),
            shape((tables, 4, CELL, QUAD * CELL), f32),
            shape((16, C), f32),
        ],
        [
            pltpu.VMEM((FRAME, C), bf16),
            pltpu.VMEM((1, C, HID), bf16),
            pltpu.VMEM((8, 4, EXTRA, BLOCK), bf16),
            pltpu.SemaphoreType.DMA((8, 4, 1)),
            pltpu.SemaphoreType.DMA((8, 4, 1)),
        ],
        20,
        prefetch=1,
    )(
        place,
        *weight,
        *extra,
        *after,
        x,
        mask,
        jnp.asarray(perm, bf16),
        jnp.asarray(perm.T, bf16),
        jnp.asarray(head_rows(), bf16),
    )


def mlp_forward_body(stacks, waits, place, *refs):
    arrays, refs = refs[:stacks], refs[stacks + waits :]
    mid, vec, result, act, slope, kept, sems = refs
    first, second = kept.at[0], kept.at[1]

    @pl.when(pl.program_id(0) == 0)
    def _():
        fetch(weight_copies(place, arrays, kept, sems))

    rows = PAIR * ROWS
    stream = mid[...].reshape(rows, C)
    unit, _ = norm(stream)
    normed = (unit * vec[5:6, :] + vec[6:7, :]).astype(bf16)
    ahead = mm(normed, first[:, 0:BLOCK])
    for c in range(8):
        cols = slice(256 * c, 256 * c + 256)
        bias = vec[8 + c // 2 : 9 + c // 2, 256 * (c % 2) : 256 * (c % 2) + 256]
        inner = ahead + bias
        if c < 7:
            ahead = mm(normed, first[:, 256 * c + 256 : 256 * c + 512])
        value, pull = gelu_pair(inner)
        act[:, :, cols] = value.astype(bf16).reshape(PAIR, ROWS, BLOCK)
        slope[:, :, cols] = pull.astype(bf16).reshape(PAIR, ROWS, BLOCK)
    total = stream + vec[7:8, :] + mm(act[...].reshape(rows, HID), second[...], NT)
    result[...] = total.reshape(PAIR, ROWS, C)


def mlp_forward(layer, place, mid, weight, vec, after):
    images = mid.shape[0]
    return call(
        partial(mlp_forward_body, len(weight), len(after)),
        f"mlp_forward_{layer}",
        (images // PAIR,),
        [HBM] * (len(weight) + len(after)) + [per_pair(ROWS, C), whole(vec.shape)],
        [per_pair(ROWS, C), per_pair(ROWS, HID), per_pair(ROWS, HID)],
        [
            shape((images, ROWS, C), f32),
            shape((images, ROWS, HID), bf16),
            shape((images, ROWS, HID), bf16),
        ],
        [
            pltpu.VMEM((2, C, HID), bf16),
            pltpu.SemaphoreType.DMA((8, 4, 2)),
        ],
        22,
        prefetch=1,
    )(place, *weight, *after, mid, vec)


def mlp_both_body(stacks, waits, place, *refs):
    arrays, refs = refs[:stacks], refs[stacks + waits :]
    grad, mid, vec, result, grad_mid, pieces, small = refs[:7]
    all_grad, all_act, all_inner, all_normed, kept, sems = refs[7:]
    first, second = kept.at[0], kept.at[1]
    i = pl.program_id(0)

    @pl.when(i == 0)
    def _():
        fetch(weight_copies(place, arrays, kept, sems, 1))
        small[...] = jnp.zeros_like(small)

    rows = PAIR * ROWS
    grad_out = grad[...].reshape(rows, C)
    here = pl.ds(pl.multiple_of(i * rows, 32), rows)
    low = grad_out.astype(bf16)
    all_grad[here, :] = low
    small[7:8, :] += column_sum(grad_out)
    stream = mid[...].reshape(rows, C)
    unit, spread = norm(stream)
    normed = (unit * vec[5:6, :] + vec[6:7, :]).astype(bf16)
    all_normed[here, :] = normed
    ahead = mm(normed, first[:, 0:BLOCK]), mm(low, second[:, 0:BLOCK])
    for c in range(8):
        cols = slice(256 * c, 256 * c + 256)
        row, lane = 8 + c // 2, 256 * (c % 2)
        bias = vec[row : row + 1, lane : lane + 256]
        inner, grad_act = ahead
        if c < 7:
            later = slice(256 * c + 256, 256 * c + 512)
            ahead = mm(normed, first[:, later]), mm(low, second[:, later])
        value, pull = gelu_pair(inner + bias)
        all_act[here, cols] = value.astype(bf16)
        inner = (grad_act * pull).astype(bf16)
        all_inner[here, cols] = inner
        small[row : row + 1, lane : lane + 256] += column_sum(inner.astype(f32))
    back = mm(all_inner[here, :], first[...], NT)
    small[5:6, :] += column_sum(back * unit)
    small[6:7, :] += column_sum(back)
    grad_mid[...] = (grad_out + norm_back(back * vec[5:6, :], unit, spread)).reshape(PAIR, ROWS, C)
    total = stream + vec[7:8, :] + mm(all_act[here, :], second[...], NT)
    for n in range(PAIR):
        alive = (i * PAIR + n < place[2]).astype(f32)
        result[n] = (total[n * ROWS : n * ROWS + TOKENS] * alive).astype(bf16)

    @pl.when(i == pl.num_programs(0) - 1)
    def _():
        mlp_weight_grads(place, all_grad, all_act, all_inner, all_normed, pieces)


def mlp_weight_grads(place, all_grad, all_act, all_inner, all_normed, *outs):
    grad_across = all_grad[...].T
    normed_across = all_normed[...].T
    for m in range(8):
        block = m if len(outs) == 1 else place[0] ^ m
        cols = pl.ds(pl.multiple_of(block * BLOCK, BLOCK), BLOCK)
        for p, total in enumerate(
            (mm(normed_across, all_inner[:, cols]), mm(grad_across, all_act[:, cols]))
        ):
            total = total.astype(bf16)
            for z in range(4):
                if len(outs) == 1:
                    outs[0][m, z, p] = total[128 * z : 128 * z + 128]
                else:
                    outs[m % 2][m // 2, z, p] = total[128 * z : 128 * z + 128]


def mlp_both(place, grad, mid, weight, vec, after):
    images = mid.shape[0]
    total = images * ROWS
    pieces = (8, 4, 2, 128, BLOCK)
    return call(
        partial(mlp_both_body, len(weight), len(after)),
        "mlp_both",
        (images // PAIR,),
        [HBM] * (len(weight) + len(after)) + [per_pair(ROWS, C), per_pair(ROWS, C), whole(vec.shape)],
        [per_pair(TOKENS, C), per_pair(ROWS, C), whole(pieces), whole((16, C))],
        [
            shape((images, TOKENS, C), bf16),
            shape((images, ROWS, C), f32),
            shape(pieces, bf16),
            shape((16, C), f32),
        ],
        [
            pltpu.VMEM((total, C), bf16),
            pltpu.VMEM((total, HID), bf16),
            pltpu.VMEM((total, HID), bf16),
            pltpu.VMEM((total, C), bf16),
            pltpu.VMEM((2, C, HID), bf16),
            pltpu.SemaphoreType.DMA((8, 4, 2)),
        ],
        45,
        prefetch=1,
    )(place, *weight, *after, grad, mid, vec)


def mlp_backward_body(stacks, waits, place, *refs):
    arrays, refs = refs[:stacks], refs[stacks + waits :]
    grad, act, slope, mid, vec, grad_mid, own, other, small = refs[:9]
    all_grad, all_act, all_inner, all_normed, kept, sems = refs[9:]
    first, second = kept.at[0], kept.at[1]
    i = pl.program_id(0)

    @pl.when(i == 0)
    def _():
        fetch(weight_copies(place, arrays, kept, sems))
        small[...] = jnp.zeros_like(small)

    rows = PAIR * ROWS
    grad_out = grad[...].reshape(rows, C)
    here = pl.ds(pl.multiple_of(i * rows, 32), rows)
    low = grad_out.astype(bf16)
    all_grad[here, :] = low
    small[7:8, :] += column_sum(low.astype(f32))
    all_act[here, :] = act[...].reshape(rows, HID)
    unit, spread = norm(mid[...].reshape(rows, C))
    all_normed[here, :] = (unit * vec[5:6, :] + vec[6:7, :]).astype(bf16)
    ahead = mm(low, second[:, 0:BLOCK])
    for c in range(8):
        cols = slice(256 * c, 256 * c + 256)
        pull = slope[:, :, cols].reshape(rows, BLOCK).astype(f32)
        grad_act = ahead
        if c < 7:
            ahead = mm(low, second[:, 256 * c + 256 : 256 * c + 512])
        inner = (grad_act * pull).astype(bf16)
        all_inner[here, cols] = inner
        row, lane = 8 + c // 2, 256 * (c % 2)
        small[row : row + 1, lane : lane + 256] += column_sum(inner.astype(f32))
    back = mm(all_inner[here, :], first[...], NT)
    small[5:6, :] += column_sum(back * unit)
    small[6:7, :] += column_sum(back)
    grad_mid[...] = (grad_out + norm_back(back * vec[5:6, :], unit, spread)).reshape(PAIR, ROWS, C)

    @pl.when(i == pl.num_programs(0) - 1)
    def _():
        mlp_weight_grads(place, all_grad, all_act, all_inner, all_normed, own, other)


def mlp_backward(layer, place, grad, act, slope, mid, weight, vec, after):
    images = mid.shape[0]
    total = images * ROWS
    pieces = (4, 4, 2, 128, BLOCK)
    return call(
        partial(mlp_backward_body, len(weight), len(after)),
        f"mlp_backward_{layer}",
        (images // PAIR,),
        [HBM] * (len(weight) + len(after))
        + [
            per_pair(grad.shape[1], C),
            per_pair(ROWS, HID),
            per_pair(ROWS, HID),
            per_pair(ROWS, C),
            whole(vec.shape),
        ],
        [per_pair(ROWS, C), whole(pieces), whole(pieces), whole((16, C))],
        [
            shape((images, ROWS, C), f32),
            shape(pieces, bf16),
            shape(pieces, bf16),
            shape((16, C), f32),
        ],
        [
            pltpu.VMEM((total, C), bf16),
            pltpu.VMEM((total, HID), bf16),
            pltpu.VMEM((total, HID), bf16),
            pltpu.VMEM((total, C), bf16),
            pltpu.VMEM((2, C, HID), bf16),
            pltpu.SemaphoreType.DMA((8, 4, 2)),
        ],
        30,
        prefetch=1,
    )(place, *weight, *after, grad, act, slope, mid, vec)


def attention_backward_body(layer, stacks, waits, resumed, ends, place, *refs):
    arrays, refs = refs[:stacks], refs[stacks + waits :]
    if resumed:
        (own_before, other_before, pairs_before), refs = refs[1:4], refs[4:]
    grad, x, qkv, merged, totals, table, vec, before = refs[:8]
    perm, perm_back, heads, rel, spread, result = refs[8:14]
    outs, refs = (refs[14:15], refs[15:]) if layer else (refs[14:16], refs[16:])
    pairs, small, framed, grad_framed, all_normed, all_packed, all_merged = refs[:7]
    across, hits, beside, kept, sems = refs[7:]
    weight = kept.at[0]
    i = pl.program_id(0)

    @pl.when(i == 0)
    def _():
        fetch(weight_copies(place, arrays, kept, sems))
        small[...] = before[...]
        pairs[...] = pairs_before[...] if resumed else jnp.zeros_like(pairs)

    stream = x[0]
    here = pl.ds(pl.multiple_of(i * ROWS, 16), ROWS)
    unit, spread_one = norm(stream)
    all_normed[here, :] = (unit * vec[0:1, :] + vec[1:2, :]).astype(bf16)
    low = grad[0].astype(bf16)
    all_packed[here, 3 * C :] = low
    all_merged[here, :] = merged[0]
    small[4:5, :] += column_sum(low.astype(f32))
    moved = mm(perm[...], low).astype(bf16)
    framed[...] = mm(moved, weight[:, 3 * C :], NT).astype(bf16)
    lane_head = lane_heads()
    at = [128 * g for g in range(4)]

    def window(w):
        rows = slice(CELL * w, CELL * w + CELL)
        keys = [qkv[0, rows, C + c : C + c + 128] for c in at]
        query = [quad_rows(qkv[0, rows, c : c + 128], heads[...]) for c in at]
        pull = [quad_rows(framed[rows, c : c + 128], heads[...]) for c in at]
        scores = [mm(keys[g], query[g], NT) for g in range(4)]
        grad_probs = [
            mm(qkv[0, rows, 2 * C + at[g] : 2 * C + at[g] + 128], pull[g], NT) for g in range(4)
        ]
        return keys, query, pull, scores, grad_probs

    ahead = window(0)
    for w in range(4):
        rows = slice(CELL * w, CELL * w + CELL)
        keys, query, pull, scores, grad_probs = ahead
        if w < 3:
            ahead = window(w + 1)
        probs, grad_scores = [], []
        for g in range(4):
            shifted = scores[g] * scale + table[w % table.shape[0], g]
            prob = jnp.exp(shifted - totals[0, 4 * w + g : 4 * w + g + 1, :])
            mean = jnp.sum(prob * grad_probs[g], 0, keepdims=True)
            grad_score = (prob * (grad_probs[g] - mean)).astype(bf16)
            pairs[g] += grad_score.astype(f32)
            probs.append(prob.astype(bf16))
            grad_scores.append(grad_score)
        for g in range(4):
            grad_value = mm(probs[g], pull[g])
            grad_framed[rows, 2 * C + at[g] : 2 * C + at[g] + 128] = grad_value.astype(bf16)
        for g in range(4):
            grad_key = mm(grad_scores[g], query[g]) * scale
            grad_framed[rows, C + at[g] : C + at[g] + 128] = grad_key.astype(bf16)
        for g in range(4):
            grad_query = pick_heads(mm(grad_scores[g], keys[g], TN), lane_head) * scale
            grad_framed[rows, at[g] : at[g] + 128] = grad_query.astype(bf16)
    for c in range(6):
        cols = slice(256 * c, 256 * c + 256)
        part = mm(perm_back[...], grad_framed[:, cols])
        all_packed[here, cols] = part.astype(bf16)
        if c < 2:
            small[2:3, cols] += column_sum(part)
        if c >= 4:
            small[3:4, 256 * (c - 4) : 256 * (c - 4) + 256] += column_sum(part)
    back = mm(all_packed[here, : 3 * C], weight[:, : 3 * C], NT)
    small[0:1, :] += column_sum(back * unit)
    small[1:2, :] += column_sum(back)
    total = grad[0] + norm_back(back * vec[0:1, :], unit, spread_one)
    result[0] = total[: result.shape[1]]

    @pl.when(i == pl.num_programs(0) - 1)
    def _():
        across[0] = all_normed[...].T
        across[1] = all_merged[...].T
        beside[...] = jnp.zeros_like(beside)
        if ends:
            hits[...] = jnp.zeros_like(hits)

            def step(r, carry):
                same = rel[...] == r
                for g in range(4):
                    kept_pairs = jnp.where(same, pairs[g], 0.0)
                    hits[pl.ds(r, 1), 256 * g : 256 * g + 256] = column_sum(kept_pairs)
                return carry

            lax.fori_loop(0, NREL, step, 0)
            for z in range(4):
                beside[0, z] = lax.dot_general(
                    spread[...],
                    hits[:, 256 * z : 256 * z + 256],
                    NT,
                    precision=lax.Precision.HIGHEST,
                    preferred_element_type=f32,
                ).astype(bf16)
                beside[1, z, :, 0:128] = small[:, 128 * z : 128 * z + 128].astype(bf16)
        for m in range(8):
            b = m if layer else place[0] ^ m
            left = across[jnp.where(b < 6, 0, 1)]
            right = all_packed[:, pl.ds(pl.multiple_of(b * BLOCK, BLOCK), BLOCK)]
            block = mm(left, right)
            for z in range(4):
                if layer:
                    out = outs[0].at[m, z, 0]
                else:
                    to = (z + 4 - place[1]) & 3
                    out = outs[m % 2].at[m // 2, to, 0]
                new = block[128 * z : 128 * z + 128]
                if resumed:
                    old = other_before if m % 2 else own_before
                    new = new + old[m // 2, to, 0, 0:128, :].astype(f32)
                out[0:128, :] = new.astype(bf16)
                out[128:144, :] = beside[jnp.minimum(b, 2), z]


def attention_backward(
    layer, place, grad, x, qkv, merged, totals, table, weight, vec, small, perm, rel, after,
    first=0, count=None, resume=None,
):
    images = grad.shape[0]
    count = count or images
    pieces = (8 if layer else 4, 4, 1, 128 + SMALL, BLOCK)
    pairs = (4, CELL, QUAD * CELL)
    total = count * ROWS
    out_rows = TOKENS if layer == 0 else ROWS

    def image(rows, cols):
        return pl.BlockSpec((1, rows, cols), lambda i, *_: (i + first, 0, 0))

    resumed = list(resume or [])
    return call(
        partial(
            attention_backward_body, layer, len(weight), len(after), bool(resumed),
            first + count == images,
        ),
        f"attention_backward_{layer}_{first}",
        (count,),
        [HBM] * (len(weight) + len(after))
        + ([HBM, whole(pieces), whole(pieces), whole(pairs)] if resumed else [])
        + [
            image(ROWS, C),
            image(x.shape[1], C),
            image(FRAME, 3 * C),
            image(ROWS, C),
            image(16, QUAD * CELL),
            whole(table.shape),
            whole(vec.shape),
            whole((16, C)),
            whole((FRAME, ROWS)),
            whole((ROWS, FRAME)),
            whole((QUAD * CELL, 128)),
            whole(rel.shape),
            whole((SMALL, QUAD * CELL)),
        ],
        [image(out_rows, C)]
        + [whole(pieces)] * (1 if layer else 2)
        + [whole(pairs), whole((16, C))],
        [shape((images, out_rows, C), f32)]
        + [shape(pieces, bf16)] * (1 if layer else 2)
        + [shape(pairs, f32), shape((16, C), f32)],
        [
            pltpu.VMEM((FRAME, C), bf16),
            pltpu.VMEM((FRAME, 3 * C), bf16),
            pltpu.VMEM((total, C), bf16),
            pltpu.VMEM((total, 4 * C), bf16),
            pltpu.VMEM((total, C), bf16),
            pltpu.VMEM((2, C, total), bf16),
            pltpu.VMEM((256, 4 * QUAD * CELL), f32),
            pltpu.VMEM((3, 4, SMALL, BLOCK), bf16),
            pltpu.VMEM((1, C, HID), bf16),
            pltpu.SemaphoreType.DMA((8, 4, 1)),
        ],
        6 * count,
        prefetch=1,
        aliases={1 + len(weight) + len(after): 0} if resumed else None,
    )(
        place,
        *weight,
        *after,
        *resumed,
        grad,
        x,
        qkv,
        merged,
        totals,
        table,
        vec,
        small,
        jnp.asarray(perm, bf16),
        jnp.asarray(perm.T, bf16),
        jnp.asarray(head_rows(), bf16),
        rel,
        jnp.asarray(head_spread(SMALL), f32),
    )


def adam_step(weight, first, second, gradient, rate, decay):
    first_new = beta_one * first + (1.0 - beta_one) * gradient
    second_new = beta_two * second + (1.0 - beta_two) * gradient * gradient
    first_hat = first_new / (1.0 - beta_one**STEP)
    second_hat = second_new / (1.0 - beta_two**STEP)
    weight_new = weight - rate * (first_hat / (jnp.sqrt(second_hat) + adam_eps) + decay * weight)
    return (weight_new, first_new, second_new)


def adam_block(grad, weight, first, second, outs, cols):
    part = grad.astype(f32)
    first_new = beta_one * first[0, :, cols] + (1.0 - beta_one) * part
    second_new = beta_two * second[0, :, cols] + (1.0 - beta_two) * part * part
    spread = second_new * (1.0 / (1.0 - beta_two**STEP))
    inverse = pltpu.reciprocal(spread * lax.rsqrt(spread) + adam_eps, approx=True)
    step = first_new * (rate_matrix / (1.0 - beta_one**STEP)) * inverse
    outs[0][0, :, cols] = weight[0, :, cols] * (1.0 - rate_matrix * weight_decay) - step
    outs[1][0, :, cols] = first_new
    outs[2][0, :, cols] = second_new


def adam_body(place, near, far, weight, first, second, *refs):
    for j in range(2):
        for k in range(2):
            block = (((place[0] // 2) & 1) ^ j) * 2 + ((place[0] & 1) ^ k)
            cols = pl.ds(pl.multiple_of(block * BLOCK, BLOCK), BLOCK)
            adam_block((far if k else near)[j], weight, first, second, refs[-3:], cols)


def adam_body_plain(place, sums, weight, first, second, *refs):
    for k in range(4):
        cols = slice(BLOCK * k, BLOCK * k + BLOCK)
        adam_block(sums[k], weight, first, second, refs[-3:], cols)


def adam(layer, part, place, sums, state, done, after):
    kept = [] if done is None else list(done)
    if len(sums) == 2:
        parts = sums[0].shape[1] // 128
        body = adam_body
        spec = pl.BlockSpec(
            (1, 128, 4 * BLOCK),
            lambda p, j, place: (layer, 0, (part + p) % 3 * 2 + ((place[0] // 4) ^ j)),
        )
        piece = pl.BlockSpec((2, 128, BLOCK), lambda p, j, place: (j, p, 0))
    else:
        parts = sums[0].shape[1] // 128
        body = adam_body_plain
        spec = pl.BlockSpec(
            (1, 128, 4 * BLOCK), lambda p, j, place: (layer, 0, (part + p) % 3 * 2 + j)
        )
        piece = pl.BlockSpec((4, 128, BLOCK), lambda p, j, place: (j, p, 0))
    return call(
        body,
        f"adam_{layer}_{part}",
        (parts, 2),
        [piece] * len(sums) + [spec] * 3 + [HBM] * (len(kept) + len(after)),
        [spec] * 3,
        [shape(state[0].shape, f32)] * 3,
        [],
        3 * parts,
        prefetch=1,
        aliases={4 + len(sums) + k: k for k in range(len(kept))},
    )(place, *sums, *state, *kept, *after)


def swap(value, bits):
    return lax.ppermute(value, "dp", [(i, i ^ bits) for i in range(8)])


def shift(value, steps):
    return lax.ppermute(value, "zero", [(i, (i + steps) % 4) for i in range(4)])


def tie(values, after):
    values = list(values)
    return list(lax.optimization_barrier((*values, *after))[: len(values)])


def stack(values, after=()):
    return jnp.stack(tie(values, after) if after else values)


def add_body(count, *refs):
    total = refs[0][...].astype(f32)
    for k in range(1, count):
        total = total + refs[k][...].astype(f32)
    refs[-1][...] = total.astype(bf16)


def add(values, after=()):
    dims = values[0].shape
    return call(
        partial(add_body, len(values)),
        "add",
        (1,),
        [whole(dims)] * len(values) + [HBM] * len(after),
        whole(dims),
        shape(dims, bf16),
        [],
        10,
        mib=24,
    )(*values, *after)


def add_split_body(count, lead, *refs):
    for k in range(4):
        if count == 2:
            refs[len(refs) - 4 + k][...] = refs[0][k] + refs[1][k]
            continue
        total = refs[0][k].astype(f32)
        for v in range(1, count):
            total = total + refs[v][k].astype(f32)
        refs[len(refs) - 4 + k][...] = total.astype(bf16)


def add_split(values, after=()):
    dims = values[0].shape
    steps = 1
    ins = (4, dims[1] // steps, *dims[2:])
    outs = dims[1:]
    zeros = (0,) * (len(dims) - 2)
    return call(
        partial(add_split_body, len(values), True),
        "add_split",
        (steps,),
        [pl.BlockSpec(ins, lambda i: (0, i, *zeros))] * len(values) + [HBM] * len(after),
        [pl.BlockSpec((outs[0] // steps, *outs[1:]), lambda i: (i, *zeros))] * 4,
        [shape(outs, bf16)] * 4,
        [],
        10,
        mib=24,
    )(*values, *after)


def join_body(*refs):
    out = refs[-1]
    at = 0
    for group in (refs[:1], refs[1:2], refs[2:6]):
        parts, rows = group[0].shape[1:3]
        for p in range(parts):
            total = group[0][:, p]
            if len(group) > 1:
                total = total.astype(f32)
                for ref in group[1:]:
                    total = total + ref[:, p].astype(f32)
            out[:, at : at + rows, :] = total.astype(bf16)
            at += rows


def join(first, second, summed, after):
    rows = sum(value.shape[1] * value.shape[2] for value in (first, second, summed[0]))
    ins = [first, second, *summed]
    return call(
        join_body,
        "join",
        (1,),
        [whole(v.shape) for v in ins] + [HBM] * len(after),
        whole((4, rows, BLOCK)),
        shape((4, rows, BLOCK), bf16),
        [],
        5,
        mib=24,
    )(*ins, *after)


def add_last_body(*refs):
    done, out = refs[0], refs[-1]
    rows = 256
    out[0:rows, :] = done[done.shape[0] - rows :, :]
    total = refs[1][0].astype(f32)
    for ref in refs[2:5]:
        total = total + ref[0].astype(f32)
    out[rows : rows + total.shape[0], :] = total.astype(bf16)


def add_last(done, values, after):
    rows = 256 + values[0].shape[1]
    return call(
        add_last_body,
        "add_last",
        (1,),
        [whole(done.shape)] + [whole(v.shape) for v in values] + [HBM] * len(after),
        whole((rows, BLOCK)),
        shape((rows, BLOCK), bf16),
        [],
        10,
        mib=24,
    )(done, *values, *after)


def send_z(piece):
    return [piece] + [shift(piece, s) for s in range(1, 4)]


def send_plane(piece):
    return [piece] + [swap(piece, 2 * j) for j in range(1, 4)]


def give_plane(parts):
    return [parts[0]] + [swap(parts[j], 2 * j) for j in range(1, 4)]


def give_z(parts):
    return [parts[0]] + [shift(parts[s], s) for s in range(1, 4)]


def gather_wide(piece, dp, extra):
    fine = dp // 8
    parts, rows = piece.shape[0], piece.shape[1] - extra
    out = lax.all_gather(piece, ("dp", "zero"), axis=0, tiled=False)
    out = out.reshape(8, fine, 4, *piece.shape)
    main = out[..., :rows, :].transpose(0, 2, 3, 1, 4, 5).reshape(8, 4, parts, 128, BLOCK)
    return [jnp.concatenate([main, out[:, 0, ..., rows:, :]], 3)]


def reduce_wide(blocks, dp, extra):
    fine = dp // 8
    blocks = blocks.reshape(8, 4, *blocks.shape[-3:])
    parts, rows = blocks.shape[2], 128 // fine
    main = blocks[..., :128, :].reshape(8, 4, parts, fine, rows, BLOCK).transpose(0, 3, 1, 2, 4, 5)
    beside = jnp.broadcast_to(
        blocks[:, None, ..., 128:, :], (8, fine, 4, parts, extra, BLOCK)
    )
    flat = jnp.concatenate([main, beside], 4).reshape(dp * 4, parts, rows + extra, BLOCK)
    mine = lax.psum_scatter(flat, ("dp", "zero"), scatter_dimension=0, tiled=True)
    out = lax.all_gather(mine[0], "dp", axis=0, tiled=False)
    out = out.reshape(8, fine, parts, rows + extra, BLOCK)
    main = out[..., :rows, :].transpose(0, 2, 1, 3, 4).reshape(8, parts, 128, BLOCK)
    out = jnp.concatenate([main, out[:, 0, :, rows:]], 2)
    return out.reshape(8, -1, BLOCK)


def shards(
    dp, images, cotangent, counts, rel_index, regions,
    mat_w, mat_m, mat_v, vec_w, vec_m, vec_v, tab_w, tab_m, tab_v,
):
    near = dp == 8
    fine = dp // 8
    rows = 128 // fine
    me = lax.axis_index("dp")
    spot = [me, lax.axis_index("zero")] if near else [0 * me, 0 * me]
    place = jnp.stack(spot + [counts[0], me // fine, me % fine]).astype(jnp.int32)

    inside = np.arange(CELL) < WIN * WIN
    zones = regions.reshape(2, WIN, 2, WIN).transpose(0, 2, 1, 3).reshape(4, WIN * WIN)
    zones = jnp.pad(zones, ((0, 0), (0, 15)))
    differ = (zones[:, :, None] != zones[:, None, :]) & inside[None, None, :]
    outside = np.where(inside, 0.0, -1e30).astype(np.float32)[None, :, None]
    mask_shifted = jnp.tile(jnp.where(differ, mask_value, 0.0) + outside, (1, 1, QUAD)).astype(f32)
    mask_plain = jnp.asarray(np.ascontiguousarray(np.broadcast_to(outside, (1, CELL, QUAD * CELL))))
    masks = (mask_plain, mask_shifted)
    perms = (frames(False), frames(True))

    packed, cut_mlp0, cut_all1, rel = pack(
        place, rows, mat_w, rel_index, tab_w, vec_w
    )
    alive = (jnp.arange(images.shape[0]) < counts[0]).astype(f32)[:, None, None]
    pad = ((0, 0), (0, ROWS - TOKENS), (0, 0))
    images = jnp.pad(images.astype(f32), pad)
    cotangent = jnp.pad(cotangent.astype(f32) * alive, pad)

    def attention(layer, stream, weight, after):
        return attention_forward(
            layer, place, stream, weight, heads0, masks[layer], perms[layer], after
        )

    early = max(1, images.shape[0] * 3 // 8)
    if near:
        sent_heads0 = send_z(packed)
        *sent_heads0, images = tie([*sent_heads0, images], [])
        z_heads0 = stack(sent_heads0)
        all1 = gather_wide(tie([cut_all1], [z_heads0])[0], dp, 0)
        sent_heads0 = send_plane(z_heads0)
        sent_mlp0 = send_z(tie([cut_mlp0], [z_heads0])[0])
        cotangent, mask_shifted = tie([cotangent, mask_shifted], [z_heads0])
        *sent_heads0, cotangent, mask_shifted = tie(
            [*sent_heads0, cotangent, mask_shifted], sent_mlp0
        )
        masks = (mask_plain, mask_shifted)
        p_heads0 = stack(sent_heads0)
        heads0 = [p_heads0, swap(p_heads0, 1)]
        z_mlp0 = stack(sent_mlp0, [p_heads0])
        sent_mlp0 = send_plane(z_mlp0)
        kept0 = attention(0, images, heads0, [z_mlp0])
        p_mlp0 = stack(sent_mlp0, [kept0[0]])
        mlp0 = [p_mlp0, swap(p_mlp0, 1)]
    else:
        heads0 = gather_wide(packed, dp, EXTRA)
        mlp0 = gather_wide(cut_mlp0, dp, 0)
        all1 = gather_wide(cut_all1, dp, 0)
        kept0 = attention(0, images, heads0, [])
    stream, act, slope = mlp_forward(0, place, kept0[0], mlp0, kept0[5], [])
    kept1 = attention(1, stream, all1, [])
    kept = (kept0, kept1)
    inputs = (images, stream)
    attention_w = (heads0, all1)

    def backward_attention(layer, gradient, small, after, *span):
        mid, qkv, merged, totals, table, vec = kept[layer]
        return attention_backward(
            layer, place, gradient, inputs[layer], qkv, merged, totals, table, attention_w[layer],
            vec, small, perms[layer], rel, after, *span,
        )

    activations, grad_mid, parts_mlp1, small = mlp_both(
        place, cotangent, kept1[0], all1, kept1[5], []
    )

    def backward_mlp0(gradient, after):
        return mlp_backward(0, place, gradient, act, slope, kept0[0], mlp0, kept0[5], after)

    state = (mat_w, mat_m, mat_v)
    def exchange(parts):
        return [parts[0], swap(parts[1], 1)]

    gradient, parts_heads1, _, _ = backward_attention(1, grad_mid, small, [])
    grad_mid, *parts_mlp0, small = backward_mlp0(gradient, [])
    if near:
        t_mlp1 = lax.psum_scatter(parts_mlp1, "dp", scatter_dimension=0, tiled=True)[0]
        parts_heads1 = tie([parts_heads1], [t_mlp1, small])[0]
        t_heads1 = lax.psum_scatter(parts_heads1, "dp", scatter_dimension=0, tiled=True)[0]
        gone_mlp0 = exchange(parts_mlp0)
        gradient, *parts_heads0, pairs, small = backward_attention(0, grad_mid, small, [], 0, early)

        s_mlp0 = add_split(gone_mlp0, [gradient])
        gone_mlp0 = give_plane(s_mlp0)
        gradient, *parts_heads0, _, small = backward_attention(
            0, grad_mid, small, [s_mlp0[0]], early, images.shape[0] - early,
            [gradient, *parts_heads0, pairs]
        )

        t_all = join(t_mlp1, t_heads1, gone_mlp0, [small])
        gone_heads0 = exchange(tie(parts_heads0, gone_mlp0))
        g_all = lax.psum_scatter(t_all, "zero", scatter_dimension=0, tiled=True)[0]
        s_heads0 = add_split(gone_heads0, [t_all])
        gone_heads0 = give_plane(s_heads0)
        across = tie([activations.transpose(1, 0, 2), gradient.transpose(1, 0, 2)], [])
        t_heads0 = add_split(gone_heads0, across)
        activations, gradient = [value.transpose(1, 0, 2) for value in across]
        gone_heads0 = give_z(t_heads0)
        g_all, *gone_heads0 = tie([g_all, *gone_heads0], [])
        g_all0 = add_last(g_all, gone_heads0, [])
        g_all = tie([g_all], [g_all0])[0]
        n_all1 = lax.all_gather(g_all[:400], "dp", axis=0, tiled=False)
        n_all0 = stack(send_plane(g_all0))
        sums0 = [n_all0, swap(n_all0, 1)]
        m = place[0] ^ np.arange(2)
        both = jnp.concatenate([half[:, 384:] for half in sums0])
        beside0 = [
            lax.dynamic_index_in_dim(both, (m[b] % 2) * 4 + m[b] // 2, 0, False) for b in range(2)
        ]
    else:
        gradient, *parts_heads0, _, _ = backward_attention(0, grad_mid, small, [])
        n_mlp1 = reduce_wide(parts_mlp1, dp, 0)
        n_heads1 = reduce_wide(parts_heads1, dp, SMALL)
        n_all1 = jnp.concatenate([n_mlp1, n_heads1], 1)
        n_mlp0 = reduce_wide(jnp.stack(parts_mlp0, 1), dp, 0)
        n_heads0 = reduce_wide(jnp.stack(parts_heads0, 1), dp, SMALL)
        sums0 = [jnp.concatenate([n_mlp0, n_heads0], 1)]
        beside0 = sums0[0][:2, 384:]
    done = adam(0, 1, place, sums0, state, None, [])
    done = adam(1, 1, place, [n_all1], state, done, [])

    def beside(block):
        return jnp.stack([beside0[block], n_all1[block, 384:]]).astype(f32)

    new_vec = adam_step(vec_w, vec_m, vec_v, beside(1)[:, 0:12, 0:128], rate_vector, 0.0)
    new_tab = adam_step(tab_w, tab_m, tab_v, beside(0)[:, 0:4, 0:NREL], rate_table, 0.0)
    return (activations, gradient, *done, *new_vec, *new_tab)


def solution(mesh):
    images = P(("dp", "zero"), None, None)
    rows = P(None, "zero", None)
    lanes = P(None, None, "zero")
    return jax.shard_map(
        partial(shards, mesh.shape["dp"]),
        mesh=mesh,
        in_specs=(images, images, P(("dp", "zero")), P(), P())
        + (rows,) * 3 + (lanes,) * 3 + (rows,) * 3,
        out_specs=(images, images) + (rows,) * 3 + (lanes,) * 3 + (rows,) * 3,
        check_vma=False,
    )
```

```python
from functools import partial

import jax
import jax.numpy as jnp
import numpy as np
from jax import lax
from jax.experimental import pallas as pl
from jax.experimental.pallas import tpu as pltpu
from jax.sharding import PartitionSpec as P

WIN = 7
SIDE = 14
STEP = 10
NREL = 169
C = 512
HID = 2048
TOKENS = SIDE * SIDE
PAIR = 2
ROWS = 208
FRAME = 256
CELL = 64
QUAD = 4
BLOCK = 256
EXTRA = 32
SMALL = 16

norm_eps = 1e-05
mask_value = -100.0
beta_one = 0.9
beta_two = 0.999
adam_eps = 1e-08
weight_decay = 0.05
rate_matrix = 0.1
rate_vector = 0.5
rate_table = 1.0
scale = 32 ** (-0.5)

bf16 = jnp.bfloat16
f32 = jnp.float32
NN = (((1,), (0,)), ((), ()))
NT = (((1,), (1,)), ((), ()))
TN = (((0,), (0,)), ((), ()))


def mm(left, right, dims=NN):
    return lax.dot_general(left, right, dims, preferred_element_type=f32)


def frames(shifted):
    move = WIN // 2 if shifted else 0
    placed = np.zeros((FRAME, ROWS), np.float32)
    for wy in range(2):
        for wx in range(2):
            for iy in range(WIN):
                for ix in range(WIN):
                    y = (wy * WIN + iy + move) % SIDE
                    x = (wx * WIN + ix + move) % SIDE
                    placed[(wy * 2 + wx) * CELL + iy * WIN + ix, y * SIDE + x] = 1
    return placed


def head_rows():
    rows = np.zeros((QUAD * CELL, 128), np.float32)
    for h in range(QUAD):
        rows[h * CELL : (h + 1) * CELL, h * 32 : (h + 1) * 32] = 1
    return rows


def head_spread(rows):
    out = np.zeros((rows, QUAD * CELL), np.float32)
    for h in range(QUAD):
        out[h, h * CELL : (h + 1) * CELL] = 1
    return out


def norm(rows):
    centred = rows - jnp.mean(rows, -1, keepdims=True)
    spread = lax.rsqrt(jnp.mean(centred * centred, -1, keepdims=True) + norm_eps)
    return centred * spread, spread


def norm_back(grad_unit, unit, spread):
    return spread * (
        grad_unit
        - jnp.mean(grad_unit, -1, keepdims=True)
        - unit * jnp.mean(grad_unit * unit, -1, keepdims=True)
    )


def column_sum(rows):
    return jnp.sum(rows, 0, keepdims=True)


def gelu_pair(u):
    size = jnp.abs(u)
    below = 1.0 + (0.3275911 * 0.5**0.5) * size
    t = pltpu.reciprocal(below, approx=True)
    bell = jnp.exp2(u * u * (-0.5 * 1.4426950408889634))
    poly = t * (
        0.127414796 + t * (-0.142248368 + t * (0.710706871 + t * (-0.726576013 + t * 0.530702714)))
    )
    tail = poly * bell
    phi = jnp.where(u >= 0, 1.0 - tail, tail)
    return u * phi, phi + u * bell * 0.3989422804014327


def quad_rows(part, heads):
    return jnp.concatenate([part] * QUAD, 0) * heads


def pick_heads(stacked, lane_head):
    low = jnp.where(lane_head == 0, stacked[:CELL], stacked[CELL : 2 * CELL])
    high = jnp.where(lane_head == 2, stacked[2 * CELL : 3 * CELL], stacked[3 * CELL :])
    return jnp.where(lane_head < 2, low, high)


def lane_heads():
    return lax.broadcasted_iota(jnp.int32, (CELL, 128), 1) // 32


def whole(shape):
    zero = (0,) * len(shape)
    return pl.BlockSpec(shape, lambda *_: zero, pipeline_mode=pl.Buffered(1))


def per_image(rows, cols):
    return pl.BlockSpec((1, rows, cols), lambda i, *_: (i, 0, 0))


def per_pair(rows, cols):
    return pl.BlockSpec((PAIR, rows, cols), lambda i, *_: (i, 0, 0))


HBM = pl.BlockSpec(memory_space=pl.ANY)


def weight_copies(place, stacks, kept, sems, part=0):
    copies = []
    for m in range(8):
        for s in range(4):
            for p in range(kept.shape[0]):
                if len(stacks) == 1:
                    source, block, owner = stacks[0].at[m, s, part + p], m, s
                else:
                    source = stacks[m % 2].at[m // 2, s, p]
                    block, owner = place[0] ^ m, (place[1] + 4 - s) & 3
                rows = pl.ds(pl.multiple_of(owner * 128, 128), 128)
                cols = pl.ds(pl.multiple_of(block * BLOCK, BLOCK), BLOCK)
                copies.append(
                    pltpu.make_async_copy(
                        source.at[pl.ds(0, 128), :], kept.at[p, rows, cols], sems.at[m, s, p]
                    )
                )
    return copies


def extra_copies(place, stacks, kept, sems):
    copies = []
    for m in range(8):
        for s in range(4):
            if len(stacks) == 1:
                source, block, owner = stacks[0].at[m, s, 0], m, s
            else:
                source = stacks[m % 2].at[m // 2, s, 0]
                block, owner = place[0] ^ m, (place[1] + 4 - s) & 3
            copies.append(
                pltpu.make_async_copy(
                    source.at[pl.ds(128, EXTRA), :], kept.at[block, owner], sems.at[m, s, 0]
                )
            )
    return copies


def fetch(copies):
    for copy in copies:
        copy.start()
    for copy in copies:
        copy.wait()


def call(
    body, name, grid, ins, outs, out_shapes, scratch, cost_us, prefetch=0, aliases=None, mib=58
):
    return pl.pallas_call(
        body,
        name=name,
        grid_spec=pltpu.PrefetchScalarGridSpec(
            num_scalar_prefetch=prefetch,
            grid=grid,
            in_specs=ins,
            out_specs=outs,
            scratch_shapes=scratch,
        ),
        out_shape=out_shapes,
        input_output_aliases=aliases or {},
        compiler_params=pltpu.CompilerParams(
            dimension_semantics=("arbitrary",) * len(grid), vmem_limit_bytes=mib * 1024 * 1024
        ),
        cost_estimate=pl.CostEstimate(
            flops=0, bytes_accessed=int(cost_us * 3.69e4), transcendentals=0
        ),
    )


def shape(dims, kind):
    return jax.ShapeDtypeStruct(dims, kind)


def pack_body(place, *refs):
    mats, (pair_index, tab, vec, spread) = refs[:6], refs[6:10]
    out, mlp0, all1, rel, spread_tab, small = refs[10:]
    rows = mats[0].shape[1]
    out[0, 0:rows, :] = mats[0][0].astype(bf16)
    for ref, at, n in ((mlp0, 0, 1), (mlp0, 1, 2), (all1, 0, 3), (all1, 1, 4), (all1, 2, 5)):
        ref[at] = mats[n][0].astype(bf16)
    rel[...] = jnp.full(rel.shape, -1, jnp.int32)
    across = pair_index[...].astype(f32).T.astype(jnp.int32)
    for h in range(QUAD):
        rel[0 : WIN * WIN, CELL * h : CELL * h + WIN * WIN] = across
    for layer in range(2):
        spread_tab[layer, 0:NREL, :] = mm(tab[layer].astype(bf16), spread[...], TN)
    pairs = rel[pl.ds(pl.multiple_of(place[3] * 8, 8), 8), :]

    def step(r, sums):
        hit = pairs == r
        return tuple(
            jnp.where(hit, spread_tab[layer, pl.ds(r, 1), :], sums[layer]) for layer in range(2)
        )

    start = jnp.zeros((8, QUAD * CELL), f32)
    first, second = lax.fori_loop(0, NREL, step, (start, start), unroll=13)
    out[0, rows : rows + 16, :] = jnp.concatenate([first, second], 0).astype(bf16)
    small[...] = jnp.zeros_like(small)
    row = jnp.minimum(place[3] * 2, 10)
    for layer in range(2):
        for k in range(2):
            small[k : k + 1, layer * 128 : (layer + 1) * 128] = vec[row + k, layer : layer + 1, :]
    out[0, rows + 16 : rows + 32, :] = small[...].astype(bf16)


def pack(place, rows, mat_w, rel_index, tab_w, vec_w):
    vec_w = vec_w.transpose(1, 0, 2)

    def block(layer, part):
        return pl.BlockSpec(
            (1, rows, BLOCK), lambda i, place: (layer, place[4], part * 8 + place[3])
        )

    dims = [(1, rows + EXTRA, BLOCK), (2, rows, BLOCK), (3, rows, BLOCK)]
    return call(
        pack_body,
        "pack",
        (1,),
        [block(layer, part) for layer in range(2) for part in range(3)]
        + [
            whole(rel_index.shape),
            whole(tab_w.shape),
            whole(vec_w.shape),
            whole((QUAD, QUAD * CELL)),
        ],
        [whole(d) for d in dims] + [whole((CELL, QUAD * CELL))],
        [shape(d, bf16) for d in dims] + [shape((CELL, QUAD * CELL), jnp.int32)],
        [pltpu.VMEM((2, 176, QUAD * CELL), f32), pltpu.VMEM((16, 256), f32)],
        4,
        prefetch=1,
    )(place, *[mat_w] * 6, rel_index, tab_w, vec_w, jnp.asarray(head_spread(QUAD), bf16))


def attention_forward_body(layer, stacks, waits, place, *refs):
    arrays, refs = refs[: stacks[0]], refs[stacks[0] :]
    extras, refs = refs[: stacks[1]], refs[stacks[1] + waits :]
    x, mask, perm, perm_back, heads = refs[:5]
    mid, qkv, merged, totals, table, vec, framed, kept, extra_kept, sems, more_sems = refs[5:]
    weight, extra = kept.at[0], extra_kept

    @pl.when(pl.program_id(0) == 0)
    def _():
        fetch(
            weight_copies(place, arrays, kept, sems)
            + extra_copies(place, extras, extra_kept, more_sems)
        )
        vec[...] = jnp.zeros_like(vec)
        for z in range(4):
            for d in range(8):
                pair = extra[d, z, 0:16, :].astype(f32)
                bias = pair[8 * layer : 8 * layer + 8]
                for w in range(table.shape[0]):
                    table[w, z, 8 * d : 8 * d + 8, :] = bias + mask[w, 8 * d : 8 * d + 8, :]
                if d < 6:
                    rows = extra[d, z, 16:32, 128 * layer : 128 * layer + 128].astype(f32)
                    vec[2 * d : 2 * d + 2, 128 * z : 128 * z + 128] = rows[0:2]

    stream = x[0]
    unit, _ = norm(stream)
    normed = (unit * vec[0:1, :] + vec[1:2, :]).astype(bf16)
    normed = mm(perm[...], normed).astype(bf16)
    for c in range(6):
        part = mm(normed, weight[:, 256 * c : 256 * c + 256])
        if c < 2:
            part = part + vec[2:3, 256 * c : 256 * c + 256]
        if c >= 4:
            part = part + vec[3:4, 256 * (c - 4) : 256 * (c - 4) + 256]
        qkv[0, :, 256 * c : 256 * c + 256] = part.astype(bf16)
    lane_head = lane_heads()

    def score(unit):
        rows, at = slice(CELL * (unit // 4), CELL * (unit // 4) + CELL), 128 * (unit % 4)
        query = quad_rows(qkv[0, rows, at : at + 128], heads[...])
        return mm(qkv[0, rows, C + at : C + at + 128], query, NT)

    ahead = score(0)
    for n in range(16):
        w, g = n // 4, n % 4
        rows, at = slice(CELL * w, CELL * w + CELL), 128 * g
        scores = ahead * scale + table[w % table.shape[0], g]
        if n < 15:
            ahead = score(n + 1)
        top = jnp.max(scores, 0, keepdims=True)
        raised = jnp.exp(scores - top)
        total = jnp.sum(raised, 0, keepdims=True)
        totals[0, n : n + 1, :] = top + jnp.log(total)
        probs = (raised * (1.0 / total)).astype(bf16)
        stacked = mm(probs, qkv[0, rows, 2 * C + at : 2 * C + at + 128], TN)
        framed[rows, at : at + 128] = pick_heads(stacked, lane_head).astype(bf16)
    gathered = mm(perm_back[...], framed[...]).astype(bf16)
    merged[0] = gathered
    mid[0] = stream + mm(gathered, weight[:, 3 * C :]) + vec[4:5, :]


def attention_forward(layer, place, x, weight, extra, mask, perm, after):
    images = x.shape[0]
    tables = mask.shape[0]
    return call(
        partial(attention_forward_body, layer, (len(weight), len(extra)), len(after)),
        f"attention_forward_{layer}",
        (images,),
        [HBM] * (len(weight) + len(extra) + len(after))
        + [
            per_image(x.shape[1], C),
            whole(mask.shape),
            whole((FRAME, ROWS)),
            whole((ROWS, FRAME)),
            whole((QUAD * CELL, 128)),
        ],
        [
            per_image(ROWS, C),
            per_image(FRAME, 3 * C),
            per_image(ROWS, C),
            per_image(16, QUAD * CELL),
            pl.BlockSpec((tables, 4, CELL, QUAD * CELL), lambda i, *_: (0, 0, 0, 0)),
            pl.BlockSpec((16, C), lambda i, *_: (0, 0)),
        ],
        [
            shape((images, ROWS, C), f32),
            shape((images, FRAME, 3 * C), bf16),
            shape((images, ROWS, C), bf16),
            shape((images, 16, QUAD * CELL), f32),
            shape((tables, 4, CELL, QUAD * CELL), f32),
            shape((16, C), f32),
        ],
        [
            pltpu.VMEM((FRAME, C), bf16),
            pltpu.VMEM((1, C, HID), bf16),
            pltpu.VMEM((8, 4, EXTRA, BLOCK), bf16),
            pltpu.SemaphoreType.DMA((8, 4, 1)),
            pltpu.SemaphoreType.DMA((8, 4, 1)),
        ],
        20,
        prefetch=1,
    )(
        place,
        *weight,
        *extra,
        *after,
        x,
        mask,
        jnp.asarray(perm, bf16),
        jnp.asarray(perm.T, bf16),
        jnp.asarray(head_rows(), bf16),
    )


def mlp_forward_body(stacks, waits, place, *refs):
    arrays, refs = refs[:stacks], refs[stacks + waits :]
    mid, vec, result, act, slope, kept, sems = refs
    first, second = kept.at[0], kept.at[1]

    @pl.when(pl.program_id(0) == 0)
    def _():
        fetch(weight_copies(place, arrays, kept, sems))

    rows = PAIR * ROWS
    stream = mid[...].reshape(rows, C)
    unit, _ = norm(stream)
    normed = (unit * vec[5:6, :] + vec[6:7, :]).astype(bf16)
    ahead = mm(normed, first[:, 0:BLOCK])
    for c in range(8):
        cols = slice(256 * c, 256 * c + 256)
        bias = vec[8 + c // 2 : 9 + c // 2, 256 * (c % 2) : 256 * (c % 2) + 256]
        inner = ahead + bias
        if c < 7:
            ahead = mm(normed, first[:, 256 * c + 256 : 256 * c + 512])
        value, pull = gelu_pair(inner)
        act[:, :, cols] = value.astype(bf16).reshape(PAIR, ROWS, BLOCK)
        slope[:, :, cols] = pull.astype(bf16).reshape(PAIR, ROWS, BLOCK)
    total = stream + vec[7:8, :] + mm(act[...].reshape(rows, HID), second[...], NT)
    result[...] = total.reshape(PAIR, ROWS, C)


def mlp_forward(layer, place, mid, weight, vec, after):
    images = mid.shape[0]
    return call(
        partial(mlp_forward_body, len(weight), len(after)),
        f"mlp_forward_{layer}",
        (images // PAIR,),
        [HBM] * (len(weight) + len(after)) + [per_pair(ROWS, C), whole(vec.shape)],
        [per_pair(ROWS, C), per_pair(ROWS, HID), per_pair(ROWS, HID)],
        [
            shape((images, ROWS, C), f32),
            shape((images, ROWS, HID), bf16),
            shape((images, ROWS, HID), bf16),
        ],
        [
            pltpu.VMEM((2, C, HID), bf16),
            pltpu.SemaphoreType.DMA((8, 4, 2)),
        ],
        22,
        prefetch=1,
    )(place, *weight, *after, mid, vec)


def mlp_both_body(stacks, waits, place, *refs):
    arrays, refs = refs[:stacks], refs[stacks + waits :]
    grad, mid, vec, result, grad_mid, pieces, small = refs[:7]
    all_grad, all_act, all_inner, all_normed, kept, sems = refs[7:]
    first, second = kept.at[0], kept.at[1]
    i = pl.program_id(0)

    @pl.when(i == 0)
    def _():
        fetch(weight_copies(place, arrays, kept, sems, 1))
        small[...] = jnp.zeros_like(small)

    rows = PAIR * ROWS
    grad_out = grad[...].reshape(rows, C)
    here = pl.ds(pl.multiple_of(i * rows, 32), rows)
    low = grad_out.astype(bf16)
    all_grad[here, :] = low
    small[7:8, :] += column_sum(grad_out)
    stream = mid[...].reshape(rows, C)
    unit, spread = norm(stream)
    normed = (unit * vec[5:6, :] + vec[6:7, :]).astype(bf16)
    all_normed[here, :] = normed
    ahead = mm(normed, first[:, 0:BLOCK]), mm(low, second[:, 0:BLOCK])
    for c in range(8):
        cols = slice(256 * c, 256 * c + 256)
        row, lane = 8 + c // 2, 256 * (c % 2)
        bias = vec[row : row + 1, lane : lane + 256]
        inner, grad_act = ahead
        if c < 7:
            later = slice(256 * c + 256, 256 * c + 512)
            ahead = mm(normed, first[:, later]), mm(low, second[:, later])
        value, pull = gelu_pair(inner + bias)
        all_act[here, cols] = value.astype(bf16)
        inner = (grad_act * pull).astype(bf16)
        all_inner[here, cols] = inner
        small[row : row + 1, lane : lane + 256] += column_sum(inner.astype(f32))
    back = mm(all_inner[here, :], first[...], NT)
    small[5:6, :] += column_sum(back * unit)
    small[6:7, :] += column_sum(back)
    grad_mid[...] = (grad_out + norm_back(back * vec[5:6, :], unit, spread)).reshape(PAIR, ROWS, C)
    total = stream + vec[7:8, :] + mm(all_act[here, :], second[...], NT)
    for n in range(PAIR):
        alive = (i * PAIR + n < place[2]).astype(f32)
        result[n] = (total[n * ROWS : n * ROWS + TOKENS] * alive).astype(bf16)

    @pl.when(i == pl.num_programs(0) - 1)
    def _():
        mlp_weight_grads(place, all_grad, all_act, all_inner, all_normed, pieces)


def mlp_weight_grads(place, all_grad, all_act, all_inner, all_normed, *outs):
    grad_across = all_grad[...].T
    normed_across = all_normed[...].T
    for m in range(8):
        block = m if len(outs) == 1 else place[0] ^ m
        cols = pl.ds(pl.multiple_of(block * BLOCK, BLOCK), BLOCK)
        for p, total in enumerate(
            (mm(normed_across, all_inner[:, cols]), mm(grad_across, all_act[:, cols]))
        ):
            total = total.astype(bf16)
            for z in range(4):
                if len(outs) == 1:
                    outs[0][m, z, p] = total[128 * z : 128 * z + 128]
                else:
                    outs[m % 2][m // 2, z, p] = total[128 * z : 128 * z + 128]


def mlp_both(place, grad, mid, weight, vec, after):
    images = mid.shape[0]
    total = images * ROWS
    pieces = (8, 4, 2, 128, BLOCK)
    return call(
        partial(mlp_both_body, len(weight), len(after)),
        "mlp_both",
        (images // PAIR,),
        [HBM] * (len(weight) + len(after)) + [per_pair(ROWS, C), per_pair(ROWS, C), whole(vec.shape)],
        [per_pair(TOKENS, C), per_pair(ROWS, C), whole(pieces), whole((16, C))],
        [
            shape((images, TOKENS, C), bf16),
            shape((images, ROWS, C), f32),
            shape(pieces, bf16),
            shape((16, C), f32),
        ],
        [
            pltpu.VMEM((total, C), bf16),
            pltpu.VMEM((total, HID), bf16),
            pltpu.VMEM((total, HID), bf16),
            pltpu.VMEM((total, C), bf16),
            pltpu.VMEM((2, C, HID), bf16),
            pltpu.SemaphoreType.DMA((8, 4, 2)),
        ],
        45,
        prefetch=1,
    )(place, *weight, *after, grad, mid, vec)


def mlp_backward_body(stacks, waits, place, *refs):
    arrays, refs = refs[:stacks], refs[stacks + waits :]
    grad, act, slope, mid, vec, grad_mid, own, other, small = refs[:9]
    all_grad, all_act, all_inner, all_normed, kept, sems = refs[9:]
    first, second = kept.at[0], kept.at[1]
    i = pl.program_id(0)

    @pl.when(i == 0)
    def _():
        fetch(weight_copies(place, arrays, kept, sems))
        small[...] = jnp.zeros_like(small)

    rows = PAIR * ROWS
    grad_out = grad[...].reshape(rows, C)
    here = pl.ds(pl.multiple_of(i * rows, 32), rows)
    low = grad_out.astype(bf16)
    all_grad[here, :] = low
    small[7:8, :] += column_sum(low.astype(f32))
    all_act[here, :] = act[...].reshape(rows, HID)
    unit, spread = norm(mid[...].reshape(rows, C))
    all_normed[here, :] = (unit * vec[5:6, :] + vec[6:7, :]).astype(bf16)
    ahead = mm(low, second[:, 0:BLOCK])
    for c in range(8):
        cols = slice(256 * c, 256 * c + 256)
        pull = slope[:, :, cols].reshape(rows, BLOCK).astype(f32)
        grad_act = ahead
        if c < 7:
            ahead = mm(low, second[:, 256 * c + 256 : 256 * c + 512])
        inner = (grad_act * pull).astype(bf16)
        all_inner[here, cols] = inner
        row, lane = 8 + c // 2, 256 * (c % 2)
        small[row : row + 1, lane : lane + 256] += column_sum(inner.astype(f32))
    back = mm(all_inner[here, :], first[...], NT)
    small[5:6, :] += column_sum(back * unit)
    small[6:7, :] += column_sum(back)
    grad_mid[...] = (grad_out + norm_back(back * vec[5:6, :], unit, spread)).reshape(PAIR, ROWS, C)

    @pl.when(i == pl.num_programs(0) - 1)
    def _():
        mlp_weight_grads(place, all_grad, all_act, all_inner, all_normed, own, other)


def mlp_backward(layer, place, grad, act, slope, mid, weight, vec, after):
    images = mid.shape[0]
    total = images * ROWS
    pieces = (4, 4, 2, 128, BLOCK)
    return call(
        partial(mlp_backward_body, len(weight), len(after)),
        f"mlp_backward_{layer}",
        (images // PAIR,),
        [HBM] * (len(weight) + len(after))
        + [
            per_pair(grad.shape[1], C),
            per_pair(ROWS, HID),
            per_pair(ROWS, HID),
            per_pair(ROWS, C),
            whole(vec.shape),
        ],
        [per_pair(ROWS, C), whole(pieces), whole(pieces), whole((16, C))],
        [
            shape((images, ROWS, C), f32),
            shape(pieces, bf16),
            shape(pieces, bf16),
            shape((16, C), f32),
        ],
        [
            pltpu.VMEM((total, C), bf16),
            pltpu.VMEM((total, HID), bf16),
            pltpu.VMEM((total, HID), bf16),
            pltpu.VMEM((total, C), bf16),
            pltpu.VMEM((2, C, HID), bf16),
            pltpu.SemaphoreType.DMA((8, 4, 2)),
        ],
        30,
        prefetch=1,
    )(place, *weight, *after, grad, act, slope, mid, vec)


def attention_backward_body(layer, stacks, waits, resumed, ends, place, *refs):
    arrays, refs = refs[:stacks], refs[stacks + waits :]
    if resumed:
        (own_before, other_before, pairs_before), refs = refs[1:4], refs[4:]
    grad, x, qkv, merged, totals, table, vec, before = refs[:8]
    perm, perm_back, heads, rel, spread, result = refs[8:14]
    outs, refs = (refs[14:15], refs[15:]) if layer else (refs[14:16], refs[16:])
    pairs, small, framed, grad_framed, all_normed, all_packed, all_merged = refs[:7]
    across, hits, beside, kept, sems = refs[7:]
    weight = kept.at[0]
    i = pl.program_id(0)

    @pl.when(i == 0)
    def _():
        fetch(weight_copies(place, arrays, kept, sems))
        small[...] = before[...]
        pairs[...] = pairs_before[...] if resumed else jnp.zeros_like(pairs)

    stream = x[0]
    here = pl.ds(pl.multiple_of(i * ROWS, 16), ROWS)
    unit, spread_one = norm(stream)
    all_normed[here, :] = (unit * vec[0:1, :] + vec[1:2, :]).astype(bf16)
    low = grad[0].astype(bf16)
    all_packed[here, 3 * C :] = low
    all_merged[here, :] = merged[0]
    small[4:5, :] += column_sum(low.astype(f32))
    moved = mm(perm[...], low).astype(bf16)
    framed[...] = mm(moved, weight[:, 3 * C :], NT).astype(bf16)
    lane_head = lane_heads()
    at = [128 * g for g in range(4)]

    def window(w):
        rows = slice(CELL * w, CELL * w + CELL)
        keys = [qkv[0, rows, C + c : C + c + 128] for c in at]
        query = [quad_rows(qkv[0, rows, c : c + 128], heads[...]) for c in at]
        pull = [quad_rows(framed[rows, c : c + 128], heads[...]) for c in at]
        scores = [mm(keys[g], query[g], NT) for g in range(4)]
        grad_probs = [
            mm(qkv[0, rows, 2 * C + at[g] : 2 * C + at[g] + 128], pull[g], NT) for g in range(4)
        ]
        return keys, query, pull, scores, grad_probs

    ahead = window(0)
    for w in range(4):
        rows = slice(CELL * w, CELL * w + CELL)
        keys, query, pull, scores, grad_probs = ahead
        if w < 3:
            ahead = window(w + 1)
        probs, grad_scores = [], []
        for g in range(4):
            shifted = scores[g] * scale + table[w % table.shape[0], g]
            prob = jnp.exp(shifted - totals[0, 4 * w + g : 4 * w + g + 1, :])
            mean = jnp.sum(prob * grad_probs[g], 0, keepdims=True)
            grad_score = (prob * (grad_probs[g] - mean)).astype(bf16)
            pairs[g] += grad_score.astype(f32)
            probs.append(prob.astype(bf16))
            grad_scores.append(grad_score)
        for g in range(4):
            grad_value = mm(probs[g], pull[g])
            grad_framed[rows, 2 * C + at[g] : 2 * C + at[g] + 128] = grad_value.astype(bf16)
        for g in range(4):
            grad_key = mm(grad_scores[g], query[g]) * scale
            grad_framed[rows, C + at[g] : C + at[g] + 128] = grad_key.astype(bf16)
        for g in range(4):
            grad_query = pick_heads(mm(grad_scores[g], keys[g], TN), lane_head) * scale
            grad_framed[rows, at[g] : at[g] + 128] = grad_query.astype(bf16)
    for c in range(6):
        cols = slice(256 * c, 256 * c + 256)
        part = mm(perm_back[...], grad_framed[:, cols])
        all_packed[here, cols] = part.astype(bf16)
        if c < 2:
            small[2:3, cols] += column_sum(part)
        if c >= 4:
            small[3:4, 256 * (c - 4) : 256 * (c - 4) + 256] += column_sum(part)
    back = mm(all_packed[here, : 3 * C], weight[:, : 3 * C], NT)
    small[0:1, :] += column_sum(back * unit)
    small[1:2, :] += column_sum(back)
    total = grad[0] + norm_back(back * vec[0:1, :], unit, spread_one)
    result[0] = total[: result.shape[1]]

    @pl.when(i == pl.num_programs(0) - 1)
    def _():
        across[0] = all_normed[...].T
        across[1] = all_merged[...].T
        beside[...] = jnp.zeros_like(beside)
        if ends:
            hits[...] = jnp.zeros_like(hits)

            def step(r, carry):
                same = rel[...] == r
                for g in range(4):
                    kept_pairs = jnp.where(same, pairs[g], 0.0)
                    hits[pl.ds(r, 1), 256 * g : 256 * g + 256] = column_sum(kept_pairs)
                return carry

            lax.fori_loop(0, NREL, step, 0)
            for z in range(4):
                beside[0, z] = lax.dot_general(
                    spread[...],
                    hits[:, 256 * z : 256 * z + 256],
                    NT,
                    precision=lax.Precision.HIGHEST,
                    preferred_element_type=f32,
                ).astype(bf16)
                beside[1, z, :, 0:128] = small[:, 128 * z : 128 * z + 128].astype(bf16)
        for m in range(8):
            b = m if layer else place[0] ^ m
            left = across[jnp.where(b < 6, 0, 1)]
            right = all_packed[:, pl.ds(pl.multiple_of(b * BLOCK, BLOCK), BLOCK)]
            block = mm(left, right)
            for z in range(4):
                if layer:
                    out = outs[0].at[m, z, 0]
                else:
                    to = (z + 4 - place[1]) & 3
                    out = outs[m % 2].at[m // 2, to, 0]
                new = block[128 * z : 128 * z + 128]
                if resumed:
                    old = other_before if m % 2 else own_before
                    new = new + old[m // 2, to, 0, 0:128, :].astype(f32)
                out[0:128, :] = new.astype(bf16)
                out[128:144, :] = beside[jnp.minimum(b, 2), z]


def attention_backward(
    layer, place, grad, x, qkv, merged, totals, table, weight, vec, small, perm, rel, after,
    first=0, count=None, resume=None,
):
    images = grad.shape[0]
    count = count or images
    pieces = (8 if layer else 4, 4, 1, 128 + SMALL, BLOCK)
    pairs = (4, CELL, QUAD * CELL)
    total = count * ROWS
    out_rows = TOKENS if layer == 0 else ROWS

    def image(rows, cols):
        return pl.BlockSpec((1, rows, cols), lambda i, *_: (i + first, 0, 0))

    resumed = list(resume or [])
    return call(
        partial(
            attention_backward_body, layer, len(weight), len(after), bool(resumed),
            first + count == images,
        ),
        f"attention_backward_{layer}_{first}",
        (count,),
        [HBM] * (len(weight) + len(after))
        + ([HBM, whole(pieces), whole(pieces), whole(pairs)] if resumed else [])
        + [
            image(ROWS, C),
            image(x.shape[1], C),
            image(FRAME, 3 * C),
            image(ROWS, C),
            image(16, QUAD * CELL),
            whole(table.shape),
            whole(vec.shape),
            whole((16, C)),
            whole((FRAME, ROWS)),
            whole((ROWS, FRAME)),
            whole((QUAD * CELL, 128)),
            whole(rel.shape),
            whole((SMALL, QUAD * CELL)),
        ],
        [image(out_rows, C)]
        + [whole(pieces)] * (1 if layer else 2)
        + [whole(pairs), whole((16, C))],
        [shape((images, out_rows, C), f32)]
        + [shape(pieces, bf16)] * (1 if layer else 2)
        + [shape(pairs, f32), shape((16, C), f32)],
        [
            pltpu.VMEM((FRAME, C), bf16),
            pltpu.VMEM((FRAME, 3 * C), bf16),
            pltpu.VMEM((total, C), bf16),
            pltpu.VMEM((total, 4 * C), bf16),
            pltpu.VMEM((total, C), bf16),
            pltpu.VMEM((2, C, total), bf16),
            pltpu.VMEM((256, 4 * QUAD * CELL), f32),
            pltpu.VMEM((3, 4, SMALL, BLOCK), bf16),
            pltpu.VMEM((1, C, HID), bf16),
            pltpu.SemaphoreType.DMA((8, 4, 1)),
        ],
        6 * count,
        prefetch=1,
        aliases={1 + len(weight) + len(after): 0} if resumed else None,
    )(
        place,
        *weight,
        *after,
        *resumed,
        grad,
        x,
        qkv,
        merged,
        totals,
        table,
        vec,
        small,
        jnp.asarray(perm, bf16),
        jnp.asarray(perm.T, bf16),
        jnp.asarray(head_rows(), bf16),
        rel,
        jnp.asarray(head_spread(SMALL), f32),
    )


def adam_step(weight, first, second, gradient, rate, decay):
    first_new = beta_one * first + (1.0 - beta_one) * gradient
    second_new = beta_two * second + (1.0 - beta_two) * gradient * gradient
    first_hat = first_new / (1.0 - beta_one**STEP)
    second_hat = second_new / (1.0 - beta_two**STEP)
    weight_new = weight - rate * (first_hat / (jnp.sqrt(second_hat) + adam_eps) + decay * weight)
    return (weight_new, first_new, second_new)


def adam_block(grad, weight, first, second, outs, cols):
    part = grad.astype(f32)
    first_new = beta_one * first[0, :, cols] + (1.0 - beta_one) * part
    second_new = beta_two * second[0, :, cols] + (1.0 - beta_two) * part * part
    spread = second_new * (1.0 / (1.0 - beta_two**STEP))
    inverse = pltpu.reciprocal(spread * lax.rsqrt(spread) + adam_eps, approx=True)
    step = first_new * (rate_matrix / (1.0 - beta_one**STEP)) * inverse
    outs[0][0, :, cols] = weight[0, :, cols] * (1.0 - rate_matrix * weight_decay) - step
    outs[1][0, :, cols] = first_new
    outs[2][0, :, cols] = second_new


def adam_body(place, near, far, weight, first, second, *refs):
    for j in range(2):
        for k in range(2):
            block = (((place[0] // 2) & 1) ^ j) * 2 + ((place[0] & 1) ^ k)
            cols = pl.ds(pl.multiple_of(block * BLOCK, BLOCK), BLOCK)
            adam_block((far if k else near)[j], weight, first, second, refs[-3:], cols)


def adam_body_plain(place, sums, weight, first, second, *refs):
    for k in range(4):
        cols = slice(BLOCK * k, BLOCK * k + BLOCK)
        adam_block(sums[k], weight, first, second, refs[-3:], cols)


def adam(layer, part, place, sums, state, done, after):
    kept = [] if done is None else list(done)
    if len(sums) == 2:
        parts = sums[0].shape[1] // 128
        body = adam_body
        spec = pl.BlockSpec(
            (1, 128, 4 * BLOCK),
            lambda p, j, place: (layer, 0, (part + p) % 3 * 2 + ((place[0] // 4) ^ j)),
        )
        piece = pl.BlockSpec((2, 128, BLOCK), lambda p, j, place: (j, p, 0))
    else:
        parts = sums[0].shape[1] // 128
        body = adam_body_plain
        spec = pl.BlockSpec(
            (1, 128, 4 * BLOCK), lambda p, j, place: (layer, 0, (part + p) % 3 * 2 + j)
        )
        piece = pl.BlockSpec((4, 128, BLOCK), lambda p, j, place: (j, p, 0))
    return call(
        body,
        f"adam_{layer}_{part}",
        (parts, 2),
        [piece] * len(sums) + [spec] * 3 + [HBM] * (len(kept) + len(after)),
        [spec] * 3,
        [shape(state[0].shape, f32)] * 3,
        [],
        3 * parts,
        prefetch=1,
        aliases={4 + len(sums) + k: k for k in range(len(kept))},
    )(place, *sums, *state, *kept, *after)


def swap(value, bits):
    return lax.ppermute(value, "dp", [(i, i ^ bits) for i in range(8)])


def shift(value, steps):
    return lax.ppermute(value, "zero", [(i, (i + steps) % 4) for i in range(4)])


def tie(values, after):
    values = list(values)
    return list(lax.optimization_barrier((*values, *after))[: len(values)])


def stack(values, after=()):
    return jnp.stack(tie(values, after) if after else values)


def add_body(count, *refs):
    total = refs[0][...].astype(f32)
    for k in range(1, count):
        total = total + refs[k][...].astype(f32)
    refs[-1][...] = total.astype(bf16)


def add(values, after=()):
    dims = values[0].shape
    return call(
        partial(add_body, len(values)),
        "add",
        (1,),
        [whole(dims)] * len(values) + [HBM] * len(after),
        whole(dims),
        shape(dims, bf16),
        [],
        10,
        mib=24,
    )(*values, *after)


def add_split_body(count, lead, *refs):
    for k in range(4):
        if count == 2:
            refs[len(refs) - 4 + k][...] = refs[0][k] + refs[1][k]
            continue
        total = refs[0][k].astype(f32)
        for v in range(1, count):
            total = total + refs[v][k].astype(f32)
        refs[len(refs) - 4 + k][...] = total.astype(bf16)


def add_split(values, after=()):
    dims = values[0].shape
    steps = 1
    ins = (4, dims[1] // steps, *dims[2:])
    outs = dims[1:]
    zeros = (0,) * (len(dims) - 2)
    return call(
        partial(add_split_body, len(values), True),
        "add_split",
        (steps,),
        [pl.BlockSpec(ins, lambda i: (0, i, *zeros))] * len(values) + [HBM] * len(after),
        [pl.BlockSpec((outs[0] // steps, *outs[1:]), lambda i: (i, *zeros))] * 4,
        [shape(outs, bf16)] * 4,
        [],
        10,
        mib=24,
    )(*values, *after)


def join_body(*refs):
    out = refs[-1]
    at = 0
    for group in (refs[:1], refs[1:2], refs[2:6]):
        parts, rows = group[0].shape[1:3]
        for p in range(parts):
            total = group[0][:, p]
            if len(group) > 1:
                total = total.astype(f32)
                for ref in group[1:]:
                    total = total + ref[:, p].astype(f32)
            out[:, at : at + rows, :] = total.astype(bf16)
            at += rows


def join(first, second, summed, after):
    rows = sum(value.shape[1] * value.shape[2] for value in (first, second, summed[0]))
    ins = [first, second, *summed]
    return call(
        join_body,
        "join",
        (1,),
        [whole(v.shape) for v in ins] + [HBM] * len(after),
        whole((4, rows, BLOCK)),
        shape((4, rows, BLOCK), bf16),
        [],
        5,
    )(*ins, *after)


def add_last_body(*refs):
    done, out = refs[0], refs[-1]
    rows = 256
    out[0:rows, :] = done[done.shape[0] - rows :, :]
    total = refs[1][0].astype(f32)
    for ref in refs[2:5]:
        total = total + ref[0].astype(f32)
    out[rows : rows + total.shape[0], :] = total.astype(bf16)


def add_last(done, values, after):
    rows = 256 + values[0].shape[1]
    return call(
        add_last_body,
        "add_last",
        (1,),
        [whole(done.shape)] + [whole(v.shape) for v in values] + [HBM] * len(after),
        whole((rows, BLOCK)),
        shape((rows, BLOCK), bf16),
        [],
        10,
        mib=24,
    )(done, *values, *after)


def send_z(piece):
    return [piece] + [shift(piece, s) for s in range(1, 4)]


def send_plane(piece):
    return [piece] + [swap(piece, 2 * j) for j in range(1, 4)]


def give_plane(parts):
    return [parts[0]] + [swap(parts[j], 2 * j) for j in range(1, 4)]


def give_z(parts):
    return [parts[0]] + [shift(parts[s], s) for s in range(1, 4)]


def gather_wide(piece, dp, extra):
    fine = dp // 8
    parts, rows = piece.shape[0], piece.shape[1] - extra
    out = lax.all_gather(piece, ("dp", "zero"), axis=0, tiled=False)
    out = out.reshape(8, fine, 4, *piece.shape)
    main = out[..., :rows, :].transpose(0, 2, 3, 1, 4, 5).reshape(8, 4, parts, 128, BLOCK)
    return [jnp.concatenate([main, out[:, 0, ..., rows:, :]], 3)]


def reduce_wide(blocks, dp, extra):
    fine = dp // 8
    blocks = blocks.reshape(8, 4, *blocks.shape[-3:])
    parts, rows = blocks.shape[2], 128 // fine
    main = blocks[..., :128, :].reshape(8, 4, parts, fine, rows, BLOCK).transpose(0, 3, 1, 2, 4, 5)
    beside = jnp.broadcast_to(
        blocks[:, None, ..., 128:, :], (8, fine, 4, parts, extra, BLOCK)
    )
    flat = jnp.concatenate([main, beside], 4).reshape(dp * 4, parts, rows + extra, BLOCK)
    mine = lax.psum_scatter(flat, ("dp", "zero"), scatter_dimension=0, tiled=True)
    out = lax.all_gather(mine[0], "dp", axis=0, tiled=False)
    out = out.reshape(8, fine, parts, rows + extra, BLOCK)
    main = out[..., :rows, :].transpose(0, 2, 1, 3, 4).reshape(8, parts, 128, BLOCK)
    out = jnp.concatenate([main, out[:, 0, :, rows:]], 2)
    return out.reshape(8, -1, BLOCK)


def shards(
    dp, images, cotangent, counts, rel_index, regions,
    mat_w, mat_m, mat_v, vec_w, vec_m, vec_v, tab_w, tab_m, tab_v,
):
    near = dp == 8
    fine = dp // 8
    rows = 128 // fine
    me = lax.axis_index("dp")
    spot = [me, lax.axis_index("zero")] if near else [0 * me, 0 * me]
    place = jnp.stack(spot + [counts[0], me // fine, me % fine]).astype(jnp.int32)

    inside = np.arange(CELL) < WIN * WIN
    zones = regions.reshape(2, WIN, 2, WIN).transpose(0, 2, 1, 3).reshape(4, WIN * WIN)
    zones = jnp.pad(zones, ((0, 0), (0, 15)))
    differ = (zones[:, :, None] != zones[:, None, :]) & inside[None, None, :]
    outside = np.where(inside, 0.0, -1e30).astype(np.float32)[None, :, None]
    mask_shifted = jnp.tile(jnp.where(differ, mask_value, 0.0) + outside, (1, 1, QUAD)).astype(f32)
    mask_plain = jnp.asarray(np.ascontiguousarray(np.broadcast_to(outside, (1, CELL, QUAD * CELL))))
    masks = (mask_plain, mask_shifted)
    perms = (frames(False), frames(True))

    packed, cut_mlp0, cut_all1, rel = pack(
        place, rows, mat_w, rel_index, tab_w, vec_w
    )
    alive = (jnp.arange(images.shape[0]) < counts[0]).astype(f32)[:, None, None]
    pad = ((0, 0), (0, ROWS - TOKENS), (0, 0))
    images = jnp.pad(images.astype(f32), pad)
    cotangent = jnp.pad(cotangent.astype(f32) * alive, pad)

    def attention(layer, stream, weight, after):
        return attention_forward(
            layer, place, stream, weight, heads0, masks[layer], perms[layer], after
        )

    early = max(1, images.shape[0] * 3 // 8)
    if near:
        sent_heads0 = send_z(packed)
        *sent_heads0, images = tie([*sent_heads0, images], [])
        z_heads0 = stack(sent_heads0)
        all1 = gather_wide(tie([cut_all1], [z_heads0])[0], dp, 0)
        sent_heads0 = send_plane(z_heads0)
        sent_mlp0 = send_z(tie([cut_mlp0], [z_heads0])[0])
        cotangent, mask_shifted = tie([cotangent, mask_shifted], [z_heads0])
        *sent_heads0, cotangent, mask_shifted = tie(
            [*sent_heads0, cotangent, mask_shifted], sent_mlp0
        )
        masks = (mask_plain, mask_shifted)
        p_heads0 = stack(sent_heads0)
        heads0 = [p_heads0, swap(p_heads0, 1)]
        z_mlp0 = stack(sent_mlp0, [p_heads0])
        sent_mlp0 = send_plane(z_mlp0)
        kept0 = attention(0, images, heads0, [z_mlp0])
        p_mlp0 = stack(sent_mlp0, [kept0[0]])
        mlp0 = [p_mlp0, swap(p_mlp0, 1)]
    else:
        heads0 = gather_wide(packed, dp, EXTRA)
        mlp0 = gather_wide(cut_mlp0, dp, 0)
        all1 = gather_wide(cut_all1, dp, 0)
        kept0 = attention(0, images, heads0, [])
    stream, act, slope = mlp_forward(0, place, kept0[0], mlp0, kept0[5], [])
    kept1 = attention(1, stream, all1, [])
    kept = (kept0, kept1)
    inputs = (images, stream)
    attention_w = (heads0, all1)

    def backward_attention(layer, gradient, small, after, *span):
        mid, qkv, merged, totals, table, vec = kept[layer]
        return attention_backward(
            layer, place, gradient, inputs[layer], qkv, merged, totals, table, attention_w[layer],
            vec, small, perms[layer], rel, after, *span,
        )

    activations, grad_mid, parts_mlp1, small = mlp_both(
        place, cotangent, kept1[0], all1, kept1[5], []
    )

    def backward_mlp0(gradient, after):
        return mlp_backward(0, place, gradient, act, slope, kept0[0], mlp0, kept0[5], after)

    state = (mat_w, mat_m, mat_v)
    def exchange(parts):
        return [parts[0], swap(parts[1], 1)]

    gradient, parts_heads1, _, _ = backward_attention(1, grad_mid, small, [])
    grad_mid, *parts_mlp0, small = backward_mlp0(gradient, [])
    if near:
        t_mlp1 = lax.psum_scatter(parts_mlp1, "dp", scatter_dimension=0, tiled=True)[0]
        parts_heads1 = tie([parts_heads1], [t_mlp1, small])[0]
        t_heads1 = lax.psum_scatter(parts_heads1, "dp", scatter_dimension=0, tiled=True)[0]
        gone_mlp0 = exchange(parts_mlp0)
        gradient, *parts_heads0, pairs, small = backward_attention(0, grad_mid, small, [], 0, early)

        s_mlp0 = add_split(gone_mlp0, [gradient])
        gone_mlp0 = give_plane(s_mlp0)
        gradient, *parts_heads0, _, small = backward_attention(
            0, grad_mid, small, [s_mlp0[0]], early, images.shape[0] - early,
            [gradient, *parts_heads0, pairs]
        )

        t_all = join(t_mlp1, t_heads1, gone_mlp0, [small])
        gone_heads0 = exchange(tie(parts_heads0, gone_mlp0))
        g_all = lax.psum_scatter(t_all, "zero", scatter_dimension=0, tiled=True)[0]
        s_heads0 = add_split(gone_heads0, [t_all])
        gone_heads0 = give_plane(s_heads0)
        across = tie([activations.transpose(1, 0, 2), gradient.transpose(1, 0, 2)], [])
        t_heads0 = add_split(gone_heads0, across)
        activations, gradient = [value.transpose(1, 0, 2) for value in across]
        gone_heads0 = give_z(t_heads0)
        g_all, *gone_heads0 = tie([g_all, *gone_heads0], [])
        g_all0 = add_last(g_all, gone_heads0, [])
        g_all = tie([g_all], [g_all0])[0]
        n_all1 = lax.all_gather(g_all[:400], "dp", axis=0, tiled=False)
        n_all0 = stack(send_plane(g_all0))
        sums0 = [n_all0, swap(n_all0, 1)]
        m = place[0] ^ np.arange(2)
        both = jnp.concatenate([half[:, 384:] for half in sums0])
        beside0 = [
            lax.dynamic_index_in_dim(both, (m[b] % 2) * 4 + m[b] // 2, 0, False) for b in range(2)
        ]
    else:
        gradient, *parts_heads0, _, _ = backward_attention(0, grad_mid, small, [])
        n_mlp1 = reduce_wide(parts_mlp1, dp, 0)
        n_heads1 = reduce_wide(parts_heads1, dp, SMALL)
        n_all1 = jnp.concatenate([n_mlp1, n_heads1], 1)
        n_mlp0 = reduce_wide(jnp.stack(parts_mlp0, 1), dp, 0)
        n_heads0 = reduce_wide(jnp.stack(parts_heads0, 1), dp, SMALL)
        sums0 = [jnp.concatenate([n_mlp0, n_heads0], 1)]
        beside0 = sums0[0][:2, 384:]
    done = adam(0, 1, place, sums0, state, None, [])
    done = adam(1, 1, place, [n_all1], state, done, [])

    def beside(block):
        return jnp.stack([beside0[block], n_all1[block, 384:]]).astype(f32)

    turned = [v.transpose(1, 0, 2) for v in (vec_w, vec_m, vec_v, beside(1)[:, 0:12, 0:128])]
    new_vec = tie(adam_step(*turned, rate_vector, 0.0), [])
    new_vec = [v.transpose(1, 0, 2) for v in new_vec]
    new_tab = adam_step(tab_w, tab_m, tab_v, beside(0)[:, 0:4, 0:NREL], rate_table, 0.0)
    return (activations, gradient, *done, *new_vec, *new_tab)


def solution(mesh):
    images = P(("dp", "zero"), None, None)
    rows = P(None, "zero", None)
    lanes = P(None, None, "zero")
    return jax.shard_map(
        partial(shards, mesh.shape["dp"]),
        mesh=mesh,
        in_specs=(images, images, P(("dp", "zero")), P(), P())
        + (rows,) * 3 + (lanes,) * 3 + (rows,) * 3,
        out_specs=(images, images) + (rows,) * 3 + (lanes,) * 3 + (rows,) * 3,
        check_vma=False,
    )
```
